32 devices in a mesh: dev: 32 (over z, y, x, core).
Axes of the slice: x: 2, y: 2, z: 4, core: 2. Of those that a mesh axis runs over, the one named last changes fastest.
Arguments:
- tokens: bfloat16 [8192, 1536], P('dev'), may hold values from -6 to 6
- positions: int32 [8192], P('dev'), may hold values from 0 to 1999, as said below
- expert_picks: int32 [8192, 8], P('dev'), may hold values from 0 to 31, all different within a row
- priority: int32 [8192, 8], P('dev'), may hold values from 0 to 2047, as said below
- first_gain: bfloat16 [1536], P('dev'), may hold values from 0.5 to 1.5
- query_weight: bfloat16 [1536, 1536], P('dev'), may hold values from -0.15625 to 0.15625
- key_projection_matrix: bfloat16 [1536, 512], P('dev'), may hold values from -0.15625 to 0.15625
- value_projection_matrix: bfloat16 [1536, 512], P('dev'), may hold values from -0.15625 to 0.15625
- output_weight: bfloat16 [1536, 1536], P('dev'), may hold values from -1.75 to 1.75
- second_gain: bfloat16 [1536], P('dev'), may hold values from 0.5 to 1.5
- router_weight: bfloat16 [1536, 32], P('dev'), may hold values from -0.078125 to 0.078125
- gate_weight: bfloat16 [1536, 16384], P(None, 'dev'), may hold values from -0.15625 to 0.15625
- up_weight: bfloat16 [1536, 16384], P(None, 'dev'), may hold values from -0.15625 to 0.15625
- down_weight: bfloat16 [16384, 1536], P('dev'), may hold values from -1 to 1
- cotangent: bfloat16 [8192, 1536], P('dev'), may hold values from -6 to 6
Outputs:
- layer_output: bfloat16 [8192, 1536], P('dev')
- tokens_gradient: float32 [8192, 1536], P('dev')
- first_gain_gradient: float32 [1536], P('dev')
- query_weight_gradient: float32 [1536, 1536], P('dev')
- key_weight_gradient: float32 [1536, 512], P('dev')
- value_weight_gradient: float32 [1536, 512], P('dev')
- output_weight_gradient: float32 [1536, 1536], P('dev')
- second_gain_gradient: float32 [1536], P('dev')
- router_weight_gradient: float32 [1536, 32], P('dev')
- gate_weight_gradient: float32 [1536, 16384], P(None, 'dev')
- up_weight_gradient: float32 [1536, 16384], P(None, 'dev')
- down_weight_gradient: float32 [16384, 1536], P('dev')
The draws below stay inside these ranges and needn't reach their ends.
Inputs may be any that keep to these rules, and one draw needn't show every extreme that they name: `positions`: each token's position counts the tokens before it in its document. Documents are runs of tokens inside aligned blocks of 8192 tokens and hold 200 to 2000 tokens, except that the last one of a block may be shorter; each block holds one document of exactly 2000 tokens. `expert_picks`: each row names 8 different experts. `priority`: within each aligned block of 256 rows the 2048 entries are all different.
All inputs are finite; a program needn't handle non-finite values.
Results may differ from the reference program's by a relative error of at most 0.015.
Values may be sent and summed in bfloat16 or wider, within the bound.
A program may use at most 512 MiB of HBM per device.

```python
import jax
import jax.numpy as jnp
from jax import lax

MODEL_DIM = 1536
QUERY_HEADS = 24
KEY_HEADS = 8
HEAD_DIM = 64
FF = 512
TOP = 8
EXPERTS = 32
TOK_DEV = 256
MINDOC = 200
MAXDOC = 2000
TOKENS = 8192
SEQLEN = 8192
CAP = 72


def draw_positions(key, part):
    sequences = TOKENS // SEQLEN
    doc_slots = SEQLEN // MINDOC + 1
    key_lengths = jax.random.fold_in(key, 11)
    key_forced = jax.random.fold_in(key, 23)
    lengths = jax.random.randint(key_lengths, (sequences, doc_slots), MINDOC, MAXDOC + 1, dtype=jnp.int32)
    forced = jax.random.randint(key_forced, (sequences, 1), 0, 3, dtype=jnp.int32)
    lengths = jnp.where(jnp.arange(doc_slots, dtype=jnp.int32)[None, :] == forced, MAXDOC, lengths)
    doc_starts = jnp.cumsum(lengths, axis=1, dtype=jnp.int32) - lengths
    offsets = jnp.arange(SEQLEN, dtype=jnp.int32)
    doc_index = jnp.sum((doc_starts[:, None, :] <= offsets[None, :, None]).astype(jnp.int32), axis=2, dtype=jnp.int32) - 1
    doc_start = jnp.take_along_axis(doc_starts, doc_index, axis=1)
    return (offsets[None, :] - doc_start).reshape(TOKENS).astype(jnp.int32)


def draw_priority(key, part):
    blocks = TOKENS // TOK_DEV
    pick_count = TOK_DEV * TOP
    block_keys = jax.random.split(jax.random.fold_in(key, 37), blocks)

    def one_block(block_key):
        return jax.random.permutation(block_key, pick_count).astype(jnp.int32)
    orders = jax.vmap(one_block)(block_keys)
    return orders.reshape(TOKENS, TOP).astype(jnp.int32)


def level_of(stream_key, dims, shards, smallest, top_value):
    gain, own = 1.0, jax.random.fold_in(stream_key, 6)
    for position, blocks in shards:
        draws = jnp.exp(jax.random.uniform(jax.random.fold_in(own, position), (blocks,), jnp.float32, smallest / len(shards), top_value / len(shards)))
        gain = gain * jnp.repeat(draws, dims[position] // blocks).reshape([-1 if axis == position else 1 for axis in range(len(dims))])
    return gain


def picks_of(stream_key, rows, amount, top, lift):
    order = jax.random.permutation(jax.random.fold_in(stream_key, 1), amount)
    boost = order
    for power in range(3):
        boost = boost * boost // amount
    boost = boost * lift // amount
    tickets = jax.random.randint(jax.random.fold_in(stream_key, 2), (rows, amount), 0, 4096) + boost
    holders = jax.random.permutation(jax.random.fold_in(stream_key, 3), rows)[jnp.arange(amount) % rows]
    tickets = jnp.where(jnp.arange(rows)[:, None] == holders[None, :], 1 << 14, tickets)
    merit = tickets * amount + jnp.arange(amount)
    return lax.top_k(merit.astype(jnp.int32), top)[1].astype(jnp.int32)


def normal_values(key, shape, deviation, most, cuts=(), kind=jnp.bfloat16):
    gain = level_of(key, shape, cuts, -0.22, 0.18) if cuts else 1.0
    entries = jax.random.normal(key, shape, jnp.float32) * deviation * gain
    return jnp.minimum(jnp.maximum(entries, -most), most).astype(kind)


def setup_inputs(seed: int = 0) -> dict:
    key_of = jax.random.split(jax.random.key(seed), 16)
    tokens = normal_values(key_of[0], (TOKENS, MODEL_DIM), 1.0, 6.0, ((0, 32),))
    positions = draw_positions(jax.random.fold_in(key_of[15], 71), 0)
    expert_picks = picks_of(key_of[2], TOKENS, EXPERTS, TOP, 2048)
    priority = draw_priority(jax.random.fold_in(key_of[15], 71), 0)
    first_gain = jnp.clip(1.0 + 0.1 * jax.random.normal(key_of[4], (MODEL_DIM,), jnp.float32), 0.5, 1.5).astype(jnp.bfloat16)
    query_weight = normal_values(key_of[5], (MODEL_DIM, QUERY_HEADS * HEAD_DIM), MODEL_DIM ** -0.5, 0.15625, ((0, 32),))
    key_projection_matrix = normal_values(key_of[6], (MODEL_DIM, KEY_HEADS * HEAD_DIM), MODEL_DIM ** -0.5, 0.15625, ((0, 32),))
    value_projection_matrix = normal_values(key_of[7], (MODEL_DIM, KEY_HEADS * HEAD_DIM), MODEL_DIM ** -0.5, 0.15625, ((0, 32),))
    output_weight = normal_values(key_of[8], (QUERY_HEADS * HEAD_DIM, MODEL_DIM), (QUERY_HEADS * HEAD_DIM // 128) ** -0.5, 1.75, ((0, 32),))
    second_gain = jnp.clip(1.0 + 0.1 * jax.random.normal(key_of[9], (MODEL_DIM,), jnp.float32), 0.5, 1.5).astype(jnp.bfloat16)
    router_weight = normal_values(key_of[10], (MODEL_DIM, EXPERTS), (4 * MODEL_DIM) ** -0.5, 0.078125, ((0, 32),))
    gate_weight = normal_values(key_of[11], (MODEL_DIM, EXPERTS * FF), MODEL_DIM ** -0.5, 0.15625, ((1, 32),))
    up_weight = normal_values(key_of[12], (MODEL_DIM, EXPERTS * FF), MODEL_DIM ** -0.5, 0.15625, ((1, 32),))
    down_weight = normal_values(key_of[13], (EXPERTS * FF, MODEL_DIM), (FF // 16) ** -0.5, 1.0, ((0, 32),))
    cotangent = normal_values(key_of[14], (TOKENS, MODEL_DIM), 1.0, 6.0, ((0, 32),))
    return {"tokens": tokens, "positions": positions, "expert_picks": expert_picks, "priority": priority, "first_gain": first_gain, "query_weight": query_weight, "key_projection_matrix": key_projection_matrix, "value_projection_matrix": value_projection_matrix, "output_weight": output_weight, "second_gain": second_gain, "router_weight": router_weight, "gate_weight": gate_weight, "up_weight": up_weight, "down_weight": down_weight, "cotangent": cotangent}


epsilon = 1e-06
masked_score = -1e+30

@jax.custom_vjp
def low(v):
    return lax.optimization_barrier(v.astype(jnp.bfloat16)).astype(jnp.float32)

@jax.custom_vjp
def low_back(v):
    return v

def low_keep(v):
    return (low(v), None)

def low_pass(kept, grad):
    return (grad,)

def back_keep(v):
    return (v, None)

def back_low(kept, grad):
    return (low(grad),)
low.defvjp(low_keep, low_pass)
low_back.defvjp(back_keep, back_low)

def matmul(first_operand, second_operand):
    return jnp.dot(first_operand, second_operand, precision=lax.Precision.HIGHEST, preferred_element_type=jnp.float32)

def rms_scale(values):
    return lax.rsqrt(lax.optimization_barrier(jnp.mean(values * values, axis=-1, keepdims=True)) + epsilon)

def rotary_tables(positions, head_size):
    half_dim = head_size // 2
    frequency = jnp.power(10000.0, -(jnp.arange(half_dim, dtype=jnp.float32) * 2.0) / head_size)
    angle = positions.astype(jnp.float32)[:, None] * frequency[None, :]
    return (jnp.cos(angle), jnp.sin(angle))

def rotate(values, cosine, sine_part):
    half_dim = cosine.shape[1]
    shaped = values.reshape(values.shape[0], -1, 2 * half_dim)
    leading = shaped[..., :half_dim]
    trailing = shaped[..., half_dim:]
    cosine_rows = cosine[:, None, :]
    sine_rows = sine_part[:, None, :]
    turned = jnp.concatenate([leading * cosine_rows - trailing * sine_rows, trailing * cosine_rows + leading * sine_rows], axis=-1)
    return turned.reshape(values.shape)

def route_slots(expert_picks, priority, experts, capacity):
    flat_picks = expert_picks.reshape(-1).astype(jnp.int32)
    flat_priority = priority.reshape(-1).astype(jnp.int32)
    pick_count = flat_picks.shape[0]
    by_priority = jnp.zeros((pick_count,), jnp.int32).at[flat_priority].set(jnp.arange(pick_count, dtype=jnp.int32))
    ordered = flat_picks[by_priority]
    matches = (ordered[:, None] == jnp.arange(experts, dtype=jnp.int32)[None, :]).astype(jnp.int32)
    running = jnp.cumsum(matches, axis=0, dtype=jnp.int32)
    ordered_rank = lax.optimization_barrier(jnp.sum(running * matches, axis=1, dtype=jnp.int32)) - 1
    pick_rank = ordered_rank[flat_priority]
    return jnp.where(pick_rank < capacity, flat_picks * capacity + pick_rank, experts * capacity).astype(jnp.int32)

def slot_sources(slot_row):
    holder = jnp.full((EXPERTS * CAP + 1,), TOK_DEV, jnp.int32)
    holder = holder.at[slot_row].set(jnp.arange(TOK_DEV * TOP, dtype=jnp.int32) // TOP)
    return holder[:EXPERTS * CAP]

def attention(query_input_rows, key_in, value_in, positions):
    rows_per_block = min(512, TOKENS)
    padding_extent = MAXDOC
    query_group_width = QUERY_HEADS // KEY_HEADS
    score_scale = HEAD_DIM ** (-0.5)
    key_with_padding = jnp.pad(key_in, ((padding_extent, 0), (0, 0)))
    value_with_padding = jnp.pad(value_in, ((padding_extent, 0), (0, 0)))

    def one_block(block_first_row):
        query_tile_rows = lax.dynamic_slice_in_dim(query_input_rows, block_first_row, rows_per_block, 0).reshape(rows_per_block, KEY_HEADS, query_group_width, HEAD_DIM)
        key_tile_rows = lax.dynamic_slice_in_dim(key_with_padding, block_first_row, rows_per_block + padding_extent, 0).reshape(rows_per_block + padding_extent, KEY_HEADS, HEAD_DIM)
        value_tile_rows = lax.dynamic_slice_in_dim(value_with_padding, block_first_row, rows_per_block + padding_extent, 0).reshape(rows_per_block + padding_extent, KEY_HEADS, HEAD_DIM)
        places = lax.dynamic_slice_in_dim(positions, block_first_row, rows_per_block, 0).astype(jnp.int32)
        query_index = block_first_row + jnp.arange(rows_per_block, dtype=jnp.int32)
        key_index = block_first_row - padding_extent + jnp.arange(rows_per_block + padding_extent, dtype=jnp.int32)
        allowed = (key_index[None, :] <= query_index[:, None]) & (key_index[None, :] >= (query_index - places)[:, None])
        scores = low_back(jnp.einsum('qhgd,khd->hgqk', query_tile_rows, key_tile_rows, precision=lax.Precision.HIGHEST) * score_scale)
        scores = jnp.where(allowed[None, None], scores, masked_score)
        row_max = lax.optimization_barrier(jnp.max(scores, axis=-1, keepdims=True))
        exponent = jnp.exp(scores - row_max)
        probability = exponent / lax.optimization_barrier(jnp.sum(exponent, axis=-1, keepdims=True))
        mixed_heads = jnp.einsum('hgqk,khd->qhgd', low(probability), value_tile_rows, precision=lax.Precision.HIGHEST)
        return mixed_heads.reshape(rows_per_block, QUERY_HEADS * HEAD_DIM)
    starts = jnp.arange(TOKENS // rows_per_block, dtype=jnp.int32) * rows_per_block
    return lax.map(jax.checkpoint(one_block), starts).reshape(TOKENS, QUERY_HEADS * HEAD_DIM)

def reference(tokens, positions, expert_picks, priority, first_gain, query_weight, key_projection_matrix, value_projection_matrix, output_weight, second_gain, router_weight, gate_weight, up_weight, down_weight, cotangent):
    block_count = TOKENS // TOK_DEV
    pick_blocks = expert_picks.reshape(block_count, TOK_DEV, TOP)
    priority_blocks = priority.reshape(block_count, TOK_DEV, TOP)

    def block_route(pick_block, order_block):
        return route_slots(pick_block, order_block, EXPERTS, CAP)
    slot_index = jax.vmap(block_route)(pick_blocks, priority_blocks)
    sources = jax.vmap(slot_sources)(slot_index)
    cosine, sine_part = rotary_tables(positions, HEAD_DIM)

    def forward(inputs, gain_one, query_matrix, key_matrix, value_matrix, output_matrix, gain_two, router_matrix, gate_matrix, up_matrix, down_matrix):
        normed_one = low(inputs * rms_scale(inputs) * gain_one)
        query_pre = low_back(matmul(normed_one, query_matrix))
        key_pre = low_back(matmul(normed_one, key_matrix))
        value_in = low(low_back(matmul(normed_one, value_matrix)))
        query_input_rows = low(rotate(query_pre, cosine, sine_part))
        key_in = low(rotate(key_pre, cosine, sine_part))
        mixed = attention(query_input_rows, key_in, value_in, positions)
        attended = low(low_back(mixed))
        residual = inputs + low_back(matmul(attended, output_matrix))
        normed_two = low(residual * rms_scale(residual) * gain_two)
        logits = low_back(matmul(normed_two, router_matrix))
        picked = jnp.take_along_axis(logits, expert_picks.astype(jnp.int32), axis=1)
        row_max = lax.optimization_barrier(jnp.max(picked, axis=-1, keepdims=True))
        exponent = jnp.exp(picked - row_max)
        pick_gates = exponent / lax.optimization_barrier(jnp.sum(exponent, axis=-1, keepdims=True))
        gate_stack = gate_matrix.reshape(MODEL_DIM, EXPERTS, FF).transpose(1, 0, 2)
        up_stack = up_matrix.reshape(MODEL_DIM, EXPERTS, FF).transpose(1, 0, 2)
        down_stack = down_matrix.reshape(EXPERTS, FF, MODEL_DIM)

        def expert_block(operands):
            normed_block, gate_block, slot_block, source_block = operands
            rows = jnp.take(normed_block, source_block, axis=0, mode='fill', fill_value=0.0).reshape(EXPERTS, CAP, MODEL_DIM)
            gate_in = low_back(jnp.einsum('ecd,edf->ecf', rows, gate_stack, precision=lax.Precision.HIGHEST))
            up_in = low_back(jnp.einsum('ecd,edf->ecf', rows, up_stack, precision=lax.Precision.HIGHEST))
            hidden = low(gate_in / (1.0 + jnp.exp(-gate_in)) * up_in)
            expert_out = low_back(jnp.einsum('ecf,efd->ecd', hidden, down_stack, precision=lax.Precision.HIGHEST))
            expert_out = expert_out.reshape(EXPERTS * CAP, MODEL_DIM)
            picked_out = jnp.take(expert_out, slot_block, axis=0, mode='fill', fill_value=0.0).reshape(TOK_DEV, TOP, MODEL_DIM)
            return lax.optimization_barrier(jnp.sum(gate_block[..., None] * picked_out, axis=1))
        mixture = lax.map(jax.checkpoint(expert_block), (normed_two.reshape(block_count, TOK_DEV, MODEL_DIM), pick_gates.reshape(block_count, TOK_DEV, TOP), slot_index, sources))
        return residual + mixture.reshape(TOKENS, MODEL_DIM)
    primals = (tokens.astype(jnp.float32), first_gain.astype(jnp.float32), query_weight.astype(jnp.float32), key_projection_matrix.astype(jnp.float32), value_projection_matrix.astype(jnp.float32), output_weight.astype(jnp.float32), second_gain.astype(jnp.float32), router_weight.astype(jnp.float32), gate_weight.astype(jnp.float32), up_weight.astype(jnp.float32), down_weight.astype(jnp.float32))
    final, pullback = jax.vjp(forward, *primals)
    gradients = pullback(cotangent.astype(jnp.float32))
    return (final.astype(jnp.bfloat16), gradients[0], gradients[1], gradients[2], gradients[3], gradients[4], gradients[5], gradients[6], gradients[7], gradients[8], gradients[9], gradients[10])
```

```python
import functools
import jax, jax.numpy as jnp
from jax import lax
from jax.experimental import pallas as pl
from jax.experimental.pallas import tpu as pltpu

MESH = pl.DeviceIdType.MESH


def place():
    me = lax.axis_index("dev")
    return lax.rem(me // 8, 4), lax.rem(me // 4, 2), lax.rem(me // 2, 2), lax.rem(me, 2)


def number(z, y, x, c):
    return ((z * 2 + y) * 2 + x) * 2 + c


def greet(partners):
    barrier = pltpu.get_barrier_semaphore()
    for partner in partners:
        pl.semaphore_signal(barrier, inc=1, device_id=(partner,), device_id_type=MESH)
    pl.semaphore_wait(barrier, len(partners))


def partners_of(z, y, x, c):
    return [
        number(z, y, x, 1 - c),
        number(z, y, 1 - x, c),
        number(z, 1 - y, x, c),
        number(lax.rem(z + 1, 4), y, x, c),
        number(lax.rem(z + 2, 4), y, x, c),
        number(lax.rem(z + 3, 4), y, x, c),
    ]


def gather_kernel(rows, pieces, x_ref, o_ref, local_sem, ss, rs):
    z, y, x, c = place()
    greet(partners_of(z, y, x, c))
    sibling = number(z, y, x, 1 - c)
    me = number(z, y, x, c)
    around = (number(z, 1 - y, x, c), number(z, y, 1 - x, c))

    def part(ref, block, p):
        r0, nr, c0, nc = pieces[p]
        return ref.at[pl.ds(pl.multiple_of(block * rows + r0, 16), nr), pl.ds(c0, nc)]

    def copy(block, p, slot, target, own=False):
        source = part(x_ref, 0, p) if own else part(o_ref, block, p)
        return pltpu.make_async_remote_copy(
            src_ref=source, dst_ref=part(o_ref, block, p),
            send_sem=ss.at[p * 31 + slot], recv_sem=rs.at[p * 31 + slot],
            device_id=(target,), device_id_type=MESH)

    pending = []

    def send(*args, **kw):
        cp = copy(*args, **kw)
        cp.start()
        pending.append(cp)

    def at(k, fy, fx):
        return number(lax.rem(z + 4 - k, 4), (1 - y) if fy else y, (1 - x) if fx else x, c)

    local = pltpu.make_async_copy(x_ref, o_ref.at[pl.ds(pl.multiple_of(me * rows, 16), rows), :], local_sem)
    local.start()
    order = (0, 1, 3, 2)
    far = ((1, 0), (0, 1))
    for k in (1, 3, 2):
        for p in range(2):
            send(me, p, k - 1, number(lax.rem(z + k, 4), y, x, c), own=True)
    for k in order:
        for p in range(2):
            block = at(k, 0, 0)
            if k:
                copy(block, p, k - 1, sibling).wait_recv()
            own = k == 0
            send(block, p, 3 + k, around[p], own=own)
            send(block, p, 7 + k, around[1 - p], own=own)
            send(block, p, 15 + k, sibling, own=own)
    for k in order:
        for p in range(2):
            fy, fx = far[p]
            block = at(k, fy, fx)
            copy(block, p, 3 + k, sibling).wait_recv()
            send(block, p, 11 + k, around[1 - p])
            send(block, p, 19 + k, sibling)
    for j, slot in ((0, 7), (1, 11)):
        for k in order:
            for p in range(2):
                fy, fx = (1, 1) if j else (1 - far[p][0], 1 - far[p][1])
                block = at(k, fy, fx)
                copy(block, p, slot + k, sibling).wait_recv()
                send(block, p, 23 + 4 * j + k, sibling)
    for k in range(4):
        for p in range(2):
            for s in (15, 19, 23, 27):
                copy(me, p, s + k, sibling).wait_recv()
    for cp in pending:
        cp.wait_send()
    local.wait()


def gather_all(block, cid, by_rows):
    rows, cols = block.shape
    if by_rows:
        pieces = ((0, rows // 2, 0, cols), (rows // 2, rows // 2, 0, cols))
    else:
        half = (cols // 256) * 128
        pieces = ((0, rows, 0, half), (0, rows, half, cols - half))
    return pl.pallas_call(
        functools.partial(gather_kernel, rows, pieces),
        out_shape=jax.ShapeDtypeStruct((32 * rows, cols), block.dtype),
        in_specs=[pl.BlockSpec(memory_space=pl.ANY)],
        out_specs=pl.BlockSpec(memory_space=pl.ANY),
        scratch_shapes=[pltpu.SemaphoreType.DMA, pltpu.SemaphoreType.DMA((62,)), pltpu.SemaphoreType.DMA((62,))],
        compiler_params=pltpu.CompilerParams(collective_id=cid, has_side_effects=True),
        name="gather_all",
    )(block)


def reduce_kernel(rows, cols, pieces, g_ref, o_ref, acc, own, ra, rb, rz, own_sem, ssem, rsem, sa, ra_sem, sb, rb_sem, sz, rz_sem):
    z, y, x, c = place()
    greet(partners_of(z, y, x, c))
    sibling = number(z, y, x, 1 - c)
    around = (number(z, y, 1 - x, c), number(z, 1 - y, x, c))
    blocks = [(dy, dx, k) for dy, dx in ((1, 1), (1, 0), (0, 1), (0, 0)) for k in (2, 1, 3, 0)]

    def where(dy, dx, k):
        return lax.rem(z + k, 4), (1 - y) if dy else y, (1 - x) if dx else x

    def lane(dy, dx, k):
        zz, yy, xx = where(dy, dx, k)
        return (zz * 2 + yy) * 2 + xx

    def chip_rows(dy, dx, k, core):
        zz, yy, xx = where(dy, dx, k)
        return g_ref.at[pl.ds(pl.multiple_of(number(zz, yy, xx, core) * rows, 16), rows), :]

    def to_sibling(n):
        dy, dx, k = blocks[n]
        return pltpu.make_async_remote_copy(
            src_ref=chip_rows(dy, dx, k, 1 - c), dst_ref=acc.at[lane(dy, dx, k)],
            send_sem=ssem.at[n], recv_sem=rsem.at[n], device_id=(sibling,), device_id_type=MESH)

    def load(n):
        return pltpu.make_async_copy(chip_rows(*blocks[n], c), own.at[n % 2], own_sem.at[n % 2])

    def part(ref, p):
        r0, nr, c0, nc = pieces[p]
        return ref.at[pl.ds(r0, nr), pl.ds(c0, nc)]

    def first(p, d2, k, dy, dx):
        return pltpu.make_async_remote_copy(
            src_ref=part(acc.at[lane(dy, dx, k)], p), dst_ref=ra.at[p, d2, k],
            send_sem=sa.at[p, d2, k], recv_sem=ra_sem.at[p, d2, k], device_id=(around[p],), device_id_type=MESH)

    def second(p, k):
        dy, dx = (1, 0) if p == 0 else (0, 1)
        return pltpu.make_async_remote_copy(
            src_ref=part(acc.at[lane(dy, dx, k)], p), dst_ref=rb.at[p, k],
            send_sem=sb.at[p, k], recv_sem=rb_sem.at[p, k], device_id=(around[1 - p],), device_id_type=MESH)

    def third(p, k):
        return pltpu.make_async_remote_copy(
            src_ref=part(acc.at[lane(0, 0, k)], p), dst_ref=rz.at[p, k - 1],
            send_sem=sz.at[p, k - 1], recv_sem=rz_sem.at[p, k - 1],
            device_id=(number(lax.rem(z + k, 4), y, x, c),), device_id_type=MESH)

    step = 16

    def add(out, terms, nr):
        def chunk(i, _):
            at = pl.ds(pl.multiple_of(i * step, step), step)
            total = terms[0][at, :].astype(jnp.float32)
            for t in terms[1:]:
                total = total + t[at, :].astype(jnp.float32)
            out[at, :] = total.astype(out.dtype)
            return 0
        lax.fori_loop(0, nr // step, chunk, 0)

    for n in range(16):
        to_sibling(n).start()
    load(0).start()
    for n in range(16):
        dy, dx, k = blocks[n]
        if n + 1 < 16:
            load(n + 1).start()
        load(n).wait()
        to_sibling(n).wait_recv()
        block = acc.at[lane(dy, dx, k)]
        add(block, [block, own.at[n % 2]], rows)
        if dx:
            first(0, dy, k, dy, dx).start()
        if dy:
            first(1, dx, k, dy, dx).start()
    for k in (2, 1, 3, 0):
        for p in range(2):
            dy, dx = (1, 0) if p == 0 else (0, 1)
            first(p, 1, k, 1, 1).wait_recv()
            block = part(acc.at[lane(dy, dx, k)], p)
            add(block, [block, ra.at[p, 1, k]], pieces[p][1])
            second(p, k).start()
    for k in (2, 1, 3, 0):
        for p in range(2):
            first(p, 0, k, 1 - p, p).wait_recv()
            second(p, k).wait_recv()
            block = part(acc.at[lane(0, 0, k)], p)
            if k:
                add(block, [block, ra.at[p, 0, k], rb.at[p, k]], pieces[p][1])
                third(p, k).start()
    for p in range(2):
        for k in range(1, 4):
            third(p, k).wait_recv()
        block = part(acc.at[lane(0, 0, 0)], p)
        add(part(o_ref, p), [block, ra.at[p, 0, 0], rb.at[p, 0]] + [rz.at[p, j] for j in range(3)], pieces[p][1])
    for n in range(16):
        to_sibling(n).wait_send()
    for p in range(2):
        for k in range(4):
            first(p, 0, k, 1 - p, p).wait_send()
            first(p, 1, k, 1, 1).wait_send()
            second(p, k).wait_send()
            if k:
                third(p, k).wait_send()


def reduce_all(dense, cid, by_rows, out_dtype=jnp.float32):
    rows, cols = dense.shape[0] // 32, dense.shape[1]
    if by_rows:
        pieces = ((0, rows // 2, 0, cols), (rows // 2, rows // 2, 0, cols))
    else:
        half = (cols // 256) * 128
        assert cols == 2 * half
        pieces = ((0, rows, 0, half), (0, rows, half, cols - half))
    pr, pc = pieces[0][1], pieces[0][3]
    dma = pltpu.SemaphoreType.DMA
    return pl.pallas_call(
        functools.partial(reduce_kernel, rows, cols, pieces),
        out_shape=jax.ShapeDtypeStruct((rows, cols), out_dtype),
        in_specs=[pl.BlockSpec(memory_space=pl.ANY)],
        out_specs=pl.BlockSpec(memory_space=pltpu.VMEM),
        scratch_shapes=[
            pltpu.VMEM((16, rows, cols), dense.dtype),
            pltpu.VMEM((2, rows, cols), dense.dtype),
            pltpu.VMEM((2, 2, 4, pr, pc), dense.dtype),
            pltpu.VMEM((2, 4, pr, pc), dense.dtype),
            pltpu.VMEM((2, 3, pr, pc), dense.dtype),
            dma((2,)), dma((16,)), dma((16,)), dma((2, 2, 4)), dma((2, 2, 4)), dma((2, 4)), dma((2, 4)), dma((2, 3)), dma((2, 3)),
        ],
        compiler_params=pltpu.CompilerParams(collective_id=cid, has_side_effects=True, vmem_limit_bytes=56 * 2**20),
        name="reduce_all",
    )(dense)


from jax.sharding import PartitionSpec as P

QUERY_HEADS = 24
KEY_HEADS = 8
HEAD_DIM = 64
GROUP = QUERY_HEADS // KEY_HEADS
TOP = 8
EXPERTS = 32
MAXDOC = 2000
EPSILON = 1e-06
MASKED = -1e30
QKV = (QUERY_HEADS + 2 * KEY_HEADS) * HEAD_DIM
F32 = jnp.float32
BF16 = jnp.bfloat16


def meshed():
    return lax.axis_size("dev") == 32


def dims(a, b, ca, cb):
    return lax.dot_general(a, b, (((ca,), (cb,)), ((), ())), preferred_element_type=F32)


def window_kernel(rows, kv_ref, o_ref, lsem, ss, rs):
    z, y, x, c = place()
    p = y * 2 + x
    sibling = number(z, y, x, 1 - c)
    up = number(lax.rem(z + 1, 4), y, x, c)
    down = number(lax.rem(z + 3, 4), y, x, c)

    def chip(q):
        return (z * 4 + q) * 2 + c

    near = [chip(lax.rem(p + d, 4)) for d in (1, 2, 3)]
    greet([sibling, up, down] + near)

    def slot(s, core):
        return o_ref.at[:, pl.ds(pl.multiple_of((2 * s + core) * rows, 16), rows), :]

    def copy(source, s, n, target):
        return pltpu.make_async_remote_copy(
            src_ref=source, dst_ref=slot(s, c), send_sem=ss.at[n], recv_sem=rs.at[n],
            device_id=(target,), device_id_type=MESH)

    own_in = pltpu.make_async_copy(kv_ref, slot(4, c), lsem.at[0])
    own_in.start()
    to_up = copy(kv_ref, 0, 0, up)

    @pl.when(z < 3)
    def _():
        to_up.start()

    stand_in = pltpu.make_async_copy(kv_ref, slot(0, c), lsem.at[1])

    @pl.when(z == 0)
    def _():
        stand_in.start()

    for d in (1, 3, 2):
        @pl.when(p + d < 4)
        def _(d=d):
            copy(kv_ref, 4 - d, d, near[d - 1]).start()

    to_sibling = {4: copy(kv_ref, 4, 4, sibling)}
    to_sibling[4].start()

    @pl.when(z == 0)
    def _():
        stand_in.wait()

    @pl.when(z > 0)
    def _():
        to_up.wait_recv()

    for d in (3, 1, 2):
        @pl.when(p + d >= 4)
        def _(d=d):
            copy(slot(0, c), 4 - d, d, near[d - 1]).start()

    to_sibling[0] = copy(slot(0, c), 0, 5, sibling)
    to_sibling[0].start()
    for d in (1, 3, 2):
        copy(kv_ref, 4 - d, d, near[d - 1]).wait_recv()
        to_sibling[4 - d] = copy(slot(4 - d, c), 4 - d, 5 + d, sibling)
        to_sibling[4 - d].start()
    for s in range(5):
        pltpu.make_async_remote_copy(
            src_ref=kv_ref, dst_ref=slot(s, 1 - c), send_sem=ss.at[0],
            recv_sem=rs.at[{4: 4, 0: 5}.get(s, 9 - s)], device_id=(sibling,), device_id_type=MESH).wait_recv()
    own_in.wait()

    @pl.when(z < 3)
    def _():
        to_up.wait_send()

    for d in (1, 2, 3):
        copy(kv_ref, 4 - d, d, near[d - 1]).wait_send()
    for s in range(5):
        to_sibling[s].wait_send()


def window_of(kv):
    rows, width = kv.shape[1:]
    if meshed():
        dma = pltpu.SemaphoreType.DMA
        full = pl.pallas_call(
            functools.partial(window_kernel, rows),
            out_shape=jax.ShapeDtypeStruct((2, 10 * rows, width), kv.dtype),
            in_specs=[pl.BlockSpec(memory_space=pl.ANY)],
            out_specs=pl.BlockSpec(memory_space=pl.ANY),
            scratch_shapes=[dma((2,)), dma((9,)), dma((9,))],
            compiler_params=pltpu.CompilerParams(collective_id=11, has_side_effects=True),
            name="window",
        )(kv)
        return full, lax.rem(lax.axis_index("dev"), 2)
    devices = lax.axis_size("dev")
    back = (MAXDOC + rows - 2) // rows
    parts = [
        lax.ppermute(kv, "dev", [(i - d, i) for i in range(d, devices)]) for d in range(back, 0, -1)
    ]
    return jnp.concatenate(parts + [kv, jnp.zeros_like(kv)], axis=1), jnp.int32(0)


def unwindow_kernel(rows, g_ref, o_ref, mine, got, near_got, far, lsem, ss, rs):
    z, y, x, c = place()
    p = y * 2 + x
    sibling = number(z, y, x, 1 - c)
    up = number(lax.rem(z + 1, 4), y, x, c)
    down = number(lax.rem(z + 3, 4), y, x, c)

    def chip(q):
        return (z * 4 + q) * 2 + c

    ahead = [chip(lax.rem(p + d, 4)) for d in (1, 2, 3)]
    behind = [chip(lax.rem(p + 4 - d, 4)) for d in (1, 2, 3)]
    greet([sibling, up, down] + ahead)

    def slot(s, core):
        return g_ref.at[:, pl.ds(pl.multiple_of((2 * s + core) * rows, 16), rows), :]

    def to_sibling(s):
        return pltpu.make_async_remote_copy(
            src_ref=slot(s, 1 - c), dst_ref=got.at[s], send_sem=ss.at[s], recv_sem=rs.at[s],
            device_id=(sibling,), device_id_type=MESH)

    def load(s):
        return pltpu.make_async_copy(slot(s, c), mine.at[s], lsem.at[s])

    def to_owner(d):
        return pltpu.make_async_remote_copy(
            src_ref=got.at[4 - d], dst_ref=near_got.at[d - 1], send_sem=ss.at[4 + d], recv_sem=rs.at[4 + d],
            device_id=(behind[d - 1],), device_id_type=MESH)

    to_down = pltpu.make_async_remote_copy(
        src_ref=got.at[0], dst_ref=far, send_sem=ss.at[8], recv_sem=rs.at[8],
        device_id=(down,), device_id_type=MESH)
    order = (3, 1, 2, 0, 4)
    for s in order:
        to_sibling(s).start()
        load(s).start()

    def rowwise(body):
        for h in range(2):
            def step(i, _, h=h):
                body(h, pl.ds(pl.multiple_of(i * 32, 32), 32))
                return 0
            lax.fori_loop(0, rows // 32, step, 0)

    for s in order:
        load(s).wait()
        to_sibling(s).wait_recv()

        def both(h, at, s=s):
            total = got[s, h, at, :].astype(F32) + mine[s, h, at, :].astype(F32)
            if s == 4:
                o_ref[h, at, :] = total
            else:
                got[s, h, at, :] = total.astype(BF16)
        rowwise(both)
        if 0 < s < 4:
            to_owner(4 - s).start()
    for d in (1, 3, 2):
        to_owner(d).wait_recv()

        @pl.when(p + d < 4)
        def _(d=d):
            def body(h, at):
                o_ref[h, at, :] += near_got[d - 1, h, at, :].astype(F32)
            rowwise(body)

        @pl.when(p + d >= 4)
        def _(d=d):
            def body(h, at):
                total = got[0, h, at, :].astype(F32) + near_got[d - 1, h, at, :].astype(F32)
                got[0, h, at, :] = total.astype(BF16)
            rowwise(body)

    @pl.when(z > 0)
    def _():
        to_down.start()

    @pl.when(z < 3)
    def _():
        to_down.wait_recv()

        def body(h, at):
            o_ref[h, at, :] += far[h, at, :].astype(F32)
        rowwise(body)

    @pl.when(z > 0)
    def _():
        to_down.wait_send()

    for s in range(5):
        to_sibling(s).wait_send()
    for d in (1, 2, 3):
        to_owner(d).wait_send()


def unwindow(grads):
    rows, width = grads.shape[1] // 10, grads.shape[2]
    if meshed():
        dma = pltpu.SemaphoreType.DMA
        return pl.pallas_call(
            functools.partial(unwindow_kernel, rows),
            out_shape=jax.ShapeDtypeStruct((2, rows, width), F32),
            in_specs=[pl.BlockSpec(memory_space=pl.ANY)],
            out_specs=pl.BlockSpec(memory_space=pltpu.VMEM),
            scratch_shapes=[
                pltpu.VMEM((5, 2, rows, width), BF16),
                pltpu.VMEM((5, 2, rows, width), BF16),
                pltpu.VMEM((3, 2, rows, width), BF16),
                pltpu.VMEM((2, rows, width), BF16),
                dma((5,)), dma((9,)), dma((9,)),
            ],
            compiler_params=pltpu.CompilerParams(collective_id=12, has_side_effects=True, vmem_limit_bytes=40 * 2**20),
            name="unwindow",
        )(grads)
    devices = lax.axis_size("dev")
    back = (MAXDOC + rows - 2) // rows
    total = grads[:, back * rows : (back + 1) * rows].astype(F32)
    for d in range(1, back + 1):
        piece = grads[:, (back - d) * rows : (back - d + 1) * rows]
        moved = lax.ppermute(piece, "dev", [(i, i - d) for i in range(d, devices)])
        total = total + moved.astype(F32)
    return total


def make_bias(bias, lo_ref, chunks, rows):
    def fill(ch, _):
        at = pl.ds(pl.multiple_of(ch * rows, rows), rows)
        relative = lax.broadcasted_iota(jnp.int32, (rows, rows), 0) + (ch - (chunks - 1)) * rows
        query = lax.broadcasted_iota(jnp.int32, (rows, rows), 1)
        allowed = (relative <= query) & (relative >= lo_ref[...])
        bias[at, :] = jnp.where(allowed, 0.0, MASKED)
        return 0
    lax.fori_loop(0, chunks, fill, 0)


def attend_kernel(chunks, rows, off_ref, lo_ref, q_ref, kv_ref, o_ref, lse_ref, bias):
    @pl.when(pl.program_id(0) == 0)
    def _():
        make_bias(bias, lo_ref, chunks, rows)

    off = off_ref[0]
    lse_ref[...] = jnp.zeros_like(lse_ref)
    for half in range(2):
        lanes = slice(half * HEAD_DIM, (half + 1) * HEAD_DIM)
        queries = [q_ref[(half * GROUP + g) * HEAD_DIM : (half * GROUP + g + 1) * HEAD_DIM, :] for g in range(GROUP)]

        def chunk(i, carry, lanes=lanes, queries=queries):
            ch = chunks - 1 - i
            at = pl.ds(pl.multiple_of((ch + off) * rows, rows), rows)
            key, value = kv_ref[0, at, lanes], kv_ref[1, at, lanes]
            shift = bias[pl.ds(pl.multiple_of(ch * rows, rows), rows), :]
            out = []
            for g in range(GROUP):
                top, total, mixed = carry[g]
                score = dims(key, queries[g], 1, 0) + shift
                new_top = jnp.maximum(top, jnp.max(score, axis=0, keepdims=True))
                weight = jnp.exp(score - new_top)
                fade = jnp.exp(top - new_top)
                total = total * fade + jnp.sum(weight, axis=0, keepdims=True)
                mixed = mixed * fade + dims(value, weight.astype(BF16), 0, 0)
                out.append((new_top, total, mixed))
            return tuple(out)

        start = tuple(
            (jnp.full((1, rows), MASKED, F32), jnp.zeros((1, rows), F32), jnp.zeros((HEAD_DIM, rows), F32))
            for _ in range(GROUP)
        )
        done = lax.fori_loop(0, chunks, chunk, start)
        for g in range(GROUP):
            top, total, mixed = done[g]
            n = half * GROUP + g
            o_ref[n * HEAD_DIM : (n + 1) * HEAD_DIM, :] = (mixed / total).astype(BF16)
            lse_ref[0, n : n + 1, :] = top + jnp.log(total)


def attend_back_kernel(
    chunks, rows, off_ref, lo_ref, cos_ref, sin_ref, q_ref, kv_ref, g_ref, lse_ref, delta_ref, dq_ref, dkv_ref, bias
):
    @pl.when(pl.program_id(0) == 0)
    def _():
        make_bias(bias, lo_ref, chunks, rows)

    off = off_ref[0]
    unused = pl.ds(pl.multiple_of((1 - off) * chunks * rows, rows), rows)
    dkv_ref[:, unused, :] = jnp.zeros((2, rows, 2 * HEAD_DIM), BF16)
    cosine, sine = cos_ref[...], sin_ref[...]
    for half in range(2):
        lanes = slice(half * HEAD_DIM, (half + 1) * HEAD_DIM)
        own = [slice((half * GROUP + g) * HEAD_DIM, (half * GROUP + g + 1) * HEAD_DIM) for g in range(GROUP)]
        queries = [q_ref[s, :] for s in own]
        grads = [g_ref[s, :] for s in own]
        lses = [lse_ref[0, half * GROUP + g : half * GROUP + g + 1, :] for g in range(GROUP)]
        deltas = [delta_ref[0, half * GROUP + g : half * GROUP + g + 1, :] for g in range(GROUP)]

        def chunk(ch, carry, lanes=lanes, queries=queries, grads=grads, lses=lses, deltas=deltas):
            at = pl.ds(pl.multiple_of((ch + off) * rows, rows), rows)
            key, value = kv_ref[0, at, lanes], kv_ref[1, at, lanes]
            shift = bias[pl.ds(pl.multiple_of(ch * rows, rows), rows), :]
            dk = jnp.zeros((rows, HEAD_DIM), F32)
            dv = jnp.zeros((rows, HEAD_DIM), F32)
            out = []
            for g in range(GROUP):
                weight = jnp.exp(dims(key, queries[g], 1, 0) + shift - lses[g])
                back = dims(value, grads[g], 1, 0)
                score_grad = (weight * (back - deltas[g])).astype(BF16)
                dv = dv + dims(weight.astype(BF16), grads[g], 1, 1)
                dk = dk + dims(score_grad, queries[g], 1, 1)
                out.append(carry[g] + dims(key, score_grad, 0, 0))
            dkv_ref[0, at, lanes] = dk.astype(BF16)
            dkv_ref[1, at, lanes] = dv.astype(BF16)
            return tuple(out)

        done = lax.fori_loop(0, chunks, chunk, tuple(jnp.zeros((HEAD_DIM, rows), F32) for _ in range(GROUP)))
        for g in range(GROUP):
            grad = done[g] * (HEAD_DIM**-0.5)
            u, w = grad[: HEAD_DIM // 2], grad[HEAD_DIM // 2 :]
            n = (half * GROUP + g) * HEAD_DIM
            dq_ref[n : n + HEAD_DIM // 2, :] = (u * cosine + w * sine).astype(BF16)
            dq_ref[n + HEAD_DIM // 2 : n + HEAD_DIM, :] = (w * cosine - u * sine).astype(BF16)


def attention_specs(rows, span):
    width = 2 * GROUP * HEAD_DIM
    return dict(
        smem=pl.BlockSpec(memory_space=pltpu.SMEM),
        row=pl.BlockSpec((1, rows), lambda j: (0, 0)),
        table=pl.BlockSpec((HEAD_DIM // 2, rows), lambda j: (0, 0)),
        query=pl.BlockSpec((width, rows), lambda j: (j, 0)),
        kv=pl.BlockSpec((2, span, 2 * HEAD_DIM), lambda j: (0, 0, j)),
        stat=pl.BlockSpec((1, 8, rows), lambda j: (j, 0, 0)),
    )


def attend(query_t, window, offset, lo):
    rows, span = query_t.shape[1], window.shape[1]
    chunks = span // rows - 1
    s = attention_specs(rows, span)
    return pl.pallas_call(
        functools.partial(attend_kernel, chunks, rows),
        grid=(KEY_HEADS // 2,),
        in_specs=[s["smem"], s["row"], s["query"], s["kv"]],
        out_specs=[s["query"], s["stat"]],
        out_shape=[
            jax.ShapeDtypeStruct(query_t.shape, BF16),
            jax.ShapeDtypeStruct((KEY_HEADS // 2, 8, rows), F32),
        ],
        scratch_shapes=[pltpu.VMEM((chunks * rows, rows), F32)],
        compiler_params=pltpu.CompilerParams(vmem_limit_bytes=40 * 2**20),
        cost_estimate=pl.CostEstimate(flops=7 * 10**9, bytes_accessed=8 * 10**6, transcendentals=15 * 10**6),
        name="attend",
    )(offset.reshape(1), lo, query_t, window)


def attend_back(query_t, window, offset, lo, grad_t, lse, delta, cos_t, sin_t):
    rows, span = query_t.shape[1], window.shape[1]
    chunks = span // rows - 1
    s = attention_specs(rows, span)
    return pl.pallas_call(
        functools.partial(attend_back_kernel, chunks, rows),
        grid=(KEY_HEADS // 2,),
        in_specs=[s["smem"], s["row"], s["table"], s["table"], s["query"], s["kv"], s["query"], s["stat"], s["stat"]],
        out_specs=[s["query"], s["kv"]],
        out_shape=[
            jax.ShapeDtypeStruct(query_t.shape, BF16),
            jax.ShapeDtypeStruct(window.shape, BF16),
        ],
        scratch_shapes=[pltpu.VMEM((chunks * rows, rows), F32)],
        compiler_params=pltpu.CompilerParams(vmem_limit_bytes=40 * 2**20),
        cost_estimate=pl.CostEstimate(flops=18 * 10**9, bytes_accessed=16 * 10**6, transcendentals=15 * 10**6),
        name="attend_back",
    )(offset.reshape(1), lo, cos_t, sin_t, query_t, window, grad_t, lse, delta)


def swap_kernel(x_ref, o_ref, lsem, ss, rs):
    me = lax.axis_index("dev")
    n = x_ref.shape[0]
    greet([lax.rem(me + d, n) for d in range(1, n)])

    def copy(d):
        target = lax.rem(me + d, n)
        return pltpu.make_async_remote_copy(
            src_ref=x_ref.at[target], dst_ref=o_ref.at[me], send_sem=ss.at[d], recv_sem=rs.at[d],
            device_id=(target,), device_id_type=MESH)

    own = pltpu.make_async_copy(x_ref.at[me], o_ref.at[me], lsem)
    own.start()

    def start(d, _):
        copy(d).start()
        return 0
    lax.fori_loop(1, n, start, 0)

    def end(d, _):
        copy(d).wait_recv()
        copy(d).wait_send()
        return 0
    lax.fori_loop(1, n, end, 0)
    own.wait()


def swap(values, cid):
    if not meshed():
        return lax.all_to_all(values, "dev", split_axis=0, concat_axis=0, tiled=True)
    n = values.shape[0]
    dma = pltpu.SemaphoreType.DMA
    return pl.pallas_call(
        swap_kernel,
        out_shape=jax.ShapeDtypeStruct(values.shape, values.dtype),
        in_specs=[pl.BlockSpec(memory_space=pltpu.VMEM)],
        out_specs=pl.BlockSpec(memory_space=pltpu.VMEM),
        scratch_shapes=[dma, dma((n,)), dma((n,))],
        compiler_params=pltpu.CompilerParams(collective_id=cid, has_side_effects=True),
        name="swap",
    )(values)


def swap_rows(values, cid):
    n, width = values.shape
    padded = jnp.pad(values.reshape(n, width // 128, 128), ((0, 0), (0, 8 - width // 128), (0, 0)))
    return swap(padded, cid)[:, : width // 128].reshape(n, width)


def hits(slot_ref, slots):
    width = slot_ref.shape[-1]
    return slot_ref[0] == lax.broadcasted_iota(jnp.int32, (slots, width), 0)


def dispatch_kernel(slot_ref, x_ref, u_ref, xo_ref, uo_ref):
    chosen = jnp.where(hits(slot_ref, xo_ref.shape[0]), 1.0, 0.0).astype(BF16)
    xo_ref[...] = dims(chosen, x_ref[...], 1, 0).astype(BF16)
    uo_ref[...] = dims(chosen, u_ref[...], 1, 0).astype(BF16)


def dispatch(slot, normed, upstream, slots):
    pairs, _, width = slot.shape
    model = normed.shape[1]
    return pl.pallas_call(
        dispatch_kernel,
        grid=(pairs,),
        in_specs=[
            pl.BlockSpec((1, 1, width), lambda i: (i, 0, 0)),
            pl.BlockSpec((width, model), lambda i: (i, 0)),
            pl.BlockSpec((width, model), lambda i: (i, 0)),
        ],
        out_specs=[pl.BlockSpec((slots, model), lambda i: (i, 0))] * 2,
        out_shape=[jax.ShapeDtypeStruct((pairs * slots, model), BF16)] * 2,
        compiler_params=pltpu.CompilerParams(vmem_limit_bytes=40 * 2**20),
        cost_estimate=pl.CostEstimate(flops=2 * 10**9, bytes_accessed=65 * 10**6, transcendentals=0),
        name="dispatch",
    )(slot, normed, upstream)


def combine_kernel(slot_ref, r_ref, o_ref):
    chosen = jnp.where(hits(slot_ref, r_ref.shape[0]), 1.0, 0.0).astype(BF16)
    o_ref[...] = dims(chosen, r_ref[...], 0, 0).astype(BF16)


def combine(slot, rows, slots):
    pairs, _, width = slot.shape
    model = rows.shape[1]
    return pl.pallas_call(
        combine_kernel,
        grid=(pairs,),
        in_specs=[
            pl.BlockSpec((1, 1, width), lambda i: (i, 0, 0)),
            pl.BlockSpec((slots, model), lambda i: (i, 0)),
        ],
        out_specs=pl.BlockSpec((width, model), lambda i: (i, 0)),
        out_shape=jax.ShapeDtypeStruct((pairs * width, model), BF16),
        compiler_params=pltpu.CompilerParams(vmem_limit_bytes=40 * 2**20),
        cost_estimate=pl.CostEstimate(flops=10**9, bytes_accessed=33 * 10**6, transcendentals=0),
        name="combine",
    )(slot, rows)


def rms_scale(values):
    return lax.rsqrt(jnp.mean(values * values, axis=-1, keepdims=True) + EPSILON)


def rotate_t(values, cosine, sine):
    half = cosine.shape[0]
    shaped = values.reshape(-1, 2, half, values.shape[1])
    u, w = shaped[:, 0], shaped[:, 1]
    turned = jnp.stack([u * cosine - w * sine, w * cosine + u * sine], axis=1)
    return turned.reshape(values.shape)


def gathered(block, cid, by_rows):
    if meshed():
        return gather_all(block, cid, by_rows)
    return lax.all_gather(block, "dev", axis=0, tiled=True)


def reduced(dense, cid, by_rows):
    if meshed():
        return reduce_all(dense, cid, by_rows)
    return lax.psum_scatter(dense, "dev", scatter_dimension=0, tiled=True).astype(F32)


def on_device(
    tokens,
    positions,
    expert_picks,
    priority,
    first_gain,
    query_weight,
    key_projection_matrix,
    value_projection_matrix,
    output_weight,
    second_gain,
    router_weight,
    gate_weight,
    up_weight,
    down_weight,
    cotangent,
):
    devices = lax.axis_size("dev")
    rows, model = tokens.shape
    split = devices // EXPERTS
    capacity = split * ((9 * rows * TOP + 8 * EXPERTS * split - 1) // (8 * EXPERTS * split))
    my_expert = lax.axis_index("dev") // split
    weight_rows = query_weight.shape[0]

    all_upstream = lax.all_gather(cotangent, "dev", axis=0, tiled=True)
    output_matrix = lax.all_gather(output_weight, "dev", axis=0, tiled=True)
    all_claims = lax.all_gather(jnp.concatenate([expert_picks, priority], axis=1), "dev", axis=0, tiled=True)

    extra = jnp.concatenate([router_weight, first_gain[:, None], second_gain[:, None]], axis=1)
    pad = (-extra.shape[1]) % 128
    packed = jnp.concatenate(
        [query_weight, key_projection_matrix, value_projection_matrix, extra, jnp.zeros((weight_rows, pad), BF16)],
        axis=1,
    )
    matrices = gathered(packed, 1, False)
    qkv_matrix = matrices[:, :QKV]
    router_matrix = matrices[:, QKV : QKV + EXPERTS]
    gain_first = matrices[:, QKV + EXPERTS].astype(F32)
    gain_second = matrices[:, QKV + EXPERTS + 1].astype(F32)

    claims = all_claims.reshape(devices, rows, 2 * TOP)
    mine = claims[:, :, :TOP] == my_expert
    picked_mine = jnp.any(mine, axis=2)
    turn = jnp.sum(jnp.where(mine, claims[:, :, TOP:], 0), axis=2)
    turn = jnp.where(picked_mine, turn, jnp.int32(2**30))
    rank = jnp.sum((turn[:, None, :] < turn[:, :, None]).astype(jnp.int32), axis=2)
    kept = picked_mine & (rank < capacity)
    slot = jnp.where(kept, rank, -1)
    pair_slot = jnp.where(
        slot.reshape(devices // 2, 2, rows) >= 0,
        slot.reshape(devices // 2, 2, rows) + jnp.array([[0], [capacity]], jnp.int32),
        -1,
    ).reshape(devices // 2, 1, 2 * rows)

    inputs = tokens.astype(F32)
    scale_one = rms_scale(inputs)
    normed_one = (inputs * scale_one * gain_first).astype(BF16)
    half_dim = HEAD_DIM // 2
    frequency = jnp.power(10000.0, -(jnp.arange(half_dim, dtype=F32) * 2.0) / HEAD_DIM)
    angle = positions.astype(F32)[None, :] * frequency[:, None]
    cos_t, sin_t = jnp.cos(angle), jnp.sin(angle)
    qkv_t = dims(qkv_matrix, normed_one, 0, 1)
    q_width, k_width = QUERY_HEADS * HEAD_DIM, KEY_HEADS * HEAD_DIM
    query_t = rotate_t(qkv_t[:q_width], cos_t, sin_t).astype(BF16) * BF16(HEAD_DIM**-0.5)
    key = rotate_t(qkv_t[q_width : q_width + k_width], cos_t, sin_t).astype(BF16).T
    value = qkv_t[q_width + k_width :].astype(BF16).T
    window, offset = window_of(jnp.stack([key, value]))
    lo = (jnp.arange(rows, dtype=jnp.int32) - positions)[None, :]
    attended_t, lse = attend(query_t, window, offset, lo)
    residual = inputs + dims(attended_t, output_matrix, 0, 0)
    scale_two = rms_scale(residual)
    normed_two = (residual * scale_two * gain_second).astype(BF16)

    logits = dims(normed_two, router_matrix, 1, 0)
    one_hot = expert_picks[:, :, None] == jnp.arange(EXPERTS, dtype=jnp.int32)
    picked_any = jnp.any(one_hot, axis=1)
    logits = jnp.where(picked_any, logits, MASKED)
    picked_exp = jnp.exp(logits - jnp.max(logits, axis=1, keepdims=True))
    gates = picked_exp / jnp.sum(picked_exp, axis=1, keepdims=True)
    gate_rows = swap_rows(jnp.repeat(gates.T, split, axis=0), 5)

    all_normed = gathered(normed_two, 2, True)
    expert_in, expert_up = dispatch(pair_slot, all_normed, all_upstream, 2 * capacity)
    slot_hit = slot[:, None, :] == jnp.arange(capacity, dtype=jnp.int32)[None, :, None]
    gate_of_slot = jnp.sum(jnp.where(slot_hit, gate_rows[:, None, :], 0.0), axis=2).reshape(-1, 1)
    gate_in = dims(expert_in, gate_weight, 1, 0)
    up_in = dims(expert_in, up_weight, 1, 0)
    sigmoid_gate = 1.0 / (1.0 + jnp.exp(-gate_in))
    silu_gate = gate_in * sigmoid_gate
    hidden = (silu_gate * up_in).astype(BF16)
    gated_hidden = (hidden.astype(F32) * gate_of_slot).astype(BF16)
    hidden_up = dims(expert_up, down_weight, 1, 1)
    hidden_grad = hidden_up * gate_of_slot
    gate_grad_slot = jnp.sum(hidden.astype(F32) * hidden_up, axis=1).reshape(devices, capacity)
    gate_in_grad = (hidden_grad * up_in * sigmoid_gate * (1.0 + gate_in * (1.0 - sigmoid_gate))).astype(BF16)
    up_in_grad = (hidden_grad * silu_gate).astype(BF16)
    partial_in = (dims(gate_in_grad, gate_weight, 1, 1) + dims(up_in_grad, up_weight, 1, 1)).astype(BF16)
    gate_grad_rows = jnp.sum(jnp.where(slot_hit, gate_grad_slot[:, :, None], 0.0), axis=1)
    returned_grad = reduced(combine(pair_slot, partial_in, 2 * capacity), 3, True)
    gate_grad = swap_rows(gate_grad_rows, 6)
    gate_grad = jnp.sum(gate_grad.reshape(EXPERTS, split, rows), axis=1).T

    partial_out = dims(gated_hidden, down_weight, 1, 0).astype(BF16)
    dense_out = combine(pair_slot, partial_out, 2 * capacity)
    mixture = lax.psum_scatter(dense_out, "dev", scatter_dimension=0, tiled=True)
    layer_output = (residual + mixture.astype(F32)).astype(BF16)
    down_gradient = dims(gated_hidden, expert_up, 0, 0)
    gate_gradient = dims(expert_in, gate_in_grad, 0, 0)
    up_gradient = dims(expert_in, up_in_grad, 0, 0)

    upstream = cotangent.astype(F32)
    logit_grad = (gates * (gate_grad - jnp.sum(gates * gate_grad, axis=1, keepdims=True))).astype(BF16)
    router_gradient = dims(normed_two, logit_grad, 0, 0)
    normed_two_grad = returned_grad + dims(logit_grad, router_matrix, 1, 1)
    weighted_two = normed_two_grad * gain_second
    second_gain_grad = jnp.sum(normed_two_grad * residual * scale_two, axis=0)
    residual_grad = (
        upstream
        + scale_two * weighted_two
        - residual * scale_two**3 * jnp.mean(weighted_two * residual, axis=-1, keepdims=True)
    )
    branch_grad = residual_grad.astype(BF16)
    output_gradient = dims(attended_t, branch_grad, 1, 0).astype(BF16)
    output_gradient = lax.psum_scatter(output_gradient, "dev", scatter_dimension=0, tiled=True).astype(F32)
    grad_t = dims(output_matrix, branch_grad, 1, 1).astype(BF16)

    delta = jnp.sum((attended_t.astype(F32) * grad_t.astype(F32)).reshape(QUERY_HEADS, HEAD_DIM, rows), axis=1)
    delta = jnp.pad(delta.reshape(KEY_HEADS // 2, 2 * GROUP, rows), ((0, 0), (0, 8 - 2 * GROUP), (0, 0)))
    query_grad_t, window_grad = attend_back(query_t, window, offset, lo, grad_t, lse, delta, cos_t, sin_t)
    key_grad, value_grad = unwindow(window_grad)
    key_grad_t = rotate_t(key_grad.T, cos_t, -sin_t).astype(BF16)
    qkv_grad_t = jnp.concatenate([query_grad_t, key_grad_t, value_grad.T.astype(BF16)], axis=0)
    qkv_gradient = dims(normed_one, qkv_grad_t, 0, 1)
    normed_one_grad = dims(qkv_grad_t, qkv_matrix, 0, 1)
    weighted_one = normed_one_grad * gain_first
    first_gain_grad = jnp.sum(normed_one_grad * inputs * scale_one, axis=0)
    tokens_gradient = (
        residual_grad
        + scale_one * weighted_one
        - inputs * scale_one**3 * jnp.mean(weighted_one * inputs, axis=-1, keepdims=True)
    )
    terms = jnp.concatenate(
        [qkv_gradient, router_gradient, first_gain_grad[:, None], second_gain_grad[:, None],
         jnp.zeros((model, (-(QKV + EXPERTS + 2)) % 256), F32)],
        axis=1,
    ).astype(BF16)
    sums = reduced(terms, 4, False)
    return (
        layer_output,
        tokens_gradient,
        sums[:, QKV + EXPERTS],
        sums[:, :q_width],
        sums[:, q_width : q_width + k_width],
        sums[:, q_width + k_width : QKV],
        output_gradient,
        sums[:, QKV + EXPERTS + 1],
        sums[:, QKV : QKV + EXPERTS],
        gate_gradient,
        up_gradient,
        down_gradient,
    )


def solution(mesh):
    rows, whole = P("dev", None), P("dev")
    columns = P(None, "dev")
    return jax.shard_map(
        on_device,
        mesh=mesh,
        in_specs=(rows, whole, rows, rows, whole, rows, rows, rows, rows, whole, rows, columns, columns, rows, rows),
        out_specs=(rows, rows, whole, rows, rows, rows, rows, whole, rows, columns, columns, rows),
        check_vma=False,
    )
```

```python
import functools
import jax, jax.numpy as jnp
from jax import lax
from jax.experimental import pallas as pl
from jax.experimental.pallas import tpu as pltpu

MESH = pl.DeviceIdType.MESH


def place():
    me = lax.axis_index("dev")
    return lax.rem(me // 8, 4), lax.rem(me // 4, 2), lax.rem(me // 2, 2), lax.rem(me, 2)


def number(z, y, x, c):
    return ((z * 2 + y) * 2 + x) * 2 + c


def greet(partners):
    barrier = pltpu.get_barrier_semaphore()
    for partner in partners:
        pl.semaphore_signal(barrier, inc=1, device_id=(partner,), device_id_type=MESH)
    pl.semaphore_wait(barrier, len(partners))


def partners_of(z, y, x, c):
    return [
        number(z, y, x, 1 - c),
        number(z, y, 1 - x, c),
        number(z, 1 - y, x, c),
        number(lax.rem(z + 1, 4), y, x, c),
        number(lax.rem(z + 2, 4), y, x, c),
        number(lax.rem(z + 3, 4), y, x, c),
    ]


def gather_kernel(rows, pieces, x_ref, o_ref, local_sem, ss, rs):
    z, y, x, c = place()
    greet(partners_of(z, y, x, c))
    sibling = number(z, y, x, 1 - c)
    me = number(z, y, x, c)
    around = (number(z, 1 - y, x, c), number(z, y, 1 - x, c))

    def part(ref, block, p):
        r0, nr, c0, nc = pieces[p]
        return ref.at[pl.ds(pl.multiple_of(block * rows + r0, 16), nr), pl.ds(c0, nc)]

    def copy(block, p, slot, target, own=False):
        source = part(x_ref, 0, p) if own else part(o_ref, block, p)
        return pltpu.make_async_remote_copy(
            src_ref=source, dst_ref=part(o_ref, block, p),
            send_sem=ss.at[p * 31 + slot], recv_sem=rs.at[p * 31 + slot],
            device_id=(target,), device_id_type=MESH)

    pending = []

    def send(*args, **kw):
        cp = copy(*args, **kw)
        cp.start()
        pending.append(cp)

    def at(k, fy, fx):
        return number(lax.rem(z + 4 - k, 4), (1 - y) if fy else y, (1 - x) if fx else x, c)

    local = pltpu.make_async_copy(x_ref, o_ref.at[pl.ds(pl.multiple_of(me * rows, 16), rows), :], local_sem)
    local.start()
    order = (0, 1, 3, 2)
    far = ((1, 0), (0, 1))
    for k in (1, 3, 2):
        for p in range(2):
            send(me, p, k - 1, number(lax.rem(z + k, 4), y, x, c), own=True)
    for k in order:
        for p in range(2):
            block = at(k, 0, 0)
            if k:
                copy(block, p, k - 1, sibling).wait_recv()
            own = k == 0
            send(block, p, 3 + k, around[p], own=own)
            send(block, p, 7 + k, around[1 - p], own=own)
            send(block, p, 15 + k, sibling, own=own)
    for k in order:
        for p in range(2):
            fy, fx = far[p]
            block = at(k, fy, fx)
            copy(block, p, 3 + k, sibling).wait_recv()
            send(block, p, 11 + k, around[1 - p])
            send(block, p, 19 + k, sibling)
    for j, slot in ((0, 7), (1, 11)):
        for k in order:
            for p in range(2):
                fy, fx = (1, 1) if j else (1 - far[p][0], 1 - far[p][1])
                block = at(k, fy, fx)
                copy(block, p, slot + k, sibling).wait_recv()
                send(block, p, 23 + 4 * j + k, sibling)
    for k in range(4):
        for p in range(2):
            for s in (15, 19, 23, 27):
                copy(me, p, s + k, sibling).wait_recv()
    for cp in pending:
        cp.wait_send()
    local.wait()


def gather_all(block, cid, by_rows):
    rows, cols = block.shape
    if by_rows:
        pieces = ((0, rows // 2, 0, cols), (rows // 2, rows // 2, 0, cols))
    else:
        half = (cols // 256) * 128
        pieces = ((0, rows, 0, half), (0, rows, half, cols - half))
    return pl.pallas_call(
        functools.partial(gather_kernel, rows, pieces),
        out_shape=jax.ShapeDtypeStruct((32 * rows, cols), block.dtype),
        in_specs=[pl.BlockSpec(memory_space=pl.ANY)],
        out_specs=pl.BlockSpec(memory_space=pl.ANY),
        scratch_shapes=[pltpu.SemaphoreType.DMA, pltpu.SemaphoreType.DMA((62,)), pltpu.SemaphoreType.DMA((62,))],
        compiler_params=pltpu.CompilerParams(collective_id=cid, has_side_effects=True),
        name="gather_all",
    )(block)


def reduce_kernel(rows, cols, pieces, g_ref, o_ref, acc, own, ra, rb, rz, own_sem, ssem, rsem, sa, ra_sem, sb, rb_sem, sz, rz_sem):
    z, y, x, c = place()
    greet(partners_of(z, y, x, c))
    sibling = number(z, y, x, 1 - c)
    around = (number(z, y, 1 - x, c), number(z, 1 - y, x, c))
    blocks = [(dy, dx, k) for dy, dx in ((1, 1), (1, 0), (0, 1), (0, 0)) for k in (2, 1, 3, 0)]

    def where(dy, dx, k):
        return lax.rem(z + k, 4), (1 - y) if dy else y, (1 - x) if dx else x

    def lane(dy, dx, k):
        zz, yy, xx = where(dy, dx, k)
        return (zz * 2 + yy) * 2 + xx

    def chip_rows(dy, dx, k, core):
        zz, yy, xx = where(dy, dx, k)
        return g_ref.at[pl.ds(pl.multiple_of(number(zz, yy, xx, core) * rows, 16), rows), :]

    def to_sibling(n):
        dy, dx, k = blocks[n]
        return pltpu.make_async_remote_copy(
            src_ref=chip_rows(dy, dx, k, 1 - c), dst_ref=acc.at[lane(dy, dx, k)],
            send_sem=ssem.at[n], recv_sem=rsem.at[n], device_id=(sibling,), device_id_type=MESH)

    def load(n):
        return pltpu.make_async_copy(chip_rows(*blocks[n], c), own.at[n % 2], own_sem.at[n % 2])

    def part(ref, p):
        r0, nr, c0, nc = pieces[p]
        return ref.at[pl.ds(r0, nr), pl.ds(c0, nc)]

    def first(p, d2, k, dy, dx):
        return pltpu.make_async_remote_copy(
            src_ref=part(acc.at[lane(dy, dx, k)], p), dst_ref=ra.at[p, d2, k],
            send_sem=sa.at[p, d2, k], recv_sem=ra_sem.at[p, d2, k], device_id=(around[p],), device_id_type=MESH)

    def second(p, k):
        dy, dx = (1, 0) if p == 0 else (0, 1)
        return pltpu.make_async_remote_copy(
            src_ref=part(acc.at[lane(dy, dx, k)], p), dst_ref=rb.at[p, k],
            send_sem=sb.at[p, k], recv_sem=rb_sem.at[p, k], device_id=(around[1 - p],), device_id_type=MESH)

    def third(p, k):
        return pltpu.make_async_remote_copy(
            src_ref=part(acc.at[lane(0, 0, k)], p), dst_ref=rz.at[p, k - 1],
            send_sem=sz.at[p, k - 1], recv_sem=rz_sem.at[p, k - 1],
            device_id=(number(lax.rem(z + k, 4), y, x, c),), device_id_type=MESH)

    step = 16

    def add(out, terms, nr):
        def chunk(i, _):
            at = pl.ds(pl.multiple_of(i * step, step), step)
            total = terms[0][at, :].astype(jnp.float32)
            for t in terms[1:]:
                total = total + t[at, :].astype(jnp.float32)
            out[at, :] = total.astype(out.dtype)
            return 0
        lax.fori_loop(0, nr // step, chunk, 0)

    for n in range(16):
        to_sibling(n).start()
    load(0).start()
    for n in range(16):
        dy, dx, k = blocks[n]
        if n + 1 < 16:
            load(n + 1).start()
        load(n).wait()
        to_sibling(n).wait_recv()
        block = acc.at[lane(dy, dx, k)]
        add(block, [block, own.at[n % 2]], rows)
        if dx:
            first(0, dy, k, dy, dx).start()
        if dy:
            first(1, dx, k, dy, dx).start()
    for k in (2, 1, 3, 0):
        for p in range(2):
            dy, dx = (1, 0) if p == 0 else (0, 1)
            first(p, 1, k, 1, 1).wait_recv()
            block = part(acc.at[lane(dy, dx, k)], p)
            add(block, [block, ra.at[p, 1, k]], pieces[p][1])
            second(p, k).start()
    for k in (2, 1, 3, 0):
        for p in range(2):
            first(p, 0, k, 1 - p, p).wait_recv()
            second(p, k).wait_recv()
            block = part(acc.at[lane(0, 0, k)], p)
            if k:
                add(block, [block, ra.at[p, 0, k], rb.at[p, k]], pieces[p][1])
                third(p, k).start()
    for p in range(2):
        for k in range(1, 4):
            third(p, k).wait_recv()
        block = part(acc.at[lane(0, 0, 0)], p)
        add(part(o_ref, p), [block, ra.at[p, 0, 0], rb.at[p, 0]] + [rz.at[p, j] for j in range(3)], pieces[p][1])
    for n in range(16):
        to_sibling(n).wait_send()
    for p in range(2):
        for k in range(4):
            first(p, 0, k, 1 - p, p).wait_send()
            first(p, 1, k, 1, 1).wait_send()
            second(p, k).wait_send()
            if k:
                third(p, k).wait_send()


def reduce_all(dense, cid, by_rows, out_dtype=jnp.float32):
    rows, cols = dense.shape[0] // 32, dense.shape[1]
    if by_rows:
        pieces = ((0, rows // 2, 0, cols), (rows // 2, rows // 2, 0, cols))
    else:
        half = (cols // 256) * 128
        assert cols == 2 * half
        pieces = ((0, rows, 0, half), (0, rows, half, cols - half))
    pr, pc = pieces[0][1], pieces[0][3]
    dma = pltpu.SemaphoreType.DMA
    return pl.pallas_call(
        functools.partial(reduce_kernel, rows, cols, pieces),
        out_shape=jax.ShapeDtypeStruct((rows, cols), out_dtype),
        in_specs=[pl.BlockSpec(memory_space=pl.ANY)],
        out_specs=pl.BlockSpec(memory_space=pltpu.VMEM),
        scratch_shapes=[
            pltpu.VMEM((16, rows, cols), dense.dtype),
            pltpu.VMEM((2, rows, cols), dense.dtype),
            pltpu.VMEM((2, 2, 4, pr, pc), dense.dtype),
            pltpu.VMEM((2, 4, pr, pc), dense.dtype),
            pltpu.VMEM((2, 3, pr, pc), dense.dtype),
            dma((2,)), dma((16,)), dma((16,)), dma((2, 2, 4)), dma((2, 2, 4)), dma((2, 4)), dma((2, 4)), dma((2, 3)), dma((2, 3)),
        ],
        compiler_params=pltpu.CompilerParams(collective_id=cid, has_side_effects=True, vmem_limit_bytes=56 * 2**20),
        name="reduce_all",
    )(dense)


from jax.sharding import PartitionSpec as P

QUERY_HEADS = 24
KEY_HEADS = 8
HEAD_DIM = 64
GROUP = QUERY_HEADS // KEY_HEADS
TOP = 8
EXPERTS = 32
MAXDOC = 2000
EPSILON = 1e-06
MASKED = -1e30
QKV = (QUERY_HEADS + 2 * KEY_HEADS) * HEAD_DIM
F32 = jnp.float32
BF16 = jnp.bfloat16


def meshed():
    return lax.axis_size("dev") == 32


def dims(a, b, ca, cb):
    return lax.dot_general(a, b, (((ca,), (cb,)), ((), ())), preferred_element_type=F32)


def window_kernel(rows, kv_ref, mine_ref, o_ref, slots_ref, lsem, ss, rs, gs, gr):
    z, y, x, c = place()
    p = y * 2 + x
    sibling = number(z, y, x, 1 - c)
    up = number(lax.rem(z + 1, 4), y, x, c)
    down = number(lax.rem(z + 3, 4), y, x, c)

    def chip(q):
        return (z * 4 + q) * 2 + c

    near = [chip(lax.rem(p + d, 4)) for d in (1, 2, 3)]
    greet_all()
    swap = Swap(lambda t: mine_ref.at[t // 8], slots_ref, gs, gr)

    def slot(s, core):
        return o_ref.at[:, pl.ds(pl.multiple_of((2 * s + core) * rows, 16), rows), :]

    def copy(source, s, n, target):
        return pltpu.make_async_remote_copy(
            src_ref=source, dst_ref=slot(s, c), send_sem=ss.at[n], recv_sem=rs.at[n],
            device_id=(target,), device_id_type=MESH)

    own_in = pltpu.make_async_copy(kv_ref, slot(4, c), lsem.at[0])
    own_in.start()
    to_up = copy(kv_ref, 0, 0, up)

    @pl.when(z < 3)
    def _():
        to_up.start()

    stand_in = pltpu.make_async_copy(kv_ref, slot(0, c), lsem.at[1])

    @pl.when(z == 0)
    def _():
        stand_in.start()

    for d in (1, 3, 2):
        @pl.when(p + d < 4)
        def _(d=d):
            copy(kv_ref, 4 - d, d, near[d - 1]).start()

    to_sibling = {4: copy(kv_ref, 4, 4, sibling)}
    to_sibling[4].start()
    swap.start()

    @pl.when(z == 0)
    def _():
        stand_in.wait()

    @pl.when(z > 0)
    def _():
        to_up.wait_recv()

    for d in (3, 1, 2):
        @pl.when(p + d >= 4)
        def _(d=d):
            copy(slot(0, c), 4 - d, d, near[d - 1]).start()

    to_sibling[0] = copy(slot(0, c), 0, 5, sibling)
    to_sibling[0].start()
    for d in (1, 3, 2):
        copy(kv_ref, 4 - d, d, near[d - 1]).wait_recv()
        to_sibling[4 - d] = copy(slot(4 - d, c), 4 - d, 5 + d, sibling)
        to_sibling[4 - d].start()
    for s in range(5):
        pltpu.make_async_remote_copy(
            src_ref=kv_ref, dst_ref=slot(s, 1 - c), send_sem=ss.at[0],
            recv_sem=rs.at[{4: 4, 0: 5}.get(s, 9 - s)], device_id=(sibling,), device_id_type=MESH).wait_recv()
    own_in.wait()

    @pl.when(z < 3)
    def _():
        to_up.wait_send()

    for d in (1, 2, 3):
        copy(kv_ref, 4 - d, d, near[d - 1]).wait_send()
    for s in range(5):
        to_sibling[s].wait_send()
    swap.wait_recv()
    swap.wait_send()


def window_of(kv, slots):
    rows, width = kv.shape[1:]
    if meshed():
        dma = pltpu.SemaphoreType.DMA
        full, plane_slots = pl.pallas_call(
            functools.partial(window_kernel, rows),
            out_shape=[
                jax.ShapeDtypeStruct((2, 10 * rows, width), kv.dtype),
                jax.ShapeDtypeStruct((32, 8, rows), F32),
            ],
            in_specs=[pl.BlockSpec(memory_space=pl.ANY), pl.BlockSpec(memory_space=pltpu.VMEM)],
            out_specs=[pl.BlockSpec(memory_space=pl.ANY), pl.BlockSpec(memory_space=pltpu.VMEM)],
            scratch_shapes=[dma((2,)), dma((9,)), dma((9,)), dma((32,)), dma((32,))],
            compiler_params=pltpu.CompilerParams(collective_id=11, has_side_effects=True),
            name="window",
        )(kv, slots)
        return full, lax.rem(lax.axis_index("dev"), 2), plane_slots
    devices = lax.axis_size("dev")
    back = (MAXDOC + rows - 2) // rows
    parts = [
        lax.ppermute(kv, "dev", [(i - d, i) for i in range(d, devices)]) for d in range(back, 0, -1)
    ]
    return jnp.concatenate(parts + [kv, jnp.zeros_like(kv)], axis=1), jnp.int32(0), None


def unwindow_kernel(rows, g_ref, o_ref, mine, got, near_got, far, lsem, ss, rs):
    z, y, x, c = place()
    p = y * 2 + x
    sibling = number(z, y, x, 1 - c)
    up = number(lax.rem(z + 1, 4), y, x, c)
    down = number(lax.rem(z + 3, 4), y, x, c)

    def chip(q):
        return (z * 4 + q) * 2 + c

    ahead = [chip(lax.rem(p + d, 4)) for d in (1, 2, 3)]
    behind = [chip(lax.rem(p + 4 - d, 4)) for d in (1, 2, 3)]
    greet([sibling, up, down] + ahead)

    def slot(s, core):
        return g_ref.at[:, pl.ds(pl.multiple_of((2 * s + core) * rows, 16), rows), :]

    def to_sibling(s):
        return pltpu.make_async_remote_copy(
            src_ref=slot(s, 1 - c), dst_ref=got.at[s], send_sem=ss.at[s], recv_sem=rs.at[s],
            device_id=(sibling,), device_id_type=MESH)

    def load(s):
        return pltpu.make_async_copy(slot(s, c), mine.at[s], lsem.at[s])

    def to_owner(d):
        return pltpu.make_async_remote_copy(
            src_ref=got.at[4 - d], dst_ref=near_got.at[d - 1], send_sem=ss.at[4 + d], recv_sem=rs.at[4 + d],
            device_id=(behind[d - 1],), device_id_type=MESH)

    to_down = pltpu.make_async_remote_copy(
        src_ref=got.at[0], dst_ref=far, send_sem=ss.at[8], recv_sem=rs.at[8],
        device_id=(down,), device_id_type=MESH)
    order = (3, 1, 2, 0, 4)
    for s in order:
        to_sibling(s).start()
        load(s).start()

    def rowwise(body):
        for h in range(2):
            def step(i, _, h=h):
                body(h, pl.ds(pl.multiple_of(i * 32, 32), 32))
                return 0
            lax.fori_loop(0, rows // 32, step, 0)

    for s in order:
        load(s).wait()
        to_sibling(s).wait_recv()

        def both(h, at, s=s):
            total = got[s, h, at, :].astype(F32) + mine[s, h, at, :].astype(F32)
            if s == 4:
                o_ref[h, at, :] = total
            else:
                got[s, h, at, :] = total.astype(BF16)
        rowwise(both)
        if 0 < s < 4:
            to_owner(4 - s).start()
    for d in (1, 3, 2):
        to_owner(d).wait_recv()

        @pl.when(p + d < 4)
        def _(d=d):
            def body(h, at):
                o_ref[h, at, :] += near_got[d - 1, h, at, :].astype(F32)
            rowwise(body)

        @pl.when(p + d >= 4)
        def _(d=d):
            def body(h, at):
                total = got[0, h, at, :].astype(F32) + near_got[d - 1, h, at, :].astype(F32)
                got[0, h, at, :] = total.astype(BF16)
            rowwise(body)

    @pl.when(z > 0)
    def _():
        to_down.start()

    @pl.when(z < 3)
    def _():
        to_down.wait_recv()

        def body(h, at):
            o_ref[h, at, :] += far[h, at, :].astype(F32)
        rowwise(body)

    @pl.when(z > 0)
    def _():
        to_down.wait_send()

    for s in range(5):
        to_sibling(s).wait_send()
    for d in (1, 2, 3):
        to_owner(d).wait_send()


def unwindow(grads):
    rows, width = grads.shape[1] // 10, grads.shape[2]
    if meshed():
        dma = pltpu.SemaphoreType.DMA
        return pl.pallas_call(
            functools.partial(unwindow_kernel, rows),
            out_shape=jax.ShapeDtypeStruct((2, rows, width), F32),
            in_specs=[pl.BlockSpec(memory_space=pl.ANY)],
            out_specs=pl.BlockSpec(memory_space=pltpu.VMEM),
            scratch_shapes=[
                pltpu.VMEM((5, 2, rows, width), BF16),
                pltpu.VMEM((5, 2, rows, width), BF16),
                pltpu.VMEM((3, 2, rows, width), BF16),
                pltpu.VMEM((2, rows, width), BF16),
                dma((5,)), dma((9,)), dma((9,)),
            ],
            compiler_params=pltpu.CompilerParams(collective_id=12, has_side_effects=True, vmem_limit_bytes=40 * 2**20),
            name="unwindow",
        )(grads)
    devices = lax.axis_size("dev")
    back = (MAXDOC + rows - 2) // rows
    total = grads[:, back * rows : (back + 1) * rows].astype(F32)
    for d in range(1, back + 1):
        piece = grads[:, (back - d) * rows : (back - d + 1) * rows]
        moved = lax.ppermute(piece, "dev", [(i, i - d) for i in range(d, devices)])
        total = total + moved.astype(F32)
    return total


def make_bias(bias, lo_ref, chunks, rows):
    def fill(ch, _):
        at = pl.ds(pl.multiple_of(ch * rows, rows), rows)
        relative = lax.broadcasted_iota(jnp.int32, (rows, rows), 0) + (ch - (chunks - 1)) * rows
        query = lax.broadcasted_iota(jnp.int32, (rows, rows), 1)
        allowed = (relative <= query) & (relative >= lo_ref[...])
        bias[at, :] = jnp.where(allowed, 0.0, MASKED)
        return 0
    lax.fori_loop(0, chunks, fill, 0)


def attend_kernel(chunks, rows, off_ref, lo_ref, q_ref, kv_ref, o_ref, lse_ref, bias):
    @pl.when(pl.program_id(0) == 0)
    def _():
        make_bias(bias, lo_ref, chunks, rows)

    off = off_ref[0]
    lse_ref[...] = jnp.zeros_like(lse_ref)
    for half in range(2):
        lanes = slice(half * HEAD_DIM, (half + 1) * HEAD_DIM)
        queries = [q_ref[(half * GROUP + g) * HEAD_DIM : (half * GROUP + g + 1) * HEAD_DIM, :] for g in range(GROUP)]

        def chunk(i, carry, lanes=lanes, queries=queries):
            ch = chunks - 1 - i
            at = pl.ds(pl.multiple_of((ch + off) * rows, rows), rows)
            key, value = kv_ref[0, at, lanes], kv_ref[1, at, lanes]
            shift = bias[pl.ds(pl.multiple_of(ch * rows, rows), rows), :]
            out = []
            for g in range(GROUP):
                top, total, mixed = carry[g]
                score = dims(key, queries[g], 1, 0) + shift
                new_top = jnp.maximum(top, jnp.max(score, axis=0, keepdims=True))
                weight = jnp.exp(score - new_top)
                fade = jnp.exp(top - new_top)
                total = total * fade + jnp.sum(weight, axis=0, keepdims=True)
                mixed = mixed * fade + dims(value, weight.astype(BF16), 0, 0)
                out.append((new_top, total, mixed))
            return tuple(out)

        start = tuple(
            (jnp.full((1, rows), MASKED, F32), jnp.zeros((1, rows), F32), jnp.zeros((HEAD_DIM, rows), F32))
            for _ in range(GROUP)
        )
        done = lax.fori_loop(0, chunks, chunk, start)
        for g in range(GROUP):
            top, total, mixed = done[g]
            n = half * GROUP + g
            o_ref[n * HEAD_DIM : (n + 1) * HEAD_DIM, :] = (mixed / total).astype(BF16)
            lse_ref[0, n : n + 1, :] = top + jnp.log(total)


def attend_back_pair(
    chunks, rows, off, cos_ref, sin_ref, q_ref, kv_ref, g_ref, lse_ref, delta_ref, dq_ref, dkv_ref, bias, between
):
    unused = pl.ds(pl.multiple_of((1 - off) * chunks * rows, rows), rows)
    dkv_ref[:, unused, :] = jnp.zeros((2, rows, 2 * HEAD_DIM), BF16)
    for half in range(2):
        lanes = slice(half * HEAD_DIM, (half + 1) * HEAD_DIM)
        own = [slice((half * GROUP + g) * HEAD_DIM, (half * GROUP + g + 1) * HEAD_DIM) for g in range(GROUP)]
        queries = [q_ref[s, :] for s in own]
        grads = [g_ref[s, :] for s in own]
        lses = [lse_ref[0, half * GROUP + g : half * GROUP + g + 1, :] for g in range(GROUP)]
        deltas = [delta_ref[0, half * GROUP + g : half * GROUP + g + 1, :] for g in range(GROUP)]

        def chunk(ch, carry, lanes=lanes, queries=queries, grads=grads, lses=lses, deltas=deltas):
            at = pl.ds(pl.multiple_of((ch + off) * rows, rows), rows)
            key, value = kv_ref[0, at, lanes], kv_ref[1, at, lanes]
            shift = bias[pl.ds(pl.multiple_of(ch * rows, rows), rows), :]
            dk = jnp.zeros((rows, HEAD_DIM), F32)
            dv = jnp.zeros((rows, HEAD_DIM), F32)
            out = []
            for g in range(GROUP):
                weight = jnp.exp(dims(key, queries[g], 1, 0) + shift - lses[g])
                back = dims(value, grads[g], 1, 0)
                score_grad = (weight * (back - deltas[g])).astype(BF16)
                dv = dv + dims(weight.astype(BF16), grads[g], 1, 1)
                dk = dk + dims(score_grad, queries[g], 1, 1)
                out.append(carry[g] + dims(key, score_grad, 0, 0))
            dkv_ref[0, at, lanes] = dk.astype(BF16)
            dkv_ref[1, at, lanes] = dv.astype(BF16)
            return tuple(out)

        done = lax.fori_loop(0, chunks, chunk, tuple(jnp.zeros((HEAD_DIM, rows), F32) for _ in range(GROUP)))
        cosine, sine = cos_ref[...], sin_ref[...]
        for g in range(GROUP):
            grad = done[g] * (HEAD_DIM**-0.5)
            u, w = grad[: HEAD_DIM // 2], grad[HEAD_DIM // 2 :]
            n = (half * GROUP + g) * HEAD_DIM
            dq_ref[n : n + HEAD_DIM // 2, :] = (u * cosine + w * sine).astype(BF16)
            dq_ref[n + HEAD_DIM // 2 : n + HEAD_DIM, :] = (w * cosine - u * sine).astype(BF16)
        between(half)


def attend_back_kernel(
    chunks, rows, off_ref, lo_ref, cos_ref, sin_ref, q_ref, kv_ref, g_ref, lse_ref, delta_ref, dq_ref, dkv_ref, bias
):
    @pl.when(pl.program_id(0) == 0)
    def _():
        make_bias(bias, lo_ref, chunks, rows)

    attend_back_pair(
        chunks, rows, off_ref[0], cos_ref, sin_ref, q_ref, kv_ref, g_ref, lse_ref, delta_ref, dq_ref, dkv_ref, bias,
        lambda half: None,
    )


def attention_specs(rows, span):
    width = 2 * GROUP * HEAD_DIM
    return dict(
        smem=pl.BlockSpec(memory_space=pltpu.SMEM),
        row=pl.BlockSpec((1, rows), lambda j: (0, 0)),
        table=pl.BlockSpec((HEAD_DIM // 2, rows), lambda j: (0, 0)),
        query=pl.BlockSpec((width, rows), lambda j: (j, 0)),
        kv=pl.BlockSpec((2, span, 2 * HEAD_DIM), lambda j: (0, 0, j)),
        stat=pl.BlockSpec((1, 8, rows), lambda j: (j, 0, 0)),
    )


def attend(query_t, window, offset, lo):
    rows, span = query_t.shape[1], window.shape[1]
    chunks = span // rows - 1
    s = attention_specs(rows, span)
    return pl.pallas_call(
        functools.partial(attend_kernel, chunks, rows),
        grid=(KEY_HEADS // 2,),
        in_specs=[s["smem"], s["row"], s["query"], s["kv"]],
        out_specs=[s["query"], s["stat"]],
        out_shape=[
            jax.ShapeDtypeStruct(query_t.shape, BF16),
            jax.ShapeDtypeStruct((KEY_HEADS // 2, 8, rows), F32),
        ],
        scratch_shapes=[pltpu.VMEM((chunks * rows, rows), F32)],
        compiler_params=pltpu.CompilerParams(vmem_limit_bytes=40 * 2**20),
        cost_estimate=pl.CostEstimate(flops=7 * 10**9, bytes_accessed=8 * 10**6, transcendentals=15 * 10**6),
        name="attend",
    )(offset.reshape(1), lo, query_t, window)


def attend_back(query_t, window, offset, lo, grad_t, lse, delta, cos_t, sin_t):
    rows, span = query_t.shape[1], window.shape[1]
    chunks = span // rows - 1
    s = attention_specs(rows, span)
    return pl.pallas_call(
        functools.partial(attend_back_kernel, chunks, rows),
        grid=(KEY_HEADS // 2,),
        in_specs=[s["smem"], s["row"], s["table"], s["table"], s["query"], s["kv"], s["query"], s["stat"], s["stat"]],
        out_specs=[s["query"], s["kv"]],
        out_shape=[
            jax.ShapeDtypeStruct(query_t.shape, BF16),
            jax.ShapeDtypeStruct(window.shape, BF16),
        ],
        scratch_shapes=[pltpu.VMEM((chunks * rows, rows), F32)],
        compiler_params=pltpu.CompilerParams(vmem_limit_bytes=40 * 2**20),
        cost_estimate=pl.CostEstimate(flops=18 * 10**9, bytes_accessed=16 * 10**6, transcendentals=15 * 10**6),
        name="attend_back",
    )(offset.reshape(1), lo, cos_t, sin_t, query_t, window, grad_t, lse, delta)


def hits(slot_ref, slots):
    width = slot_ref.shape[-1]
    return slot_ref[0] == lax.broadcasted_iota(jnp.int32, (slots, width), 0)


def dispatch_kernel(slot_ref, x_ref, u_ref, xo_ref, uo_ref):
    chosen = jnp.where(hits(slot_ref, xo_ref.shape[0]), 1.0, 0.0).astype(BF16)
    xo_ref[...] = dims(chosen, x_ref[...], 1, 0).astype(BF16)
    uo_ref[...] = dims(chosen, u_ref[...], 1, 0).astype(BF16)


def dispatch(slot, normed, upstream, slots):
    pairs, _, width = slot.shape
    model = normed.shape[1]
    return pl.pallas_call(
        dispatch_kernel,
        grid=(pairs,),
        in_specs=[
            pl.BlockSpec((1, 1, width), lambda i: (i, 0, 0)),
            pl.BlockSpec((width, model), lambda i: (i, 0)),
            pl.BlockSpec((width, model), lambda i: (i, 0)),
        ],
        out_specs=[pl.BlockSpec((slots, model), lambda i: (i, 0))] * 2,
        out_shape=[jax.ShapeDtypeStruct((pairs * slots, model), BF16)] * 2,
        compiler_params=pltpu.CompilerParams(vmem_limit_bytes=40 * 2**20),
        cost_estimate=pl.CostEstimate(flops=2 * 10**9, bytes_accessed=65 * 10**6, transcendentals=0),
        name="dispatch",
    )(slot, normed, upstream)


def combine_kernel(slot_ref, r_ref, o_ref):
    chosen = jnp.where(hits(slot_ref, r_ref.shape[0]), 1.0, 0.0).astype(BF16)
    o_ref[...] = dims(chosen, r_ref[...], 0, 0).astype(BF16)


def combine(slot, rows, slots):
    pairs, _, width = slot.shape
    model = rows.shape[1]
    return pl.pallas_call(
        combine_kernel,
        grid=(pairs,),
        in_specs=[
            pl.BlockSpec((1, 1, width), lambda i: (i, 0, 0)),
            pl.BlockSpec((slots, model), lambda i: (i, 0)),
        ],
        out_specs=pl.BlockSpec((width, model), lambda i: (i, 0)),
        out_shape=jax.ShapeDtypeStruct((pairs * width, model), BF16),
        compiler_params=pltpu.CompilerParams(vmem_limit_bytes=40 * 2**20),
        cost_estimate=pl.CostEstimate(flops=10**9, bytes_accessed=33 * 10**6, transcendentals=0),
        name="combine",
    )(slot, rows)


SLOTS = 80


def order_of(i):
    return jnp.where(i < 2, i, 5 - i)


def far_first(i):
    return jnp.where(i == 0, 2, jnp.where(i == 3, 0, 2 * i - 1))


def greet_all():
    me = lax.axis_index("dev")
    barrier = pltpu.get_barrier_semaphore()

    def signal(d, _):
        pl.semaphore_signal(barrier, inc=1, device_id=(lax.rem(me + d, 32),), device_id_type=MESH)
        return 0
    lax.fori_loop(1, 32, signal, 0)
    pl.semaphore_wait(barrier, 31)


class Swap:
    def __init__(self, source, into, ss, rs):
        self.me = lax.axis_index("dev")
        self.source, self.into, self.ss, self.rs = source, into, ss, rs

    def copy(self, d):
        target = lax.rem(self.me + d, 32)
        return pltpu.make_async_remote_copy(
            src_ref=self.source(target), dst_ref=self.into.at[self.me], send_sem=self.ss.at[d], recv_sem=self.rs.at[d],
            device_id=(target,), device_id_type=MESH)

    def start(self):
        def one(d, _):
            self.copy(d).start()
            return 0
        lax.fori_loop(1, 32, one, 0)
        self.into[self.me] = self.source(self.me)[...]

    def wait_recv(self):
        def one(d, _):
            self.copy(d).wait_recv()
            return 0
        lax.fori_loop(1, 32, one, 0)

    def wait_send(self):
        def one(d, _):
            self.copy(d).wait_send()
            return 0
        lax.fori_loop(1, 32, one, 0)


def in_plane(y, x, c):
    return (y * 2 + x) * 2 + c


def chosen_rows(slots_ref, block, expert):
    row = slots_ref[block, pl.ds(expert, 1), :]
    return row == lax.broadcasted_iota(jnp.int32, (SLOTS, row.shape[1]), 0).astype(F32)


def experts_kernel(
    x_ref, gates_ref, slots_ref, u_ref, wg_ref, wu_ref, wd_ref,
    xi_out, ui_out, dx_out, y_out, hg_ref, dg_ref, du_ref, gg_ref,
    gates, land, stage, xi, ubuf, ui_buf, dx_buf, y_buf,
    gs, gr, zs, zr, fs, fr, cs, cr, own_sem, usem, xsem, osem,
):
    z, y, x, c = place()
    rows, model = x_ref.shape
    half = model // 2
    sibling = number(z, y, x, 1 - c)
    greet_all()
    swap = Swap(lambda t: gates_ref.at[t], gates, gs, gr)
    cols = [pl.ds(0, half), pl.ds(half, half)]
    beside = [number(z, 1 - y, x, c), number(z, y, 1 - x, c)]
    across = [(y, 1 - x), (1 - y, x)]

    def to_z(p, d):
        return pltpu.make_async_remote_copy(
            src_ref=x_ref.at[:, cols[p]], dst_ref=land.at[p, 0, d], send_sem=zs.at[p, d], recv_sem=zr.at[p, d],
            device_id=(number(lax.rem(z + d, 4), y, x, c),), device_id_type=MESH)

    def hop(p, k):
        return pltpu.make_async_remote_copy(
            src_ref=land.at[p, 0, k], dst_ref=land.at[p, 1, k], send_sem=fs.at[p, k], recv_sem=fr.at[p, k],
            device_id=(beside[p],), device_id_type=MESH)

    def block_of(p, h, k, yy, xx, cc):
        zz = lax.rem(z + 4 - k, 4)
        if p == 0:
            return number(zz, (1 - yy) if h else yy, xx, cc)
        return number(zz, yy, (1 - xx) if h else xx, cc)

    def served(p, h, k, t):
        block = block_of(p, h, k, y, x, c)
        ay, ax = across[p]
        target = [number(z, y, x, 1 - c), number(z, ay, ax, c), number(z, ay, ax, 1 - c)][t]
        return pltpu.make_async_remote_copy(
            src_ref=stage.at[p, h, k, t],
            dst_ref=xi.at[pl.ds(pl.multiple_of(block * SLOTS, 16), SLOTS), cols[p]],
            send_sem=cs.at[p, h, k, t], recv_sem=cr.at[p, h, k, t], device_id=(target,), device_id_type=MESH)

    def serve(p, h, k):
        block = block_of(p, h, k, y, x, c)
        source = land[p, h, k]
        ay, ax = across[p]
        for t, expert in enumerate([in_plane(y, x, 1 - c), in_plane(ay, ax, c), in_plane(ay, ax, 1 - c), in_plane(y, x, c)]):
            chosen = jnp.where(chosen_rows(slots_ref, block, expert), 1.0, 0.0).astype(BF16)
            got = dims(chosen, source, 1, 0).astype(BF16)
            if t < 3:
                stage[p, h, k, t] = got
                served(p, h, k, t).start()
            else:
                xi[pl.ds(pl.multiple_of(block * SLOTS, 16), SLOTS), cols[p]] = got

    own = [pltpu.make_async_copy(x_ref.at[:, cols[p]], land.at[p, 0, 0], own_sem.at[p]) for p in range(2)]
    for p in range(2):
        own[p].start()
    for d in (1, 3, 2):
        for p in range(2):
            to_z(p, d).start()

    def chip_of(u):
        group, k = u // 4, order_of(lax.rem(u, 4))
        dy, dx = lax.rem(group, 2), group // 2
        zz = lax.rem(z + 4 - k, 4)
        yy = jnp.where(dy == 1, 1 - y, y)
        xx = jnp.where(dx == 1, 1 - x, x)
        return (zz * 2 + yy) * 2 + xx

    def load_up(u):
        at = pl.ds(pl.multiple_of(chip_of(u) * 2 * rows, 16), 2 * rows)
        return pltpu.make_async_copy(u_ref.at[at, :], ubuf.at[lax.rem(u, 2)], usem.at[lax.rem(u, 2)])

    load_up(0).start()
    swap.start()
    for p in range(2):
        own[p].wait()
        hop(p, 0).start()

    def first_stage(i, _):
        k = order_of(i)
        for p in range(2):
            @pl.when(i > 0)
            def _(p=p):
                to_z(p, k).wait_recv()
                hop(p, k).start()
            serve(p, 0, k)
        return 0
    lax.fori_loop(0, 4, first_stage, 0)
    swap.wait_recv()

    def store(n, buf, out, u):
        at = pl.ds(pl.multiple_of(chip_of(u) * 2 * SLOTS, 16), 2 * SLOTS)
        return pltpu.make_async_copy(buf.at[lax.rem(u, 2)], out.at[at, :], osem.at[n, lax.rem(u, 2)])

    def stores(u):
        return [store(0, ui_buf, ui_out, u), store(1, dx_buf, dx_out, u), store(2, y_buf, y_out, u)]

    def keep(u):
        at = pl.ds(pl.multiple_of(chip_of(u) * 2 * SLOTS, 16), 2 * SLOTS)
        return pltpu.make_async_copy(xi.at[at, :], xi_out.at[at, :], xsem.at[u])

    def unit(u, _):
        group, k = u // 4, order_of(lax.rem(u, 4))
        slot = lax.rem(u, 2)
        chip = chip_of(u)

        @pl.when(u < 15)
        def _():
            load_up(u + 1).start()

        @pl.when(group == 0)
        def _():
            for p in range(2):
                hop(p, k).wait_recv()
                serve(p, 1, k)
            for p in range(2):
                served(p, 0, k, 0).wait_recv()

        @pl.when(group == 1)
        def _():
            served(0, 1, k, 0).wait_recv()
            served(1, 0, k, 1).wait_recv()
            served(1, 0, k, 2).wait_recv()

        @pl.when(group == 2)
        def _():
            served(1, 1, k, 0).wait_recv()
            served(0, 0, k, 1).wait_recv()
            served(0, 0, k, 2).wait_recv()

        @pl.when(group == 3)
        def _():
            for p in range(2):
                served(p, 1, k, 1).wait_recv()
                served(p, 1, k, 2).wait_recv()

        @pl.when(u >= 2)
        def _():
            for s in stores(u - 2):
                s.wait()

        load_up(u).wait()
        at = pl.ds(pl.multiple_of(chip * 2 * SLOTS, 16), 2 * SLOTS)
        expert = in_plane(y, x, c)
        picks, gate, up_rows = [], [], []
        for core in range(2):
            block = chip * 2 + core
            hit = chosen_rows(slots_ref, block, expert)
            picks.append(hit)
            gate_row = jnp.concatenate([gates[block, 0:1, :], gates[block, 1:2, :]], axis=1)
            gate.append(jnp.sum(jnp.where(hit, gate_row, 0.0), axis=1, keepdims=True))
            up_rows.append(
                dims(jnp.where(hit, 1.0, 0.0).astype(BF16), ubuf[slot, core * rows : (core + 1) * rows, :], 1, 0).astype(BF16)
            )
        gate_of_slot = jnp.concatenate(gate, axis=0)
        ui = jnp.concatenate(up_rows, axis=0)
        ui_buf[slot] = ui
        hidden_up = dims(ui, wd_ref[...], 1, 1)
        rows_in = xi[at, :]
        gate_in = dims(rows_in, wg_ref[...], 1, 0)
        up_in = dims(rows_in, wu_ref[...], 1, 0)
        sig = 1.0 / (1.0 + jnp.exp(-gate_in))
        silu = gate_in * sig
        hidden = (silu * up_in).astype(BF16).astype(F32)
        gated = (hidden * gate_of_slot).astype(BF16)
        hidden_grad = hidden_up * gate_of_slot
        gate_back = (hidden_grad * up_in * sig * (1.0 + gate_in * (1.0 - sig))).astype(BF16)
        up_back = (hidden_grad * silu).astype(BF16)
        hg_ref[at, :] = gated
        dg_ref[at, :] = gate_back
        du_ref[at, :] = up_back
        dx_buf[slot] = (dims(gate_back, wg_ref[...], 1, 1) + dims(up_back, wu_ref[...], 1, 1)).astype(BF16)
        y_buf[slot] = dims(gated, wd_ref[...], 1, 0).astype(BF16)
        gate_grad = jnp.sum(hidden * hidden_up, axis=1, keepdims=True)
        for core in range(2):
            block = chip * 2 + core
            row = jnp.sum(jnp.where(picks[core], gate_grad[core * SLOTS : (core + 1) * SLOTS], 0.0), axis=0, keepdims=True)
            gg_ref[block, 0:1, :] = row[:, :128]
            gg_ref[block, 1:2, :] = row[:, 128:]
        for s in stores(u):
            s.start()
        keep(u).start()
        return 0

    lax.fori_loop(0, 16, unit, 0)
    for u in (14, 15):
        for s in stores(u):
            s.wait()

    def last(u, _):
        keep(u).wait()
        return 0
    lax.fori_loop(0, 16, last, 0)

    def sent(k, _):
        for p in range(2):
            hop(p, k).wait_send()

            @pl.when(k > 0)
            def _(p=p):
                to_z(p, k).wait_send()
            for h in range(2):
                for t in range(3):
                    served(p, h, k, t).wait_send()
        return 0
    lax.fori_loop(0, 4, sent, 0)
    swap.wait_send()


def run_experts(normed, gates, slots, upstream, gate_weight, up_weight, down_weight):
    rows, model = normed.shape
    ff = gate_weight.shape[1]
    half = model // 2
    n = 32 * SLOTS
    hbm, vmem = pl.BlockSpec(memory_space=pl.ANY), pl.BlockSpec(memory_space=pltpu.VMEM)
    dma = pltpu.SemaphoreType.DMA
    long = jax.ShapeDtypeStruct((n, model), BF16)
    short = jax.ShapeDtypeStruct((n, ff), BF16)
    return pl.pallas_call(
        experts_kernel,
        in_specs=[hbm, vmem, vmem, hbm, vmem, vmem, vmem],
        out_specs=[hbm] * 4 + [vmem] * 4,
        out_shape=[long] * 4 + [short] * 3 + [jax.ShapeDtypeStruct((32, 8, 128), F32)],
        scratch_shapes=[
            pltpu.VMEM((32, 8, 128), F32),
            pltpu.VMEM((2, 2, 4, rows, half), BF16),
            pltpu.VMEM((2, 2, 4, 3, SLOTS, half), BF16),
            pltpu.VMEM((n, model), BF16),
            pltpu.VMEM((2, 2 * rows, model), BF16),
            pltpu.VMEM((2, 2 * SLOTS, model), BF16),
            pltpu.VMEM((2, 2 * SLOTS, model), BF16),
            pltpu.VMEM((2, 2 * SLOTS, model), BF16),
            dma((32,)), dma((32,)), dma((2, 4)), dma((2, 4)), dma((2, 4)), dma((2, 4)),
            dma((2, 2, 4, 3)), dma((2, 2, 4, 3)), dma((2,)), dma((2,)), dma((16,)), dma((3, 2)),
        ],
        compiler_params=pltpu.CompilerParams(collective_id=13, has_side_effects=True, vmem_limit_bytes=56 * 2**20),
        name="experts",
    )(normed, gates, slots, upstream, gate_weight, up_weight, down_weight)


class Back:
    scratch = staticmethod(lambda rows, half: [
        pltpu.VMEM((2, 2, 4, SLOTS, half), BF16),
        pltpu.VMEM((2, 3, 2, 4, SLOTS, half), BF16),
        pltpu.VMEM((2, 4, rows, half), BF16),
        pltpu.VMEM((2, 4, rows, half), BF16),
        pltpu.VMEM((2, 4, rows, half), BF16),
        pltpu.VMEM((2, 4, rows, half), BF16),
        pltpu.SemaphoreType.DMA((2, 2, 4)),
        pltpu.SemaphoreType.DMA((2, 3, 2, 4)), pltpu.SemaphoreType.DMA((2, 3, 2, 4)),
        pltpu.SemaphoreType.DMA((2, 4)), pltpu.SemaphoreType.DMA((2, 4)),
        pltpu.SemaphoreType.DMA((2, 4)), pltpu.SemaphoreType.DMA((2, 4)),
    ])
    n_scratch = 13

    def __init__(self, rows_ref, slots_ref, o_ref, scratch):
        self.rows_ref, self.slots_ref, self.o_ref = rows_ref, slots_ref, o_ref
        (self.own, self.rin, self.sout, self.rb, self.zout, self.rz,
         self.own_sem, self.ts, self.tr, self.bs, self.br, self.zs, self.zr) = scratch
        self.z, self.y, self.x, self.c = place()
        half = rows_ref.shape[1] // 2
        self.cols = [pl.ds(0, half), pl.ds(half, half)]

    def block(self, p, h, k, yy, xx, cc):
        zz = lax.rem(self.z + k, 4)
        if p == 0:
            return number(zz, (1 - yy) if h else yy, xx, cc)
        return number(zz, yy, (1 - xx) if h else xx, cc)

    def sources(self, p):
        y, x, c = self.y, self.x, self.c
        ay, ax = (y, 1 - x) if p == 0 else (1 - y, x)
        return [(y, x, 1 - c), (ay, ax, c), (ay, ax, 1 - c)]

    def slot_rows(self, block, p):
        return self.rows_ref.at[pl.ds(pl.multiple_of(block * SLOTS, 16), SLOTS), self.cols[p]]

    def to(self, p, t, h, k):
        place_of = self.sources(p)[t]
        return pltpu.make_async_remote_copy(
            src_ref=self.slot_rows(self.block(p, h, k, *place_of), p), dst_ref=self.rin.at[p, t, h, k],
            send_sem=self.ts.at[p, t, h, k], recv_sem=self.tr.at[p, t, h, k],
            device_id=(number(self.z, *place_of),), device_id_type=MESH)

    def mine(self, p, h, k):
        return pltpu.make_async_copy(
            self.slot_rows(self.block(p, h, k, self.y, self.x, self.c), p), self.own.at[p, h, k], self.own_sem.at[p, h, k])

    def second(self, p, k):
        z, y, x, c = self.z, self.y, self.x, self.c
        target = number(z, 1 - y, x, c) if p == 0 else number(z, y, 1 - x, c)
        return pltpu.make_async_remote_copy(
            src_ref=self.sout.at[p, k], dst_ref=self.rb.at[p, k], send_sem=self.bs.at[p, k], recv_sem=self.br.at[p, k],
            device_id=(target,), device_id_type=MESH)

    def third(self, p, k):
        target = number(lax.rem(self.z + k, 4), self.y, self.x, self.c)
        return pltpu.make_async_remote_copy(
            src_ref=self.zout.at[p, k], dst_ref=self.rz.at[p, k], send_sem=self.zs.at[p, k], recv_sem=self.zr.at[p, k],
            device_id=(target,), device_id_type=MESH)

    def start(self):
        for h in (1, 0):
            def one(i, _, h=h):
                k = far_first(i)
                for p in range(2):
                    for t in (1, 2, 0):
                        self.to(p, t, h, k).start()
                    self.mine(p, h, k).start()
                return 0
            lax.fori_loop(0, 4, one, 0)

    def dense(self, p, h, k):
        self.mine(p, h, k).wait()
        for t in range(3):
            self.to(p, t, h, k).wait_recv()
        block = self.block(p, h, k, self.y, self.x, self.c)
        total = None
        for t, who in enumerate([(self.y, self.x, self.c)] + self.sources(p)):
            hit = chosen_rows(self.slots_ref, block, in_plane(*who))
            chosen = jnp.where(hit, 1.0, 0.0).astype(BF16)
            values = self.own[p, h, k] if t == 0 else self.rin[p, t - 1, h, k]
            term = dims(chosen, values, 0, 0)
            total = term if total is None else total + term
        return total

    def step(self, u):
        k = far_first(lax.rem(u, 4))

        @pl.when(u < 4)
        def _():
            for p in range(2):
                self.sout[p, k] = self.dense(p, 1, k).astype(BF16)
                self.second(p, k).start()

        @pl.when(u >= 4)
        def _():
            for p in range(2):
                total = self.dense(p, 0, k)
                self.second(p, k).wait_recv()
                total = total + self.rb[p, k].astype(F32)

                @pl.when(k > 0)
                def _(p=p, total=total):
                    self.zout[p, k] = total.astype(BF16)
                    self.third(p, k).start()

                @pl.when(k == 0)
                def _(p=p, total=total):
                    self.o_ref[:, self.cols[p]] = total

    def finish(self):
        for p in range(2):
            for k in range(1, 4):
                self.third(p, k).wait_recv()
            self.o_ref[:, self.cols[p]] += (
                self.rz[p, 1].astype(F32) + self.rz[p, 2].astype(F32) + self.rz[p, 3].astype(F32)
            )

        def one(k, _):
            for p in range(2):
                self.second(p, k).wait_send()

                @pl.when(k > 0)
                def _(p=p):
                    self.third(p, k).wait_send()
                for t in range(3):
                    for h in range(2):
                        self.to(p, t, h, k).wait_send()
            return 0
        lax.fori_loop(0, 4, one, 0)


def grads_kernel(
    dx_ref, slots_ref, gg_ref, xi_ref, ui_ref, hg_ref, dg_ref, du_ref,
    o_ref, back_ref, wg_out, wu_out, wd_out, xcol, ucol, gout, uout, dout, gs, gr, isem, osem, *scratch,
):
    greet_all()
    swap = Swap(lambda t: gg_ref.at[t], back_ref, gs, gr)
    rs = Back(dx_ref, slots_ref, o_ref, scratch)
    rs.start()
    swap.start()

    def col(i):
        return pl.ds(pl.multiple_of(i * 256, 256), 256)

    def loads(i):
        s = lax.rem(i, 2)
        return [
            pltpu.make_async_copy(xi_ref.at[:, col(i)], xcol.at[s], isem.at[0, s]),
            pltpu.make_async_copy(ui_ref.at[:, col(i)], ucol.at[s], isem.at[1, s]),
        ]

    def stores(i):
        s = lax.rem(i, 2)
        return [
            pltpu.make_async_copy(gout.at[s], wg_out.at[col(i), :], osem.at[0, s]),
            pltpu.make_async_copy(uout.at[s], wu_out.at[col(i), :], osem.at[1, s]),
            pltpu.make_async_copy(dout.at[s], wd_out.at[:, col(i)], osem.at[2, s]),
        ]

    for cp in loads(0):
        cp.start()

    def one(u, _):
        @pl.when(u < 6)
        def _():
            s = lax.rem(u, 2)

            @pl.when(u < 5)
            def _():
                for cp in loads(u + 1):
                    cp.start()

            for cp in loads(u):
                cp.wait()

            @pl.when(u >= 2)
            def _():
                for cp in stores(u - 2):
                    cp.wait()

            rows_in = xcol[s]
            gout[s] = dims(rows_in, dg_ref[...], 0, 0)
            uout[s] = dims(rows_in, du_ref[...], 0, 0)
            dout[s] = dims(hg_ref[...], ucol[s], 0, 0)
            for cp in stores(u):
                cp.start()

        rs.step(u)
        return 0

    lax.fori_loop(0, 8, one, 0)
    for i in (4, 5):
        for cp in stores(i):
            cp.wait()
    swap.wait_recv()
    rs.finish()
    swap.wait_send()


def run_grads(dx, slots, gg, xi, ui, hg, dg, du):
    rows, model = slots.shape[2], dx.shape[1]
    ff = hg.shape[1]
    n = dx.shape[0]
    hbm, vmem = pl.BlockSpec(memory_space=pl.ANY), pl.BlockSpec(memory_space=pltpu.VMEM)
    dma = pltpu.SemaphoreType.DMA
    return pl.pallas_call(
        grads_kernel,
        in_specs=[hbm, vmem, vmem, hbm, hbm, vmem, vmem, vmem],
        out_specs=[vmem, vmem, hbm, hbm, hbm],
        out_shape=[
            jax.ShapeDtypeStruct((rows, model), F32),
            jax.ShapeDtypeStruct((32, 8, 128), F32),
            jax.ShapeDtypeStruct((model, ff), F32),
            jax.ShapeDtypeStruct((model, ff), F32),
            jax.ShapeDtypeStruct((ff, model), F32),
        ],
        scratch_shapes=[
            pltpu.VMEM((2, n, 256), BF16), pltpu.VMEM((2, n, 256), BF16),
            pltpu.VMEM((2, 256, ff), F32), pltpu.VMEM((2, 256, ff), F32), pltpu.VMEM((2, ff, 256), F32),
            dma((32,)), dma((32,)), dma((2, 2)), dma((3, 2)),
        ] + Back.scratch(rows, model // 2),
        compiler_params=pltpu.CompilerParams(collective_id=14, has_side_effects=True, vmem_limit_bytes=56 * 2**20),
        name="grads",
    )(dx, slots, gg, xi, ui, hg, dg, du)


def attend_back_mesh_kernel(
    chunks, rows, lo_ref, cos_ref, sin_ref, q_ref, kv_ref, g_ref, lse_ref, delta_ref, y_ref, slots_ref,
    dq_ref, dkv_ref, o_ref, bias, *scratch,
):
    greet_all()
    rs = Back(y_ref, slots_ref, o_ref, scratch)
    rs.start()
    make_bias(bias, lo_ref, chunks, rows)
    width = 2 * GROUP * HEAD_DIM

    def pair(j, _):
        lanes = pl.ds(pl.multiple_of(j * 2 * HEAD_DIM, 2 * HEAD_DIM), 2 * HEAD_DIM)
        head = pl.ds(pl.multiple_of(j * width, width), width)

        def between(half):
            rs.step(2 * j + half)

        attend_back_pair(
            chunks, rows, lax.rem(lax.axis_index("dev"), 2), cos_ref, sin_ref, q_ref.at[head, :], kv_ref.at[:, :, lanes], g_ref.at[head, :],
            lse_ref.at[pl.ds(j, 1)], delta_ref.at[pl.ds(j, 1)], dq_ref.at[head, :], dkv_ref.at[:, :, lanes], bias, between,
        )
        return 0

    lax.fori_loop(0, KEY_HEADS // 2, pair, 0)
    rs.finish()


def attend_back_mesh(query_t, window, lo, grad_t, lse, delta, cos_t, sin_t, y, slots):
    rows, span = query_t.shape[1], window.shape[1]
    chunks = span // rows - 1
    model = y.shape[1]
    hbm, vmem = pl.BlockSpec(memory_space=pl.ANY), pl.BlockSpec(memory_space=pltpu.VMEM)
    return pl.pallas_call(
        functools.partial(attend_back_mesh_kernel, chunks, rows),
        in_specs=[vmem] * 8 + [hbm, vmem],
        out_specs=[vmem] * 3,
        out_shape=[
            jax.ShapeDtypeStruct(query_t.shape, BF16),
            jax.ShapeDtypeStruct(window.shape, BF16),
            jax.ShapeDtypeStruct((rows, model), F32),
        ],
        scratch_shapes=[pltpu.VMEM((chunks * rows, rows), F32)] + Back.scratch(rows, model // 2),
        compiler_params=pltpu.CompilerParams(collective_id=15, has_side_effects=True, vmem_limit_bytes=56 * 2**20),
        name="attend_back",
    )(lo, cos_t, sin_t, query_t, window, grad_t, lse, delta, y, slots)


def rms_scale(values):
    return lax.rsqrt(jnp.mean(values * values, axis=-1, keepdims=True) + EPSILON)


def rotate_t(values, cosine, sine):
    half = cosine.shape[0]
    shaped = values.reshape(-1, 2, half, values.shape[1])
    u, w = shaped[:, 0], shaped[:, 1]
    turned = jnp.stack([u * cosine - w * sine, w * cosine + u * sine], axis=1)
    return turned.reshape(values.shape)


def gathered(block, cid, by_rows):
    if meshed():
        return gather_all(block, cid, by_rows)
    return lax.all_gather(block, "dev", axis=0, tiled=True)


def reduced(dense, cid, by_rows):
    if meshed():
        return reduce_all(dense, cid, by_rows)
    return lax.psum_scatter(dense, "dev", scatter_dimension=0, tiled=True).astype(F32)


def on_device(
    tokens,
    positions,
    expert_picks,
    priority,
    first_gain,
    query_weight,
    key_projection_matrix,
    value_projection_matrix,
    output_weight,
    second_gain,
    router_weight,
    gate_weight,
    up_weight,
    down_weight,
    cotangent,
):
    devices = lax.axis_size("dev")
    rows, model = tokens.shape
    split = devices // EXPERTS
    capacity = split * ((9 * rows * TOP + 8 * EXPERTS * split - 1) // (8 * EXPERTS * split))
    weight_rows = query_weight.shape[0]

    all_upstream = lax.all_gather(cotangent, "dev", axis=0, tiled=True)
    output_matrix = lax.all_gather(output_weight, "dev", axis=0, tiled=True)

    extra = jnp.concatenate([router_weight, first_gain[:, None], second_gain[:, None]], axis=1)
    pad = (-extra.shape[1]) % 128
    packed = jnp.concatenate(
        [query_weight, key_projection_matrix, value_projection_matrix, extra, jnp.zeros((weight_rows, pad), BF16)],
        axis=1,
    )
    matrices = gathered(packed, 1, False)
    qkv_matrix = matrices[:, :QKV]
    router_matrix = matrices[:, QKV : QKV + EXPERTS]
    gain_first = matrices[:, QKV + EXPERTS].astype(F32)
    gain_second = matrices[:, QKV + EXPERTS + 1].astype(F32)

    one_hot = expert_picks[:, :, None] == jnp.arange(EXPERTS, dtype=jnp.int32)
    picked_any = jnp.any(one_hot, axis=1)
    turn = jnp.sum(jnp.where(one_hot, priority[:, :, None], 0), axis=1)
    turn = jnp.where(picked_any, turn, jnp.int32(2**30)).T
    rank = jnp.sum((turn[:, None, :] < turn[:, :, None]).astype(jnp.int32), axis=2)
    slot_rows = jnp.where(picked_any.T & (rank < capacity), rank, -1).astype(F32)

    inputs = tokens.astype(F32)
    scale_one = rms_scale(inputs)
    normed_one = (inputs * scale_one * gain_first).astype(BF16)
    half_dim = HEAD_DIM // 2
    frequency = jnp.power(10000.0, -(jnp.arange(half_dim, dtype=F32) * 2.0) / HEAD_DIM)
    angle = positions.astype(F32)[None, :] * frequency[:, None]
    cos_t, sin_t = jnp.cos(angle), jnp.sin(angle)
    qkv_t = dims(qkv_matrix, normed_one, 0, 1)
    q_width, k_width = QUERY_HEADS * HEAD_DIM, KEY_HEADS * HEAD_DIM
    query_t = rotate_t(qkv_t[:q_width], cos_t, sin_t).astype(BF16) * BF16(HEAD_DIM**-0.5)
    key = rotate_t(qkv_t[q_width : q_width + k_width], cos_t, sin_t).astype(BF16).T
    value = qkv_t[q_width + k_width :].astype(BF16).T
    window, offset, plane_slots = window_of(jnp.stack([key, value]), slot_rows.reshape(-1, 8, rows))
    lo = (jnp.arange(rows, dtype=jnp.int32) - positions)[None, :]
    attended_t, lse = attend(query_t, window, offset, lo)
    residual = inputs + dims(attended_t, output_matrix, 0, 0)
    scale_two = rms_scale(residual)
    normed_two = (residual * scale_two * gain_second).astype(BF16)

    logits = dims(normed_two, router_matrix, 1, 0)
    logits = jnp.where(picked_any, logits, MASKED)
    picked_exp = jnp.exp(logits - jnp.max(logits, axis=1, keepdims=True))
    gates = picked_exp / jnp.sum(picked_exp, axis=1, keepdims=True)

    if meshed():
        gate_rows = jnp.pad(gates.T.reshape(EXPERTS, rows // 128, 128), ((0, 0), (0, 8 - rows // 128), (0, 0)))
        expert_in, expert_up, grad_rows, out_rows, gated_hidden, gate_in_grad, up_in_grad, gate_grad_rows = run_experts(
            normed_two, gate_rows, plane_slots, all_upstream, gate_weight, up_weight, down_weight
        )
        returned_grad, gate_grad, gate_gradient, up_gradient, down_gradient = run_grads(
            grad_rows, plane_slots, gate_grad_rows, expert_in, expert_up, gated_hidden, gate_in_grad, up_in_grad
        )
        gate_grad = gate_grad[:, : rows // 128].reshape(EXPERTS, rows).T
    else:
        gate_rows, slot = (
            lax.all_to_all(jnp.repeat(v, split, axis=0), "dev", split_axis=0, concat_axis=0, tiled=True)
            for v in (gates.T, slot_rows)
        )
        pair_slot = jnp.where(
            slot.reshape(devices // 2, 2, rows) >= 0,
            slot.reshape(devices // 2, 2, rows) + jnp.array([[0], [capacity]], F32),
            -1.0,
        ).astype(jnp.int32).reshape(devices // 2, 1, 2 * rows)
        all_normed = lax.all_gather(normed_two, "dev", axis=0, tiled=True)
        expert_in, expert_up = dispatch(pair_slot, all_normed, all_upstream, 2 * capacity)
        slot_hit = slot[:, None, :] == jnp.arange(capacity, dtype=F32)[None, :, None]
        gate_of_slot = jnp.sum(jnp.where(slot_hit, gate_rows[:, None, :], 0.0), axis=2).reshape(-1, 1)
        gate_in = dims(expert_in, gate_weight, 1, 0)
        up_in = dims(expert_in, up_weight, 1, 0)
        sigmoid_gate = 1.0 / (1.0 + jnp.exp(-gate_in))
        silu_gate = gate_in * sigmoid_gate
        hidden = (silu_gate * up_in).astype(BF16)
        gated_hidden = (hidden.astype(F32) * gate_of_slot).astype(BF16)
        hidden_up = dims(expert_up, down_weight, 1, 1)
        hidden_grad = hidden_up * gate_of_slot
        gate_grad_slot = jnp.sum(hidden.astype(F32) * hidden_up, axis=1).reshape(devices, capacity)
        gate_in_grad = (hidden_grad * up_in * sigmoid_gate * (1.0 + gate_in * (1.0 - sigmoid_gate))).astype(BF16)
        up_in_grad = (hidden_grad * silu_gate).astype(BF16)
        partial_in = (dims(gate_in_grad, gate_weight, 1, 1) + dims(up_in_grad, up_weight, 1, 1)).astype(BF16)
        gate_grad_rows = jnp.sum(jnp.where(slot_hit, gate_grad_slot[:, :, None], 0.0), axis=1)
        returned_grad = lax.psum_scatter(
            combine(pair_slot, partial_in, 2 * capacity), "dev", scatter_dimension=0, tiled=True
        ).astype(F32)
        gate_grad = lax.all_to_all(gate_grad_rows, "dev", split_axis=0, concat_axis=0, tiled=True)
        gate_grad = jnp.sum(gate_grad.reshape(EXPERTS, split, rows), axis=1).T
        partial_out = dims(gated_hidden, down_weight, 1, 0).astype(BF16)
        dense_out = combine(pair_slot, partial_out, 2 * capacity)
        mixture = lax.psum_scatter(dense_out, "dev", scatter_dimension=0, tiled=True).astype(F32)
        down_gradient = dims(gated_hidden, expert_up, 0, 0)
        gate_gradient = dims(expert_in, gate_in_grad, 0, 0)
        up_gradient = dims(expert_in, up_in_grad, 0, 0)

    upstream = cotangent.astype(F32)
    logit_grad = (gates * (gate_grad - jnp.sum(gates * gate_grad, axis=1, keepdims=True))).astype(BF16)
    router_gradient = dims(normed_two, logit_grad, 0, 0)
    normed_two_grad = returned_grad + dims(logit_grad, router_matrix, 1, 1)
    weighted_two = normed_two_grad * gain_second
    second_gain_grad = jnp.sum(normed_two_grad * residual * scale_two, axis=0)
    residual_grad = (
        upstream
        + scale_two * weighted_two
        - residual * scale_two**3 * jnp.mean(weighted_two * residual, axis=-1, keepdims=True)
    )
    branch_grad = residual_grad.astype(BF16)
    output_gradient = dims(attended_t, branch_grad, 1, 0).astype(BF16)
    output_gradient = lax.psum_scatter(output_gradient, "dev", scatter_dimension=0, tiled=True).astype(F32)
    grad_t = dims(output_matrix, branch_grad, 1, 1).astype(BF16)

    delta = jnp.sum((attended_t.astype(F32) * grad_t.astype(F32)).reshape(QUERY_HEADS, HEAD_DIM, rows), axis=1)
    delta = jnp.pad(delta.reshape(KEY_HEADS // 2, 2 * GROUP, rows), ((0, 0), (0, 8 - 2 * GROUP), (0, 0)))
    if meshed():
        query_grad_t, window_grad, mixture = attend_back_mesh(
            query_t, window, lo, grad_t, lse, delta, cos_t, sin_t, out_rows, plane_slots
        )
    else:
        query_grad_t, window_grad = attend_back(query_t, window, offset, lo, grad_t, lse, delta, cos_t, sin_t)
    layer_output = (residual + mixture).astype(BF16)
    key_grad, value_grad = unwindow(window_grad)
    key_grad_t = rotate_t(key_grad.T, cos_t, -sin_t).astype(BF16)
    qkv_grad_t = jnp.concatenate([query_grad_t, key_grad_t, value_grad.T.astype(BF16)], axis=0)
    qkv_gradient = dims(normed_one, qkv_grad_t, 0, 1)
    normed_one_grad = dims(qkv_grad_t, qkv_matrix, 0, 1)
    weighted_one = normed_one_grad * gain_first
    first_gain_grad = jnp.sum(normed_one_grad * inputs * scale_one, axis=0)
    tokens_gradient = (
        residual_grad
        + scale_one * weighted_one
        - inputs * scale_one**3 * jnp.mean(weighted_one * inputs, axis=-1, keepdims=True)
    )
    terms = jnp.concatenate(
        [qkv_gradient, router_gradient, first_gain_grad[:, None], second_gain_grad[:, None],
         jnp.zeros((model, (-(QKV + EXPERTS + 2)) % 256), F32)],
        axis=1,
    ).astype(BF16)
    sums = reduced(terms, 4, False)
    return (
        layer_output,
        tokens_gradient,
        sums[:, QKV + EXPERTS],
        sums[:, :q_width],
        sums[:, q_width : q_width + k_width],
        sums[:, q_width + k_width : QKV],
        output_gradient,
        sums[:, QKV + EXPERTS + 1],
        sums[:, QKV : QKV + EXPERTS],
        gate_gradient,
        up_gradient,
        down_gradient,
    )


def solution(mesh):
    rows, whole = P("dev", None), P("dev")
    columns = P(None, "dev")
    return jax.shard_map(
        on_device,
        mesh=mesh,
        in_specs=(rows, whole, rows, rows, whole, rows, rows, rows, rows, whole, rows, columns, columns, rows, rows),
        out_specs=(rows, rows, whole, rows, rows, rows, rows, whole, rows, columns, columns, rows),
        check_vma=False,
    )
```

```python
import functools
import jax, jax.numpy as jnp
from jax import lax
from jax.experimental import pallas as pl
from jax.experimental.pallas import tpu as pltpu

MESH = pl.DeviceIdType.MESH


def place():
    me = lax.axis_index("dev")
    return lax.rem(me // 8, 4), lax.rem(me // 4, 2), lax.rem(me // 2, 2), lax.rem(me, 2)


def number(z, y, x, c):
    return ((z * 2 + y) * 2 + x) * 2 + c


def greet(partners):
    barrier = pltpu.get_barrier_semaphore()
    for partner in partners:
        pl.semaphore_signal(barrier, inc=1, device_id=(partner,), device_id_type=MESH)
    pl.semaphore_wait(barrier, len(partners))


def partners_of(z, y, x, c):
    return [
        number(z, y, x, 1 - c),
        number(z, y, 1 - x, c),
        number(z, 1 - y, x, c),
        number(lax.rem(z + 1, 4), y, x, c),
        number(lax.rem(z + 2, 4), y, x, c),
        number(lax.rem(z + 3, 4), y, x, c),
    ]


def gather_kernel(rows, pieces, x_ref, o_ref, local_sem, ss, rs):
    z, y, x, c = place()
    greet(partners_of(z, y, x, c))
    sibling = number(z, y, x, 1 - c)
    me = number(z, y, x, c)
    around = (number(z, 1 - y, x, c), number(z, y, 1 - x, c))

    def part(ref, block, p):
        r0, nr, c0, nc = pieces[p]
        return ref.at[pl.ds(pl.multiple_of(block * rows + r0, 16), nr), pl.ds(c0, nc)]

    def copy(block, p, slot, target, own=False):
        source = part(x_ref, 0, p) if own else part(o_ref, block, p)
        return pltpu.make_async_remote_copy(
            src_ref=source, dst_ref=part(o_ref, block, p),
            send_sem=ss.at[p * 31 + slot], recv_sem=rs.at[p * 31 + slot],
            device_id=(target,), device_id_type=MESH)

    pending = []

    def send(*args, **kw):
        cp = copy(*args, **kw)
        cp.start()
        pending.append(cp)

    def at(k, fy, fx):
        return number(lax.rem(z + 4 - k, 4), (1 - y) if fy else y, (1 - x) if fx else x, c)

    local = pltpu.make_async_copy(x_ref, o_ref.at[pl.ds(pl.multiple_of(me * rows, 16), rows), :], local_sem)
    local.start()
    order = (0, 1, 3, 2)
    far = ((1, 0), (0, 1))
    for k in (1, 3, 2):
        for p in range(2):
            send(me, p, k - 1, number(lax.rem(z + k, 4), y, x, c), own=True)
    for k in order:
        for p in range(2):
            block = at(k, 0, 0)
            if k:
                copy(block, p, k - 1, sibling).wait_recv()
            own = k == 0
            send(block, p, 3 + k, around[p], own=own)
            send(block, p, 7 + k, around[1 - p], own=own)
            send(block, p, 15 + k, sibling, own=own)
    for k in order:
        for p in range(2):
            fy, fx = far[p]
            block = at(k, fy, fx)
            copy(block, p, 3 + k, sibling).wait_recv()
            send(block, p, 11 + k, around[1 - p])
            send(block, p, 19 + k, sibling)
    for j, slot in ((0, 7), (1, 11)):
        for k in order:
            for p in range(2):
                fy, fx = (1, 1) if j else (1 - far[p][0], 1 - far[p][1])
                block = at(k, fy, fx)
                copy(block, p, slot + k, sibling).wait_recv()
                send(block, p, 23 + 4 * j + k, sibling)
    for k in range(4):
        for p in range(2):
            for s in (15, 19, 23, 27):
                copy(me, p, s + k, sibling).wait_recv()
    for cp in pending:
        cp.wait_send()
    local.wait()


def gather_all(block, cid, by_rows):
    rows, cols = block.shape
    if by_rows:
        pieces = ((0, rows // 2, 0, cols), (rows // 2, rows // 2, 0, cols))
    else:
        half = (cols // 256) * 128
        pieces = ((0, rows, 0, half), (0, rows, half, cols - half))
    return pl.pallas_call(
        functools.partial(gather_kernel, rows, pieces),
        out_shape=jax.ShapeDtypeStruct((32 * rows, cols), block.dtype),
        in_specs=[pl.BlockSpec(memory_space=pl.ANY)],
        out_specs=pl.BlockSpec(memory_space=pl.ANY),
        scratch_shapes=[pltpu.SemaphoreType.DMA, pltpu.SemaphoreType.DMA((62,)), pltpu.SemaphoreType.DMA((62,))],
        compiler_params=pltpu.CompilerParams(collective_id=cid, has_side_effects=True),
        name="gather_all",
    )(block)


def reduce_kernel(rows, cols, pieces, g_ref, more_ref, o_ref, acc, own, ra, rb, rz, own_sem, ssem, rsem, sa, ra_sem, sb, rb_sem, sz, rz_sem):
    z, y, x, c = place()
    greet(partners_of(z, y, x, c))
    sibling = number(z, y, x, 1 - c)
    around = (number(z, y, 1 - x, c), number(z, 1 - y, x, c))
    blocks = [(dy, dx, k) for dy, dx in ((1, 1), (1, 0), (0, 1), (0, 0)) for k in (2, 1, 3, 0)]

    def where(dy, dx, k):
        return lax.rem(z + k, 4), (1 - y) if dy else y, (1 - x) if dx else x

    def lane(dy, dx, k):
        zz, yy, xx = where(dy, dx, k)
        return (zz * 2 + yy) * 2 + xx

    main = g_ref.shape[1]
    sides = ((g_ref, pl.ds(0, main)), (more_ref, pl.ds(main, cols - main)))

    def chip_rows(ref, dy, dx, k, core):
        zz, yy, xx = where(dy, dx, k)
        return ref.at[pl.ds(pl.multiple_of(number(zz, yy, xx, core) * rows, 16), rows), :]

    def to_sibling(n):
        return [
            pltpu.make_async_remote_copy(
                src_ref=chip_rows(ref, *blocks[n], 1 - c), dst_ref=acc.at[lane(*blocks[n]), :, at],
                send_sem=ssem.at[n, i], recv_sem=rsem.at[n, i], device_id=(sibling,), device_id_type=MESH)
            for i, (ref, at) in enumerate(sides)
        ]

    def load(n):
        return [
            pltpu.make_async_copy(chip_rows(ref, *blocks[n], c), own.at[n % 2, :, at], own_sem.at[n % 2, i])
            for i, (ref, at) in enumerate(sides)
        ]

    def part(ref, p):
        r0, nr, c0, nc = pieces[p]
        return ref.at[pl.ds(r0, nr), pl.ds(c0, nc)]

    def first(p, d2, k, dy, dx):
        return pltpu.make_async_remote_copy(
            src_ref=part(acc.at[lane(dy, dx, k)], p), dst_ref=ra.at[p, d2, k],
            send_sem=sa.at[p, d2, k], recv_sem=ra_sem.at[p, d2, k], device_id=(around[p],), device_id_type=MESH)

    def second(p, k):
        dy, dx = (1, 0) if p == 0 else (0, 1)
        return pltpu.make_async_remote_copy(
            src_ref=part(acc.at[lane(dy, dx, k)], p), dst_ref=rb.at[p, k],
            send_sem=sb.at[p, k], recv_sem=rb_sem.at[p, k], device_id=(around[1 - p],), device_id_type=MESH)

    def third(p, k):
        return pltpu.make_async_remote_copy(
            src_ref=part(acc.at[lane(0, 0, k)], p), dst_ref=rz.at[p, k - 1],
            send_sem=sz.at[p, k - 1], recv_sem=rz_sem.at[p, k - 1],
            device_id=(number(lax.rem(z + k, 4), y, x, c),), device_id_type=MESH)

    step = 16

    def add(out, terms, nr):
        def chunk(i, _):
            at = pl.ds(pl.multiple_of(i * step, step), step)
            total = terms[0][at, :].astype(jnp.float32)
            for t in terms[1:]:
                total = total + t[at, :].astype(jnp.float32)
            out[at, :] = total.astype(out.dtype)
            return 0
        lax.fori_loop(0, nr // step, chunk, 0)

    for n in range(16):
        for cp in to_sibling(n):
            cp.start()
    for cp in load(0):
        cp.start()
    for n in range(16):
        dy, dx, k = blocks[n]
        if n + 1 < 16:
            for cp in load(n + 1):
                cp.start()
        for cp in load(n):
            cp.wait()
        for cp in to_sibling(n):
            cp.wait_recv()
        block = acc.at[lane(dy, dx, k)]
        add(block, [block, own.at[n % 2]], rows)
        if dx:
            first(0, dy, k, dy, dx).start()
        if dy:
            first(1, dx, k, dy, dx).start()
    for k in (2, 1, 3, 0):
        for p in range(2):
            dy, dx = (1, 0) if p == 0 else (0, 1)
            first(p, 1, k, 1, 1).wait_recv()
            block = part(acc.at[lane(dy, dx, k)], p)
            add(block, [block, ra.at[p, 1, k]], pieces[p][1])
            second(p, k).start()
    for k in (2, 1, 3, 0):
        for p in range(2):
            first(p, 0, k, 1 - p, p).wait_recv()
            second(p, k).wait_recv()
            block = part(acc.at[lane(0, 0, k)], p)
            if k:
                add(block, [block, ra.at[p, 0, k], rb.at[p, k]], pieces[p][1])
                third(p, k).start()
    for p in range(2):
        for k in range(1, 4):
            third(p, k).wait_recv()
        block = part(acc.at[lane(0, 0, 0)], p)
        add(part(o_ref, p), [block, ra.at[p, 0, 0], rb.at[p, 0]] + [rz.at[p, j] for j in range(3)], pieces[p][1])
    for n in range(16):
        for cp in to_sibling(n):
            cp.wait_send()
    for p in range(2):
        for k in range(4):
            first(p, 0, k, 1 - p, p).wait_send()
            first(p, 1, k, 1, 1).wait_send()
            second(p, k).wait_send()
            if k:
                third(p, k).wait_send()


def reduce_all(dense, more, cid):
    rows, cols = dense.shape[0] // 32, dense.shape[1] + more.shape[1]
    half = cols // 2
    pieces = ((0, rows, 0, half), (0, rows, half, half))
    dma = pltpu.SemaphoreType.DMA
    return pl.pallas_call(
        functools.partial(reduce_kernel, rows, cols, pieces),
        out_shape=jax.ShapeDtypeStruct((rows, cols), jnp.float32),
        in_specs=[pl.BlockSpec(memory_space=pl.ANY)] * 2,
        out_specs=pl.BlockSpec(memory_space=pltpu.VMEM),
        scratch_shapes=[
            pltpu.VMEM((16, rows, cols), dense.dtype),
            pltpu.VMEM((2, rows, cols), dense.dtype),
            pltpu.VMEM((2, 2, 4, rows, half), dense.dtype),
            pltpu.VMEM((2, 4, rows, half), dense.dtype),
            pltpu.VMEM((2, 3, rows, half), dense.dtype),
            dma((2, 2)), dma((16, 2)), dma((16, 2)), dma((2, 2, 4)), dma((2, 2, 4)), dma((2, 4)), dma((2, 4)), dma((2, 3)), dma((2, 3)),
        ],
        compiler_params=pltpu.CompilerParams(collective_id=cid, has_side_effects=True, vmem_limit_bytes=56 * 2**20),
        name="reduce_all",
    )(dense, more)


from jax.sharding import PartitionSpec as P

QUERY_HEADS = 24
KEY_HEADS = 8
HEAD_DIM = 64
GROUP = QUERY_HEADS // KEY_HEADS
TOP = 8
EXPERTS = 32
MAXDOC = 2000
EPSILON = 1e-06
MASKED = -1e30
QKV = (QUERY_HEADS + 2 * KEY_HEADS) * HEAD_DIM
F32 = jnp.float32
BF16 = jnp.bfloat16


def meshed():
    return lax.axis_size("dev") == 32


def dims(a, b, ca, cb):
    return lax.dot_general(a, b, (((ca,), (cb,)), ((), ())), preferred_element_type=F32)


class Window:
    scratch = [pltpu.SemaphoreType.DMA((2,)), pltpu.SemaphoreType.DMA((9,)), pltpu.SemaphoreType.DMA((9,))]

    def __init__(self, rows, kv_ref, out, scratch):
        self.rows, self.kv_ref, self.out = rows, kv_ref, out
        self.lsem, self.ss, self.rs = scratch
        self.z, self.y, self.x, self.c = place()
        self.p = self.y * 2 + self.x
        self.sibling = number(self.z, self.y, self.x, 1 - self.c)
        self.near = [(self.z * 4 + lax.rem(self.p + d, 4)) * 2 + self.c for d in (1, 2, 3)]
        self.own_in = pltpu.make_async_copy(kv_ref, self.slot(4, self.c), self.lsem.at[0])
        self.stand_in = pltpu.make_async_copy(kv_ref, self.slot(0, self.c), self.lsem.at[1])
        self.to_up = self.copy(kv_ref, 0, 0, number(lax.rem(self.z + 1, 4), self.y, self.x, self.c))

    def slot(self, s, core):
        return self.out.at[:, pl.ds(pl.multiple_of((2 * s + core) * self.rows, 16), self.rows), :]

    def copy(self, source, s, n, target):
        return pltpu.make_async_remote_copy(
            src_ref=source, dst_ref=self.slot(s, self.c), send_sem=self.ss.at[n], recv_sem=self.rs.at[n],
            device_id=(target,), device_id_type=MESH)

    def own_near(self, d):
        return self.copy(self.kv_ref, 4 - d, d, self.near[d - 1])

    def across(self, s):
        source = self.kv_ref if s == 4 else self.slot(s, self.c)
        return self.copy(source, s, {4: 4, 0: 5}.get(s, 9 - s), self.sibling)

    def start(self):
        self.own_in.start()

        @pl.when(self.z < 3)
        def _():
            self.to_up.start()

        @pl.when(self.z == 0)
        def _():
            self.stand_in.start()

        for d in (1, 3, 2):
            @pl.when(self.p + d < 4)
            def _(d=d):
                self.own_near(d).start()
        self.across(4).start()

    def previous(self):
        @pl.when(self.z == 0)
        def _():
            self.stand_in.wait()

        @pl.when(self.z > 0)
        def _():
            self.to_up.wait_recv()

        for d in (3, 1, 2):
            @pl.when(self.p + d >= 4)
            def _(d=d):
                self.copy(self.slot(0, self.c), 4 - d, d, self.near[d - 1]).start()
        self.across(0).start()

    def pass_on(self):
        for d in (1, 3, 2):
            self.own_near(d).wait_recv()
            self.across(4 - d).start()

    def end(self):
        for s in range(5):
            pltpu.make_async_remote_copy(
                src_ref=self.kv_ref, dst_ref=self.slot(s, 1 - self.c), send_sem=self.ss.at[0],
                recv_sem=self.rs.at[{4: 4, 0: 5}.get(s, 9 - s)], device_id=(self.sibling,), device_id_type=MESH).wait_recv()
        self.own_in.wait()

    def sent(self):
        @pl.when(self.z < 3)
        def _():
            self.to_up.wait_send()

        for d in (1, 2, 3):
            self.own_near(d).wait_send()
        for s in range(5):
            self.across(s).wait_send()


def window_of(kv):
    rows = kv.shape[1]
    devices = lax.axis_size("dev")
    back = (MAXDOC + rows - 2) // rows
    parts = [
        lax.ppermute(kv, "dev", [(i - d, i) for i in range(d, devices)]) for d in range(back, 0, -1)
    ]
    return jnp.concatenate(parts + [kv, jnp.zeros_like(kv)], axis=1)


def unwindow_kernel(rows, g_ref, o_ref, mine, got, near_got, far, lsem, ss, rs):
    z, y, x, c = place()
    p = y * 2 + x
    sibling = number(z, y, x, 1 - c)
    up = number(lax.rem(z + 1, 4), y, x, c)
    down = number(lax.rem(z + 3, 4), y, x, c)

    def chip(q):
        return (z * 4 + q) * 2 + c

    ahead = [chip(lax.rem(p + d, 4)) for d in (1, 2, 3)]
    behind = [chip(lax.rem(p + 4 - d, 4)) for d in (1, 2, 3)]
    greet([sibling, up, down] + ahead)

    def slot(s, core):
        return g_ref.at[:, pl.ds(pl.multiple_of((2 * s + core) * rows, 16), rows), :]

    def to_sibling(s):
        return pltpu.make_async_remote_copy(
            src_ref=slot(s, 1 - c), dst_ref=got.at[s], send_sem=ss.at[s], recv_sem=rs.at[s],
            device_id=(sibling,), device_id_type=MESH)

    def load(s):
        return pltpu.make_async_copy(slot(s, c), mine.at[s], lsem.at[s])

    def to_owner(d):
        return pltpu.make_async_remote_copy(
            src_ref=got.at[4 - d], dst_ref=near_got.at[d - 1], send_sem=ss.at[4 + d], recv_sem=rs.at[4 + d],
            device_id=(behind[d - 1],), device_id_type=MESH)

    to_down = pltpu.make_async_remote_copy(
        src_ref=got.at[0], dst_ref=far, send_sem=ss.at[8], recv_sem=rs.at[8],
        device_id=(down,), device_id_type=MESH)
    order = (3, 1, 2, 0, 4)
    for s in order:
        to_sibling(s).start()
        load(s).start()

    def rowwise(body):
        for h in range(2):
            def step(i, _, h=h):
                body(h, pl.ds(pl.multiple_of(i * 32, 32), 32))
                return 0
            lax.fori_loop(0, rows // 32, step, 0)

    for s in order:
        load(s).wait()
        to_sibling(s).wait_recv()

        def both(h, at, s=s):
            total = got[s, h, at, :].astype(F32) + mine[s, h, at, :].astype(F32)
            if s == 4:
                o_ref[h, at, :] = total
            else:
                got[s, h, at, :] = total.astype(BF16)
        rowwise(both)
        if 0 < s < 4:
            to_owner(4 - s).start()
    for d in (1, 3, 2):
        to_owner(d).wait_recv()

        @pl.when(p + d < 4)
        def _(d=d):
            def body(h, at):
                o_ref[h, at, :] += near_got[d - 1, h, at, :].astype(F32)
            rowwise(body)

        @pl.when(p + d >= 4)
        def _(d=d):
            def body(h, at):
                total = got[0, h, at, :].astype(F32) + near_got[d - 1, h, at, :].astype(F32)
                got[0, h, at, :] = total.astype(BF16)
            rowwise(body)

    @pl.when(z > 0)
    def _():
        to_down.start()

    @pl.when(z < 3)
    def _():
        to_down.wait_recv()

        def body(h, at):
            o_ref[h, at, :] += far[h, at, :].astype(F32)
        rowwise(body)

    @pl.when(z > 0)
    def _():
        to_down.wait_send()

    for s in range(5):
        to_sibling(s).wait_send()
    for d in (1, 2, 3):
        to_owner(d).wait_send()


def unwindow(grads):
    rows, width = grads.shape[1] // 10, grads.shape[2]
    if meshed():
        dma = pltpu.SemaphoreType.DMA
        return pl.pallas_call(
            functools.partial(unwindow_kernel, rows),
            out_shape=jax.ShapeDtypeStruct((2, rows, width), F32),
            in_specs=[pl.BlockSpec(memory_space=pl.ANY)],
            out_specs=pl.BlockSpec(memory_space=pltpu.VMEM),
            scratch_shapes=[
                pltpu.VMEM((5, 2, rows, width), BF16),
                pltpu.VMEM((5, 2, rows, width), BF16),
                pltpu.VMEM((3, 2, rows, width), BF16),
                pltpu.VMEM((2, rows, width), BF16),
                dma((5,)), dma((9,)), dma((9,)),
            ],
            compiler_params=pltpu.CompilerParams(collective_id=12, has_side_effects=True, vmem_limit_bytes=40 * 2**20),
            name="unwindow",
        )(grads)
    devices = lax.axis_size("dev")
    back = (MAXDOC + rows - 2) // rows
    total = grads[:, back * rows : (back + 1) * rows].astype(F32)
    for d in range(1, back + 1):
        piece = grads[:, (back - d) * rows : (back - d + 1) * rows]
        moved = lax.ppermute(piece, "dev", [(i, i - d) for i in range(d, devices)])
        total = total + moved.astype(F32)
    return total


def make_bias(bias, lo_ref, chunks, rows):
    def fill(ch, _):
        at = pl.ds(pl.multiple_of(ch * rows, rows), rows)
        relative = lax.broadcasted_iota(jnp.int32, (rows, rows), 0) + (ch - (chunks - 1)) * rows
        query = lax.broadcasted_iota(jnp.int32, (rows, rows), 1)
        allowed = (relative <= query) & (relative >= lo_ref[...])
        bias[at, :] = jnp.where(allowed, 0.0, MASKED)
        return 0
    lax.fori_loop(0, chunks, fill, 0)


def side_by_side(ref, half):
    first = half * GROUP
    return jnp.concatenate(
        [ref[(first + g) * HEAD_DIM : (first + g + 1) * HEAD_DIM, :] for g in range(GROUP)], axis=1
    )


def stats_of(ref, half):
    return jnp.concatenate([ref[0, half * GROUP + g : half * GROUP + g + 1, :] for g in range(GROUP)], axis=1)


def attend_pair(chunks, rows, off, q_ref, kv_ref, o_ref, lse_ref, bias, between):
    lse_ref[...] = jnp.zeros_like(lse_ref)
    width = GROUP * rows
    for half in range(2):
        lanes = slice(half * HEAD_DIM, (half + 1) * HEAD_DIM)
        queries = side_by_side(q_ref, half)

        def chunk(i, carry, lanes=lanes, queries=queries):
            ch = chunks - 1 - i
            at = pl.ds(pl.multiple_of((ch + off) * rows, rows), rows)
            key, value = kv_ref[0, at, lanes], kv_ref[1, at, lanes]
            shift = bias[pl.ds(pl.multiple_of(ch * rows, rows), rows), :]
            top, total, mixed = carry
            score = dims(key, queries, 1, 0) + jnp.concatenate([shift] * GROUP, axis=1)
            new_top = jnp.maximum(top, jnp.max(score, axis=0, keepdims=True))
            weight = jnp.exp(score - new_top)
            fade = jnp.exp(top - new_top)
            total = total * fade + jnp.sum(weight, axis=0, keepdims=True)
            mixed = mixed * fade + dims(value, weight.astype(BF16), 0, 0)
            return new_top, total, mixed

        start = (jnp.full((1, width), MASKED, F32), jnp.zeros((1, width), F32), jnp.zeros((HEAD_DIM, width), F32))
        top, total, mixed = lax.fori_loop(0, chunks, chunk, start, unroll=3)
        mixed = (mixed / total).astype(BF16)
        lse = top + jnp.log(total)
        for g in range(GROUP):
            n = half * GROUP + g
            o_ref[n * HEAD_DIM : (n + 1) * HEAD_DIM, :] = mixed[:, g * rows : (g + 1) * rows]
            lse_ref[0, n : n + 1, :] = lse[:, g * rows : (g + 1) * rows]
        between(half)


def attend_kernel(chunks, rows, off_ref, lo_ref, q_ref, kv_ref, o_ref, lse_ref, bias):
    @pl.when(pl.program_id(0) == 0)
    def _():
        make_bias(bias, lo_ref, chunks, rows)

    attend_pair(chunks, rows, off_ref[0], q_ref, kv_ref, o_ref, lse_ref, bias, lambda half: None)


def attend_back_pair(
    chunks, rows, off, cos_ref, sin_ref, q_ref, kv_ref, g_ref, lse_ref, delta_ref, dq_ref, dkv_ref, bias, between
):
    unused = pl.ds(pl.multiple_of((1 - off) * chunks * rows, rows), rows)
    dkv_ref[:, unused, :] = jnp.zeros((2, rows, 2 * HEAD_DIM), BF16)
    for half in range(2):
        lanes = slice(half * HEAD_DIM, (half + 1) * HEAD_DIM)
        queries, grads = side_by_side(q_ref, half), side_by_side(g_ref, half)
        lse, delta = stats_of(lse_ref, half), stats_of(delta_ref, half)

        def chunk(ch, query_grad, lanes=lanes, queries=queries, grads=grads, lse=lse, delta=delta):
            at = pl.ds(pl.multiple_of((ch + off) * rows, rows), rows)
            key, value = kv_ref[0, at, lanes], kv_ref[1, at, lanes]
            shift = bias[pl.ds(pl.multiple_of(ch * rows, rows), rows), :]
            score = dims(key, queries, 1, 0) + jnp.concatenate([shift] * GROUP, axis=1)
            weight = jnp.exp(score - lse)
            score_grad = (weight * (dims(value, grads, 1, 0) - delta)).astype(BF16)
            dkv_ref[0, at, lanes] = dims(score_grad, queries, 1, 1).astype(BF16)
            dkv_ref[1, at, lanes] = dims(weight.astype(BF16), grads, 1, 1).astype(BF16)
            return query_grad + dims(key, score_grad, 0, 0)

        done = lax.fori_loop(0, chunks, chunk, jnp.zeros((HEAD_DIM, GROUP * rows), F32), unroll=3)
        done = done * (HEAD_DIM**-0.5)
        cosine, sine = cos_ref[...], sin_ref[...]
        for g in range(GROUP):
            grad = done[:, g * rows : (g + 1) * rows]
            u, w = grad[: HEAD_DIM // 2], grad[HEAD_DIM // 2 :]
            n = (half * GROUP + g) * HEAD_DIM
            dq_ref[n : n + HEAD_DIM // 2, :] = (u * cosine + w * sine).astype(BF16)
            dq_ref[n + HEAD_DIM // 2 : n + HEAD_DIM, :] = (w * cosine - u * sine).astype(BF16)
        between(half)


def attend_back_kernel(
    chunks, rows, off_ref, lo_ref, cos_ref, sin_ref, q_ref, kv_ref, g_ref, lse_ref, delta_ref, dq_ref, dkv_ref, bias
):
    @pl.when(pl.program_id(0) == 0)
    def _():
        make_bias(bias, lo_ref, chunks, rows)

    attend_back_pair(
        chunks, rows, off_ref[0], cos_ref, sin_ref, q_ref, kv_ref, g_ref, lse_ref, delta_ref, dq_ref, dkv_ref, bias,
        lambda half: None,
    )


def attention_specs(rows, span):
    width = 2 * GROUP * HEAD_DIM
    return dict(
        smem=pl.BlockSpec(memory_space=pltpu.SMEM),
        row=pl.BlockSpec((1, rows), lambda j: (0, 0)),
        table=pl.BlockSpec((HEAD_DIM // 2, rows), lambda j: (0, 0)),
        query=pl.BlockSpec((width, rows), lambda j: (j, 0)),
        kv=pl.BlockSpec((2, span, 2 * HEAD_DIM), lambda j: (0, 0, j)),
        stat=pl.BlockSpec((1, 8, rows), lambda j: (j, 0, 0)),
    )


def attend(query_t, window, offset, lo):
    rows, span = query_t.shape[1], window.shape[1]
    chunks = span // rows - 1
    s = attention_specs(rows, span)
    return pl.pallas_call(
        functools.partial(attend_kernel, chunks, rows),
        grid=(KEY_HEADS // 2,),
        in_specs=[s["smem"], s["row"], s["query"], s["kv"]],
        out_specs=[s["query"], s["stat"]],
        out_shape=[
            jax.ShapeDtypeStruct(query_t.shape, BF16),
            jax.ShapeDtypeStruct((KEY_HEADS // 2, 8, rows), F32),
        ],
        scratch_shapes=[pltpu.VMEM((chunks * rows, rows), F32)],
        compiler_params=pltpu.CompilerParams(vmem_limit_bytes=40 * 2**20),
        cost_estimate=pl.CostEstimate(flops=7 * 10**9, bytes_accessed=8 * 10**6, transcendentals=15 * 10**6),
        name="attend",
    )(offset.reshape(1), lo, query_t, window)


def attend_back(query_t, window, offset, lo, grad_t, lse, delta, cos_t, sin_t):
    rows, span = query_t.shape[1], window.shape[1]
    chunks = span // rows - 1
    s = attention_specs(rows, span)
    return pl.pallas_call(
        functools.partial(attend_back_kernel, chunks, rows),
        grid=(KEY_HEADS // 2,),
        in_specs=[s["smem"], s["row"], s["table"], s["table"], s["query"], s["kv"], s["query"], s["stat"], s["stat"]],
        out_specs=[s["query"], s["kv"]],
        out_shape=[
            jax.ShapeDtypeStruct(query_t.shape, BF16),
            jax.ShapeDtypeStruct(window.shape, BF16),
        ],
        scratch_shapes=[pltpu.VMEM((chunks * rows, rows), F32)],
        compiler_params=pltpu.CompilerParams(vmem_limit_bytes=40 * 2**20),
        cost_estimate=pl.CostEstimate(flops=18 * 10**9, bytes_accessed=16 * 10**6, transcendentals=15 * 10**6),
        name="attend_back",
    )(offset.reshape(1), lo, cos_t, sin_t, query_t, window, grad_t, lse, delta)


def hits(slot_ref, slots):
    width = slot_ref.shape[-1]
    return slot_ref[0] == lax.broadcasted_iota(jnp.int32, (slots, width), 0)


def dispatch_kernel(slot_ref, x_ref, u_ref, xo_ref, uo_ref):
    chosen = jnp.where(hits(slot_ref, xo_ref.shape[0]), 1.0, 0.0).astype(BF16)
    xo_ref[...] = dims(chosen, x_ref[...], 1, 0).astype(BF16)
    uo_ref[...] = dims(chosen, u_ref[...], 1, 0).astype(BF16)


def dispatch(slot, normed, upstream, slots):
    pairs, _, width = slot.shape
    model = normed.shape[1]
    return pl.pallas_call(
        dispatch_kernel,
        grid=(pairs,),
        in_specs=[
            pl.BlockSpec((1, 1, width), lambda i: (i, 0, 0)),
            pl.BlockSpec((width, model), lambda i: (i, 0)),
            pl.BlockSpec((width, model), lambda i: (i, 0)),
        ],
        out_specs=[pl.BlockSpec((slots, model), lambda i: (i, 0))] * 2,
        out_shape=[jax.ShapeDtypeStruct((pairs * slots, model), BF16)] * 2,
        compiler_params=pltpu.CompilerParams(vmem_limit_bytes=40 * 2**20),
        cost_estimate=pl.CostEstimate(flops=2 * 10**9, bytes_accessed=65 * 10**6, transcendentals=0),
        name="dispatch",
    )(slot, normed, upstream)


def combine_kernel(slot_ref, r_ref, o_ref):
    chosen = jnp.where(hits(slot_ref, r_ref.shape[0]), 1.0, 0.0).astype(BF16)
    o_ref[...] = dims(chosen, r_ref[...], 0, 0).astype(BF16)


def combine(slot, rows, slots):
    pairs, _, width = slot.shape
    model = rows.shape[1]
    return pl.pallas_call(
        combine_kernel,
        grid=(pairs,),
        in_specs=[
            pl.BlockSpec((1, 1, width), lambda i: (i, 0, 0)),
            pl.BlockSpec((slots, model), lambda i: (i, 0)),
        ],
        out_specs=pl.BlockSpec((width, model), lambda i: (i, 0)),
        out_shape=jax.ShapeDtypeStruct((pairs * width, model), BF16),
        compiler_params=pltpu.CompilerParams(vmem_limit_bytes=40 * 2**20),
        cost_estimate=pl.CostEstimate(flops=10**9, bytes_accessed=33 * 10**6, transcendentals=0),
        name="combine",
    )(slot, rows)


SLOTS = 80


def far_first(i):
    return jnp.where(i == 0, 2, jnp.where(i == 3, 0, 2 * i - 1))


def greet_all():
    me = lax.axis_index("dev")
    barrier = pltpu.get_barrier_semaphore()

    def signal(d, _):
        pl.semaphore_signal(barrier, inc=1, device_id=(lax.rem(me + d, 32),), device_id_type=MESH)
        return 0
    lax.fori_loop(1, 32, signal, 0)
    pl.semaphore_wait(barrier, 31)


class Swap:
    def __init__(self, source, into, ss, rs):
        self.me = lax.axis_index("dev")
        self.source, self.into, self.ss, self.rs = source, into, ss, rs

    def copy(self, d):
        target = lax.rem(self.me + d, 32)
        return pltpu.make_async_remote_copy(
            src_ref=self.source(target), dst_ref=self.into.at[self.me], send_sem=self.ss.at[d], recv_sem=self.rs.at[d],
            device_id=(target,), device_id_type=MESH)

    def start(self):
        def one(d, _):
            self.copy(d).start()
            return 0
        lax.fori_loop(1, 32, one, 0)
        self.into[self.me] = self.source(self.me)[...]

    def wait_recv(self):
        def one(d, _):
            self.copy(d).wait_recv()
            return 0
        lax.fori_loop(1, 32, one, 0)

    def wait_send(self):
        def one(d, _):
            self.copy(d).wait_send()
            return 0
        lax.fori_loop(1, 32, one, 0)


def in_plane(y, x, c):
    return (y * 2 + x) * 2 + c


def chosen_rows(slots_ref, block, expert):
    row = slots_ref[block, pl.ds(expert, 1), :]
    return row == lax.broadcasted_iota(jnp.int32, (SLOTS, row.shape[1]), 0).astype(F32)


def greet_near():
    z, y, x, c = place()
    greet(
        [number(z, y, x, 1 - c)]
        + [number(z, 1 - y, x, cc) for cc in (c, 1 - c)]
        + [number(z, y, 1 - x, cc) for cc in (c, 1 - c)]
        + [number(lax.rem(z + d, 4), y, x, c) for d in (1, 2, 3)]
    )


class Forth:
    scratch = staticmethod(lambda rows, half: [
        pltpu.VMEM((2, 2, 4, rows, half), BF16),
        pltpu.VMEM((2, 2, 4, 4, SLOTS, half), BF16),
        pltpu.SemaphoreType.DMA((2, 2, 4)), pltpu.SemaphoreType.DMA((2, 4)),
        pltpu.SemaphoreType.DMA((2, 4)), pltpu.SemaphoreType.DMA((2, 4)),
        pltpu.SemaphoreType.DMA((2, 2, 4, 4)), pltpu.SemaphoreType.DMA((2, 2, 4, 3)), pltpu.SemaphoreType.DMA((2,)),
    ])
    n_scratch = 9

    def __init__(self, x_ref, slots_ref, xi, scratch):
        self.x_ref, self.slots_ref, self.xi = x_ref, slots_ref, xi
        self.land, self.stage, self.zs, self.zr, self.fs, self.fr, self.cs, self.cr, self.own_sem = scratch
        self.z, self.y, self.x, self.c = place()
        half = x_ref.shape[1] // 2
        self.cols = [pl.ds(0, half), pl.ds(half, half)]

    def turn(self, i):
        middle = jnp.where(i < 2, i, 5 - i)
        return jnp.where(self.z == 0, lax.rem(4 - i, 4), jnp.where(self.z == 3, i, middle))

    def to_z(self, p, up, k, own=False):
        step = 1 if up else 3
        source = self.x_ref.at[:, self.cols[p]] if own else self.land.at[p, 0, k]
        there = lax.rem(k + step, 4)
        return pltpu.make_async_remote_copy(
            src_ref=source, dst_ref=self.land.at[p, 0, there],
            send_sem=self.zs.at[p, int(up), k], recv_sem=self.zr.at[p, there],
            device_id=(number(lax.rem(self.z + step, 4), self.y, self.x, self.c),), device_id_type=MESH)

    def hop(self, p, k):
        z, y, x, c = self.z, self.y, self.x, self.c
        beside = number(z, 1 - y, x, c) if p == 0 else number(z, y, 1 - x, c)
        return pltpu.make_async_remote_copy(
            src_ref=self.land.at[p, 0, k], dst_ref=self.land.at[p, 1, k],
            send_sem=self.fs.at[p, k], recv_sem=self.fr.at[p, k], device_id=(beside,), device_id_type=MESH)

    def block(self, p, h, k):
        zz = lax.rem(self.z + 4 - k, 4)
        if p == 0:
            return number(zz, (1 - self.y) if h else self.y, self.x, self.c)
        return number(zz, self.y, (1 - self.x) if h else self.x, self.c)

    def who(self, p):
        y, x, c = self.y, self.x, self.c
        ay, ax = (y, 1 - x) if p == 0 else (1 - y, x)
        return [(y, x, 1 - c), (ay, ax, c), (ay, ax, 1 - c), (y, x, c)]

    def slots_at(self, p, h, k):
        return self.xi.at[pl.ds(pl.multiple_of(self.block(p, h, k) * SLOTS, 16), SLOTS), self.cols[p]]

    def served(self, p, h, k, t):
        return pltpu.make_async_remote_copy(
            src_ref=self.stage.at[p, h, k, t], dst_ref=self.slots_at(p, h, k),
            send_sem=self.cs.at[p, h, k, t], recv_sem=self.cr.at[p, h, k, t],
            device_id=(number(self.z, *self.who(p)[t]),), device_id_type=MESH)

    def kept(self, p, h, k):
        return pltpu.make_async_copy(self.stage.at[p, h, k, 3], self.slots_at(p, h, k), self.cs.at[p, h, k, 3])

    def serve(self, p, h, k):
        block = self.block(p, h, k)
        source = self.land[p, h, k]
        for t, to in enumerate(self.who(p)):
            chosen = jnp.where(chosen_rows(self.slots_ref, block, in_plane(*to)), 1.0, 0.0).astype(BF16)
            self.stage[p, h, k, t] = dims(chosen, source, 1, 0).astype(BF16)
            if t < 3:
                self.served(p, h, k, t).start()
            else:
                self.kept(p, h, k).start()

    def own(self, p):
        return pltpu.make_async_copy(self.x_ref.at[:, self.cols[p]], self.land.at[p, 0, 0], self.own_sem.at[p])

    def along(self, i, use):
        k = self.turn(i)
        zz = lax.rem(self.z + 4 - k, 4)
        for p in range(2):
            @pl.when((zz < self.z) & (self.z < 3))
            def _(p=p):
                use(self.to_z(p, True, k))

            @pl.when((zz > self.z) & (self.z > 0))
            def _(p=p):
                use(self.to_z(p, False, k))

    def along_own(self, use):
        for p in range(2):
            @pl.when(self.z < 3)
            def _(p=p):
                use(self.to_z(p, True, 0, own=True))

            @pl.when(self.z > 0)
            def _(p=p):
                use(self.to_z(p, False, 0, own=True))

    def start(self):
        for p in range(2):
            self.own(p).start()
        self.along_own(lambda cp: cp.start())

    def one(self, i):
        k = self.turn(i)

        @pl.when(i == 0)
        def _():
            for p in range(2):
                self.own(p).wait()

        @pl.when(i > 0)
        def _():
            for p in range(2):
                self.to_z(p, True, lax.rem(k + 3, 4)).wait_recv()

        self.along(i, lambda cp: cp.start())
        for p in range(2):
            self.hop(p, k).start()
        for p in range(2):
            self.serve(p, 0, k)

    def two(self, i):
        k = self.turn(i)
        for p in range(2):
            self.hop(p, k).wait_recv()
            self.serve(p, 1, k)

    def arrived(self, group, i):
        k = self.turn(i)

        @pl.when(group == 0)
        def _():
            for p in range(2):
                self.served(p, 0, k, 0).wait_recv()
                self.kept(p, 0, k).wait()

        @pl.when(group == 1)
        def _():
            self.kept(0, 1, k).wait()
            self.served(0, 1, k, 0).wait_recv()
            self.served(1, 0, k, 1).wait_recv()
            self.served(1, 0, k, 2).wait_recv()

        @pl.when(group == 2)
        def _():
            self.kept(1, 1, k).wait()
            self.served(1, 1, k, 0).wait_recv()
            self.served(0, 0, k, 1).wait_recv()
            self.served(0, 0, k, 2).wait_recv()

        @pl.when(group == 3)
        def _():
            for p in range(2):
                self.served(p, 1, k, 1).wait_recv()
                self.served(p, 1, k, 2).wait_recv()

    def chip(self, group, i):
        dy, dx = lax.rem(group, 2), group // 2
        zz = lax.rem(self.z + 4 - self.turn(i), 4)
        yy = jnp.where(dy == 1, 1 - self.y, self.y)
        xx = jnp.where(dx == 1, 1 - self.x, self.x)
        return (zz * 2 + yy) * 2 + xx

    def sent(self):
        self.along_own(lambda cp: cp.wait_send())

        def each(i, _):
            k = self.turn(i)
            self.along(i, lambda cp: cp.wait_send())
            for p in range(2):
                self.hop(p, k).wait_send()
                for h in range(2):
                    for t in range(3):
                        self.served(p, h, k, t).wait_send()
            return 0
        lax.fori_loop(0, 4, each, 0)


def experts_kernel(
    x_ref, gates_ref, slots_ref, ui_ref, wg_ref, wu_ref, wd_ref,
    xi_out, dx_out, y_out, hg_ref, dg_ref, du_ref, gg_ref,
    gates, xi, ubuf, dx_buf, y_buf, gs, gr, usem, xsem, osem, *scratch,
):
    z, y, x, c = place()
    rows = x_ref.shape[0]
    greet_all()
    swap = Swap(lambda t: gates_ref.at[t], gates, gs, gr)
    ag = Forth(x_ref, slots_ref, xi, scratch)
    ag.start()

    def chip_of(u):
        return ag.chip(lax.rem(u, 4), u // 4)

    def at_chip(u):
        return pl.ds(pl.multiple_of(chip_of(u) * 2 * SLOTS, 16), 2 * SLOTS)

    def load_up(u):
        return pltpu.make_async_copy(ui_ref.at[at_chip(u), :], ubuf.at[lax.rem(u, 2)], usem.at[lax.rem(u, 2)])

    load_up(0).start()
    swap.start()
    ag.one(0)
    swap.wait_recv()

    def store(n, buf, out, u):
        return pltpu.make_async_copy(buf.at[lax.rem(u, 2)], out.at[at_chip(u), :], osem.at[n, lax.rem(u, 2)])

    def stores(u):
        return [store(0, dx_buf, dx_out, u), store(1, y_buf, y_out, u)]

    def keep(u):
        return pltpu.make_async_copy(xi.at[at_chip(u), :], xi_out.at[at_chip(u), :], xsem.at[u])

    def unit(u):
        slot = lax.rem(u, 2)
        chip = chip_of(u)

        @pl.when(u < 15)
        def _():
            load_up(u + 1).start()

        ag.arrived(lax.rem(u, 4), u // 4)

        @pl.when(u >= 2)
        def _():
            for s in stores(u - 2):
                s.wait()

        load_up(u).wait()
        at = at_chip(u)
        expert = in_plane(y, x, c)
        picks, gate = [], []
        for core in range(2):
            block = chip * 2 + core
            hit = chosen_rows(slots_ref, block, expert)
            picks.append(hit)
            gate_row = jnp.concatenate([gates[block, 0:1, :], gates[block, 1:2, :]], axis=1)
            gate.append(jnp.sum(jnp.where(hit, gate_row, 0.0), axis=1, keepdims=True))
        gate_of_slot = jnp.concatenate(gate, axis=0)
        hidden_up = dims(ubuf[slot], wd_ref[...], 1, 1)
        rows_in = xi[at, :]
        gate_in = dims(rows_in, wg_ref[...], 1, 0)
        up_in = dims(rows_in, wu_ref[...], 1, 0)
        sig = 1.0 / (1.0 + jnp.exp(-gate_in))
        silu = gate_in * sig
        hidden = (silu * up_in).astype(BF16).astype(F32)
        gated = (hidden * gate_of_slot).astype(BF16)
        hidden_grad = hidden_up * gate_of_slot
        gate_back = (hidden_grad * up_in * sig * (1.0 + gate_in * (1.0 - sig))).astype(BF16)
        up_back = (hidden_grad * silu).astype(BF16)
        hg_ref[at, :] = gated
        dg_ref[at, :] = gate_back
        du_ref[at, :] = up_back
        dx_buf[slot] = (dims(gate_back, wg_ref[...], 1, 1) + dims(up_back, wu_ref[...], 1, 1)).astype(BF16)
        y_buf[slot] = dims(gated, wd_ref[...], 1, 0).astype(BF16)
        gate_grad = jnp.sum(hidden * hidden_up, axis=1, keepdims=True)
        for core in range(2):
            block = chip * 2 + core
            row = jnp.sum(jnp.where(picks[core], gate_grad[core * SLOTS : (core + 1) * SLOTS], 0.0), axis=0, keepdims=True)
            gg_ref[block, 0:1, :] = row[:, :128]
            gg_ref[block, 1:2, :] = row[:, 128:]
        for s in stores(u):
            s.start()
        keep(u).start()

    def each(v, _):
        i, group = v // 4, lax.rem(v, 4)

        @pl.when((group == 0) & (i < 3))
        def _():
            ag.one(i + 1)

        @pl.when((group == 0) & (i < 4))
        def _():
            ag.two(i)

        @pl.when(v >= 4)
        def _():
            unit(v - 4)
        return 0

    lax.fori_loop(0, 20, each, 0)
    for u in (14, 15):
        for s in stores(u):
            s.wait()

    def last(u, _):
        keep(u).wait()
        return 0
    lax.fori_loop(0, 16, last, 0)
    ag.sent()
    swap.wait_send()


def run_experts(normed, gates, slots, ui, gate_weight, up_weight, down_weight):
    rows, model = normed.shape
    ff = gate_weight.shape[1]
    n = 32 * SLOTS
    hbm, vmem = pl.BlockSpec(memory_space=pl.ANY), pl.BlockSpec(memory_space=pltpu.VMEM)
    dma = pltpu.SemaphoreType.DMA
    long = jax.ShapeDtypeStruct((n, model), BF16)
    short = jax.ShapeDtypeStruct((n, ff), BF16)
    return pl.pallas_call(
        experts_kernel,
        in_specs=[hbm, vmem, vmem, hbm, vmem, vmem, vmem],
        out_specs=[hbm] * 3 + [vmem] * 4,
        out_shape=[long] * 3 + [short] * 3 + [jax.ShapeDtypeStruct((32, 8, 128), F32)],
        scratch_shapes=[
            pltpu.VMEM((32, 8, 128), F32),
            pltpu.VMEM((n, model), BF16),
            pltpu.VMEM((2, 2 * SLOTS, model), BF16),
            pltpu.VMEM((2, 2 * SLOTS, model), BF16),
            pltpu.VMEM((2, 2 * SLOTS, model), BF16),
            dma((32,)), dma((32,)), dma((2,)), dma((16,)), dma((2, 2)),
        ] + Forth.scratch(rows, model // 2),
        compiler_params=pltpu.CompilerParams(collective_id=13, has_side_effects=True, vmem_limit_bytes=56 * 2**20),
        name="experts",
    )(normed, gates, slots, ui, gate_weight, up_weight, down_weight)


class Back:
    scratch = staticmethod(lambda rows, half: [
        pltpu.VMEM((2, 2, 4, SLOTS, half), BF16),
        pltpu.VMEM((2, 3, 2, 4, SLOTS, half), BF16),
        pltpu.VMEM((2, 4, rows, half), BF16),
        pltpu.VMEM((2, 4, rows, half), BF16),
        pltpu.VMEM((2, 4, rows, half), BF16),
        pltpu.VMEM((2, 4, rows, half), BF16),
        pltpu.SemaphoreType.DMA((2, 2, 4)),
        pltpu.SemaphoreType.DMA((2, 3, 2, 4)), pltpu.SemaphoreType.DMA((2, 3, 2, 4)),
        pltpu.SemaphoreType.DMA((2, 4)), pltpu.SemaphoreType.DMA((2, 4)),
        pltpu.SemaphoreType.DMA((2, 4)), pltpu.SemaphoreType.DMA((2, 4)),
    ])
    n_scratch = 13

    def __init__(self, rows_ref, slots_ref, o_ref, scratch):
        self.rows_ref, self.slots_ref, self.o_ref = rows_ref, slots_ref, o_ref
        (self.own, self.rin, self.sout, self.rb, self.zout, self.rz,
         self.own_sem, self.ts, self.tr, self.bs, self.br, self.zs, self.zr) = scratch
        self.z, self.y, self.x, self.c = place()
        half = rows_ref.shape[1] // 2
        self.cols = [pl.ds(0, half), pl.ds(half, half)]

    def block(self, p, h, k, yy, xx, cc):
        zz = lax.rem(self.z + k, 4)
        if p == 0:
            return number(zz, (1 - yy) if h else yy, xx, cc)
        return number(zz, yy, (1 - xx) if h else xx, cc)

    def sources(self, p):
        y, x, c = self.y, self.x, self.c
        ay, ax = (y, 1 - x) if p == 0 else (1 - y, x)
        return [(y, x, 1 - c), (ay, ax, c), (ay, ax, 1 - c)]

    def slot_rows(self, block, p):
        return self.rows_ref.at[pl.ds(pl.multiple_of(block * SLOTS, 16), SLOTS), self.cols[p]]

    def to(self, p, t, h, k):
        place_of = self.sources(p)[t]
        return pltpu.make_async_remote_copy(
            src_ref=self.slot_rows(self.block(p, h, k, *place_of), p), dst_ref=self.rin.at[p, t, h, k],
            send_sem=self.ts.at[p, t, h, k], recv_sem=self.tr.at[p, t, h, k],
            device_id=(number(self.z, *place_of),), device_id_type=MESH)

    def mine(self, p, h, k):
        return pltpu.make_async_copy(
            self.slot_rows(self.block(p, h, k, self.y, self.x, self.c), p), self.own.at[p, h, k], self.own_sem.at[p, h, k])

    def second(self, p, k):
        z, y, x, c = self.z, self.y, self.x, self.c
        target = number(z, 1 - y, x, c) if p == 0 else number(z, y, 1 - x, c)
        return pltpu.make_async_remote_copy(
            src_ref=self.sout.at[p, k], dst_ref=self.rb.at[p, k], send_sem=self.bs.at[p, k], recv_sem=self.br.at[p, k],
            device_id=(target,), device_id_type=MESH)

    def third(self, p, k):
        target = number(lax.rem(self.z + k, 4), self.y, self.x, self.c)
        return pltpu.make_async_remote_copy(
            src_ref=self.zout.at[p, k], dst_ref=self.rz.at[p, k], send_sem=self.zs.at[p, k], recv_sem=self.zr.at[p, k],
            device_id=(target,), device_id_type=MESH)

    def issue(self, h, i):
        k = far_first(i)
        for p in range(2):
            for t in (1, 2, 0):
                self.to(p, t, h, k).start()
            self.mine(p, h, k).start()

    def start(self):
        self.issue(1, 0)
        self.issue(0, 0)

    def dense(self, p, h, k):
        self.mine(p, h, k).wait()
        for t in range(3):
            self.to(p, t, h, k).wait_recv()
        block = self.block(p, h, k, self.y, self.x, self.c)
        total = None
        for t, who in enumerate([(self.y, self.x, self.c)] + self.sources(p)):
            hit = chosen_rows(self.slots_ref, block, in_plane(*who))
            chosen = jnp.where(hit, 1.0, 0.0).astype(BF16)
            values = self.own[p, h, k] if t == 0 else self.rin[p, t - 1, h, k]
            term = dims(chosen, values, 0, 0)
            total = term if total is None else total + term
        return total

    def step(self, u):
        i = u // 2
        k = far_first(i)
        early = lax.rem(u, 2) == 0

        @pl.when(early)
        def _():
            for p in range(2):
                self.sout[p, k] = self.dense(p, 1, k).astype(BF16)
                self.second(p, k).start()

            @pl.when(i < 3)
            def _():
                self.issue(1, i + 1)

        @pl.when(jnp.logical_not(early))
        def _():
            for p in range(2):
                total = self.dense(p, 0, k)
                self.second(p, k).wait_recv()
                total = total + self.rb[p, k].astype(F32)

                @pl.when(k > 0)
                def _(p=p, total=total):
                    self.zout[p, k] = total.astype(BF16)
                    self.third(p, k).start()

                @pl.when(k == 0)
                def _(p=p, total=total):
                    self.o_ref[:, self.cols[p]] = total

            @pl.when(i < 3)
            def _():
                self.issue(0, i + 1)

    def finish(self):
        for p in range(2):
            for k in range(1, 4):
                self.third(p, k).wait_recv()
            self.o_ref[:, self.cols[p]] += (
                self.rz[p, 1].astype(F32) + self.rz[p, 2].astype(F32) + self.rz[p, 3].astype(F32)
            )

        def one(k, _):
            for p in range(2):
                self.second(p, k).wait_send()

                @pl.when(k > 0)
                def _(p=p):
                    self.third(p, k).wait_send()
                for t in range(3):
                    for h in range(2):
                        self.to(p, t, h, k).wait_send()
            return 0
        lax.fori_loop(0, 4, one, 0)


def grads_kernel(
    dx_ref, slots_ref, gg_ref, xi_ref, ui_ref, hg_ref, dg_ref, du_ref,
    o_ref, back_ref, wg_out, wu_out, wd_out, xcol, ucol, gout, uout, dout, gs, gr, isem, osem, *scratch,
):
    greet_all()
    swap = Swap(lambda t: gg_ref.at[t], back_ref, gs, gr)
    rs = Back(dx_ref, slots_ref, o_ref, scratch)
    rs.start()
    swap.start()

    def col(i):
        return pl.ds(pl.multiple_of(i * 256, 256), 256)

    def loads(i):
        s = lax.rem(i, 2)
        return [
            pltpu.make_async_copy(xi_ref.at[:, col(i)], xcol.at[s], isem.at[0, s]),
            pltpu.make_async_copy(ui_ref.at[:, col(i)], ucol.at[s], isem.at[1, s]),
        ]

    def stores(i):
        s = lax.rem(i, 2)
        return [
            pltpu.make_async_copy(gout.at[s], wg_out.at[col(i), :], osem.at[0, s]),
            pltpu.make_async_copy(uout.at[s], wu_out.at[col(i), :], osem.at[1, s]),
            pltpu.make_async_copy(dout.at[s], wd_out.at[:, col(i)], osem.at[2, s]),
        ]

    for cp in loads(0):
        cp.start()

    def one(u, _):
        @pl.when(u < 6)
        def _():
            s = lax.rem(u, 2)

            @pl.when(u < 5)
            def _():
                for cp in loads(u + 1):
                    cp.start()

            for cp in loads(u):
                cp.wait()

            @pl.when(u >= 2)
            def _():
                for cp in stores(u - 2):
                    cp.wait()

            rows_in = xcol[s]
            gout[s] = dims(rows_in, dg_ref[...], 0, 0)
            uout[s] = dims(rows_in, du_ref[...], 0, 0)
            dout[s] = dims(hg_ref[...], ucol[s], 0, 0)
            for cp in stores(u):
                cp.start()

        rs.step(u)
        return 0

    lax.fori_loop(0, 8, one, 0)
    for i in (4, 5):
        for cp in stores(i):
            cp.wait()
    swap.wait_recv()
    rs.finish()
    swap.wait_send()


def run_grads(dx, slots, gg, xi, ui, hg, dg, du):
    rows, model = slots.shape[2], dx.shape[1]
    ff = hg.shape[1]
    n = dx.shape[0]
    hbm, vmem = pl.BlockSpec(memory_space=pl.ANY), pl.BlockSpec(memory_space=pltpu.VMEM)
    dma = pltpu.SemaphoreType.DMA
    return pl.pallas_call(
        grads_kernel,
        in_specs=[hbm, vmem, vmem, hbm, hbm, vmem, vmem, vmem],
        out_specs=[vmem, vmem, hbm, hbm, hbm],
        out_shape=[
            jax.ShapeDtypeStruct((rows, model), F32),
            jax.ShapeDtypeStruct((32, 8, 128), F32),
            jax.ShapeDtypeStruct((model, ff), F32),
            jax.ShapeDtypeStruct((model, ff), F32),
            jax.ShapeDtypeStruct((ff, model), F32),
        ],
        scratch_shapes=[
            pltpu.VMEM((2, n, 256), BF16), pltpu.VMEM((2, n, 256), BF16),
            pltpu.VMEM((2, 256, ff), F32), pltpu.VMEM((2, 256, ff), F32), pltpu.VMEM((2, ff, 256), F32),
            dma((32,)), dma((32,)), dma((2, 2)), dma((3, 2)),
        ] + Back.scratch(rows, model // 2),
        compiler_params=pltpu.CompilerParams(collective_id=14, has_side_effects=True, vmem_limit_bytes=56 * 2**20),
        name="grads",
    )(dx, slots, gg, xi, ui, hg, dg, du)


def attend_mesh_kernel(
    chunks, rows, lo_ref, q_ref, kv_ref, u_ref, mine_ref, o_ref, lse_ref, window, slots_ref, ui_ref,
    bias, gs, gr, lsem, ws, wr, *scratch,
):
    greet_all()
    swap = Swap(lambda t: mine_ref.at[t // 8], slots_ref, gs, gr)
    keys = Window(rows, kv_ref, window, (lsem, ws, wr))
    ag = Forth(u_ref, slots_ref, ui_ref, scratch)
    keys.start()
    swap.start()
    ag.start()
    make_bias(bias, lo_ref, chunks, rows)
    keys.previous()
    swap.wait_recv()
    ag.one(0)
    keys.pass_on()
    ag.one(1)
    keys.end()
    width = 2 * GROUP * HEAD_DIM

    def pair(j, _):
        lanes = pl.ds(pl.multiple_of(j * 2 * HEAD_DIM, 2 * HEAD_DIM), 2 * HEAD_DIM)
        head = pl.ds(pl.multiple_of(j * width, width), width)

        def between(half):
            u = 2 * j + half + 2

            @pl.when((u == 3) | (u == 5))
            def _():
                ag.one((u + 1) // 2)

            @pl.when((u == 2) | (u == 4) | (u == 6) | (u == 7))
            def _():
                ag.two(jnp.where(u == 7, 3, u // 2 - 1))

        attend_pair(
            chunks, rows, lax.rem(lax.axis_index("dev"), 2), q_ref.at[head, :], window.at[:, :, lanes],
            o_ref.at[head, :], lse_ref.at[pl.ds(j, 1)], bias, between,
        )
        return 0

    lax.fori_loop(0, KEY_HEADS // 2, pair, 0)

    def last(u, _):
        ag.arrived(lax.rem(u, 4), u // 4)
        return 0
    lax.fori_loop(0, 16, last, 0)
    ag.sent()
    keys.sent()
    swap.wait_send()


def attend_mesh(query_t, kv, lo, upstream, mine):
    rows = query_t.shape[1]
    chunks = 9
    model = upstream.shape[1]
    hbm, vmem = pl.BlockSpec(memory_space=pl.ANY), pl.BlockSpec(memory_space=pltpu.VMEM)
    dma = pltpu.SemaphoreType.DMA
    return pl.pallas_call(
        functools.partial(attend_mesh_kernel, chunks, rows),
        in_specs=[vmem] * 2 + [hbm, hbm, vmem],
        out_specs=[vmem] * 4 + [hbm],
        out_shape=[
            jax.ShapeDtypeStruct(query_t.shape, BF16),
            jax.ShapeDtypeStruct((KEY_HEADS // 2, 8, rows), F32),
            jax.ShapeDtypeStruct((2, 10 * rows, kv.shape[2]), BF16),
            jax.ShapeDtypeStruct((32, 8, rows), F32),
            jax.ShapeDtypeStruct((32 * SLOTS, model), BF16),
        ],
        scratch_shapes=[pltpu.VMEM((chunks * rows, rows), F32), dma((32,)), dma((32,))]
        + Window.scratch + Forth.scratch(rows, model // 2),
        compiler_params=pltpu.CompilerParams(collective_id=16, has_side_effects=True, vmem_limit_bytes=56 * 2**20),
        name="attend",
    )(lo, query_t, kv, upstream, mine)


def attend_back_mesh_kernel(
    chunks, rows, lo_ref, cos_ref, sin_ref, q_ref, kv_ref, g_ref, lse_ref, delta_ref, y_ref, slots_ref,
    dq_ref, dkv_ref, o_ref, bias, *scratch,
):
    greet_near()
    rs = Back(y_ref, slots_ref, o_ref, scratch)
    rs.start()
    make_bias(bias, lo_ref, chunks, rows)
    width = 2 * GROUP * HEAD_DIM

    def pair(j, _):
        lanes = pl.ds(pl.multiple_of(j * 2 * HEAD_DIM, 2 * HEAD_DIM), 2 * HEAD_DIM)
        head = pl.ds(pl.multiple_of(j * width, width), width)

        def between(half):
            rs.step(2 * j + half)

        attend_back_pair(
            chunks, rows, lax.rem(lax.axis_index("dev"), 2), cos_ref, sin_ref, q_ref.at[head, :], kv_ref.at[:, :, lanes], g_ref.at[head, :],
            lse_ref.at[pl.ds(j, 1)], delta_ref.at[pl.ds(j, 1)], dq_ref.at[head, :], dkv_ref.at[:, :, lanes], bias, between,
        )
        return 0

    lax.fori_loop(0, KEY_HEADS // 2, pair, 0)
    rs.finish()


def attend_back_mesh(query_t, window, lo, grad_t, lse, delta, cos_t, sin_t, y, slots):
    rows, span = query_t.shape[1], window.shape[1]
    chunks = span // rows - 1
    model = y.shape[1]
    hbm, vmem = pl.BlockSpec(memory_space=pl.ANY), pl.BlockSpec(memory_space=pltpu.VMEM)
    return pl.pallas_call(
        functools.partial(attend_back_mesh_kernel, chunks, rows),
        in_specs=[vmem] * 8 + [hbm, vmem],
        out_specs=[vmem] * 3,
        out_shape=[
            jax.ShapeDtypeStruct(query_t.shape, BF16),
            jax.ShapeDtypeStruct(window.shape, BF16),
            jax.ShapeDtypeStruct((rows, model), F32),
        ],
        scratch_shapes=[pltpu.VMEM((chunks * rows, rows), F32)] + Back.scratch(rows, model // 2),
        compiler_params=pltpu.CompilerParams(collective_id=15, has_side_effects=True, vmem_limit_bytes=56 * 2**20),
        name="attend_back",
    )(lo, cos_t, sin_t, query_t, window, grad_t, lse, delta, y, slots)


def rms_scale(values):
    return lax.rsqrt(jnp.mean(values * values, axis=-1, keepdims=True) + EPSILON)


def rotate_t(values, cosine, sine):
    half = cosine.shape[0]
    shaped = values.reshape(-1, 2, half, values.shape[1])
    u, w = shaped[:, 0], shaped[:, 1]
    turned = jnp.stack([u * cosine - w * sine, w * cosine + u * sine], axis=1)
    return turned.reshape(values.shape)


def gathered(block, cid, by_rows):
    if meshed():
        return gather_all(block, cid, by_rows)
    return lax.all_gather(block, "dev", axis=0, tiled=True)


def reduced(dense, more, cid):
    if meshed():
        return reduce_all(dense, more, cid)
    dense = jnp.concatenate([dense, more], axis=1)
    return lax.psum_scatter(dense, "dev", scatter_dimension=0, tiled=True).astype(F32)


def on_device(
    tokens,
    positions,
    expert_picks,
    priority,
    first_gain,
    query_weight,
    key_projection_matrix,
    value_projection_matrix,
    output_weight,
    second_gain,
    router_weight,
    gate_weight,
    up_weight,
    down_weight,
    cotangent,
):
    devices = lax.axis_size("dev")
    rows, model = tokens.shape
    split = devices // EXPERTS
    capacity = split * ((9 * rows * TOP + 8 * EXPERTS * split - 1) // (8 * EXPERTS * split))
    weight_rows = query_weight.shape[0]

    output_matrix = lax.all_gather(output_weight, "dev", axis=0, tiled=True)

    extra = jnp.concatenate([router_weight, first_gain[:, None], second_gain[:, None]], axis=1)
    pad = (-extra.shape[1]) % 128
    packed = jnp.concatenate(
        [query_weight, key_projection_matrix, value_projection_matrix, extra, jnp.zeros((weight_rows, pad), BF16)],
        axis=1,
    )
    matrices = gathered(packed, 1, False)
    qkv_matrix = matrices[:, :QKV]
    router_matrix = matrices[:, QKV : QKV + EXPERTS]
    gain_first = matrices[:, QKV + EXPERTS].astype(F32)
    gain_second = matrices[:, QKV + EXPERTS + 1].astype(F32)

    one_hot = expert_picks[:, :, None] == jnp.arange(EXPERTS, dtype=jnp.int32)
    picked_any = jnp.any(one_hot, axis=1)
    turn = jnp.sum(jnp.where(one_hot, priority[:, :, None], 0), axis=1)
    turn = jnp.where(picked_any, turn, jnp.int32(2**30)).T
    rank = jnp.sum((turn[:, None, :] < turn[:, :, None]).astype(jnp.int32), axis=2)
    slot_rows = jnp.where(picked_any.T & (rank < capacity), rank, -1).astype(F32)

    inputs = tokens.astype(F32)
    scale_one = rms_scale(inputs)
    normed_one = (inputs * scale_one * gain_first).astype(BF16)
    half_dim = HEAD_DIM // 2
    frequency = jnp.power(10000.0, -(jnp.arange(half_dim, dtype=F32) * 2.0) / HEAD_DIM)
    angle = positions.astype(F32)[None, :] * frequency[:, None]
    cos_t, sin_t = jnp.cos(angle), jnp.sin(angle)
    qkv_t = dims(qkv_matrix, normed_one, 0, 1)
    q_width, k_width = QUERY_HEADS * HEAD_DIM, KEY_HEADS * HEAD_DIM
    query_t = rotate_t(qkv_t[:q_width], cos_t, sin_t).astype(BF16) * BF16(HEAD_DIM**-0.5)
    key = rotate_t(qkv_t[q_width : q_width + k_width], cos_t, sin_t).astype(BF16).T
    value = qkv_t[q_width + k_width :].astype(BF16).T
    kv = jnp.stack([key, value])
    lo = (jnp.arange(rows, dtype=jnp.int32) - positions)[None, :]
    if meshed():
        attended_t, lse, window, plane_slots, expert_up = attend_mesh(
            query_t, kv, lo, cotangent, slot_rows.reshape(-1, 8, rows)
        )
    else:
        window, offset = window_of(kv), jnp.int32(0)
        attended_t, lse = attend(query_t, window, offset, lo)
    residual = inputs + dims(attended_t, output_matrix, 0, 0)
    scale_two = rms_scale(residual)
    normed_two = (residual * scale_two * gain_second).astype(BF16)

    logits = dims(normed_two, router_matrix, 1, 0)
    logits = jnp.where(picked_any, logits, MASKED)
    picked_exp = jnp.exp(logits - jnp.max(logits, axis=1, keepdims=True))
    gates = picked_exp / jnp.sum(picked_exp, axis=1, keepdims=True)

    if meshed():
        gate_rows = jnp.pad(gates.T.reshape(EXPERTS, rows // 128, 128), ((0, 0), (0, 8 - rows // 128), (0, 0)))
        expert_in, grad_rows, out_rows, gated_hidden, gate_in_grad, up_in_grad, gate_grad_rows = run_experts(
            normed_two, gate_rows, plane_slots, expert_up, gate_weight, up_weight, down_weight
        )
        returned_grad, gate_grad, gate_gradient, up_gradient, down_gradient = run_grads(
            grad_rows, plane_slots, gate_grad_rows, expert_in, expert_up, gated_hidden, gate_in_grad, up_in_grad
        )
        gate_grad = gate_grad[:, : rows // 128].reshape(EXPERTS, rows).T
    else:
        gate_rows, slot = (
            lax.all_to_all(jnp.repeat(v, split, axis=0), "dev", split_axis=0, concat_axis=0, tiled=True)
            for v in (gates.T, slot_rows)
        )
        pair_slot = jnp.where(
            slot.reshape(devices // 2, 2, rows) >= 0,
            slot.reshape(devices // 2, 2, rows) + jnp.array([[0], [capacity]], F32),
            -1.0,
        ).astype(jnp.int32).reshape(devices // 2, 1, 2 * rows)
        all_upstream = lax.all_gather(cotangent, "dev", axis=0, tiled=True)
        all_normed = lax.all_gather(normed_two, "dev", axis=0, tiled=True)
        expert_in, expert_up = dispatch(pair_slot, all_normed, all_upstream, 2 * capacity)
        slot_hit = slot[:, None, :] == jnp.arange(capacity, dtype=F32)[None, :, None]
        gate_of_slot = jnp.sum(jnp.where(slot_hit, gate_rows[:, None, :], 0.0), axis=2).reshape(-1, 1)
        gate_in = dims(expert_in, gate_weight, 1, 0)
        up_in = dims(expert_in, up_weight, 1, 0)
        sigmoid_gate = 1.0 / (1.0 + jnp.exp(-gate_in))
        silu_gate = gate_in * sigmoid_gate
        hidden = (silu_gate * up_in).astype(BF16)
        gated_hidden = (hidden.astype(F32) * gate_of_slot).astype(BF16)
        hidden_up = dims(expert_up, down_weight, 1, 1)
        hidden_grad = hidden_up * gate_of_slot
        gate_grad_slot = jnp.sum(hidden.astype(F32) * hidden_up, axis=1).reshape(devices, capacity)
        gate_in_grad = (hidden_grad * up_in * sigmoid_gate * (1.0 + gate_in * (1.0 - sigmoid_gate))).astype(BF16)
        up_in_grad = (hidden_grad * silu_gate).astype(BF16)
        partial_in = (dims(gate_in_grad, gate_weight, 1, 1) + dims(up_in_grad, up_weight, 1, 1)).astype(BF16)
        gate_grad_rows = jnp.sum(jnp.where(slot_hit, gate_grad_slot[:, :, None], 0.0), axis=1)
        returned_grad = lax.psum_scatter(
            combine(pair_slot, partial_in, 2 * capacity), "dev", scatter_dimension=0, tiled=True
        ).astype(F32)
        gate_grad = lax.all_to_all(gate_grad_rows, "dev", split_axis=0, concat_axis=0, tiled=True)
        gate_grad = jnp.sum(gate_grad.reshape(EXPERTS, split, rows), axis=1).T
        partial_out = dims(gated_hidden, down_weight, 1, 0).astype(BF16)
        dense_out = combine(pair_slot, partial_out, 2 * capacity)
        mixture = lax.psum_scatter(dense_out, "dev", scatter_dimension=0, tiled=True).astype(F32)
        down_gradient = dims(gated_hidden, expert_up, 0, 0)
        gate_gradient = dims(expert_in, gate_in_grad, 0, 0)
        up_gradient = dims(expert_in, up_in_grad, 0, 0)

    upstream = cotangent.astype(F32)
    logit_grad = (gates * (gate_grad - jnp.sum(gates * gate_grad, axis=1, keepdims=True))).astype(BF16)
    router_gradient = dims(normed_two, logit_grad, 0, 0)
    normed_two_grad = returned_grad + dims(logit_grad, router_matrix, 1, 1)
    weighted_two = normed_two_grad * gain_second
    second_gain_grad = jnp.sum(normed_two_grad * residual * scale_two, axis=0)
    residual_grad = (
        upstream
        + scale_two * weighted_two
        - residual * scale_two**3 * jnp.mean(weighted_two * residual, axis=-1, keepdims=True)
    )
    branch_grad = residual_grad.astype(BF16)
    output_gradient = dims(attended_t, branch_grad, 1, 0).astype(BF16)
    output_gradient = lax.psum_scatter(output_gradient, "dev", scatter_dimension=0, tiled=True).astype(F32)
    grad_t = dims(output_matrix, branch_grad, 1, 1).astype(BF16)

    delta = jnp.sum((attended_t.astype(F32) * grad_t.astype(F32)).reshape(QUERY_HEADS, HEAD_DIM, rows), axis=1)
    delta = jnp.pad(delta.reshape(KEY_HEADS // 2, 2 * GROUP, rows), ((0, 0), (0, 8 - 2 * GROUP), (0, 0)))
    if meshed():
        query_grad_t, window_grad, mixture = attend_back_mesh(
            query_t, window, lo, grad_t, lse, delta, cos_t, sin_t, out_rows, plane_slots
        )
    else:
        query_grad_t, window_grad = attend_back(query_t, window, offset, lo, grad_t, lse, delta, cos_t, sin_t)
    layer_output = (residual + mixture).astype(BF16)
    key_grad, value_grad = unwindow(window_grad)
    key_grad_t = rotate_t(key_grad.T, cos_t, -sin_t).astype(BF16)
    qkv_grad_t = jnp.concatenate([query_grad_t, key_grad_t, value_grad.T.astype(BF16)], axis=0)
    qkv_gradient = dims(normed_one, qkv_grad_t, 0, 1)
    normed_one_grad = dims(qkv_grad_t, qkv_matrix, 0, 1)
    weighted_one = normed_one_grad * gain_first
    first_gain_grad = jnp.sum(normed_one_grad * inputs * scale_one, axis=0)
    tokens_gradient = (
        residual_grad
        + scale_one * weighted_one
        - inputs * scale_one**3 * jnp.mean(weighted_one * inputs, axis=-1, keepdims=True)
    )
    terms = qkv_gradient.astype(BF16)
    more = jnp.concatenate(
        [router_gradient, first_gain_grad[:, None], second_gain_grad[:, None],
         jnp.zeros((model, (-(EXPERTS + 2)) % 256), F32)],
        axis=1,
    ).astype(BF16)
    sums = reduced(terms, more, 4)
    return (
        layer_output,
        tokens_gradient,
        sums[:, QKV + EXPERTS],
        sums[:, :q_width],
        sums[:, q_width : q_width + k_width],
        sums[:, q_width + k_width : QKV],
        output_gradient,
        sums[:, QKV + EXPERTS + 1],
        sums[:, QKV : QKV + EXPERTS],
        gate_gradient,
        up_gradient,
        down_gradient,
    )


def solution(mesh):
    rows, whole = P("dev", None), P("dev")
    columns = P(None, "dev")
    return jax.shard_map(
        on_device,
        mesh=mesh,
        in_specs=(rows, whole, rows, rows, whole, rows, rows, rows, rows, whole, rows, columns, columns, rows, rows),
        out_specs=(rows, rows, whole, rows, rows, rows, rows, whole, rows, columns, columns, rows),
        check_vma=False,
    )
```

```python
import functools
import jax, jax.numpy as jnp
from jax import lax
from jax.experimental import pallas as pl
from jax.experimental.pallas import tpu as pltpu

MESH = pl.DeviceIdType.MESH


def place():
    me = lax.axis_index("dev")
    return lax.rem(me // 8, 4), lax.rem(me // 4, 2), lax.rem(me // 2, 2), lax.rem(me, 2)


def number(z, y, x, c):
    return ((z * 2 + y) * 2 + x) * 2 + c


def greet(partners):
    barrier = pltpu.get_barrier_semaphore()
    for partner in partners:
        pl.semaphore_signal(barrier, inc=1, device_id=(partner,), device_id_type=MESH)
    pl.semaphore_wait(barrier, len(partners))


def partners_of(z, y, x, c):
    return [
        number(z, y, x, 1 - c),
        number(z, y, 1 - x, c),
        number(z, 1 - y, x, c),
        number(lax.rem(z + 1, 4), y, x, c),
        number(lax.rem(z + 2, 4), y, x, c),
        number(lax.rem(z + 3, 4), y, x, c),
    ]


def gather_kernel(rows, pieces, x_ref, o_ref, local_sem, ss, rs):
    z, y, x, c = place()
    greet(partners_of(z, y, x, c))
    sibling = number(z, y, x, 1 - c)
    me = number(z, y, x, c)
    around = (number(z, 1 - y, x, c), number(z, y, 1 - x, c))

    def part(ref, block, p):
        r0, nr, c0, nc = pieces[p]
        return ref.at[pl.ds(pl.multiple_of(block * rows + r0, 16), nr), pl.ds(c0, nc)]

    def copy(block, p, slot, target, own=False):
        source = part(x_ref, 0, p) if own else part(o_ref, block, p)
        return pltpu.make_async_remote_copy(
            src_ref=source, dst_ref=part(o_ref, block, p),
            send_sem=ss.at[p * 31 + slot], recv_sem=rs.at[p * 31 + slot],
            device_id=(target,), device_id_type=MESH)

    pending = []

    def send(*args, **kw):
        cp = copy(*args, **kw)
        cp.start()
        pending.append(cp)

    def at(k, fy, fx):
        return number(lax.rem(z + 4 - k, 4), (1 - y) if fy else y, (1 - x) if fx else x, c)

    local = pltpu.make_async_copy(x_ref, o_ref.at[pl.ds(pl.multiple_of(me * rows, 16), rows), :], local_sem)
    local.start()
    order = (0, 1, 3, 2)
    far = ((1, 0), (0, 1))
    for k in (1, 3, 2):
        for p in range(2):
            send(me, p, k - 1, number(lax.rem(z + k, 4), y, x, c), own=True)
    for k in order:
        for p in range(2):
            block = at(k, 0, 0)
            if k:
                copy(block, p, k - 1, sibling).wait_recv()
            own = k == 0
            send(block, p, 3 + k, around[p], own=own)
            send(block, p, 7 + k, around[1 - p], own=own)
            send(block, p, 15 + k, sibling, own=own)
    for k in order:
        for p in range(2):
            fy, fx = far[p]
            block = at(k, fy, fx)
            copy(block, p, 3 + k, sibling).wait_recv()
            send(block, p, 11 + k, around[1 - p])
            send(block, p, 19 + k, sibling)
    for j, slot in ((0, 7), (1, 11)):
        for k in order:
            for p in range(2):
                fy, fx = (1, 1) if j else (1 - far[p][0], 1 - far[p][1])
                block = at(k, fy, fx)
                copy(block, p, slot + k, sibling).wait_recv()
                send(block, p, 23 + 4 * j + k, sibling)
    for k in range(4):
        for p in range(2):
            for s in (15, 19, 23, 27):
                copy(me, p, s + k, sibling).wait_recv()
    for cp in pending:
        cp.wait_send()
    local.wait()


def gather_all(block, cid, by_rows):
    rows, cols = block.shape
    if by_rows:
        pieces = ((0, rows // 2, 0, cols), (rows // 2, rows // 2, 0, cols))
    else:
        half = (cols // 256) * 128
        pieces = ((0, rows, 0, half), (0, rows, half, cols - half))
    return pl.pallas_call(
        functools.partial(gather_kernel, rows, pieces),
        out_shape=jax.ShapeDtypeStruct((32 * rows, cols), block.dtype),
        in_specs=[pl.BlockSpec(memory_space=pl.ANY)],
        out_specs=pl.BlockSpec(memory_space=pl.ANY),
        scratch_shapes=[pltpu.SemaphoreType.DMA, pltpu.SemaphoreType.DMA((62,)), pltpu.SemaphoreType.DMA((62,))],
        compiler_params=pltpu.CompilerParams(collective_id=cid, has_side_effects=True),
        name="gather_all",
    )(block)


from jax.sharding import PartitionSpec as P

QUERY_HEADS = 24
KEY_HEADS = 8
HEAD_DIM = 64
GROUP = QUERY_HEADS // KEY_HEADS
TOP = 8
EXPERTS = 32
MAXDOC = 2000
EPSILON = 1e-06
MASKED = -1e30
QKV = (QUERY_HEADS + 2 * KEY_HEADS) * HEAD_DIM
F32 = jnp.float32
BF16 = jnp.bfloat16


def meshed():
    return lax.axis_size("dev") == 32


def dims(a, b, ca, cb):
    return lax.dot_general(a, b, (((ca,), (cb,)), ((), ())), preferred_element_type=F32)


class Window:
    scratch = [pltpu.SemaphoreType.DMA((2,)), pltpu.SemaphoreType.DMA((9,)), pltpu.SemaphoreType.DMA((9,))]

    def __init__(self, rows, kv_ref, out, scratch):
        self.rows, self.kv_ref, self.out = rows, kv_ref, out
        self.lsem, self.ss, self.rs = scratch
        self.z, self.y, self.x, self.c = place()
        self.p = self.y * 2 + self.x
        self.sibling = number(self.z, self.y, self.x, 1 - self.c)
        self.near = [(self.z * 4 + lax.rem(self.p + d, 4)) * 2 + self.c for d in (1, 2, 3)]
        self.own_in = pltpu.make_async_copy(kv_ref, self.slot(4, self.c), self.lsem.at[0])
        self.stand_in = pltpu.make_async_copy(kv_ref, self.slot(0, self.c), self.lsem.at[1])
        self.to_up = self.copy(kv_ref, 0, 0, number(lax.rem(self.z + 1, 4), self.y, self.x, self.c))

    def slot(self, s, core):
        return self.out.at[:, pl.ds(pl.multiple_of((2 * s + core) * self.rows, 16), self.rows), :]

    def copy(self, source, s, n, target):
        return pltpu.make_async_remote_copy(
            src_ref=source, dst_ref=self.slot(s, self.c), send_sem=self.ss.at[n], recv_sem=self.rs.at[n],
            device_id=(target,), device_id_type=MESH)

    def own_near(self, d):
        return self.copy(self.kv_ref, 4 - d, d, self.near[d - 1])

    def across(self, s):
        source = self.kv_ref if s == 4 else self.slot(s, self.c)
        return self.copy(source, s, {4: 4, 0: 5}.get(s, 9 - s), self.sibling)

    def start(self):
        self.own_in.start()

        @pl.when(self.z < 3)
        def _():
            self.to_up.start()

        @pl.when(self.z == 0)
        def _():
            self.stand_in.start()

        for d in (1, 3, 2):
            @pl.when(self.p + d < 4)
            def _(d=d):
                self.own_near(d).start()
        self.across(4).start()

    def previous(self):
        @pl.when(self.z == 0)
        def _():
            self.stand_in.wait()

        @pl.when(self.z > 0)
        def _():
            self.to_up.wait_recv()

        for d in (3, 1, 2):
            @pl.when(self.p + d >= 4)
            def _(d=d):
                self.copy(self.slot(0, self.c), 4 - d, d, self.near[d - 1]).start()
        self.across(0).start()

    def pass_on(self):
        for d in (1, 3, 2):
            self.own_near(d).wait_recv()
            self.across(4 - d).start()

    def end(self):
        for s in range(5):
            pltpu.make_async_remote_copy(
                src_ref=self.kv_ref, dst_ref=self.slot(s, 1 - self.c), send_sem=self.ss.at[0],
                recv_sem=self.rs.at[{4: 4, 0: 5}.get(s, 9 - s)], device_id=(self.sibling,), device_id_type=MESH).wait_recv()
        self.own_in.wait()

    def sent(self):
        @pl.when(self.z < 3)
        def _():
            self.to_up.wait_send()

        for d in (1, 2, 3):
            self.own_near(d).wait_send()
        for s in range(5):
            self.across(s).wait_send()


def window_of(kv):
    rows = kv.shape[1]
    devices = lax.axis_size("dev")
    back = (MAXDOC + rows - 2) // rows
    parts = [
        lax.ppermute(kv, "dev", [(i - d, i) for i in range(d, devices)]) for d in range(back, 0, -1)
    ]
    return jnp.concatenate(parts + [kv, jnp.zeros_like(kv)], axis=1)


class Unwindow:
    @staticmethod
    def scratch(rows, width):
        return [
            pltpu.VMEM((5, 2, rows, width), BF16),
            pltpu.VMEM((3, 2, rows, width), BF16),
            pltpu.VMEM((2, rows, width), BF16),
            pltpu.SemaphoreType.DMA((9,)), pltpu.SemaphoreType.DMA((9,)),
        ]

    n_scratch = 5
    order = (3, 1, 2, 0, 4)

    def __init__(self, rows, grads, o_ref, scratch):
        self.rows, self.grads, self.o_ref = rows, grads, o_ref
        self.got, self.near_got, self.far, self.ss, self.rs = scratch
        self.z, self.y, self.x, self.c = place()
        self.p = self.y * 2 + self.x
        self.sibling = number(self.z, self.y, self.x, 1 - self.c)
        self.to_down = pltpu.make_async_remote_copy(
            src_ref=self.got.at[0], dst_ref=self.far, send_sem=self.ss.at[8], recv_sem=self.rs.at[8],
            device_id=(number(lax.rem(self.z + 3, 4), self.y, self.x, self.c),), device_id_type=MESH)

    def to_sibling(self, s):
        at = pl.ds(pl.multiple_of((2 * s + 1 - self.c) * self.rows, 16), self.rows)
        return pltpu.make_async_remote_copy(
            src_ref=self.grads.at[:, at, :], dst_ref=self.got.at[s], send_sem=self.ss.at[s], recv_sem=self.rs.at[s],
            device_id=(self.sibling,), device_id_type=MESH)

    def to_owner(self, d):
        owner = (self.z * 4 + lax.rem(self.p + 4 - d, 4)) * 2 + self.c
        return pltpu.make_async_remote_copy(
            src_ref=self.got.at[4 - d], dst_ref=self.near_got.at[d - 1], send_sem=self.ss.at[4 + d], recv_sem=self.rs.at[4 + d],
            device_id=(owner,), device_id_type=MESH)

    def rowwise(self, body):
        for h in range(2):
            def step(i, _, h=h):
                body(h, pl.multiple_of(i * 32, 32))
                return 0
            lax.fori_loop(0, self.rows // 32, step, 0)

    def start(self):
        for s in self.order:
            self.to_sibling(s).start()

    def sums(self):
        for s in self.order:
            self.to_sibling(s).wait_recv()
            first = (2 * s + self.c) * self.rows

            def both(h, r, s=s, first=first):
                at = pl.ds(r, 32)
                mine = self.grads[h, pl.ds(pl.multiple_of(first + r, 32), 32), :]
                total = self.got[s, h, at, :].astype(F32) + mine.astype(F32)
                if s == 4:
                    self.o_ref[h, at, :] = total
                else:
                    self.got[s, h, at, :] = total.astype(BF16)
            self.rowwise(both)
            if 0 < s < 4:
                self.to_owner(4 - s).start()

    def near(self):
        for d in (1, 3, 2):
            self.to_owner(d).wait_recv()

            @pl.when(self.p + d < 4)
            def _(d=d):
                def body(h, r):
                    at = pl.ds(r, 32)
                    self.o_ref[h, at, :] += self.near_got[d - 1, h, at, :].astype(F32)
                self.rowwise(body)

            @pl.when(self.p + d >= 4)
            def _(d=d):
                def body(h, r):
                    at = pl.ds(r, 32)
                    total = self.got[0, h, at, :].astype(F32) + self.near_got[d - 1, h, at, :].astype(F32)
                    self.got[0, h, at, :] = total.astype(BF16)
                self.rowwise(body)

        @pl.when(self.z > 0)
        def _():
            self.to_down.start()

    def end(self):
        @pl.when(self.z < 3)
        def _():
            self.to_down.wait_recv()

            def body(h, r):
                at = pl.ds(r, 32)
                self.o_ref[h, at, :] += self.far[h, at, :].astype(F32)
            self.rowwise(body)

        @pl.when(self.z > 0)
        def _():
            self.to_down.wait_send()

        for s in range(5):
            self.to_sibling(s).wait_send()
        for d in (1, 2, 3):
            self.to_owner(d).wait_send()


def unwindow(grads):
    rows = grads.shape[1] // 10
    devices = lax.axis_size("dev")
    back = (MAXDOC + rows - 2) // rows
    total = grads[:, back * rows : (back + 1) * rows].astype(F32)
    for d in range(1, back + 1):
        piece = grads[:, (back - d) * rows : (back - d + 1) * rows]
        moved = lax.ppermute(piece, "dev", [(i, i - d) for i in range(d, devices)])
        total = total + moved.astype(F32)
    return total


def make_bias(bias, lo_ref, chunks, rows):
    def fill(ch, _):
        at = pl.ds(pl.multiple_of(ch * rows, rows), rows)
        relative = lax.broadcasted_iota(jnp.int32, (rows, rows), 0) + (ch - (chunks - 1)) * rows
        query = lax.broadcasted_iota(jnp.int32, (rows, rows), 1)
        allowed = (relative <= query) & (relative >= lo_ref[...])
        bias[at, :] = jnp.where(allowed, 0.0, MASKED)
        return 0
    lax.fori_loop(0, chunks, fill, 0)


def side_by_side(ref, half):
    first = half * GROUP
    return jnp.concatenate(
        [ref[(first + g) * HEAD_DIM : (first + g + 1) * HEAD_DIM, :] for g in range(GROUP)], axis=1
    )


def stats_of(ref, half):
    return jnp.concatenate([ref[0, half * GROUP + g : half * GROUP + g + 1, :] for g in range(GROUP)], axis=1)


def attend_pair(chunks, rows, off, q_ref, kv_ref, o_ref, lse_ref, bias, between):
    lse_ref[...] = jnp.zeros_like(lse_ref)
    width = GROUP * rows
    for half in range(2):
        lanes = slice(half * HEAD_DIM, (half + 1) * HEAD_DIM)
        queries = side_by_side(q_ref, half)

        def chunk(i, carry, lanes=lanes, queries=queries):
            ch = chunks - 1 - i
            at = pl.ds(pl.multiple_of((ch + off) * rows, rows), rows)
            key, value = kv_ref[0, at, lanes], kv_ref[1, at, lanes]
            shift = bias[pl.ds(pl.multiple_of(ch * rows, rows), rows), :]
            top, total, mixed = carry
            score = dims(key, queries, 1, 0) + jnp.concatenate([shift] * GROUP, axis=1)
            new_top = jnp.maximum(top, jnp.max(score, axis=0, keepdims=True))
            weight = jnp.exp(score - new_top)
            fade = jnp.exp(top - new_top)
            total = total * fade + jnp.sum(weight, axis=0, keepdims=True)
            mixed = mixed * fade + dims(value, weight.astype(BF16), 0, 0)
            return new_top, total, mixed

        start = (jnp.full((1, width), MASKED, F32), jnp.zeros((1, width), F32), jnp.zeros((HEAD_DIM, width), F32))
        top, total, mixed = lax.fori_loop(0, chunks, chunk, start, unroll=3)
        mixed = (mixed / total).astype(BF16)
        lse = top + jnp.log(total)
        for g in range(GROUP):
            n = half * GROUP + g
            o_ref[n * HEAD_DIM : (n + 1) * HEAD_DIM, :] = mixed[:, g * rows : (g + 1) * rows]
            lse_ref[0, n : n + 1, :] = lse[:, g * rows : (g + 1) * rows]
        between(half)


def attend_kernel(chunks, rows, off_ref, lo_ref, q_ref, kv_ref, o_ref, lse_ref, bias):
    @pl.when(pl.program_id(0) == 0)
    def _():
        make_bias(bias, lo_ref, chunks, rows)

    attend_pair(chunks, rows, off_ref[0], q_ref, kv_ref, o_ref, lse_ref, bias, lambda half: None)


def attend_back_pair(
    chunks, rows, off, cos_ref, sin_ref, q_ref, kv_ref, g_ref, lse_ref, out_ref, dq_ref, dkv_ref, bias, between
):
    unused = pl.ds(pl.multiple_of((1 - off) * chunks * rows, rows), rows)
    dkv_ref[:, unused, :] = jnp.zeros((2, rows, 2 * HEAD_DIM), BF16)
    for half in range(2):
        lanes = slice(half * HEAD_DIM, (half + 1) * HEAD_DIM)
        queries, grads = side_by_side(q_ref, half), side_by_side(g_ref, half)
        lse = stats_of(lse_ref, half)
        mixed = side_by_side(out_ref, half).astype(F32)
        delta = jnp.sum(mixed * grads.astype(F32), axis=0, keepdims=True)

        def chunk(ch, query_grad, lanes=lanes, queries=queries, grads=grads, lse=lse, delta=delta):
            at = pl.ds(pl.multiple_of((ch + off) * rows, rows), rows)
            key, value = kv_ref[0, at, lanes], kv_ref[1, at, lanes]
            shift = bias[pl.ds(pl.multiple_of(ch * rows, rows), rows), :]
            score = dims(key, queries, 1, 0) + jnp.concatenate([shift] * GROUP, axis=1)
            weight = jnp.exp(score - lse)
            score_grad = (weight * (dims(value, grads, 1, 0) - delta)).astype(BF16)
            dkv_ref[0, at, lanes] = dims(score_grad, queries, 1, 1).astype(BF16)
            dkv_ref[1, at, lanes] = dims(weight.astype(BF16), grads, 1, 1).astype(BF16)
            return query_grad + dims(key, score_grad, 0, 0)

        done = lax.fori_loop(0, chunks, chunk, jnp.zeros((HEAD_DIM, GROUP * rows), F32), unroll=3)
        done = done * (HEAD_DIM**-0.5)
        cosine, sine = cos_ref[...], sin_ref[...]
        for g in range(GROUP):
            grad = done[:, g * rows : (g + 1) * rows]
            u, w = grad[: HEAD_DIM // 2], grad[HEAD_DIM // 2 :]
            n = (half * GROUP + g) * HEAD_DIM
            dq_ref[n : n + HEAD_DIM // 2, :] = (u * cosine + w * sine).astype(BF16)
            dq_ref[n + HEAD_DIM // 2 : n + HEAD_DIM, :] = (w * cosine - u * sine).astype(BF16)
        between(half)


def attend_back_kernel(
    chunks, rows, off_ref, lo_ref, cos_ref, sin_ref, q_ref, kv_ref, g_ref, lse_ref, out_ref, dq_ref, dkv_ref, bias
):
    @pl.when(pl.program_id(0) == 0)
    def _():
        make_bias(bias, lo_ref, chunks, rows)

    attend_back_pair(
        chunks, rows, off_ref[0], cos_ref, sin_ref, q_ref, kv_ref, g_ref, lse_ref, out_ref, dq_ref, dkv_ref, bias,
        lambda half: None,
    )


def attention_specs(rows, span):
    width = 2 * GROUP * HEAD_DIM
    return dict(
        smem=pl.BlockSpec(memory_space=pltpu.SMEM),
        row=pl.BlockSpec((1, rows), lambda j: (0, 0)),
        table=pl.BlockSpec((HEAD_DIM // 2, rows), lambda j: (0, 0)),
        query=pl.BlockSpec((width, rows), lambda j: (j, 0)),
        kv=pl.BlockSpec((2, span, 2 * HEAD_DIM), lambda j: (0, 0, j)),
        stat=pl.BlockSpec((1, 8, rows), lambda j: (j, 0, 0)),
    )


def attend(query_t, window, offset, lo):
    rows, span = query_t.shape[1], window.shape[1]
    chunks = span // rows - 1
    s = attention_specs(rows, span)
    return pl.pallas_call(
        functools.partial(attend_kernel, chunks, rows),
        grid=(KEY_HEADS // 2,),
        in_specs=[s["smem"], s["row"], s["query"], s["kv"]],
        out_specs=[s["query"], s["stat"]],
        out_shape=[
            jax.ShapeDtypeStruct(query_t.shape, BF16),
            jax.ShapeDtypeStruct((KEY_HEADS // 2, 8, rows), F32),
        ],
        scratch_shapes=[pltpu.VMEM((chunks * rows, rows), F32)],
        compiler_params=pltpu.CompilerParams(vmem_limit_bytes=40 * 2**20),
        cost_estimate=pl.CostEstimate(flops=7 * 10**9, bytes_accessed=8 * 10**6, transcendentals=15 * 10**6),
        name="attend",
    )(offset.reshape(1), lo, query_t, window)


def attend_back(query_t, window, offset, lo, grad_t, lse, attended_t, cos_t, sin_t):
    rows, span = query_t.shape[1], window.shape[1]
    chunks = span // rows - 1
    s = attention_specs(rows, span)
    return pl.pallas_call(
        functools.partial(attend_back_kernel, chunks, rows),
        grid=(KEY_HEADS // 2,),
        in_specs=[s["smem"], s["row"], s["table"], s["table"], s["query"], s["kv"], s["query"], s["stat"], s["query"]],
        out_specs=[s["query"], s["kv"]],
        out_shape=[
            jax.ShapeDtypeStruct(query_t.shape, BF16),
            jax.ShapeDtypeStruct(window.shape, BF16),
        ],
        scratch_shapes=[pltpu.VMEM((chunks * rows, rows), F32)],
        compiler_params=pltpu.CompilerParams(vmem_limit_bytes=40 * 2**20),
        cost_estimate=pl.CostEstimate(flops=18 * 10**9, bytes_accessed=16 * 10**6, transcendentals=15 * 10**6),
        name="attend_back",
    )(offset.reshape(1), lo, cos_t, sin_t, query_t, window, grad_t, lse, attended_t)


def hits(slot_ref, slots):
    width = slot_ref.shape[-1]
    return slot_ref[0] == lax.broadcasted_iota(jnp.int32, (slots, width), 0)


def dispatch_kernel(slot_ref, x_ref, u_ref, xo_ref, uo_ref):
    chosen = jnp.where(hits(slot_ref, xo_ref.shape[0]), 1.0, 0.0).astype(BF16)
    xo_ref[...] = dims(chosen, x_ref[...], 1, 0).astype(BF16)
    uo_ref[...] = dims(chosen, u_ref[...], 1, 0).astype(BF16)


def dispatch(slot, normed, upstream, slots):
    pairs, _, width = slot.shape
    model = normed.shape[1]
    return pl.pallas_call(
        dispatch_kernel,
        grid=(pairs,),
        in_specs=[
            pl.BlockSpec((1, 1, width), lambda i: (i, 0, 0)),
            pl.BlockSpec((width, model), lambda i: (i, 0)),
            pl.BlockSpec((width, model), lambda i: (i, 0)),
        ],
        out_specs=[pl.BlockSpec((slots, model), lambda i: (i, 0))] * 2,
        out_shape=[jax.ShapeDtypeStruct((pairs * slots, model), BF16)] * 2,
        compiler_params=pltpu.CompilerParams(vmem_limit_bytes=40 * 2**20),
        cost_estimate=pl.CostEstimate(flops=2 * 10**9, bytes_accessed=65 * 10**6, transcendentals=0),
        name="dispatch",
    )(slot, normed, upstream)


def combine_kernel(slot_ref, r_ref, o_ref):
    chosen = jnp.where(hits(slot_ref, r_ref.shape[0]), 1.0, 0.0).astype(BF16)
    o_ref[...] = dims(chosen, r_ref[...], 0, 0).astype(BF16)


def combine(slot, rows, slots):
    pairs, _, width = slot.shape
    model = rows.shape[1]
    return pl.pallas_call(
        combine_kernel,
        grid=(pairs,),
        in_specs=[
            pl.BlockSpec((1, 1, width), lambda i: (i, 0, 0)),
            pl.BlockSpec((slots, model), lambda i: (i, 0)),
        ],
        out_specs=pl.BlockSpec((width, model), lambda i: (i, 0)),
        out_shape=jax.ShapeDtypeStruct((pairs * width, model), BF16),
        compiler_params=pltpu.CompilerParams(vmem_limit_bytes=40 * 2**20),
        cost_estimate=pl.CostEstimate(flops=10**9, bytes_accessed=33 * 10**6, transcendentals=0),
        name="combine",
    )(slot, rows)


SLOTS = 80


def far_first(i):
    return jnp.where(i == 0, 2, jnp.where(i == 3, 0, 2 * i - 1))


def greet_all():
    me = lax.axis_index("dev")
    barrier = pltpu.get_barrier_semaphore()

    def signal(d, _):
        pl.semaphore_signal(barrier, inc=1, device_id=(lax.rem(me + d, 32),), device_id_type=MESH)
        return 0
    lax.fori_loop(1, 32, signal, 0)
    pl.semaphore_wait(barrier, 31)


class Swap:
    def __init__(self, source, into, ss, rs):
        self.me = lax.axis_index("dev")
        self.source, self.into, self.ss, self.rs = source, into, ss, rs

    def copy(self, d):
        target = lax.rem(self.me + d, 32)
        return pltpu.make_async_remote_copy(
            src_ref=self.source(target), dst_ref=self.into.at[self.me], send_sem=self.ss.at[d], recv_sem=self.rs.at[d],
            device_id=(target,), device_id_type=MESH)

    def start(self):
        def one(d, _):
            self.copy(d).start()
            return 0
        lax.fori_loop(1, 32, one, 0)
        self.into[self.me] = self.source(self.me)[...]

    def wait_recv(self):
        def one(d, _):
            self.copy(d).wait_recv()
            return 0
        lax.fori_loop(1, 32, one, 0)

    def wait_send(self):
        def one(d, _):
            self.copy(d).wait_send()
            return 0
        lax.fori_loop(1, 32, one, 0)


def in_plane(y, x, c):
    return (y * 2 + x) * 2 + c


def chosen_rows(slots_ref, block, expert):
    row = slots_ref[block, pl.ds(expert, 1), :]
    return row == lax.broadcasted_iota(jnp.int32, (SLOTS, row.shape[1]), 0).astype(F32)


def greet_near():
    z, y, x, c = place()
    greet(
        [number(z, y, x, 1 - c)]
        + [number(z, 1 - y, x, cc) for cc in (c, 1 - c)]
        + [number(z, y, 1 - x, cc) for cc in (c, 1 - c)]
        + [number(z, 1 - y, 1 - x, c)]
        + [number(lax.rem(z + d, 4), y, x, c) for d in (1, 2, 3)]
    )


class Forth:
    scratch = staticmethod(lambda rows, half: [
        pltpu.VMEM((2, 2, 4, rows, half), BF16),
        pltpu.VMEM((2, 2, 4, 4, SLOTS, half), BF16),
        pltpu.SemaphoreType.DMA((2, 2, 4)), pltpu.SemaphoreType.DMA((2, 4)),
        pltpu.SemaphoreType.DMA((2, 4)), pltpu.SemaphoreType.DMA((2, 4)),
        pltpu.SemaphoreType.DMA((2, 2, 4, 4)), pltpu.SemaphoreType.DMA((2, 2, 4, 3)), pltpu.SemaphoreType.DMA((2,)),
    ])
    n_scratch = 9

    def __init__(self, x_ref, slots_ref, xi, scratch):
        self.x_ref, self.slots_ref, self.xi = x_ref, slots_ref, xi
        self.land, self.stage, self.zs, self.zr, self.fs, self.fr, self.cs, self.cr, self.own_sem = scratch
        self.z, self.y, self.x, self.c = place()
        half = x_ref.shape[1] // 2
        self.cols = [pl.ds(0, half), pl.ds(half, half)]

    def turn(self, i):
        middle = jnp.where(i < 2, i, 5 - i)
        return jnp.where(self.z == 0, lax.rem(4 - i, 4), jnp.where(self.z == 3, i, middle))

    def to_z(self, p, up, k, own=False):
        step = 1 if up else 3
        source = self.x_ref.at[:, self.cols[p]] if own else self.land.at[p, 0, k]
        there = lax.rem(k + step, 4)
        return pltpu.make_async_remote_copy(
            src_ref=source, dst_ref=self.land.at[p, 0, there],
            send_sem=self.zs.at[p, int(up), k], recv_sem=self.zr.at[p, there],
            device_id=(number(lax.rem(self.z + step, 4), self.y, self.x, self.c),), device_id_type=MESH)

    def hop(self, p, k):
        z, y, x, c = self.z, self.y, self.x, self.c
        beside = number(z, 1 - y, x, c) if p == 0 else number(z, y, 1 - x, c)
        return pltpu.make_async_remote_copy(
            src_ref=self.land.at[p, 0, k], dst_ref=self.land.at[p, 1, k],
            send_sem=self.fs.at[p, k], recv_sem=self.fr.at[p, k], device_id=(beside,), device_id_type=MESH)

    def block(self, p, h, k):
        zz = lax.rem(self.z + 4 - k, 4)
        if p == 0:
            return number(zz, (1 - self.y) if h else self.y, self.x, self.c)
        return number(zz, self.y, (1 - self.x) if h else self.x, self.c)

    def who(self, p):
        y, x, c = self.y, self.x, self.c
        ay, ax = (y, 1 - x) if p == 0 else (1 - y, x)
        return [(y, x, 1 - c), (ay, ax, c), (ay, ax, 1 - c), (y, x, c)]

    def slots_at(self, p, h, k):
        return self.xi.at[pl.ds(pl.multiple_of(self.block(p, h, k) * SLOTS, 16), SLOTS), self.cols[p]]

    def served(self, p, h, k, t):
        return pltpu.make_async_remote_copy(
            src_ref=self.stage.at[p, h, k, t], dst_ref=self.slots_at(p, h, k),
            send_sem=self.cs.at[p, h, k, t], recv_sem=self.cr.at[p, h, k, t],
            device_id=(number(self.z, *self.who(p)[t]),), device_id_type=MESH)

    def kept(self, p, h, k):
        return pltpu.make_async_copy(self.stage.at[p, h, k, 3], self.slots_at(p, h, k), self.cs.at[p, h, k, 3])

    def serve(self, p, h, k):
        block = self.block(p, h, k)
        source = self.land[p, h, k]
        for t, to in enumerate(self.who(p)):
            chosen = jnp.where(chosen_rows(self.slots_ref, block, in_plane(*to)), 1.0, 0.0).astype(BF16)
            self.stage[p, h, k, t] = dims(chosen, source, 1, 0).astype(BF16)
            if t < 3:
                self.served(p, h, k, t).start()
            else:
                self.kept(p, h, k).start()

    def own(self, p):
        return pltpu.make_async_copy(self.x_ref.at[:, self.cols[p]], self.land.at[p, 0, 0], self.own_sem.at[p])

    def along(self, i, use):
        k = self.turn(i)
        zz = lax.rem(self.z + 4 - k, 4)
        for p in range(2):
            @pl.when((zz < self.z) & (self.z < 3))
            def _(p=p):
                use(self.to_z(p, True, k))

            @pl.when((zz > self.z) & (self.z > 0))
            def _(p=p):
                use(self.to_z(p, False, k))

    def along_own(self, use):
        for p in range(2):
            @pl.when(self.z < 3)
            def _(p=p):
                use(self.to_z(p, True, 0, own=True))

            @pl.when(self.z > 0)
            def _(p=p):
                use(self.to_z(p, False, 0, own=True))

    def start(self):
        for p in range(2):
            self.own(p).start()
        self.along_own(lambda cp: cp.start())

    def one(self, i):
        k = self.turn(i)

        @pl.when(i == 0)
        def _():
            for p in range(2):
                self.own(p).wait()

        @pl.when(i > 0)
        def _():
            for p in range(2):
                self.to_z(p, True, lax.rem(k + 3, 4)).wait_recv()

        self.along(i, lambda cp: cp.start())
        for p in range(2):
            self.hop(p, k).start()
        for p in range(2):
            self.serve(p, 0, k)

    def two(self, i):
        k = self.turn(i)
        for p in range(2):
            self.hop(p, k).wait_recv()
            self.serve(p, 1, k)

    def arrived(self, group, i):
        k = self.turn(i)

        @pl.when(group == 0)
        def _():
            for p in range(2):
                self.served(p, 0, k, 0).wait_recv()
                self.kept(p, 0, k).wait()

        @pl.when(group == 1)
        def _():
            self.kept(0, 1, k).wait()
            self.served(0, 1, k, 0).wait_recv()
            self.served(1, 0, k, 1).wait_recv()
            self.served(1, 0, k, 2).wait_recv()

        @pl.when(group == 2)
        def _():
            self.kept(1, 1, k).wait()
            self.served(1, 1, k, 0).wait_recv()
            self.served(0, 0, k, 1).wait_recv()
            self.served(0, 0, k, 2).wait_recv()

        @pl.when(group == 3)
        def _():
            for p in range(2):
                self.served(p, 1, k, 1).wait_recv()
                self.served(p, 1, k, 2).wait_recv()

    def chip(self, group, i):
        dy, dx = lax.rem(group, 2), group // 2
        zz = lax.rem(self.z + 4 - self.turn(i), 4)
        yy = jnp.where(dy == 1, 1 - self.y, self.y)
        xx = jnp.where(dx == 1, 1 - self.x, self.x)
        return (zz * 2 + yy) * 2 + xx

    def sent(self):
        self.along_own(lambda cp: cp.wait_send())

        def each(i, _):
            k = self.turn(i)
            self.along(i, lambda cp: cp.wait_send())
            for p in range(2):
                self.hop(p, k).wait_send()
                for h in range(2):
                    for t in range(3):
                        self.served(p, h, k, t).wait_send()
            return 0
        lax.fori_loop(0, 4, each, 0)


def experts_kernel(
    x_ref, gates_ref, slots_ref, ui_ref, wg_ref, wu_ref, wd_ref,
    xi_out, dx_out, y_out, hg_ref, dg_ref, du_ref, gg_ref,
    gates, xi, ubuf, dx_buf, y_buf, gs, gr, usem, xsem, osem, *scratch,
):
    z, y, x, c = place()
    rows = x_ref.shape[0]
    greet_all()
    swap = Swap(lambda t: gates_ref.at[t], gates, gs, gr)
    ag = Forth(x_ref, slots_ref, xi, scratch)
    ag.start()

    def chip_of(u):
        return ag.chip(lax.rem(u, 4), u // 4)

    def at_chip(u):
        return pl.ds(pl.multiple_of(chip_of(u) * 2 * SLOTS, 16), 2 * SLOTS)

    def load_up(u):
        return pltpu.make_async_copy(ui_ref.at[at_chip(u), :], ubuf.at[lax.rem(u, 2)], usem.at[lax.rem(u, 2)])

    load_up(0).start()
    swap.start()
    ag.one(0)
    swap.wait_recv()

    def store(n, buf, out, u):
        return pltpu.make_async_copy(buf.at[lax.rem(u, 2)], out.at[at_chip(u), :], osem.at[n, lax.rem(u, 2)])

    def stores(u):
        return [store(0, dx_buf, dx_out, u), store(1, y_buf, y_out, u)]

    def keep(u):
        return pltpu.make_async_copy(xi.at[at_chip(u), :], xi_out.at[at_chip(u), :], xsem.at[u])

    def unit(u):
        slot = lax.rem(u, 2)
        chip = chip_of(u)

        @pl.when(u < 15)
        def _():
            load_up(u + 1).start()

        ag.arrived(lax.rem(u, 4), u // 4)

        @pl.when(u >= 2)
        def _():
            for s in stores(u - 2):
                s.wait()

        load_up(u).wait()
        at = at_chip(u)
        expert = in_plane(y, x, c)
        picks, gate = [], []
        for core in range(2):
            block = chip * 2 + core
            hit = chosen_rows(slots_ref, block, expert)
            picks.append(hit)
            gate_row = jnp.concatenate([gates[block, 0:1, :], gates[block, 1:2, :]], axis=1)
            gate.append(jnp.sum(jnp.where(hit, gate_row, 0.0), axis=1, keepdims=True))
        gate_of_slot = jnp.concatenate(gate, axis=0)
        hidden_up = dims(ubuf[slot], wd_ref[...], 1, 1)
        rows_in = xi[at, :]
        gate_in = dims(rows_in, wg_ref[...], 1, 0)
        up_in = dims(rows_in, wu_ref[...], 1, 0)
        sig = 1.0 / (1.0 + jnp.exp(-gate_in))
        silu = gate_in * sig
        hidden = (silu * up_in).astype(BF16).astype(F32)
        gated = (hidden * gate_of_slot).astype(BF16)
        hidden_grad = hidden_up * gate_of_slot
        gate_back = (hidden_grad * up_in * sig * (1.0 + gate_in * (1.0 - sig))).astype(BF16)
        up_back = (hidden_grad * silu).astype(BF16)
        hg_ref[at, :] = gated
        dg_ref[at, :] = gate_back
        du_ref[at, :] = up_back
        dx_buf[slot] = (dims(gate_back, wg_ref[...], 1, 1) + dims(up_back, wu_ref[...], 1, 1)).astype(BF16)
        y_buf[slot] = dims(gated, wd_ref[...], 1, 0).astype(BF16)
        gate_grad = jnp.sum(hidden * hidden_up, axis=1, keepdims=True)
        for core in range(2):
            block = chip * 2 + core
            row = jnp.sum(jnp.where(picks[core], gate_grad[core * SLOTS : (core + 1) * SLOTS], 0.0), axis=0, keepdims=True)
            gg_ref[block, 0:1, :] = row[:, :128]
            gg_ref[block, 1:2, :] = row[:, 128:]
        for s in stores(u):
            s.start()
        keep(u).start()

    def each(v, _):
        i, group = v // 4, lax.rem(v, 4)

        @pl.when((group == 0) & (i < 3))
        def _():
            ag.one(i + 1)

        @pl.when((group == 0) & (i < 4))
        def _():
            ag.two(i)

        @pl.when(v >= 4)
        def _():
            unit(v - 4)
        return 0

    lax.fori_loop(0, 20, each, 0)
    for u in (14, 15):
        for s in stores(u):
            s.wait()

    def last(u, _):
        keep(u).wait()
        return 0
    lax.fori_loop(0, 16, last, 0)
    ag.sent()
    swap.wait_send()


def run_experts(normed, gates, slots, ui, gate_weight, up_weight, down_weight):
    rows, model = normed.shape
    ff = gate_weight.shape[1]
    n = 32 * SLOTS
    hbm, vmem = pl.BlockSpec(memory_space=pl.ANY), pl.BlockSpec(memory_space=pltpu.VMEM)
    dma = pltpu.SemaphoreType.DMA
    long = jax.ShapeDtypeStruct((n, model), BF16)
    short = jax.ShapeDtypeStruct((n, ff), BF16)
    return pl.pallas_call(
        experts_kernel,
        in_specs=[hbm, vmem, vmem, hbm, vmem, vmem, vmem],
        out_specs=[hbm] * 3 + [vmem] * 4,
        out_shape=[long] * 3 + [short] * 3 + [jax.ShapeDtypeStruct((32, 8, 128), F32)],
        scratch_shapes=[
            pltpu.VMEM((32, 8, 128), F32),
            pltpu.VMEM((n, model), BF16),
            pltpu.VMEM((2, 2 * SLOTS, model), BF16),
            pltpu.VMEM((2, 2 * SLOTS, model), BF16),
            pltpu.VMEM((2, 2 * SLOTS, model), BF16),
            dma((32,)), dma((32,)), dma((2,)), dma((16,)), dma((2, 2)),
        ] + Forth.scratch(rows, model // 2),
        compiler_params=pltpu.CompilerParams(collective_id=13, has_side_effects=True, vmem_limit_bytes=56 * 2**20),
        name="experts",
    )(normed, gates, slots, ui, gate_weight, up_weight, down_weight)


class Back:
    scratch = staticmethod(lambda rows, half: [
        pltpu.VMEM((2, 2, 4, SLOTS, half), BF16),
        pltpu.VMEM((2, 3, 2, 4, SLOTS, half), BF16),
        pltpu.VMEM((2, 4, rows, half), BF16),
        pltpu.VMEM((2, 4, rows, half), BF16),
        pltpu.VMEM((2, 4, rows, half), BF16),
        pltpu.VMEM((2, 4, rows, half), BF16),
        pltpu.SemaphoreType.DMA((2, 2, 4)),
        pltpu.SemaphoreType.DMA((2, 3, 2, 4)), pltpu.SemaphoreType.DMA((2, 3, 2, 4)),
        pltpu.SemaphoreType.DMA((2, 4)), pltpu.SemaphoreType.DMA((2, 4)),
        pltpu.SemaphoreType.DMA((2, 4)), pltpu.SemaphoreType.DMA((2, 4)),
    ])
    n_scratch = 13

    def __init__(self, rows_ref, slots_ref, o_ref, scratch):
        self.rows_ref, self.slots_ref, self.o_ref = rows_ref, slots_ref, o_ref
        (self.own, self.rin, self.sout, self.rb, self.zout, self.rz,
         self.own_sem, self.ts, self.tr, self.bs, self.br, self.zs, self.zr) = scratch
        self.z, self.y, self.x, self.c = place()
        half = rows_ref.shape[1] // 2
        self.cols = [pl.ds(0, half), pl.ds(half, half)]

    def block(self, p, h, k, yy, xx, cc):
        zz = lax.rem(self.z + k, 4)
        if p == 0:
            return number(zz, (1 - yy) if h else yy, xx, cc)
        return number(zz, yy, (1 - xx) if h else xx, cc)

    def sources(self, p):
        y, x, c = self.y, self.x, self.c
        ay, ax = (y, 1 - x) if p == 0 else (1 - y, x)
        return [(y, x, 1 - c), (ay, ax, c), (ay, ax, 1 - c)]

    def slot_rows(self, block, p):
        return self.rows_ref.at[pl.ds(pl.multiple_of(block * SLOTS, 16), SLOTS), self.cols[p]]

    def to(self, p, t, h, k):
        place_of = self.sources(p)[t]
        return pltpu.make_async_remote_copy(
            src_ref=self.slot_rows(self.block(p, h, k, *place_of), p), dst_ref=self.rin.at[p, t, h, k],
            send_sem=self.ts.at[p, t, h, k], recv_sem=self.tr.at[p, t, h, k],
            device_id=(number(self.z, *place_of),), device_id_type=MESH)

    def mine(self, p, h, k):
        return pltpu.make_async_copy(
            self.slot_rows(self.block(p, h, k, self.y, self.x, self.c), p), self.own.at[p, h, k], self.own_sem.at[p, h, k])

    def second(self, p, k):
        z, y, x, c = self.z, self.y, self.x, self.c
        target = number(z, 1 - y, x, c) if p == 0 else number(z, y, 1 - x, c)
        return pltpu.make_async_remote_copy(
            src_ref=self.sout.at[p, k], dst_ref=self.rb.at[p, k], send_sem=self.bs.at[p, k], recv_sem=self.br.at[p, k],
            device_id=(target,), device_id_type=MESH)

    def third(self, p, k):
        target = number(lax.rem(self.z + k, 4), self.y, self.x, self.c)
        return pltpu.make_async_remote_copy(
            src_ref=self.zout.at[p, k], dst_ref=self.rz.at[p, k], send_sem=self.zs.at[p, k], recv_sem=self.zr.at[p, k],
            device_id=(target,), device_id_type=MESH)

    def issue(self, h, i):
        k = far_first(i)
        for p in range(2):
            for t in (1, 2, 0):
                self.to(p, t, h, k).start()
            self.mine(p, h, k).start()

    def start(self):
        self.issue(1, 0)
        self.issue(0, 0)

    def dense(self, p, h, k):
        self.mine(p, h, k).wait()
        for t in range(3):
            self.to(p, t, h, k).wait_recv()
        block = self.block(p, h, k, self.y, self.x, self.c)
        total = None
        for t, who in enumerate([(self.y, self.x, self.c)] + self.sources(p)):
            hit = chosen_rows(self.slots_ref, block, in_plane(*who))
            chosen = jnp.where(hit, 1.0, 0.0).astype(BF16)
            values = self.own[p, h, k] if t == 0 else self.rin[p, t - 1, h, k]
            term = dims(chosen, values, 0, 0)
            total = term if total is None else total + term
        return total

    def step(self, u):
        u = jnp.int32(u)
        i = u // 2
        k = far_first(i)
        early = lax.rem(u, 2) == 0

        @pl.when(early)
        def _():
            for p in range(2):
                self.sout[p, k] = self.dense(p, 1, k).astype(BF16)
                self.second(p, k).start()

            @pl.when(i < 3)
            def _():
                self.issue(1, i + 1)

        @pl.when(jnp.logical_not(early))
        def _():
            for p in range(2):
                total = self.dense(p, 0, k)
                self.second(p, k).wait_recv()
                total = total + self.rb[p, k].astype(F32)

                @pl.when(k > 0)
                def _(p=p, total=total):
                    self.zout[p, k] = total.astype(BF16)
                    self.third(p, k).start()

                @pl.when(k == 0)
                def _(p=p, total=total):
                    self.o_ref[:, self.cols[p]] = total

            @pl.when(i < 3)
            def _():
                self.issue(0, i + 1)

    def finish(self):
        for p in range(2):
            for k in range(1, 4):
                self.third(p, k).wait_recv()
            self.o_ref[:, self.cols[p]] += (
                self.rz[p, 1].astype(F32) + self.rz[p, 2].astype(F32) + self.rz[p, 3].astype(F32)
            )

        def one(k, _):
            for p in range(2):
                self.second(p, k).wait_send()

                @pl.when(k > 0)
                def _(p=p):
                    self.third(p, k).wait_send()
                for t in range(3):
                    for h in range(2):
                        self.to(p, t, h, k).wait_send()
            return 0
        lax.fori_loop(0, 4, one, 0)


def grads_kernel(
    dx_ref, slots_ref, gg_ref, xi_ref, ui_ref, hg_ref, dg_ref, du_ref,
    o_ref, back_ref, wg_out, wu_out, wd_out, xcol, ucol, gout, uout, dout, gs, gr, isem, osem, *scratch,
):
    greet_all()
    swap = Swap(lambda t: gg_ref.at[t], back_ref, gs, gr)
    rs = Back(dx_ref, slots_ref, o_ref, scratch)
    rs.start()
    swap.start()

    def col(i):
        return pl.ds(pl.multiple_of(i * 256, 256), 256)

    def loads(i):
        s = lax.rem(i, 2)
        return [
            pltpu.make_async_copy(xi_ref.at[:, col(i)], xcol.at[s], isem.at[0, s]),
            pltpu.make_async_copy(ui_ref.at[:, col(i)], ucol.at[s], isem.at[1, s]),
        ]

    def stores(i):
        s = lax.rem(i, 2)
        return [
            pltpu.make_async_copy(gout.at[s], wg_out.at[col(i), :], osem.at[0, s]),
            pltpu.make_async_copy(uout.at[s], wu_out.at[col(i), :], osem.at[1, s]),
            pltpu.make_async_copy(dout.at[s], wd_out.at[:, col(i)], osem.at[2, s]),
        ]

    for cp in loads(0):
        cp.start()

    def one(u, _):
        @pl.when(u < 6)
        def _():
            s = lax.rem(u, 2)

            @pl.when(u < 5)
            def _():
                for cp in loads(u + 1):
                    cp.start()

            for cp in loads(u):
                cp.wait()

            @pl.when(u >= 2)
            def _():
                for cp in stores(u - 2):
                    cp.wait()

            rows_in = xcol[s]
            gout[s] = dims(rows_in, dg_ref[...], 0, 0)
            uout[s] = dims(rows_in, du_ref[...], 0, 0)
            dout[s] = dims(hg_ref[...], ucol[s], 0, 0)
            for cp in stores(u):
                cp.start()

        rs.step(u)
        return 0

    lax.fori_loop(0, 8, one, 0)
    for i in (4, 5):
        for cp in stores(i):
            cp.wait()
    swap.wait_recv()
    rs.finish()
    swap.wait_send()


def run_grads(dx, slots, gg, xi, ui, hg, dg, du):
    rows, model = slots.shape[2], dx.shape[1]
    ff = hg.shape[1]
    n = dx.shape[0]
    hbm, vmem = pl.BlockSpec(memory_space=pl.ANY), pl.BlockSpec(memory_space=pltpu.VMEM)
    dma = pltpu.SemaphoreType.DMA
    return pl.pallas_call(
        grads_kernel,
        in_specs=[hbm, vmem, vmem, hbm, hbm, vmem, vmem, vmem],
        out_specs=[vmem, vmem, hbm, hbm, hbm],
        out_shape=[
            jax.ShapeDtypeStruct((rows, model), F32),
            jax.ShapeDtypeStruct((32, 8, 128), F32),
            jax.ShapeDtypeStruct((model, ff), F32),
            jax.ShapeDtypeStruct((model, ff), F32),
            jax.ShapeDtypeStruct((ff, model), F32),
        ],
        scratch_shapes=[
            pltpu.VMEM((2, n, 256), BF16), pltpu.VMEM((2, n, 256), BF16),
            pltpu.VMEM((2, 256, ff), F32), pltpu.VMEM((2, 256, ff), F32), pltpu.VMEM((2, ff, 256), F32),
            dma((32,)), dma((32,)), dma((2, 2)), dma((3, 2)),
        ] + Back.scratch(rows, model // 2),
        compiler_params=pltpu.CompilerParams(collective_id=14, has_side_effects=True, vmem_limit_bytes=56 * 2**20),
        name="grads",
    )(dx, slots, gg, xi, ui, hg, dg, du)


def attend_mesh_kernel(
    chunks, rows, lo_ref, q_ref, kv_ref, u_ref, mine_ref, o_ref, lse_ref, window, slots_ref, ui_ref,
    bias, gs, gr, lsem, ws, wr, *scratch,
):
    greet_all()
    swap = Swap(lambda t: mine_ref.at[t // 8], slots_ref, gs, gr)
    keys = Window(rows, kv_ref, window, (lsem, ws, wr))
    ag = Forth(u_ref, slots_ref, ui_ref, scratch)
    keys.start()
    swap.start()
    ag.start()
    make_bias(bias, lo_ref, chunks, rows)
    keys.previous()
    swap.wait_recv()
    ag.one(0)
    keys.pass_on()
    ag.one(1)
    keys.end()
    width = 2 * GROUP * HEAD_DIM

    def pair(j, _):
        lanes = pl.ds(pl.multiple_of(j * 2 * HEAD_DIM, 2 * HEAD_DIM), 2 * HEAD_DIM)
        head = pl.ds(pl.multiple_of(j * width, width), width)

        def between(half):
            u = 2 * j + half + 2

            @pl.when((u == 3) | (u == 5))
            def _():
                ag.one((u + 1) // 2)

            @pl.when((u == 2) | (u == 4) | (u == 6) | (u == 7))
            def _():
                ag.two(jnp.where(u == 7, 3, u // 2 - 1))

        attend_pair(
            chunks, rows, lax.rem(lax.axis_index("dev"), 2), q_ref.at[head, :], window.at[:, :, lanes],
            o_ref.at[head, :], lse_ref.at[pl.ds(j, 1)], bias, between,
        )
        return 0

    lax.fori_loop(0, KEY_HEADS // 2, pair, 0)

    def last(u, _):
        ag.arrived(lax.rem(u, 4), u // 4)
        return 0
    lax.fori_loop(0, 16, last, 0)
    ag.sent()
    keys.sent()
    swap.wait_send()


def attend_mesh(query_t, kv, lo, upstream, mine):
    rows = query_t.shape[1]
    chunks = 9
    model = upstream.shape[1]
    hbm, vmem = pl.BlockSpec(memory_space=pl.ANY), pl.BlockSpec(memory_space=pltpu.VMEM)
    dma = pltpu.SemaphoreType.DMA
    return pl.pallas_call(
        functools.partial(attend_mesh_kernel, chunks, rows),
        in_specs=[vmem] * 2 + [hbm, hbm, vmem],
        out_specs=[vmem] * 4 + [hbm],
        out_shape=[
            jax.ShapeDtypeStruct(query_t.shape, BF16),
            jax.ShapeDtypeStruct((KEY_HEADS // 2, 8, rows), F32),
            jax.ShapeDtypeStruct((2, 10 * rows, kv.shape[2]), BF16),
            jax.ShapeDtypeStruct((32, 8, rows), F32),
            jax.ShapeDtypeStruct((32 * SLOTS, model), BF16),
        ],
        scratch_shapes=[pltpu.VMEM((chunks * rows, rows), F32), dma((32,)), dma((32,))]
        + Window.scratch + Forth.scratch(rows, model // 2),
        compiler_params=pltpu.CompilerParams(collective_id=16, has_side_effects=True, vmem_limit_bytes=56 * 2**20),
        name="attend",
    )(lo, query_t, kv, upstream, mine)


def attend_back_mesh_kernel(
    chunks, rows, lo_ref, cos_ref, sin_ref, q_ref, kv_ref, g_ref, lse_ref, out_ref, y_ref, slots_ref, residual_ref,
    grad_out, layer_ref, bias, dkv, sums_ref, gt_ref, o_ref, *scratch,
):
    greet_near()
    rs = Back(y_ref, slots_ref, o_ref, scratch[: Back.n_scratch])
    keys = Unwindow(rows, dkv, sums_ref, scratch[Back.n_scratch :])
    rs.start()
    make_bias(bias, lo_ref, chunks, rows)
    width = 2 * GROUP * HEAD_DIM

    def pair(j, _):
        lanes = pl.ds(pl.multiple_of(j * 2 * HEAD_DIM, 2 * HEAD_DIM), 2 * HEAD_DIM)
        head = pl.ds(pl.multiple_of(j * width, width), width)

        def between(half):
            if half == 0:
                rs.step(j)

        attend_back_pair(
            chunks, rows, lax.rem(lax.axis_index("dev"), 2), cos_ref, sin_ref, q_ref.at[head, :], kv_ref.at[:, :, lanes], g_ref.at[head, :],
            lse_ref.at[pl.ds(j, 1)], out_ref.at[head, :], gt_ref.at[head, :], dkv.at[:, :, lanes], bias, between,
        )
        return 0

    lax.fori_loop(0, KEY_HEADS // 2, pair, 0)
    keys.start()

    def turned(first, last):
        for n in range(first, last, 256):
            grad_out[:, n : n + 256] = gt_ref[n : n + 256, :].T

    def rest(u, _):
        rs.step(u)

        @pl.when(u == 4)
        def _():
            keys.sums()

        @pl.when(u == 6)
        def _():
            keys.near()
            turned(0, QUERY_HEADS * HEAD_DIM)
        return 0

    lax.fori_loop(4, 8, rest, 0)
    keys.end()
    base = QUERY_HEADS * HEAD_DIM
    key_t = sums_ref[0].T
    cosine, sine = cos_ref[...], sin_ref[...]
    for n in range(KEY_HEADS):
        first, middle = n * HEAD_DIM, n * HEAD_DIM + HEAD_DIM // 2
        u, w = key_t[first:middle], key_t[middle : first + HEAD_DIM]
        gt_ref[base + first : base + middle, :] = (u * cosine + w * sine).astype(BF16)
        gt_ref[base + middle : base + first + HEAD_DIM, :] = (w * cosine - u * sine).astype(BF16)
    turned(base, base + KEY_HEADS * HEAD_DIM)
    grad_out[:, base + KEY_HEADS * HEAD_DIM :] = sums_ref[1].astype(BF16)
    rs.finish()
    layer_ref[...] = (residual_ref[...] + o_ref[...]).astype(BF16)


def attend_back_mesh(query_t, window, lo, grad_t, lse, attended_t, cos_t, sin_t, y, slots, residual):
    rows, span, keys = query_t.shape[1], window.shape[1], window.shape[2]
    chunks = span // rows - 1
    model = y.shape[1]
    hbm, vmem = pl.BlockSpec(memory_space=pl.ANY), pl.BlockSpec(memory_space=pltpu.VMEM)
    return pl.pallas_call(
        functools.partial(attend_back_mesh_kernel, chunks, rows),
        in_specs=[vmem] * 8 + [hbm, vmem, vmem],
        out_specs=[vmem] * 2,
        out_shape=[
            jax.ShapeDtypeStruct((rows, QKV), BF16),
            jax.ShapeDtypeStruct((rows, model), BF16),
        ],
        scratch_shapes=[
            pltpu.VMEM((chunks * rows, rows), F32), pltpu.VMEM(window.shape, BF16), pltpu.VMEM((2, rows, keys), F32),
            pltpu.VMEM((QKV, rows), BF16), pltpu.VMEM((rows, model), F32),
        ]
        + Back.scratch(rows, model // 2) + Unwindow.scratch(rows, keys),
        compiler_params=pltpu.CompilerParams(collective_id=15, has_side_effects=True, vmem_limit_bytes=56 * 2**20),
        name="attend_back",
    )(lo, cos_t, sin_t, query_t, window, grad_t, lse, attended_t, y, slots, residual)


def finish_kernel(
    rows, n_ref, g_ref, w_ref, more_ref, gain_ref, scale_ref, x_ref, rg_ref,
    oq_ref, ok_ref, ov_ref, om_ref, tg_ref, fg_ref, dense, acc, ra, rb, rz, out, ng, mine, theirs,
    ssem, rsem, sa, ra_sem, sb, rb_sem, sz, rz_sem, gs, gr,
):
    z, y, x, c = place()
    greet_all()
    sibling = number(z, y, x, 1 - c)
    cols = acc.shape[2]
    main = g_ref.shape[1]
    half = cols // 2
    pieces = [pl.ds(0, half), pl.ds(half, half)]
    around = (number(z, y, 1 - x, c), number(z, 1 - y, x, c))
    swap = Swap(lambda t: mine.at[t], theirs, gs, gr)

    def lane(dy, dx, k):
        yy = 1 - y if dy else y
        xx = 1 - x if dx else x
        return (lax.rem(z + k, 4) * 2 + yy) * 2 + xx

    def to_sibling(dy, dx, k):
        chip = lane(dy, dx, k)
        n = (k, dy, dx)
        sides = (
            (dense.at[chip, pl.ds(pl.multiple_of((1 - c) * rows, 16), rows), :], pl.ds(0, main)),
            (more_ref.at[pl.ds(pl.multiple_of((2 * chip + 1 - c) * rows, 16), rows), :], pl.ds(main, cols - main)),
        )
        return [
            pltpu.make_async_remote_copy(
                src_ref=source, dst_ref=acc.at[chip, :, at], send_sem=ssem.at[(*n, i)], recv_sem=rsem.at[(*n, i)],
                device_id=(sibling,), device_id_type=MESH)
            for i, (source, at) in enumerate(sides)
        ]

    def first(p, d2, k, dy, dx):
        return pltpu.make_async_remote_copy(
            src_ref=acc.at[lane(dy, dx, k), :, pieces[p]], dst_ref=ra.at[p, d2, k],
            send_sem=sa.at[p, d2, k], recv_sem=ra_sem.at[p, d2, k], device_id=(around[p],), device_id_type=MESH)

    def second(p, k):
        dy, dx = (1, 0) if p == 0 else (0, 1)
        return pltpu.make_async_remote_copy(
            src_ref=acc.at[lane(dy, dx, k), :, pieces[p]], dst_ref=rb.at[p, k],
            send_sem=sb.at[p, k], recv_sem=rb_sem.at[p, k], device_id=(around[1 - p],), device_id_type=MESH)

    def third(p, k):
        return pltpu.make_async_remote_copy(
            src_ref=acc.at[lane(0, 0, k), :, pieces[p]], dst_ref=rz.at[p, k],
            send_sem=sz.at[p, k], recv_sem=rz_sem.at[p, k],
            device_id=(number(lax.rem(z + k, 4), y, x, c),), device_id_type=MESH)

    quarter = ((1, 1), (1, 0), (0, 1), (0, 0))

    def product(i, _):
        k = far_first(i)
        zz = lax.rem(z + k, 4)
        at = pl.ds(pl.multiple_of(zz * 8 * rows, 128), 8 * rows)
        part = dims(n_ref[:, at], g_ref[...], 0, 0).astype(BF16)
        for chip in range(4):
            dense[zz * 4 + chip] = part[chip * 2 * rows : (chip + 1) * 2 * rows]
        for dy, dx in quarter:
            for cp in to_sibling(dy, dx, k):
                cp.start()
        return 0

    def own_sums(k):
        for dy, dx in quarter:
            chip = lane(dy, dx, k)
            for cp in to_sibling(dy, dx, k):
                cp.wait_recv()
            acc[chip, :, :main] = (
                acc[chip, :, :main].astype(F32) + dense[chip, pl.ds(pl.multiple_of(c * rows, 16), rows), :].astype(F32)
            ).astype(BF16)
            acc[chip, :, main:] = (
                acc[chip, :, main:].astype(F32)
                + more_ref[pl.ds(pl.multiple_of((2 * chip + c) * rows, 16), rows), :].astype(F32)
            ).astype(BF16)
            if dx:
                first(0, dy, k, dy, dx).start()
            if dy:
                first(1, dx, k, dy, dx).start()

    def middle(k):
        for p in range(2):
            dy, dx = (1, 0) if p == 0 else (0, 1)
            first(p, 1, k, 1, 1).wait_recv()
            block = acc.at[lane(dy, dx, k), :, pieces[p]]
            block[...] = (block[...].astype(F32) + ra[p, 1, k].astype(F32)).astype(BF16)
            second(p, k).start()

    def late(k):
        for p in range(2):
            first(p, 0, k, 1 - p, p).wait_recv()
            second(p, k).wait_recv()
            block = acc.at[lane(0, 0, k), :, pieces[p]]
            total = block[...].astype(F32) + ra[p, 0, k].astype(F32) + rb[p, k].astype(F32)

            @pl.when(k > 0)
            def _(p=p, block=block, total=total):
                block[...] = total.astype(BF16)
                third(p, k).start()

            @pl.when(k == 0)
            def _(p=p, total=total):
                out[:, pieces[p]] = total

    def rest_of_tokens():
        ng[...] = dims(g_ref[...], w_ref[:, :main], 1, 1)

        def tail(i, total):
            at = pl.ds(pl.multiple_of(i * 32, 32), 32)
            grad, scale, values = ng[at, :], scale_ref[at, :], x_ref[at, :].astype(F32)
            weighted = grad * gain_ref[...]
            scaled = values * scale
            mean = jnp.mean(weighted * values, axis=1, keepdims=True)
            tg_ref[at, :] = rg_ref[at, :] + scale * weighted - scaled * (scale * scale * mean)
            return total + jnp.sum(grad * scaled, axis=0, keepdims=True)
        total = lax.fori_loop(0, x_ref.shape[0] // 32, tail, jnp.zeros(gain_ref.shape, F32))
        mine[...] = jnp.zeros_like(mine)
        for t in range(32):
            mine[t, 0:1, 0:rows] = total[:, t * rows : (t + 1) * rows]
        swap.start()

    lax.fori_loop(0, 4, product, 0)

    def steps(i, _):
        @pl.when(i < 4)
        def _():
            own_sums(far_first(i))

        @pl.when(i == 3)
        def _():
            rest_of_tokens()

        @pl.when((i >= 1) & (i < 5))
        def _():
            middle(far_first(i - 1))

        @pl.when(i >= 2)
        def _():
            late(far_first(i - 2))
        return 0
    lax.fori_loop(0, 6, steps, 0)
    swap.wait_recv()
    fg_ref[...] = jnp.sum(theirs[...], axis=0)
    for p in range(2):
        for k in range(1, 4):
            third(p, k).wait_recv()
        out[:, pieces[p]] += rz[p, 1].astype(F32) + rz[p, 2].astype(F32) + rz[p, 3].astype(F32)
    at = 0
    for ref in (oq_ref, ok_ref, ov_ref, om_ref):
        ref[...] = out[:, at : at + ref.shape[1]]
        at += ref.shape[1]

    def sent(k, _):
        for dy, dx in quarter:
            for cp in to_sibling(dy, dx, k):
                cp.wait_send()
        for p in range(2):
            first(p, 0, k, 1 - p, p).wait_send()
            first(p, 1, k, 1, 1).wait_send()
            second(p, k).wait_send()

            @pl.when(k > 0)
            def _(p=p):
                third(p, k).wait_send()
        return 0
    lax.fori_loop(0, 4, sent, 0)
    swap.wait_send()


def finish(normed, grad, matrices, more, gain, scale, tokens, residual_grad):
    count, model = normed.shape
    rows = model // 32
    main, cols = grad.shape[1], grad.shape[1] + more.shape[1]
    half = cols // 2
    dma = pltpu.SemaphoreType.DMA
    vmem = pl.BlockSpec(memory_space=pltpu.VMEM)
    widths = [QUERY_HEADS * HEAD_DIM, KEY_HEADS * HEAD_DIM, KEY_HEADS * HEAD_DIM, more.shape[1]]
    return pl.pallas_call(
        functools.partial(finish_kernel, rows),
        in_specs=[vmem] * 8,
        out_specs=[vmem] * 6,
        out_shape=[jax.ShapeDtypeStruct((rows, w), F32) for w in widths] + [
            jax.ShapeDtypeStruct((count, model), F32),
            jax.ShapeDtypeStruct((8, 128), F32),
        ],
        scratch_shapes=[
            pltpu.VMEM((16, 2 * rows, main), BF16),
            pltpu.VMEM((16, rows, cols), BF16),
            pltpu.VMEM((2, 2, 4, rows, half), BF16),
            pltpu.VMEM((2, 4, rows, half), BF16),
            pltpu.VMEM((2, 4, rows, half), BF16),
            pltpu.VMEM((rows, cols), F32),
            pltpu.VMEM((count, model), F32),
            pltpu.VMEM((32, 8, 128), F32),
            pltpu.VMEM((32, 8, 128), F32),
            dma((4, 2, 2, 2)), dma((4, 2, 2, 2)), dma((2, 2, 4)), dma((2, 2, 4)), dma((2, 4)), dma((2, 4)), dma((2, 4)), dma((2, 4)),
            dma((32,)), dma((32,)),
        ],
        compiler_params=pltpu.CompilerParams(collective_id=17, has_side_effects=True, vmem_limit_bytes=56 * 2**20),
        name="finish",
    )(normed, grad, matrices, more, gain, scale, tokens, residual_grad)


def hand_over_kernel(count, *refs):
    sources, outs, held = refs[:count], refs[count : 2 * count], refs[2 * count : 3 * count]
    sems = refs[3 * count]
    into = [pltpu.make_async_copy(sources[i], held[i], sems.at[0, i]) for i in range(count)]
    out = [pltpu.make_async_copy(held[i], outs[i], sems.at[1, i]) for i in range(count)]
    for cp in into:
        cp.start()
    for a, b in zip(into, out, strict=True):
        a.wait()
        b.start()
    for cp in out:
        cp.wait()


def hand_over(*arrays):
    hbm = pl.BlockSpec(memory_space=pl.ANY)
    return pl.pallas_call(
        functools.partial(hand_over_kernel, len(arrays)),
        in_specs=[hbm] * len(arrays),
        out_specs=[hbm] * len(arrays),
        out_shape=[jax.ShapeDtypeStruct(a.shape, a.dtype) for a in arrays],
        scratch_shapes=[pltpu.VMEM(a.shape, a.dtype) for a in arrays] + [pltpu.SemaphoreType.DMA((2, len(arrays)))],
        compiler_params=pltpu.CompilerParams(vmem_limit_bytes=60 * 2**20),
        name="hand_over",
    )(*arrays)


def rms_scale(values):
    return lax.rsqrt(jnp.mean(values * values, axis=-1, keepdims=True) + EPSILON)


def rotate_t(values, cosine, sine):
    half = cosine.shape[0]
    shaped = values.reshape(-1, 2, half, values.shape[1])
    u, w = shaped[:, 0], shaped[:, 1]
    turned = jnp.stack([u * cosine - w * sine, w * cosine + u * sine], axis=1)
    return turned.reshape(values.shape)


def gathered(block, cid, by_rows):
    if meshed():
        return gather_all(block, cid, by_rows)
    return lax.all_gather(block, "dev", axis=0, tiled=True)


def on_device(
    tokens,
    positions,
    expert_picks,
    priority,
    first_gain,
    query_weight,
    key_projection_matrix,
    value_projection_matrix,
    output_weight,
    second_gain,
    router_weight,
    gate_weight,
    up_weight,
    down_weight,
    cotangent,
):
    devices = lax.axis_size("dev")
    rows, model = tokens.shape
    split = devices // EXPERTS
    capacity = split * ((9 * rows * TOP + 8 * EXPERTS * split - 1) // (8 * EXPERTS * split))
    weight_rows = query_weight.shape[0]

    output_matrix = lax.all_gather(output_weight, "dev", axis=0, tiled=True)

    extra = jnp.concatenate([router_weight, first_gain[:, None], second_gain[:, None]], axis=1)
    pad = (-extra.shape[1]) % 128
    packed = jnp.concatenate(
        [query_weight, key_projection_matrix, value_projection_matrix, extra, jnp.zeros((weight_rows, pad), BF16)],
        axis=1,
    )
    matrices = gathered(packed, 1, False)
    qkv_matrix = matrices[:, :QKV]
    router_matrix = matrices[:, QKV : QKV + EXPERTS]
    gain_first = matrices[:, QKV + EXPERTS].astype(F32)
    gain_second = matrices[:, QKV + EXPERTS + 1].astype(F32)

    one_hot = expert_picks[:, :, None] == jnp.arange(EXPERTS, dtype=jnp.int32)
    picked_any = jnp.any(one_hot, axis=1)
    turn = jnp.sum(jnp.where(one_hot, priority[:, :, None], 0), axis=1)
    turn = jnp.where(picked_any, turn, jnp.int32(2**30)).T
    rank = jnp.sum((turn[:, None, :] < turn[:, :, None]).astype(jnp.int32), axis=2)
    slot_rows = jnp.where(picked_any.T & (rank < capacity), rank, -1).astype(F32)

    inputs = tokens.astype(F32)
    scale_one = rms_scale(inputs)
    normed_one = (inputs * scale_one * gain_first).astype(BF16)
    half_dim = HEAD_DIM // 2
    frequency = jnp.power(10000.0, -(jnp.arange(half_dim, dtype=F32) * 2.0) / HEAD_DIM)
    angle = positions.astype(F32)[None, :] * frequency[:, None]
    cos_t, sin_t = jnp.cos(angle), jnp.sin(angle)
    qkv_t = dims(qkv_matrix, normed_one, 0, 1)
    q_width, k_width = QUERY_HEADS * HEAD_DIM, KEY_HEADS * HEAD_DIM
    query_t = rotate_t(qkv_t[:q_width], cos_t, sin_t).astype(BF16) * BF16(HEAD_DIM**-0.5)
    key = rotate_t(qkv_t[q_width : q_width + k_width], cos_t, sin_t).astype(BF16).T
    value = qkv_t[q_width + k_width :].astype(BF16).T
    kv = jnp.stack([key, value])
    lo = (jnp.arange(rows, dtype=jnp.int32) - positions)[None, :]
    if meshed():
        attended_t, lse, window, plane_slots, expert_up = attend_mesh(
            query_t, kv, lo, cotangent, slot_rows.reshape(-1, 8, rows)
        )
    else:
        window, offset = window_of(kv), jnp.int32(0)
        attended_t, lse = attend(query_t, window, offset, lo)
    residual = inputs + dims(attended_t, output_matrix, 0, 0)
    scale_two = rms_scale(residual)
    normed_two = (residual * scale_two * gain_second).astype(BF16)

    logits = dims(normed_two, router_matrix, 1, 0)
    logits = jnp.where(picked_any, logits, MASKED)
    picked_exp = jnp.exp(logits - jnp.max(logits, axis=1, keepdims=True))
    gates = picked_exp / jnp.sum(picked_exp, axis=1, keepdims=True)

    if meshed():
        gate_rows = jnp.pad(gates.T.reshape(EXPERTS, rows // 128, 128), ((0, 0), (0, 8 - rows // 128), (0, 0)))
        expert_in, grad_rows, out_rows, gated_hidden, gate_in_grad, up_in_grad, gate_grad_rows = run_experts(
            normed_two, gate_rows, plane_slots, expert_up, gate_weight, up_weight, down_weight
        )
        returned_grad, gate_grad, gate_gradient, up_gradient, down_gradient = run_grads(
            grad_rows, plane_slots, gate_grad_rows, expert_in, expert_up, gated_hidden, gate_in_grad, up_in_grad
        )
        gate_grad = gate_grad[:, : rows // 128].reshape(EXPERTS, rows).T
    else:
        gate_rows, slot = (
            lax.all_to_all(jnp.repeat(v, split, axis=0), "dev", split_axis=0, concat_axis=0, tiled=True)
            for v in (gates.T, slot_rows)
        )
        pair_slot = jnp.where(
            slot.reshape(devices // 2, 2, rows) >= 0,
            slot.reshape(devices // 2, 2, rows) + jnp.array([[0], [capacity]], F32),
            -1.0,
        ).astype(jnp.int32).reshape(devices // 2, 1, 2 * rows)
        all_upstream = lax.all_gather(cotangent, "dev", axis=0, tiled=True)
        all_normed = lax.all_gather(normed_two, "dev", axis=0, tiled=True)
        expert_in, expert_up = dispatch(pair_slot, all_normed, all_upstream, 2 * capacity)
        slot_hit = slot[:, None, :] == jnp.arange(capacity, dtype=F32)[None, :, None]
        gate_of_slot = jnp.sum(jnp.where(slot_hit, gate_rows[:, None, :], 0.0), axis=2).reshape(-1, 1)
        gate_in = dims(expert_in, gate_weight, 1, 0)
        up_in = dims(expert_in, up_weight, 1, 0)
        sigmoid_gate = 1.0 / (1.0 + jnp.exp(-gate_in))
        silu_gate = gate_in * sigmoid_gate
        hidden = (silu_gate * up_in).astype(BF16)
        gated_hidden = (hidden.astype(F32) * gate_of_slot).astype(BF16)
        hidden_up = dims(expert_up, down_weight, 1, 1)
        hidden_grad = hidden_up * gate_of_slot
        gate_grad_slot = jnp.sum(hidden.astype(F32) * hidden_up, axis=1).reshape(devices, capacity)
        gate_in_grad = (hidden_grad * up_in * sigmoid_gate * (1.0 + gate_in * (1.0 - sigmoid_gate))).astype(BF16)
        up_in_grad = (hidden_grad * silu_gate).astype(BF16)
        partial_in = (dims(gate_in_grad, gate_weight, 1, 1) + dims(up_in_grad, up_weight, 1, 1)).astype(BF16)
        gate_grad_rows = jnp.sum(jnp.where(slot_hit, gate_grad_slot[:, :, None], 0.0), axis=1)
        returned_grad = lax.psum_scatter(
            combine(pair_slot, partial_in, 2 * capacity), "dev", scatter_dimension=0, tiled=True
        ).astype(F32)
        gate_grad = lax.all_to_all(gate_grad_rows, "dev", split_axis=0, concat_axis=0, tiled=True)
        gate_grad = jnp.sum(gate_grad.reshape(EXPERTS, split, rows), axis=1).T
        partial_out = dims(gated_hidden, down_weight, 1, 0).astype(BF16)
        dense_out = combine(pair_slot, partial_out, 2 * capacity)
        mixture = lax.psum_scatter(dense_out, "dev", scatter_dimension=0, tiled=True).astype(F32)
        down_gradient = dims(gated_hidden, expert_up, 0, 0)
        gate_gradient = dims(expert_in, gate_in_grad, 0, 0)
        up_gradient = dims(expert_in, up_in_grad, 0, 0)

    upstream = cotangent.astype(F32)
    logit_grad = (gates * (gate_grad - jnp.sum(gates * gate_grad, axis=1, keepdims=True))).astype(BF16)
    router_gradient = dims(normed_two, logit_grad, 0, 0)
    normed_two_grad = returned_grad + dims(logit_grad, router_matrix, 1, 1)
    weighted_two = normed_two_grad * gain_second
    second_gain_grad = jnp.sum(normed_two_grad * residual * scale_two, axis=0)
    residual_grad = (
        upstream
        + scale_two * weighted_two
        - residual * scale_two**3 * jnp.mean(weighted_two * residual, axis=-1, keepdims=True)
    )
    branch_grad = residual_grad.astype(BF16)
    output_gradient = dims(attended_t, branch_grad, 1, 0).astype(BF16)
    output_gradient = lax.psum_scatter(output_gradient, "dev", scatter_dimension=0, tiled=True).astype(F32)
    grad_t = dims(output_matrix, branch_grad, 1, 1).astype(BF16)

    if meshed():
        qkv_grad, layer_output = attend_back_mesh(
            query_t, window, lo, grad_t, lse, attended_t, cos_t, sin_t, out_rows, plane_slots, residual
        )
    else:
        query_grad_t, window_grad = attend_back(query_t, window, offset, lo, grad_t, lse, attended_t, cos_t, sin_t)
        key_grad, value_grad = unwindow(window_grad)
        key_grad_t = rotate_t(key_grad.T, cos_t, -sin_t).astype(BF16)
        qkv_grad_t = jnp.concatenate([query_grad_t, key_grad_t, value_grad.T.astype(BF16)], axis=0)
        layer_output = (residual + mixture).astype(BF16)
    more = jnp.concatenate(
        [router_gradient, second_gain_grad[:, None], jnp.zeros((model, (-(EXPERTS + 1)) % 256), F32)], axis=1
    ).astype(BF16)
    if meshed():
        query_sums, key_sums, value_sums, more_sums, tokens_gradient, first_sums = finish(
            normed_one, qkv_grad, matrices, more, gain_first[None, :], scale_one, tokens, residual_grad
        )
        first_sums = first_sums[0, :weight_rows]
        (
            gate_gradient, up_gradient, down_gradient, layer_output, tokens_gradient, query_sums, key_sums, value_sums
        ) = hand_over(
            gate_gradient, up_gradient, down_gradient, layer_output, tokens_gradient, query_sums, key_sums, value_sums
        )
    else:
        qkv_gradient = dims(normed_one, qkv_grad_t, 0, 1).astype(BF16)
        normed_one_grad = dims(qkv_grad_t, qkv_matrix, 0, 1)
        weighted_one = normed_one_grad * gain_first
        tokens_gradient = (
            residual_grad
            + scale_one * weighted_one
            - inputs * scale_one**3 * jnp.mean(weighted_one * inputs, axis=-1, keepdims=True)
        )
        sums = lax.psum_scatter(
            jnp.concatenate([qkv_gradient, more], axis=1), "dev", scatter_dimension=0, tiled=True
        ).astype(F32)
        query_sums, key_sums, value_sums, more_sums = jnp.split(sums, [q_width, q_width + k_width, QKV], axis=1)
        first_sums = lax.psum_scatter(
            jnp.sum(normed_one_grad * inputs * scale_one, axis=0), "dev", scatter_dimension=0, tiled=True
        )
    return (
        layer_output,
        tokens_gradient,
        first_sums,
        query_sums,
        key_sums,
        value_sums,
        output_gradient,
        more_sums[:, EXPERTS],
        more_sums[:, :EXPERTS],
        gate_gradient,
        up_gradient,
        down_gradient,
    )


def solution(mesh):
    rows, whole = P("dev", None), P("dev")
    columns = P(None, "dev")
    return jax.shard_map(
        on_device,
        mesh=mesh,
        in_specs=(rows, whole, rows, rows, whole, rows, rows, rows, rows, whole, rows, columns, columns, rows, rows),
        out_specs=(rows, rows, whole, rows, rows, rows, rows, whole, rows, columns, columns, rows),
        check_vma=False,
    )
```

```python
import functools
import jax, jax.numpy as jnp
from jax import lax
from jax.experimental import pallas as pl
from jax.experimental.pallas import tpu as pltpu

MESH = pl.DeviceIdType.MESH


def place():
    me = lax.axis_index("dev")
    return lax.rem(me // 8, 4), lax.rem(me // 4, 2), lax.rem(me // 2, 2), lax.rem(me, 2)


def number(z, y, x, c):
    return ((z * 2 + y) * 2 + x) * 2 + c


def greet(partners):
    barrier = pltpu.get_barrier_semaphore()
    for partner in partners:
        pl.semaphore_signal(barrier, inc=1, device_id=(partner,), device_id_type=MESH)
    pl.semaphore_wait(barrier, len(partners))


def partners_of(z, y, x, c):
    return [
        number(z, y, x, 1 - c),
        number(z, y, 1 - x, c),
        number(z, 1 - y, x, c),
        number(lax.rem(z + 1, 4), y, x, c),
        number(lax.rem(z + 2, 4), y, x, c),
        number(lax.rem(z + 3, 4), y, x, c),
    ]


class Whole:
    scratch = [pltpu.SemaphoreType.DMA] + [
        pltpu.SemaphoreType.DMA(shape)
        for shape in ((2, 2, 4), (2, 4), (2, 3, 4), (2, 3, 4), (2, 4, 4), (2, 4, 4))
    ]

    def __init__(self, x_ref, o_ref, scratch):
        self.x_ref, self.o_ref = x_ref, o_ref
        self.local_sem, self.zs, self.zr, self.fs, self.fr, self.cs, self.cr = scratch
        self.z, self.y, self.x, self.c = z, y, x, c = place()
        self.rows, cols = x_ref.shape
        half = (cols // 256) * 128
        self.pieces = (pl.ds(0, half), pl.ds(half, cols - half))
        self.sibling = number(z, y, x, 1 - c)
        self.me = number(z, y, x, c)
        self.around = (number(z, 1 - y, x, c), number(z, y, 1 - x, c))
        self.far = ((1, 0), (0, 1))
        self.local = pltpu.make_async_copy(x_ref, self.there(self.me), self.local_sem)

    def turn(self, i):
        middle = i if i < 2 else 5 - i
        return jnp.where(self.z == 0, (4 - i) % 4, jnp.where(self.z == 3, i, middle))

    def there(self, block, p=None):
        at = pl.ds(pl.multiple_of(block * self.rows, 16), self.rows)
        return self.o_ref.at[at, :] if p is None else self.o_ref.at[at, self.pieces[p]]

    def copy(self, source, block, p, send_sem, recv_sem, target):
        return pltpu.make_async_remote_copy(
            src_ref=source, dst_ref=self.there(block, p), send_sem=send_sem, recv_sem=recv_sem,
            device_id=(target,), device_id_type=MESH)

    def block(self, k, fy=0, fx=0):
        return number(lax.rem(self.z + 4 - k, 4), (1 - self.y) if fy else self.y, (1 - self.x) if fx else self.x, self.c)

    def along(self, i, use):
        k = self.turn(i)
        zz = lax.rem(self.z + 4 - k, 4)
        for up, step in ((1, 1), (0, 3)):
            go = (zz <= self.z) & (self.z < 3) if up else (zz >= self.z) & (self.z > 0)

            @pl.when(go)
            def _(up=up, step=step):
                block = self.block(k)
                target = number(lax.rem(self.z + step, 4), self.y, self.x, self.c)
                for p in range(2):
                    source = self.x_ref.at[:, self.pieces[p]] if i == 0 else self.there(block, p)
                    use(self.copy(
                        source, block, p, self.zs.at[p, up, k], self.zr.at[p, lax.rem(k + step, 4)], target))

    def hop(self, p, n, k):
        block = self.block(k, *self.far[p]) if n == 2 else self.block(k)
        target = self.around[p] if n == 0 else self.around[1 - p]
        return self.copy(self.there(block, p), block, p, self.fs.at[p, n, k], self.fr.at[p, n, k], target)

    def across(self, p, n, k):
        fy, fx = ((0, 0), self.far[p], (1 - self.far[p][0], 1 - self.far[p][1]), (1, 1))[n]
        block = self.block(k, fy, fx)
        return self.copy(self.there(block, p), block, p, self.cs.at[p, n, k], self.cr.at[p, n, k], self.sibling)

    def start(self):
        self.local.start()
        self.along(0, lambda cp: cp.start())

    def one(self, i):
        k = self.turn(i)
        if i == 0:
            self.local.wait()
        else:
            block = self.block(k)
            for p in range(2):
                self.copy(self.there(block, p), block, p, self.zs.at[p, 0, 0], self.zr.at[p, k], self.sibling).wait_recv()
            self.along(i, lambda cp: cp.start())
        for p in range(2):
            self.hop(p, 0, k).start()
            self.hop(p, 1, k).start()
            self.across(p, 0, k).start()

    def two(self, i):
        k = self.turn(i)
        for p in range(2):
            self.hop(p, 0, k).wait_recv()
            self.hop(p, 2, k).start()
            self.across(p, 1, k).start()

    def three(self, i):
        k = self.turn(i)
        for n in (1, 2):
            for p in range(2):
                self.hop(p, n, k).wait_recv()
                self.across(p, n + 1, k).start()

    def end(self):
        for k in range(4):
            for p in range(2):
                for n in range(4):
                    self.across(p, n, k).wait_recv()

    def sent(self):
        for i in range(4):
            self.along(i, lambda cp: cp.wait_send())
        for k in range(4):
            for p in range(2):
                for n in range(3):
                    self.hop(p, n, k).wait_send()
                for n in range(4):
                    self.across(p, n, k).wait_send()


from jax.sharding import PartitionSpec as P

QUERY_HEADS = 24
KEY_HEADS = 8
HEAD_DIM = 64
GROUP = QUERY_HEADS // KEY_HEADS
TOP = 8
EXPERTS = 32
MAXDOC = 2000
EPSILON = 1e-06
UNPICKED = 1e9
CAPACITY = 72
MASKED = -1e30
QKV = (QUERY_HEADS + 2 * KEY_HEADS) * HEAD_DIM
F32 = jnp.float32
BF16 = jnp.bfloat16


def meshed():
    return lax.axis_size("dev") == 32


def dims(a, b, ca, cb):
    return lax.dot_general(a, b, (((ca,), (cb,)), ((), ())), preferred_element_type=F32)


class Window:
    scratch = [pltpu.SemaphoreType.DMA((2,)), pltpu.SemaphoreType.DMA((9,)), pltpu.SemaphoreType.DMA((9,))]

    def __init__(self, rows, kv_ref, out, scratch):
        self.rows, self.kv_ref, self.out = rows, kv_ref, out
        self.lsem, self.ss, self.rs = scratch
        self.z, self.y, self.x, self.c = place()
        self.p = self.y * 2 + self.x
        self.sibling = number(self.z, self.y, self.x, 1 - self.c)
        self.near = [(self.z * 4 + lax.rem(self.p + d, 4)) * 2 + self.c for d in (1, 2, 3)]
        self.own_in = pltpu.make_async_copy(kv_ref, self.slot(4, self.c), self.lsem.at[0])
        self.stand_in = pltpu.make_async_copy(kv_ref, self.slot(0, self.c), self.lsem.at[1])
        self.to_up = self.copy(kv_ref, 0, 0, number(lax.rem(self.z + 1, 4), self.y, self.x, self.c))

    def slot(self, s, core):
        return self.out.at[:, pl.ds(pl.multiple_of((2 * s + core) * self.rows, 16), self.rows), :]

    def copy(self, source, s, n, target):
        return pltpu.make_async_remote_copy(
            src_ref=source, dst_ref=self.slot(s, self.c), send_sem=self.ss.at[n], recv_sem=self.rs.at[n],
            device_id=(target,), device_id_type=MESH)

    def own_near(self, d):
        return self.copy(self.kv_ref, 4 - d, d, self.near[d - 1])

    def across(self, s):
        source = self.kv_ref if s == 4 else self.slot(s, self.c)
        return self.copy(source, s, {4: 4, 0: 5}.get(s, 9 - s), self.sibling)

    def start(self):
        self.own_in.start()

        @pl.when(self.z < 3)
        def _():
            self.to_up.start()

        @pl.when(self.z == 0)
        def _():
            self.stand_in.start()

        for d in (1, 3, 2):
            @pl.when(self.p + d < 4)
            def _(d=d):
                self.own_near(d).start()
        self.across(4).start()

    def previous(self):
        @pl.when(self.z == 0)
        def _():
            self.stand_in.wait()

        @pl.when(self.z > 0)
        def _():
            self.to_up.wait_recv()

        for d in (3, 1, 2):
            @pl.when(self.p + d >= 4)
            def _(d=d):
                self.copy(self.slot(0, self.c), 4 - d, d, self.near[d - 1]).start()
        self.across(0).start()

    def pass_on(self):
        for d in (1, 3, 2):
            self.own_near(d).wait_recv()
            self.across(4 - d).start()

    def end(self):
        for s in range(5):
            pltpu.make_async_remote_copy(
                src_ref=self.kv_ref, dst_ref=self.slot(s, 1 - self.c), send_sem=self.ss.at[0],
                recv_sem=self.rs.at[{4: 4, 0: 5}.get(s, 9 - s)], device_id=(self.sibling,), device_id_type=MESH).wait_recv()
        self.own_in.wait()

    def sent(self):
        @pl.when(self.z < 3)
        def _():
            self.to_up.wait_send()

        for d in (1, 2, 3):
            self.own_near(d).wait_send()
        for s in range(5):
            self.across(s).wait_send()


def window_of(kv):
    rows = kv.shape[1]
    devices = lax.axis_size("dev")
    back = (MAXDOC + rows - 2) // rows
    parts = [
        lax.ppermute(kv, "dev", [(i - d, i) for i in range(d, devices)]) for d in range(back, 0, -1)
    ]
    return jnp.concatenate(parts + [kv, jnp.zeros_like(kv)], axis=1)


class Unwindow:
    @staticmethod
    def scratch(rows, width):
        return [
            pltpu.VMEM((5, 2, rows, width), BF16),
            pltpu.VMEM((3, 2, rows, width), BF16),
            pltpu.VMEM((2, rows, width), BF16),
            pltpu.SemaphoreType.DMA((9,)), pltpu.SemaphoreType.DMA((9,)),
        ]

    n_scratch = 5
    order = (3, 1, 2, 0, 4)

    def __init__(self, rows, grads, o_ref, scratch):
        self.rows, self.grads, self.o_ref = rows, grads, o_ref
        self.got, self.near_got, self.far, self.ss, self.rs = scratch
        self.z, self.y, self.x, self.c = place()
        self.p = self.y * 2 + self.x
        self.sibling = number(self.z, self.y, self.x, 1 - self.c)
        self.to_down = pltpu.make_async_remote_copy(
            src_ref=self.got.at[0], dst_ref=self.far, send_sem=self.ss.at[8], recv_sem=self.rs.at[8],
            device_id=(number(lax.rem(self.z + 3, 4), self.y, self.x, self.c),), device_id_type=MESH)

    def to_sibling(self, s):
        at = pl.ds(pl.multiple_of((2 * s + 1 - self.c) * self.rows, 16), self.rows)
        return pltpu.make_async_remote_copy(
            src_ref=self.grads.at[:, at, :], dst_ref=self.got.at[s], send_sem=self.ss.at[s], recv_sem=self.rs.at[s],
            device_id=(self.sibling,), device_id_type=MESH)

    def to_owner(self, d):
        owner = (self.z * 4 + lax.rem(self.p + 4 - d, 4)) * 2 + self.c
        return pltpu.make_async_remote_copy(
            src_ref=self.got.at[4 - d], dst_ref=self.near_got.at[d - 1], send_sem=self.ss.at[4 + d], recv_sem=self.rs.at[4 + d],
            device_id=(owner,), device_id_type=MESH)

    def rowwise(self, body):
        for h in range(2):
            def step(i, _, h=h):
                body(h, pl.multiple_of(i * 32, 32))
                return 0
            lax.fori_loop(0, self.rows // 32, step, 0)

    def start(self):
        for s in self.order:
            self.to_sibling(s).start()

    def sums(self):
        for s in self.order:
            self.to_sibling(s).wait_recv()
            first = (2 * s + self.c) * self.rows

            def both(h, r, s=s, first=first):
                at = pl.ds(r, 32)
                mine = self.grads[h, pl.ds(pl.multiple_of(first + r, 32), 32), :]
                total = self.got[s, h, at, :].astype(F32) + mine.astype(F32)
                if s == 4:
                    self.o_ref[h, at, :] = total
                else:
                    self.got[s, h, at, :] = total.astype(BF16)
            self.rowwise(both)
            if 0 < s < 4:
                self.to_owner(4 - s).start()

    def near(self):
        for d in (1, 3, 2):
            self.to_owner(d).wait_recv()

            @pl.when(self.p + d < 4)
            def _(d=d):
                def body(h, r):
                    at = pl.ds(r, 32)
                    self.o_ref[h, at, :] += self.near_got[d - 1, h, at, :].astype(F32)
                self.rowwise(body)

            @pl.when(self.p + d >= 4)
            def _(d=d):
                def body(h, r):
                    at = pl.ds(r, 32)
                    total = self.got[0, h, at, :].astype(F32) + self.near_got[d - 1, h, at, :].astype(F32)
                    self.got[0, h, at, :] = total.astype(BF16)
                self.rowwise(body)

        @pl.when(self.z > 0)
        def _():
            self.to_down.start()

    def end(self):
        @pl.when(self.z < 3)
        def _():
            self.to_down.wait_recv()

            def body(h, r):
                at = pl.ds(r, 32)
                self.o_ref[h, at, :] += self.far[h, at, :].astype(F32)
            self.rowwise(body)

        @pl.when(self.z > 0)
        def _():
            self.to_down.wait_send()

        for s in range(5):
            self.to_sibling(s).wait_send()
        for d in (1, 2, 3):
            self.to_owner(d).wait_send()


def unwindow(grads):
    rows = grads.shape[1] // 10
    devices = lax.axis_size("dev")
    back = (MAXDOC + rows - 2) // rows
    total = grads[:, back * rows : (back + 1) * rows].astype(F32)
    for d in range(1, back + 1):
        piece = grads[:, (back - d) * rows : (back - d + 1) * rows]
        moved = lax.ppermute(piece, "dev", [(i, i - d) for i in range(d, devices)])
        total = total + moved.astype(F32)
    return total


def make_bias(bias, lo_ref, chunks, rows):
    def fill(ch, _):
        at = pl.ds(pl.multiple_of(ch * rows, rows), rows)
        relative = lax.broadcasted_iota(jnp.int32, (rows, rows), 0) + (ch - (chunks - 1)) * rows
        query = lax.broadcasted_iota(jnp.int32, (rows, rows), 1)
        allowed = (relative <= query) & (relative >= lo_ref[...])
        bias[at, :] = jnp.where(allowed, 0.0, MASKED)
        return 0
    lax.fori_loop(0, chunks, fill, 0)


def side_by_side(ref, half):
    first = half * GROUP
    return jnp.concatenate(
        [ref[(first + g) * HEAD_DIM : (first + g + 1) * HEAD_DIM, :] for g in range(GROUP)], axis=1
    )


def stats_of(ref, half):
    return jnp.concatenate([ref[0, half * GROUP + g : half * GROUP + g + 1, :] for g in range(GROUP)], axis=1)


def attend_pair(chunks, rows, off, q_ref, kv_ref, o_ref, lse_ref, bias, between):
    lse_ref[...] = jnp.zeros_like(lse_ref)
    width = GROUP * rows
    for half in range(2):
        lanes = slice(half * HEAD_DIM, (half + 1) * HEAD_DIM)
        queries = side_by_side(q_ref, half)

        def chunk(i, carry, lanes=lanes, queries=queries):
            ch = chunks - 1 - i
            at = pl.ds(pl.multiple_of((ch + off) * rows, rows), rows)
            key, value = kv_ref[0, at, lanes], kv_ref[1, at, lanes]
            shift = bias[pl.ds(pl.multiple_of(ch * rows, rows), rows), :]
            top, total, mixed = carry
            score = dims(key, queries, 1, 0) + jnp.concatenate([shift] * GROUP, axis=1)
            new_top = jnp.maximum(top, jnp.max(score, axis=0, keepdims=True))
            weight = jnp.exp(score - new_top)
            fade = jnp.exp(top - new_top)
            total = total * fade + jnp.sum(weight, axis=0, keepdims=True)
            mixed = mixed * fade + dims(value, weight.astype(BF16), 0, 0)
            return new_top, total, mixed

        start = (jnp.full((1, width), MASKED, F32), jnp.zeros((1, width), F32), jnp.zeros((HEAD_DIM, width), F32))
        top, total, mixed = lax.fori_loop(0, chunks, chunk, start, unroll=3)
        mixed = (mixed / total).astype(BF16)
        lse = top + jnp.log(total)
        for g in range(GROUP):
            n = half * GROUP + g
            o_ref[n * HEAD_DIM : (n + 1) * HEAD_DIM, :] = mixed[:, g * rows : (g + 1) * rows]
            lse_ref[0, n : n + 1, :] = lse[:, g * rows : (g + 1) * rows]
        between(half)


def attend_kernel(chunks, rows, off_ref, lo_ref, q_ref, kv_ref, o_ref, lse_ref, bias):
    @pl.when(pl.program_id(0) == 0)
    def _():
        make_bias(bias, lo_ref, chunks, rows)

    attend_pair(chunks, rows, off_ref[0], q_ref, kv_ref, o_ref, lse_ref, bias, lambda half: None)


def attend_back_pair(
    chunks, rows, off, cos_ref, sin_ref, q_ref, kv_ref, g_ref, lse_ref, out_ref, dq_ref, dkv_ref, bias, between
):
    unused = pl.ds(pl.multiple_of((1 - off) * chunks * rows, rows), rows)
    dkv_ref[:, unused, :] = jnp.zeros((2, rows, 2 * HEAD_DIM), BF16)
    for half in range(2):
        lanes = slice(half * HEAD_DIM, (half + 1) * HEAD_DIM)
        queries, grads = side_by_side(q_ref, half), side_by_side(g_ref, half)
        lse = stats_of(lse_ref, half)
        mixed = side_by_side(out_ref, half).astype(F32)
        delta = jnp.sum(mixed * grads.astype(F32), axis=0, keepdims=True)

        def chunk(ch, query_grad, lanes=lanes, queries=queries, grads=grads, lse=lse, delta=delta):
            at = pl.ds(pl.multiple_of((ch + off) * rows, rows), rows)
            key, value = kv_ref[0, at, lanes], kv_ref[1, at, lanes]
            shift = bias[pl.ds(pl.multiple_of(ch * rows, rows), rows), :]
            score = dims(key, queries, 1, 0) + jnp.concatenate([shift] * GROUP, axis=1)
            weight = jnp.exp(score - lse)
            score_grad = (weight * (dims(value, grads, 1, 0) - delta)).astype(BF16)
            dkv_ref[0, at, lanes] = dims(score_grad, queries, 1, 1).astype(BF16)
            dkv_ref[1, at, lanes] = dims(weight.astype(BF16), grads, 1, 1).astype(BF16)
            return query_grad + dims(key, score_grad, 0, 0)

        done = lax.fori_loop(0, chunks, chunk, jnp.zeros((HEAD_DIM, GROUP * rows), F32), unroll=3)
        done = done * (HEAD_DIM**-0.5)
        cosine, sine = cos_ref[...], sin_ref[...]
        for g in range(GROUP):
            grad = done[:, g * rows : (g + 1) * rows]
            u, w = grad[: HEAD_DIM // 2], grad[HEAD_DIM // 2 :]
            n = (half * GROUP + g) * HEAD_DIM
            dq_ref[n : n + HEAD_DIM // 2, :] = (u * cosine + w * sine).astype(BF16)
            dq_ref[n + HEAD_DIM // 2 : n + HEAD_DIM, :] = (w * cosine - u * sine).astype(BF16)
        between(half)


def attend_back_kernel(
    chunks, rows, off_ref, lo_ref, cos_ref, sin_ref, q_ref, kv_ref, g_ref, lse_ref, out_ref, dq_ref, dkv_ref, bias
):
    @pl.when(pl.program_id(0) == 0)
    def _():
        make_bias(bias, lo_ref, chunks, rows)

    attend_back_pair(
        chunks, rows, off_ref[0], cos_ref, sin_ref, q_ref, kv_ref, g_ref, lse_ref, out_ref, dq_ref, dkv_ref, bias,
        lambda half: None,
    )


def attention_specs(rows, span):
    width = 2 * GROUP * HEAD_DIM
    return dict(
        smem=pl.BlockSpec(memory_space=pltpu.SMEM),
        row=pl.BlockSpec((1, rows), lambda j: (0, 0)),
        table=pl.BlockSpec((HEAD_DIM // 2, rows), lambda j: (0, 0)),
        query=pl.BlockSpec((width, rows), lambda j: (j, 0)),
        kv=pl.BlockSpec((2, span, 2 * HEAD_DIM), lambda j: (0, 0, j)),
        stat=pl.BlockSpec((1, 8, rows), lambda j: (j, 0, 0)),
    )


def attend(query_t, window, offset, lo):
    rows, span = query_t.shape[1], window.shape[1]
    chunks = span // rows - 1
    s = attention_specs(rows, span)
    return pl.pallas_call(
        functools.partial(attend_kernel, chunks, rows),
        grid=(KEY_HEADS // 2,),
        in_specs=[s["smem"], s["row"], s["query"], s["kv"]],
        out_specs=[s["query"], s["stat"]],
        out_shape=[
            jax.ShapeDtypeStruct(query_t.shape, BF16),
            jax.ShapeDtypeStruct((KEY_HEADS // 2, 8, rows), F32),
        ],
        scratch_shapes=[pltpu.VMEM((chunks * rows, rows), F32)],
        compiler_params=pltpu.CompilerParams(vmem_limit_bytes=40 * 2**20),
        cost_estimate=pl.CostEstimate(flops=7 * 10**9, bytes_accessed=8 * 10**6, transcendentals=15 * 10**6),
        name="attend",
    )(offset.reshape(1), lo, query_t, window)


def attend_back(query_t, window, offset, lo, grad_t, lse, attended_t, cos_t, sin_t):
    rows, span = query_t.shape[1], window.shape[1]
    chunks = span // rows - 1
    s = attention_specs(rows, span)
    return pl.pallas_call(
        functools.partial(attend_back_kernel, chunks, rows),
        grid=(KEY_HEADS // 2,),
        in_specs=[s["smem"], s["row"], s["table"], s["table"], s["query"], s["kv"], s["query"], s["stat"], s["query"]],
        out_specs=[s["query"], s["kv"]],
        out_shape=[
            jax.ShapeDtypeStruct(query_t.shape, BF16),
            jax.ShapeDtypeStruct(window.shape, BF16),
        ],
        scratch_shapes=[pltpu.VMEM((chunks * rows, rows), F32)],
        compiler_params=pltpu.CompilerParams(vmem_limit_bytes=40 * 2**20),
        cost_estimate=pl.CostEstimate(flops=18 * 10**9, bytes_accessed=16 * 10**6, transcendentals=15 * 10**6),
        name="attend_back",
    )(offset.reshape(1), lo, cos_t, sin_t, query_t, window, grad_t, lse, attended_t)


def hits(slot_ref, slots):
    width = slot_ref.shape[-1]
    return slot_ref[0] == lax.broadcasted_iota(jnp.int32, (slots, width), 0)


def dispatch_kernel(slot_ref, x_ref, u_ref, xo_ref, uo_ref):
    chosen = jnp.where(hits(slot_ref, xo_ref.shape[0]), 1.0, 0.0).astype(BF16)
    xo_ref[...] = dims(chosen, x_ref[...], 1, 0).astype(BF16)
    uo_ref[...] = dims(chosen, u_ref[...], 1, 0).astype(BF16)


def dispatch(slot, normed, upstream, slots):
    pairs, _, width = slot.shape
    model = normed.shape[1]
    return pl.pallas_call(
        dispatch_kernel,
        grid=(pairs,),
        in_specs=[
            pl.BlockSpec((1, 1, width), lambda i: (i, 0, 0)),
            pl.BlockSpec((width, model), lambda i: (i, 0)),
            pl.BlockSpec((width, model), lambda i: (i, 0)),
        ],
        out_specs=[pl.BlockSpec((slots, model), lambda i: (i, 0))] * 2,
        out_shape=[jax.ShapeDtypeStruct((pairs * slots, model), BF16)] * 2,
        compiler_params=pltpu.CompilerParams(vmem_limit_bytes=40 * 2**20),
        cost_estimate=pl.CostEstimate(flops=2 * 10**9, bytes_accessed=65 * 10**6, transcendentals=0),
        name="dispatch",
    )(slot, normed, upstream)


def combine_kernel(slot_ref, r_ref, o_ref):
    chosen = jnp.where(hits(slot_ref, r_ref.shape[0]), 1.0, 0.0).astype(BF16)
    o_ref[...] = dims(chosen, r_ref[...], 0, 0).astype(BF16)


def combine(slot, rows, slots):
    pairs, _, width = slot.shape
    model = rows.shape[1]
    return pl.pallas_call(
        combine_kernel,
        grid=(pairs,),
        in_specs=[
            pl.BlockSpec((1, 1, width), lambda i: (i, 0, 0)),
            pl.BlockSpec((slots, model), lambda i: (i, 0)),
        ],
        out_specs=pl.BlockSpec((width, model), lambda i: (i, 0)),
        out_shape=jax.ShapeDtypeStruct((pairs * width, model), BF16),
        compiler_params=pltpu.CompilerParams(vmem_limit_bytes=40 * 2**20),
        cost_estimate=pl.CostEstimate(flops=10**9, bytes_accessed=33 * 10**6, transcendentals=0),
        name="combine",
    )(slot, rows)


SLOTS = 80


def far_first(i):
    return jnp.where(i == 0, 2, jnp.where(i == 3, 0, 2 * i - 1))


def greet_all():
    me = lax.axis_index("dev")
    barrier = pltpu.get_barrier_semaphore()

    def signal(d, _):
        pl.semaphore_signal(barrier, inc=1, device_id=(lax.rem(me + d, 32),), device_id_type=MESH)
        return 0
    lax.fori_loop(1, 32, signal, 0)
    pl.semaphore_wait(barrier, 31)


class Swap:
    def __init__(self, source, into, ss, rs):
        self.me = lax.axis_index("dev")
        self.source, self.into, self.ss, self.rs = source, into, ss, rs

    def copy(self, d):
        target = lax.rem(self.me + d, 32)
        return pltpu.make_async_remote_copy(
            src_ref=self.source(target), dst_ref=self.into.at[self.me], send_sem=self.ss.at[d], recv_sem=self.rs.at[d],
            device_id=(target,), device_id_type=MESH)

    def start(self):
        def one(d, _):
            self.copy(d).start()
            return 0
        lax.fori_loop(1, 32, one, 0)
        self.into[self.me] = self.source(self.me)[...]

    def wait_recv(self):
        def one(d, _):
            self.copy(d).wait_recv()
            return 0
        lax.fori_loop(1, 32, one, 0)

    def wait_send(self):
        def one(d, _):
            self.copy(d).wait_send()
            return 0
        lax.fori_loop(1, 32, one, 0)


def in_plane(y, x, c):
    return (y * 2 + x) * 2 + c


def chosen_rows(slots_ref, block, expert):
    row = slots_ref[block, pl.ds(expert, 1), :]
    return row == lax.broadcasted_iota(jnp.int32, (SLOTS, row.shape[1]), 0).astype(F32)


def greet_near():
    z, y, x, c = place()
    greet(
        [number(z, y, x, 1 - c)]
        + [number(z, 1 - y, x, cc) for cc in (c, 1 - c)]
        + [number(z, y, 1 - x, cc) for cc in (c, 1 - c)]
        + [number(z, 1 - y, 1 - x, c)]
        + [number(lax.rem(z + d, 4), y, x, c) for d in (1, 2, 3)]
    )


class Forth:
    scratch = staticmethod(lambda rows, half: [
        pltpu.VMEM((2, 2, 4, rows, half), BF16),
        pltpu.VMEM((2, 2, 4, 4, SLOTS, half), BF16),
        pltpu.SemaphoreType.DMA((2, 2, 4)), pltpu.SemaphoreType.DMA((2, 4)),
        pltpu.SemaphoreType.DMA((2, 4)), pltpu.SemaphoreType.DMA((2, 4)),
        pltpu.SemaphoreType.DMA((2, 2, 4, 4)), pltpu.SemaphoreType.DMA((2, 2, 4, 3)), pltpu.SemaphoreType.DMA((2,)),
    ])
    n_scratch = 9

    def __init__(self, x_ref, slots_ref, xi, scratch):
        self.x_ref, self.slots_ref, self.xi = x_ref, slots_ref, xi
        self.land, self.stage, self.zs, self.zr, self.fs, self.fr, self.cs, self.cr, self.own_sem = scratch
        self.z, self.y, self.x, self.c = place()
        half = x_ref.shape[1] // 2
        self.cols = [pl.ds(0, half), pl.ds(half, half)]

    def turn(self, i):
        middle = jnp.where(i < 2, i, 5 - i)
        return jnp.where(self.z == 0, lax.rem(4 - i, 4), jnp.where(self.z == 3, i, middle))

    def to_z(self, p, up, k, own=False):
        step = 1 if up else 3
        source = self.x_ref.at[:, self.cols[p]] if own else self.land.at[p, 0, k]
        there = lax.rem(k + step, 4)
        return pltpu.make_async_remote_copy(
            src_ref=source, dst_ref=self.land.at[p, 0, there],
            send_sem=self.zs.at[p, int(up), k], recv_sem=self.zr.at[p, there],
            device_id=(number(lax.rem(self.z + step, 4), self.y, self.x, self.c),), device_id_type=MESH)

    def hop(self, p, k):
        z, y, x, c = self.z, self.y, self.x, self.c
        beside = number(z, 1 - y, x, c) if p == 0 else number(z, y, 1 - x, c)
        return pltpu.make_async_remote_copy(
            src_ref=self.land.at[p, 0, k], dst_ref=self.land.at[p, 1, k],
            send_sem=self.fs.at[p, k], recv_sem=self.fr.at[p, k], device_id=(beside,), device_id_type=MESH)

    def block(self, p, h, k):
        zz = lax.rem(self.z + 4 - k, 4)
        if p == 0:
            return number(zz, (1 - self.y) if h else self.y, self.x, self.c)
        return number(zz, self.y, (1 - self.x) if h else self.x, self.c)

    def who(self, p):
        y, x, c = self.y, self.x, self.c
        ay, ax = (y, 1 - x) if p == 0 else (1 - y, x)
        return [(y, x, 1 - c), (ay, ax, c), (ay, ax, 1 - c), (y, x, c)]

    def slots_at(self, p, h, k):
        return self.xi.at[pl.ds(pl.multiple_of(self.block(p, h, k) * SLOTS, 16), SLOTS), self.cols[p]]

    def served(self, p, h, k, t):
        return pltpu.make_async_remote_copy(
            src_ref=self.stage.at[p, h, k, t], dst_ref=self.slots_at(p, h, k),
            send_sem=self.cs.at[p, h, k, t], recv_sem=self.cr.at[p, h, k, t],
            device_id=(number(self.z, *self.who(p)[t]),), device_id_type=MESH)

    def kept(self, p, h, k):
        return pltpu.make_async_copy(self.stage.at[p, h, k, 3], self.slots_at(p, h, k), self.cs.at[p, h, k, 3])

    def serve(self, p, h, k):
        block = self.block(p, h, k)
        source = self.land[p, h, k]
        for t, to in enumerate(self.who(p)):
            chosen = jnp.where(chosen_rows(self.slots_ref, block, in_plane(*to)), 1.0, 0.0).astype(BF16)
            self.stage[p, h, k, t] = dims(chosen, source, 1, 0).astype(BF16)
            if t < 3:
                self.served(p, h, k, t).start()
            else:
                self.kept(p, h, k).start()

    def own(self, p):
        return pltpu.make_async_copy(self.x_ref.at[:, self.cols[p]], self.land.at[p, 0, 0], self.own_sem.at[p])

    def along(self, i, use):
        k = self.turn(i)
        zz = lax.rem(self.z + 4 - k, 4)
        for p in range(2):
            @pl.when((zz < self.z) & (self.z < 3))
            def _(p=p):
                use(self.to_z(p, True, k))

            @pl.when((zz > self.z) & (self.z > 0))
            def _(p=p):
                use(self.to_z(p, False, k))

    def along_own(self, use):
        for p in range(2):
            @pl.when(self.z < 3)
            def _(p=p):
                use(self.to_z(p, True, 0, own=True))

            @pl.when(self.z > 0)
            def _(p=p):
                use(self.to_z(p, False, 0, own=True))

    def start(self):
        for p in range(2):
            self.own(p).start()
        self.along_own(lambda cp: cp.start())

    def come(self, i):
        k = self.turn(i)
        for p in range(2):
            self.to_z(p, True, lax.rem(k + 3, 4)).wait_recv()
        self.along(i, lambda cp: cp.start())

    def one(self, i, come=True):
        k = self.turn(i)

        @pl.when(i == 0)
        def _():
            for p in range(2):
                self.own(p).wait()

        if come:
            @pl.when(i > 0)
            def _():
                self.come(i)

        for p in range(2):
            self.hop(p, k).start()
        for p in range(2):
            self.serve(p, 0, k)

    def two(self, i):
        k = self.turn(i)
        for p in range(2):
            self.hop(p, k).wait_recv()
            self.serve(p, 1, k)

    def arrived(self, group, i):
        k = self.turn(i)

        @pl.when(group == 0)
        def _():
            for p in range(2):
                self.served(p, 0, k, 0).wait_recv()
                self.kept(p, 0, k).wait()

        @pl.when(group == 1)
        def _():
            self.kept(0, 1, k).wait()
            self.served(0, 1, k, 0).wait_recv()
            self.served(1, 0, k, 1).wait_recv()
            self.served(1, 0, k, 2).wait_recv()

        @pl.when(group == 2)
        def _():
            self.kept(1, 1, k).wait()
            self.served(1, 1, k, 0).wait_recv()
            self.served(0, 0, k, 1).wait_recv()
            self.served(0, 0, k, 2).wait_recv()

        @pl.when(group == 3)
        def _():
            for p in range(2):
                self.served(p, 1, k, 1).wait_recv()
                self.served(p, 1, k, 2).wait_recv()

    def chip(self, group, i):
        dy, dx = lax.rem(group, 2), group // 2
        zz = lax.rem(self.z + 4 - self.turn(i), 4)
        yy = jnp.where(dy == 1, 1 - self.y, self.y)
        xx = jnp.where(dx == 1, 1 - self.x, self.x)
        return (zz * 2 + yy) * 2 + xx

    def sent(self):
        self.along_own(lambda cp: cp.wait_send())

        def each(i, _):
            k = self.turn(i)
            self.along(i, lambda cp: cp.wait_send())
            for p in range(2):
                self.hop(p, k).wait_send()
                for h in range(2):
                    for t in range(3):
                        self.served(p, h, k, t).wait_send()
            return 0
        lax.fori_loop(0, 4, each, 0)


BEFORE_UNIT = {0: ("o1", "t0", "o2", "t1"), 4: ("o3", "t2"), 8: ("t3",)}


def experts_kernel(
    x_ref, gates_ref, slots_ref, ui_ref, wg_in, wu_in, wd_in,
    xi_out, dx_out, y_out, hg_out, dg_out, du_out, gg_ref,
    gates, xi, ubuf, dx_buf, y_buf, hg_ref, dg_ref, du_ref, wg_ref, wu_ref, wd_ref, wgt, wut, wdt,
    gs, gr, usem, xsem, osem, wsem, *scratch,
):
    z, y, x, c = place()
    rows = x_ref.shape[0]
    greet_all()
    swap = Swap(lambda t: gates_ref.at[t], gates, gs, gr)
    ag = Forth(x_ref, slots_ref, xi, scratch)
    ag.start()

    def chip_of(u):
        return ag.chip(lax.rem(u, 4), u // 4)

    def at_chip(u):
        return pl.ds(pl.multiple_of(chip_of(u) * 2 * SLOTS, 16), 2 * SLOTS)

    def load_up(u):
        return pltpu.make_async_copy(ui_ref.at[at_chip(u), :], ubuf.at[lax.rem(u, 2)], usem.at[lax.rem(u, 2)])

    load_up(0).start()
    swap.start()
    loads = [
        pltpu.make_async_copy(source, into, wsem.at[i])
        for i, (source, into) in enumerate(((wg_in, wg_ref), (wu_in, wu_ref), (wd_in, wd_ref)))
    ]
    for cp in loads:
        cp.start()
    ag.one(0)
    for cp, source, into in zip(loads, (wg_ref, wu_ref, wd_ref), (wgt, wut, wdt), strict=True):
        cp.wait()
        into[...] = source[...].T
    swap.wait_recv()

    def store(n, buf, out, u):
        return pltpu.make_async_copy(buf.at[lax.rem(u, 2)], out.at[at_chip(u), :], osem.at[n, lax.rem(u, 2)])

    def stores(u):
        return [store(0, dx_buf, dx_out, u), store(1, y_buf, y_out, u)]

    def keep(u):
        return [
            pltpu.make_async_copy(held.at[at_chip(u), :], out.at[at_chip(u), :], xsem.at[i, u])
            for i, (held, out) in enumerate(((xi, xi_out), (hg_ref, hg_out), (dg_ref, dg_out), (du_ref, du_out)))
        ]

    def unit(u):
        slot = lax.rem(u, 2)
        chip = chip_of(u)

        @pl.when(u < 15)
        def _():
            load_up(u + 1).start()

        ag.arrived(lax.rem(u, 4), u // 4)

        @pl.when(u >= 2)
        def _():
            for s in stores(u - 2):
                s.wait()

        load_up(u).wait()
        at = at_chip(u)
        expert = in_plane(y, x, c)
        picks, gate = [], []
        for core in range(2):
            block = chip * 2 + core
            hit = chosen_rows(slots_ref, block, expert)
            picks.append(hit)
            gate_row = jnp.concatenate([gates[block, 0:1, :], gates[block, 1:2, :]], axis=1)
            gate.append(jnp.sum(jnp.where(hit, gate_row, 0.0), axis=1, keepdims=True))
        gate_of_slot = jnp.concatenate(gate, axis=0)
        hidden_up = dims(ubuf[slot], wdt[...], 1, 0)
        rows_in = xi[at, :]
        gate_in = dims(rows_in, wg_ref[...], 1, 0)
        up_in = dims(rows_in, wu_ref[...], 1, 0)
        sig = 1.0 / (1.0 + jnp.exp(-gate_in))
        silu = gate_in * sig
        hidden = (silu * up_in).astype(BF16).astype(F32)
        gated = (hidden * gate_of_slot).astype(BF16)
        hidden_grad = hidden_up * gate_of_slot
        gate_back = (hidden_grad * up_in * sig * (1.0 + gate_in * (1.0 - sig))).astype(BF16)
        up_back = (hidden_grad * silu).astype(BF16)
        hg_ref[at, :] = gated
        dg_ref[at, :] = gate_back
        du_ref[at, :] = up_back
        dx_buf[slot] = (dims(gate_back, wgt[...], 1, 0) + dims(up_back, wut[...], 1, 0)).astype(BF16)
        y_buf[slot] = dims(gated, wd_ref[...], 1, 0).astype(BF16)
        gate_grad = jnp.sum(hidden * hidden_up, axis=1, keepdims=True)
        for core in range(2):
            block = chip * 2 + core
            row = jnp.sum(jnp.where(picks[core], gate_grad[core * SLOTS : (core + 1) * SLOTS], 0.0), axis=0, keepdims=True)
            gg_ref[block, 0:1, :] = row[:, :128]
            gg_ref[block, 1:2, :] = row[:, 128:]
        for s in stores(u):
            s.start()
        for s in keep(u):
            s.start()

    step = {}
    for i in range(4):
        step[f"o{i}"] = functools.partial(ag.one, jnp.int32(i))
        step[f"c{i}"] = functools.partial(ag.come, jnp.int32(i))
        step[f"s{i}"] = functools.partial(ag.one, jnp.int32(i), False)
        step[f"t{i}"] = functools.partial(ag.two, jnp.int32(i))

    def each(u, _):
        for when, names in BEFORE_UNIT.items():
            @pl.when(u == when)
            def _(names=names):
                for name in names:
                    step[name]()

        unit(u)
        return 0

    lax.fori_loop(0, 16, each, 0)
    for u in (14, 15):
        for s in stores(u):
            s.wait()

    def last(u, _):
        for s in keep(u):
            s.wait()
        return 0
    lax.fori_loop(0, 16, last, 0)
    ag.sent()
    swap.wait_send()


def run_experts(normed, gates, slots, ui, gate_weight, up_weight, down_weight):
    rows, model = normed.shape
    ff = gate_weight.shape[1]
    n = 32 * SLOTS
    hbm, vmem = pl.BlockSpec(memory_space=pl.ANY), pl.BlockSpec(memory_space=pltpu.VMEM)
    dma = pltpu.SemaphoreType.DMA
    long = jax.ShapeDtypeStruct((n, model), BF16)
    short = jax.ShapeDtypeStruct((n, ff), BF16)
    return pl.pallas_call(
        experts_kernel,
        in_specs=[hbm, vmem, vmem, hbm, hbm, hbm, hbm],
        out_specs=[hbm] * 6 + [vmem],
        out_shape=[long] * 3 + [short] * 3 + [jax.ShapeDtypeStruct((32, 8, 128), F32)],
        scratch_shapes=[
            pltpu.VMEM((32, 8, 128), F32),
            pltpu.VMEM((n, model), BF16),
            pltpu.VMEM((2, 2 * SLOTS, model), BF16),
            pltpu.VMEM((2, 2 * SLOTS, model), BF16),
            pltpu.VMEM((2, 2 * SLOTS, model), BF16),
            pltpu.VMEM((n, ff), BF16), pltpu.VMEM((n, ff), BF16), pltpu.VMEM((n, ff), BF16),
            pltpu.VMEM((model, ff), BF16), pltpu.VMEM((model, ff), BF16), pltpu.VMEM((ff, model), BF16),
            pltpu.VMEM((ff, model), BF16), pltpu.VMEM((ff, model), BF16), pltpu.VMEM((model, ff), BF16),
            dma((32,)), dma((32,)), dma((2,)), dma((4, 16)), dma((2, 2)), dma((3,)),
        ] + Forth.scratch(rows, model // 2),
        compiler_params=pltpu.CompilerParams(collective_id=13, has_side_effects=True, vmem_limit_bytes=56 * 2**20),
        name="experts",
    )(normed, gates, slots, ui, gate_weight, up_weight, down_weight)


class Back:
    scratch = staticmethod(lambda rows, half: [
        pltpu.VMEM((2, 2, 4, SLOTS, half), BF16),
        pltpu.VMEM((2, 3, 2, 4, SLOTS, half), BF16),
        pltpu.VMEM((2, 4, rows, half), BF16),
        pltpu.VMEM((2, 4, rows, half), BF16),
        pltpu.VMEM((2, 4, rows, half), BF16),
        pltpu.VMEM((2, 4, rows, half), BF16),
        pltpu.SemaphoreType.DMA((2, 2, 4)),
        pltpu.SemaphoreType.DMA((2, 3, 2, 4)), pltpu.SemaphoreType.DMA((2, 3, 2, 4)),
        pltpu.SemaphoreType.DMA((2, 4)), pltpu.SemaphoreType.DMA((2, 4)),
        pltpu.SemaphoreType.DMA((2, 4)), pltpu.SemaphoreType.DMA((2, 4)),
    ])
    n_scratch = 13

    def __init__(self, rows_ref, slots_ref, o_ref, scratch):
        self.rows_ref, self.slots_ref, self.o_ref = rows_ref, slots_ref, o_ref
        (self.own, self.rin, self.sout, self.rb, self.zout, self.rz,
         self.own_sem, self.ts, self.tr, self.bs, self.br, self.zs, self.zr) = scratch
        self.z, self.y, self.x, self.c = place()
        half = rows_ref.shape[1] // 2
        self.cols = [pl.ds(0, half), pl.ds(half, half)]

    def block(self, p, h, k, yy, xx, cc):
        zz = lax.rem(self.z + k, 4)
        if p == 0:
            return number(zz, (1 - yy) if h else yy, xx, cc)
        return number(zz, yy, (1 - xx) if h else xx, cc)

    def sources(self, p):
        y, x, c = self.y, self.x, self.c
        ay, ax = (y, 1 - x) if p == 0 else (1 - y, x)
        return [(y, x, 1 - c), (ay, ax, c), (ay, ax, 1 - c)]

    def slot_rows(self, block, p):
        return self.rows_ref.at[pl.ds(pl.multiple_of(block * SLOTS, 16), SLOTS), self.cols[p]]

    def to(self, p, t, h, k):
        place_of = self.sources(p)[t]
        return pltpu.make_async_remote_copy(
            src_ref=self.slot_rows(self.block(p, h, k, *place_of), p), dst_ref=self.rin.at[p, t, h, k],
            send_sem=self.ts.at[p, t, h, k], recv_sem=self.tr.at[p, t, h, k],
            device_id=(number(self.z, *place_of),), device_id_type=MESH)

    def mine(self, p, h, k):
        return pltpu.make_async_copy(
            self.slot_rows(self.block(p, h, k, self.y, self.x, self.c), p), self.own.at[p, h, k], self.own_sem.at[p, h, k])

    def second(self, p, k):
        z, y, x, c = self.z, self.y, self.x, self.c
        target = number(z, 1 - y, x, c) if p == 0 else number(z, y, 1 - x, c)
        return pltpu.make_async_remote_copy(
            src_ref=self.sout.at[p, k], dst_ref=self.rb.at[p, k], send_sem=self.bs.at[p, k], recv_sem=self.br.at[p, k],
            device_id=(target,), device_id_type=MESH)

    def third(self, p, k):
        target = number(lax.rem(self.z + k, 4), self.y, self.x, self.c)
        return pltpu.make_async_remote_copy(
            src_ref=self.zout.at[p, k], dst_ref=self.rz.at[p, k], send_sem=self.zs.at[p, k], recv_sem=self.zr.at[p, k],
            device_id=(target,), device_id_type=MESH)

    def issue(self, h, i):
        k = far_first(i)
        for p in range(2):
            for t in (1, 2, 0):
                self.to(p, t, h, k).start()
            self.mine(p, h, k).start()

    def start(self):
        self.issue(1, 0)
        self.issue(0, 0)

    def dense(self, p, h, k):
        self.mine(p, h, k).wait()
        for t in range(3):
            self.to(p, t, h, k).wait_recv()
        block = self.block(p, h, k, self.y, self.x, self.c)
        total = None
        for t, who in enumerate([(self.y, self.x, self.c)] + self.sources(p)):
            hit = chosen_rows(self.slots_ref, block, in_plane(*who))
            chosen = jnp.where(hit, 1.0, 0.0).astype(BF16)
            values = self.own[p, h, k] if t == 0 else self.rin[p, t - 1, h, k]
            term = dims(chosen, values, 0, 0)
            total = term if total is None else total + term
        return total

    def step(self, u):
        i = u // 2
        k = far_first(jnp.int32(i))
        early = u % 2 == 0

        @pl.when(early)
        def _():
            for p in range(2):
                self.sout[p, k] = self.dense(p, 1, k).astype(BF16)
                self.second(p, k).start()

            @pl.when(i < 3)
            def _():
                self.issue(1, i + 1)

        @pl.when(u % 2 == 1)
        def _():
            for p in range(2):
                total = self.dense(p, 0, k)
                self.second(p, k).wait_recv()
                total = total + self.rb[p, k].astype(F32)

                @pl.when(k > 0)
                def _(p=p, total=total):
                    self.zout[p, k] = total.astype(BF16)
                    self.third(p, k).start()

                @pl.when(k == 0)
                def _(p=p, total=total):
                    self.o_ref[:, self.cols[p]] = total

            @pl.when(i < 3)
            def _():
                self.issue(0, i + 1)

    def finish(self):
        for p in range(2):
            for k in range(1, 4):
                self.third(p, k).wait_recv()
            self.o_ref[:, self.cols[p]] += (
                self.rz[p, 1].astype(F32) + self.rz[p, 2].astype(F32) + self.rz[p, 3].astype(F32)
            )

        def one(k, _):
            for p in range(2):
                self.second(p, k).wait_send()

                @pl.when(k > 0)
                def _(p=p):
                    self.third(p, k).wait_send()
                for t in range(3):
                    for h in range(2):
                        self.to(p, t, h, k).wait_send()
            return 0
        lax.fori_loop(0, 4, one, 0)


def grads_kernel(
    dx_ref, slots_ref, gg_ref, xi_ref, ui_ref, hg_in, dg_in, du_in,
    o_ref, back_ref, wg_out, wu_out, wd_out, xcol, ucol, gout, uout, dout, hg_ref, dg_ref, du_ref,
    gs, gr, isem, osem, wsem, *scratch,
):
    greet_all()
    swap = Swap(lambda t: gg_ref.at[t], back_ref, gs, gr)
    rs = Back(dx_ref, slots_ref, o_ref, scratch)
    rs.start()
    swap.start()

    def col(i):
        return pl.ds(pl.multiple_of(i * 256, 256), 256)

    def loads(i):
        s = lax.rem(i, 2)
        return [
            pltpu.make_async_copy(xi_ref.at[:, col(i)], xcol.at[s], isem.at[0, s]),
            pltpu.make_async_copy(ui_ref.at[:, col(i)], ucol.at[s], isem.at[1, s]),
        ]

    def stores(i):
        s = lax.rem(i, 2)
        return [
            pltpu.make_async_copy(gout.at[s], wg_out.at[col(i), :], osem.at[0, s]),
            pltpu.make_async_copy(uout.at[s], wu_out.at[col(i), :], osem.at[1, s]),
            pltpu.make_async_copy(dout.at[s], wd_out.at[:, col(i)], osem.at[2, s]),
        ]

    for cp in loads(0):
        cp.start()
    whole = [
        pltpu.make_async_copy(source, into, wsem.at[i])
        for i, (source, into) in enumerate(((hg_in, hg_ref), (dg_in, dg_ref), (du_in, du_ref)))
    ]
    for cp in whole:
        cp.start()
    for cp in whole:
        cp.wait()

    def one(u, _):
        @pl.when(u < 6)
        def _():
            s = lax.rem(u, 2)

            @pl.when(u < 5)
            def _():
                for cp in loads(u + 1):
                    cp.start()

            for cp in loads(u):
                cp.wait()

            @pl.when(u >= 2)
            def _():
                for cp in stores(u - 2):
                    cp.wait()

            rows_in = xcol[s]
            gout[s] = dims(rows_in, dg_ref[...], 0, 0)
            uout[s] = dims(rows_in, du_ref[...], 0, 0)
            dout[s] = dims(hg_ref[...], ucol[s], 0, 0)
            for cp in stores(u):
                cp.start()

        rs.step(u)
        return 0

    lax.fori_loop(0, 8, one, 0)
    for i in (4, 5):
        for cp in stores(i):
            cp.wait()
    swap.wait_recv()
    rs.finish()
    swap.wait_send()


def run_grads(dx, slots, gg, xi, ui, hg, dg, du):
    rows, model = slots.shape[2], dx.shape[1]
    ff = hg.shape[1]
    n = dx.shape[0]
    hbm, vmem = pl.BlockSpec(memory_space=pl.ANY), pl.BlockSpec(memory_space=pltpu.VMEM)
    dma = pltpu.SemaphoreType.DMA
    return pl.pallas_call(
        grads_kernel,
        in_specs=[hbm, vmem, vmem, hbm, hbm, hbm, hbm, hbm],
        out_specs=[vmem, vmem, hbm, hbm, hbm],
        out_shape=[
            jax.ShapeDtypeStruct((rows, model), F32),
            jax.ShapeDtypeStruct((32, 8, 128), F32),
            jax.ShapeDtypeStruct((model, ff), F32),
            jax.ShapeDtypeStruct((model, ff), F32),
            jax.ShapeDtypeStruct((ff, model), F32),
        ],
        scratch_shapes=[
            pltpu.VMEM((2, n, 256), BF16), pltpu.VMEM((2, n, 256), BF16),
            pltpu.VMEM((2, 256, ff), F32), pltpu.VMEM((2, 256, ff), F32), pltpu.VMEM((2, ff, 256), F32),
            pltpu.VMEM((n, ff), BF16), pltpu.VMEM((n, ff), BF16), pltpu.VMEM((n, ff), BF16),
            dma((32,)), dma((32,)), dma((2, 2)), dma((3, 2)), dma((3,)),
        ] + Back.scratch(rows, model // 2),
        compiler_params=pltpu.CompilerParams(collective_id=14, has_side_effects=True, vmem_limit_bytes=56 * 2**20),
        name="grads",
    )(dx, slots, gg, xi, ui, hg, dg, du)


BEFORE_HEADS = (
    "w0", "rank", "w1", "v0", "w2", "v1", "w3", "v2", "v3", "bias", "gains", "norm", "u0", "u1",
    "u2", "u3", "wend", "kv", "ag", "o0", "q", "prev", "o1", "pass", "t0", "kend",
)
AFTER_HEAD = ("o2", "t1", "o3", "t2", "", "t3", "", "")


def front_kernel(
    chunks, rows, lo_ref, cos_ref, sin_ref, x_ref, wq_ref, wk_ref, wv_ref, router_ref, u_ref, turn_ref, turn_t_ref,
    gain_one_ref, gain_two_ref, q_out, o_ref, lse_ref, window_out, slots_ref, ui_ref, w_out, n_ref, gains_ref, scale_ref,
    q_ref, window, w_ref, part_ref, bias, mine, kv, key_t, insem, outsem, gs, gr, lsem, ws, wr, *scratch,
):
    loads, at = [], 0
    for i, ref in enumerate((wq_ref, wk_ref, wv_ref)):
        loads.append(pltpu.make_async_copy(ref, part_ref.at[:, pl.ds(at, ref.shape[1])], insem.at[i]))
        at += ref.shape[1]
    for cp in loads:
        cp.start()
    part_ref[:, at:] = jnp.zeros((part_ref.shape[0], part_ref.shape[1] - at), BF16)
    part_ref[:, at : at + EXPERTS] = router_ref[...]
    greet_all()
    weights = Whole(part_ref, w_ref, scratch[:7])
    swap = Swap(lambda t: mine.at[t // 8], slots_ref, gs, gr)
    keys = Window(rows, kv, window, (lsem, ws, wr))
    ag = Forth(u_ref, slots_ref, ui_ref, scratch[7:])
    cosine, sine = cos_ref[...], sin_ref[...]
    q_width, k_width = QUERY_HEADS * HEAD_DIM, KEY_HEADS * HEAD_DIM

    def rank():
        for e in range(EXPERTS):
            own = turn_t_ref[e : e + 1, :]
            place_of = jnp.sum(jnp.where(turn_ref[:, e : e + 1] < own, 1.0, 0.0), axis=0, keepdims=True)
            slot = jnp.where((own < UNPICKED) & (place_of < CAPACITY), place_of, -1.0)
            mine[e // 8, e % 8 : e % 8 + 1, :] = slot
        mine[:, 8:16, :] = jnp.zeros((4, 8, rows), F32)
        for plane in range(4):
            mine[plane, 8:9, 0 : part_ref.shape[0]] = gain_one_ref[...].astype(F32)
            mine[plane, 9:10, 0 : part_ref.shape[0]] = gain_two_ref[...].astype(F32)
        swap.start()

    def gains():
        swap.wait_recv()
        part = part_ref.shape[0]
        for t in range(32):
            gains_ref[0:8, t * part : (t + 1) * part] = slots_ref[t, 8:16, 0:part]

    def norm():
        def some(i, _):
            at = pl.ds(pl.multiple_of(i * 32, 32), 32)
            values = x_ref[at, :].astype(F32)
            scale = lax.rsqrt(jnp.mean(values * values, axis=1, keepdims=True) + EPSILON)
            scale_ref[at, :] = scale
            n_ref[at, :] = (values * scale * gains_ref[0:1, :]).astype(BF16)
            return 0
        lax.fori_loop(0, rows // 32, some, 0)

    def roped(values, into, first):
        turned = values.T
        for n in range(256 // HEAD_DIM):
            u = turned[n * HEAD_DIM : n * HEAD_DIM + HEAD_DIM // 2]
            w = turned[n * HEAD_DIM + HEAD_DIM // 2 : (n + 1) * HEAD_DIM]
            at = first + n * HEAD_DIM
            into[pl.ds(pl.multiple_of(at, 32), 32), :] = (u * cosine - w * sine).astype(BF16)
            into[pl.ds(pl.multiple_of(at + 32, 32), 32), :] = (w * cosine + u * sine).astype(BF16)

    def keys_and_values():
        for n in range(k_width // 256):
            roped(dims(n_ref[...], w_ref[:, q_width + n * 256 : q_width + (n + 1) * 256], 1, 0), key_t, n * 256)
            kv[0, :, n * 256 : (n + 1) * 256] = key_t[n * 256 : (n + 1) * 256, :].T
        kv[1] = dims(n_ref[...], w_ref[:, q_width + k_width : QKV], 1, 0).astype(BF16)
        keys.start()

    def queries():
        def some(i, _):
            at = pl.ds(pl.multiple_of(i * 256, 256), 256)
            roped(dims(n_ref[...], w_ref[:, at], 1, 0), q_ref, i * 256)
            q_ref[at, :] = (q_ref[at, :].astype(F32) * HEAD_DIM**-0.5).astype(BF16)
            return 0
        lax.fori_loop(0, q_width // 256, some, 0)

    def whole():
        weights.end()
        outs[0].start()

    def queried():
        queries()
        outs[1].start()

    def windowed():
        keys.end()
        outs[2].start()

    outs = [
        pltpu.make_async_copy(held, out, outsem.at[i])
        for i, (held, out) in enumerate(((w_ref, w_out), (q_ref, q_out), (window, window_out)))
    ]
    step = {
        "rank": rank, "gains": gains, "norm": norm, "kv": keys_and_values, "q": queried,
        "ag": ag.start, "bias": lambda: make_bias(bias, lo_ref, chunks, rows), "wend": whole,
        "prev": keys.previous, "pass": keys.pass_on, "kend": windowed,
    }
    for i in range(4):
        step[f"w{i}"] = functools.partial(weights.one, i)
        step[f"v{i}"] = functools.partial(weights.two, i)
        step[f"u{i}"] = functools.partial(weights.three, i)
        step[f"c{i}"] = functools.partial(ag.come, jnp.int32(i))
        step[f"s{i}"] = functools.partial(ag.one, jnp.int32(i), False)
        step[f"o{i}"] = functools.partial(ag.one, jnp.int32(i))
        step[f"t{i}"] = functools.partial(ag.two, jnp.int32(i))

    for cp in loads:
        cp.wait()
    weights.start()
    for name in BEFORE_HEADS:
        step[name]()
    width = 2 * GROUP * HEAD_DIM

    def pair(j, _):
        lanes = pl.ds(pl.multiple_of(j * 2 * HEAD_DIM, 2 * HEAD_DIM), 2 * HEAD_DIM)
        head = pl.ds(pl.multiple_of(j * width, width), width)

        def between(half):
            for u in range(half, 8, 2):
                if AFTER_HEAD[u]:
                    @pl.when(2 * j + half == u)
                    def _(u=u):
                        step[AFTER_HEAD[u]]()

        attend_pair(
            chunks, rows, lax.rem(lax.axis_index("dev"), 2), q_ref.at[head, :], window.at[:, :, lanes],
            o_ref.at[head, :], lse_ref.at[pl.ds(j, 1)], bias, between,
        )
        return 0

    lax.fori_loop(0, KEY_HEADS // 2, pair, 0)

    def last(u, _):
        ag.arrived(lax.rem(u, 4), u // 4)
        return 0
    lax.fori_loop(0, 16, last, 0)
    ag.sent()
    keys.sent()
    swap.wait_send()
    weights.sent()
    for cp in outs:
        cp.wait()


def front(lo, cos_t, sin_t, tokens, projections, router, upstream, turn, gain_one, gain_two):
    rows, model = tokens.shape
    chunks = 9
    keys = KEY_HEADS * HEAD_DIM
    part = jax.ShapeDtypeStruct((router.shape[0], -(-(QKV + EXPERTS) // 128) * 128), BF16)
    hbm, vmem = pl.BlockSpec(memory_space=pl.ANY), pl.BlockSpec(memory_space=pltpu.VMEM)
    dma = pltpu.SemaphoreType.DMA
    return pl.pallas_call(
        functools.partial(front_kernel, chunks, rows),
        in_specs=[vmem] * 4 + [hbm] * 3 + [vmem, hbm] + [vmem] * 4,
        out_specs=[hbm, vmem, vmem, hbm, vmem, hbm, hbm, vmem, vmem, vmem],
        out_shape=[
            jax.ShapeDtypeStruct((QUERY_HEADS * HEAD_DIM, rows), BF16),
            jax.ShapeDtypeStruct((QUERY_HEADS * HEAD_DIM, rows), BF16),
            jax.ShapeDtypeStruct((KEY_HEADS // 2, 8, rows), F32),
            jax.ShapeDtypeStruct((2, 10 * rows, keys), BF16),
            jax.ShapeDtypeStruct((32, 16, rows), F32),
            jax.ShapeDtypeStruct((32 * SLOTS, model), BF16),
            jax.ShapeDtypeStruct((32 * part.shape[0], part.shape[1]), BF16),
            jax.ShapeDtypeStruct((rows, model), BF16),
            jax.ShapeDtypeStruct((8, model), F32),
            jax.ShapeDtypeStruct((rows, 1), F32),
        ],
        scratch_shapes=[
            pltpu.VMEM((QUERY_HEADS * HEAD_DIM, rows), BF16), pltpu.VMEM((2, 10 * rows, keys), BF16),
            pltpu.VMEM((32 * part.shape[0], part.shape[1]), BF16), pltpu.VMEM(part.shape, BF16),
            pltpu.VMEM((chunks * rows, rows), F32), pltpu.VMEM((4, 16, rows), F32), pltpu.VMEM((2, rows, keys), BF16),
            pltpu.VMEM((keys, rows), BF16), dma((3,)), dma((3,)), dma((32,)), dma((32,)),
        ]
        + Window.scratch + Whole.scratch + Forth.scratch(rows, model // 2),
        compiler_params=pltpu.CompilerParams(collective_id=16, has_side_effects=True, vmem_limit_bytes=58 * 2**20),
        name="front",
    )(lo, cos_t, sin_t, tokens, *projections, router, upstream, turn, turn.T, gain_one, gain_two)


IN_PAIRS = {0: (0,), 2: (1,), 4: (2,), 6: (3,)}
AFTER_PAIRS = (4, "sums", 5, 6, "near", "turn", 7)


def attend_back_mesh_kernel(
    chunks, rows, lo_ref, cos_ref, sin_ref, q_ref, kv_in, branch_ref, wo_in, lse_ref, out_ref, y_ref, slots_ref, residual_in,
    grad_out, layer_ref, wo, g_ref, wsem, kv_ref, residual_ref, insem, bias, dkv, sums_ref, gt_ref, o_ref, *scratch,
):
    greet_near()
    rs = Back(y_ref, slots_ref, o_ref, scratch[: Back.n_scratch])
    keys = Unwindow(rows, dkv, sums_ref, scratch[Back.n_scratch :])
    rs.start()
    kv_load = pltpu.make_async_copy(kv_in, kv_ref, insem.at[0])
    residual_load = pltpu.make_async_copy(residual_in, residual_ref, insem.at[1])
    kv_load.start()
    residual_load.start()
    step = wo.shape[1]

    def wo_load(i):
        return pltpu.make_async_copy(wo_in.at[pl.ds(i * step, step), :], wo.at[i % 2], wsem.at[i % 2])

    wo_load(0).start()
    make_bias(bias, lo_ref, chunks, rows)
    for i in range(wo_in.shape[0] // step):
        if (i + 1) * step < wo_in.shape[0]:
            wo_load(i + 1).start()
        wo_load(i).wait()
        g_ref[i * step : (i + 1) * step, :] = dims(wo[i % 2], branch_ref[...], 1, 1).astype(BF16)
    kv_load.wait()
    residual_load.wait()
    width = 2 * GROUP * HEAD_DIM

    def pair(j, _):
        lanes = pl.ds(pl.multiple_of(j * 2 * HEAD_DIM, 2 * HEAD_DIM), 2 * HEAD_DIM)
        head = pl.ds(pl.multiple_of(j * width, width), width)

        def between(half):
            for n, names in IN_PAIRS.items():
                if n % 2 == half:
                    @pl.when(2 * j + half == n)
                    def _(names=names):
                        for name in names:
                            rs.step(name)

        attend_back_pair(
            chunks, rows, lax.rem(lax.axis_index("dev"), 2), cos_ref, sin_ref, q_ref.at[head, :], kv_ref.at[:, :, lanes], g_ref.at[head, :],
            lse_ref.at[pl.ds(j, 1)], out_ref.at[head, :], gt_ref.at[head, :], dkv.at[:, :, lanes], bias, between,
        )
        return 0

    lax.fori_loop(0, KEY_HEADS // 2, pair, 0)

    def turned(first, last):
        for n in range(first, last, 256):
            grad_out[:, n : n + 256] = gt_ref[n : n + 256, :].T

    keys.start()
    for name in AFTER_PAIRS:
        if isinstance(name, int):
            rs.step(name)
        elif name == "sums":
            keys.sums()
        elif name == "turn":
            turned(0, QUERY_HEADS * HEAD_DIM)
        else:
            keys.near()
    keys.end()
    base = QUERY_HEADS * HEAD_DIM
    key_t = sums_ref[0].T
    cosine, sine = cos_ref[...], sin_ref[...]
    for n in range(KEY_HEADS):
        first, middle = n * HEAD_DIM, n * HEAD_DIM + HEAD_DIM // 2
        u, w = key_t[first:middle], key_t[middle : first + HEAD_DIM]
        gt_ref[base + first : base + middle, :] = (u * cosine + w * sine).astype(BF16)
        gt_ref[base + middle : base + first + HEAD_DIM, :] = (w * cosine - u * sine).astype(BF16)
    turned(base, base + KEY_HEADS * HEAD_DIM)
    grad_out[:, base + KEY_HEADS * HEAD_DIM :] = sums_ref[1].astype(BF16)
    rs.finish()
    layer_ref[...] = (residual_ref[...] + o_ref[...]).astype(BF16)


def attend_back_mesh(query_t, window, lo, branch_grad, output_matrix, lse, attended_t, cos_t, sin_t, y, slots, residual):
    rows, span, keys = query_t.shape[1], window.shape[1], window.shape[2]
    chunks = span // rows - 1
    model = y.shape[1]
    hbm, vmem = pl.BlockSpec(memory_space=pl.ANY), pl.BlockSpec(memory_space=pltpu.VMEM)
    return pl.pallas_call(
        functools.partial(attend_back_mesh_kernel, chunks, rows),
        in_specs=[vmem] * 4 + [hbm, vmem, hbm] + [vmem] * 2 + [hbm, vmem, hbm],
        out_specs=[vmem] * 2,
        out_shape=[
            jax.ShapeDtypeStruct((rows, QKV), BF16),
            jax.ShapeDtypeStruct((rows, model), BF16),
        ],
        scratch_shapes=[
            pltpu.VMEM((2, 384, model), BF16), pltpu.VMEM(query_t.shape, BF16), pltpu.SemaphoreType.DMA((2,)),
            pltpu.VMEM(window.shape, BF16), pltpu.VMEM((rows, model), F32), pltpu.SemaphoreType.DMA((2,)),
            pltpu.VMEM((chunks * rows, rows), F32), pltpu.VMEM(window.shape, BF16), pltpu.VMEM((2, rows, keys), F32),
            pltpu.VMEM((QKV, rows), BF16), pltpu.VMEM((rows, model), F32),
        ]
        + Back.scratch(rows, model // 2) + Unwindow.scratch(rows, keys),
        compiler_params=pltpu.CompilerParams(collective_id=15, has_side_effects=True, vmem_limit_bytes=60 * 2**20),
        name="attend_back",
    )(lo, cos_t, sin_t, query_t, window, branch_grad, output_matrix, lse, attended_t, y, slots, residual)


def finish_kernel(
    rows, n_ref, g_ref, w_in, more_ref, gain_ref, scale_ref, x_in, rg_in,
    oq_ref, ok_ref, ov_ref, om_ref, tg_ref, fg_ref, w_ref, x_ref, rg_ref, insem,
    dense, acc, ra, rb, rz, out, ng, mine, theirs, ssem, rsem, sa, ra_sem, sb, rb_sem, sz, rz_sem, gs, gr,
):
    z, y, x, c = place()
    greet_all()
    sibling = number(z, y, x, 1 - c)
    cols = acc.shape[2]
    main = g_ref.shape[1]
    half = cols // 2
    pieces = [pl.ds(0, half), pl.ds(half, half)]
    around = (number(z, y, 1 - x, c), number(z, 1 - y, x, c))
    swap = Swap(lambda t: mine.at[t], theirs, gs, gr)

    def lane(dy, dx, k):
        yy = 1 - y if dy else y
        xx = 1 - x if dx else x
        return (lax.rem(z + k, 4) * 2 + yy) * 2 + xx

    def to_sibling(dy, dx, k):
        chip = lane(dy, dx, k)
        n = (k, dy, dx)
        sides = (
            (dense.at[chip, pl.ds(pl.multiple_of((1 - c) * rows, 16), rows), :], pl.ds(0, main)),
            (more_ref.at[pl.ds(pl.multiple_of((2 * chip + 1 - c) * rows, 16), rows), :], pl.ds(main, cols - main)),
        )
        return [
            pltpu.make_async_remote_copy(
                src_ref=source, dst_ref=acc.at[chip, :, at], send_sem=ssem.at[(*n, i)], recv_sem=rsem.at[(*n, i)],
                device_id=(sibling,), device_id_type=MESH)
            for i, (source, at) in enumerate(sides)
        ]

    def first(p, d2, k, dy, dx):
        return pltpu.make_async_remote_copy(
            src_ref=acc.at[lane(dy, dx, k), :, pieces[p]], dst_ref=ra.at[p, d2, k],
            send_sem=sa.at[p, d2, k], recv_sem=ra_sem.at[p, d2, k], device_id=(around[p],), device_id_type=MESH)

    def second(p, k):
        dy, dx = (1, 0) if p == 0 else (0, 1)
        return pltpu.make_async_remote_copy(
            src_ref=acc.at[lane(dy, dx, k), :, pieces[p]], dst_ref=rb.at[p, k],
            send_sem=sb.at[p, k], recv_sem=rb_sem.at[p, k], device_id=(around[1 - p],), device_id_type=MESH)

    def third(p, k):
        return pltpu.make_async_remote_copy(
            src_ref=acc.at[lane(0, 0, k), :, pieces[p]], dst_ref=rz.at[p, k],
            send_sem=sz.at[p, k], recv_sem=rz_sem.at[p, k],
            device_id=(number(lax.rem(z + k, 4), y, x, c),), device_id_type=MESH)

    quarter = ((1, 1), (1, 0), (0, 1), (0, 0))

    def product(i, _):
        k = far_first(i)
        zz = lax.rem(z + k, 4)
        at = pl.ds(pl.multiple_of(zz * 8 * rows, 128), 8 * rows)
        part = dims(n_ref[:, at], g_ref[...], 0, 0).astype(BF16)
        for chip in range(4):
            dense[zz * 4 + chip] = part[chip * 2 * rows : (chip + 1) * 2 * rows]
        for dy, dx in quarter:
            for cp in to_sibling(dy, dx, k):
                cp.start()
        return 0

    def own_sums(k):
        for dy, dx in quarter:
            chip = lane(dy, dx, k)
            for cp in to_sibling(dy, dx, k):
                cp.wait_recv()
            acc[chip, :, :main] = (
                acc[chip, :, :main].astype(F32) + dense[chip, pl.ds(pl.multiple_of(c * rows, 16), rows), :].astype(F32)
            ).astype(BF16)
            acc[chip, :, main:] = (
                acc[chip, :, main:].astype(F32)
                + more_ref[pl.ds(pl.multiple_of((2 * chip + c) * rows, 16), rows), :].astype(F32)
            ).astype(BF16)
            if dx:
                first(0, dy, k, dy, dx).start()
            if dy:
                first(1, dx, k, dy, dx).start()

    def middle(k):
        for p in range(2):
            dy, dx = (1, 0) if p == 0 else (0, 1)
            first(p, 1, k, 1, 1).wait_recv()
            block = acc.at[lane(dy, dx, k), :, pieces[p]]
            block[...] = (block[...].astype(F32) + ra[p, 1, k].astype(F32)).astype(BF16)
            second(p, k).start()

    def late(k):
        for p in range(2):
            first(p, 0, k, 1 - p, p).wait_recv()
            second(p, k).wait_recv()
            block = acc.at[lane(0, 0, k), :, pieces[p]]
            total = block[...].astype(F32) + ra[p, 0, k].astype(F32) + rb[p, k].astype(F32)

            @pl.when(k > 0)
            def _(p=p, block=block, total=total):
                block[...] = total.astype(BF16)
                third(p, k).start()

            @pl.when(k == 0)
            def _(p=p, total=total):
                out[:, pieces[p]] = total

    def rest_of_tokens():
        ng[...] = dims(g_ref[...], w_ref[:, :main], 1, 1)

        def tail(i, total):
            at = pl.ds(pl.multiple_of(i * 32, 32), 32)
            grad, scale, values = ng[at, :], scale_ref[at, :], x_ref[at, :].astype(F32)
            weighted = grad * gain_ref[...]
            scaled = values * scale
            mean = jnp.mean(weighted * values, axis=1, keepdims=True)
            tg_ref[at, :] = rg_ref[at, :] + scale * weighted - scaled * (scale * scale * mean)
            return total + jnp.sum(grad * scaled, axis=0, keepdims=True)
        total = lax.fori_loop(0, x_ref.shape[0] // 32, tail, jnp.zeros(gain_ref.shape, F32))
        mine[...] = jnp.zeros_like(mine)
        for t in range(32):
            mine[t, 0:1, 0:rows] = total[:, t * rows : (t + 1) * rows]
        swap.start()

    loads = [
        pltpu.make_async_copy(source, into, insem.at[i])
        for i, (source, into) in enumerate(((w_in, w_ref), (x_in, x_ref), (rg_in, rg_ref)))
    ]
    for cp in loads:
        cp.start()
    lax.fori_loop(0, 4, product, 0)
    for cp in loads:
        cp.wait()

    def steps(i, _):
        @pl.when(i < 4)
        def _():
            own_sums(far_first(i))

        @pl.when(i == 3)
        def _():
            rest_of_tokens()

        @pl.when((i >= 1) & (i < 5))
        def _():
            middle(far_first(i - 1))

        @pl.when(i >= 2)
        def _():
            late(far_first(i - 2))
        return 0
    lax.fori_loop(0, 6, steps, 0)
    swap.wait_recv()
    fg_ref[...] = jnp.sum(theirs[...], axis=0)
    for p in range(2):
        for k in range(1, 4):
            third(p, k).wait_recv()
        out[:, pieces[p]] += rz[p, 1].astype(F32) + rz[p, 2].astype(F32) + rz[p, 3].astype(F32)
    at = 0
    for ref in (oq_ref, ok_ref, ov_ref, om_ref):
        ref[...] = out[:, at : at + ref.shape[1]]
        at += ref.shape[1]

    def sent(k, _):
        for dy, dx in quarter:
            for cp in to_sibling(dy, dx, k):
                cp.wait_send()
        for p in range(2):
            first(p, 0, k, 1 - p, p).wait_send()
            first(p, 1, k, 1, 1).wait_send()
            second(p, k).wait_send()

            @pl.when(k > 0)
            def _(p=p):
                third(p, k).wait_send()
        return 0
    lax.fori_loop(0, 4, sent, 0)
    swap.wait_send()


def finish(normed, grad, matrices, more, gain, scale, tokens, residual_grad):
    count, model = normed.shape
    rows = model // 32
    main, cols = grad.shape[1], grad.shape[1] + more.shape[1]
    half = cols // 2
    dma = pltpu.SemaphoreType.DMA
    hbm, vmem = pl.BlockSpec(memory_space=pl.ANY), pl.BlockSpec(memory_space=pltpu.VMEM)
    widths = [QUERY_HEADS * HEAD_DIM, KEY_HEADS * HEAD_DIM, KEY_HEADS * HEAD_DIM, more.shape[1]]
    return pl.pallas_call(
        functools.partial(finish_kernel, rows),
        in_specs=[vmem, vmem, hbm, vmem, vmem, vmem, hbm, hbm],
        out_specs=[vmem] * 6,
        out_shape=[jax.ShapeDtypeStruct((rows, w), F32) for w in widths] + [
            jax.ShapeDtypeStruct((count, model), F32),
            jax.ShapeDtypeStruct((8, 128), F32),
        ],
        scratch_shapes=[
            pltpu.VMEM(matrices.shape, BF16), pltpu.VMEM((count, model), BF16), pltpu.VMEM((count, model), F32), dma((3,)),
            pltpu.VMEM((16, 2 * rows, main), BF16),
            pltpu.VMEM((16, rows, cols), BF16),
            pltpu.VMEM((2, 2, 4, rows, half), BF16),
            pltpu.VMEM((2, 4, rows, half), BF16),
            pltpu.VMEM((2, 4, rows, half), BF16),
            pltpu.VMEM((rows, cols), F32),
            pltpu.VMEM((count, model), F32),
            pltpu.VMEM((32, 8, 128), F32),
            pltpu.VMEM((32, 8, 128), F32),
            dma((4, 2, 2, 2)), dma((4, 2, 2, 2)), dma((2, 2, 4)), dma((2, 2, 4)), dma((2, 4)), dma((2, 4)), dma((2, 4)), dma((2, 4)),
            dma((32,)), dma((32,)),
        ],
        compiler_params=pltpu.CompilerParams(collective_id=17, has_side_effects=True, vmem_limit_bytes=42 * 2**20),
        name="finish",
    )(normed, grad, matrices, more, gain, scale, tokens, residual_grad)


def chunks_of(shape):
    rows = shape[0]
    count = 1
    while rows % (32 * count) == 0 and rows // count * shape[1] > 2**18:
        count *= 2
    return [(i * (rows // count), rows // count) for i in range(count)]


def hand_over_kernel(count, *refs):
    sources, outs, held = refs[:count], refs[count : 2 * count], refs[2 * count : 3 * count]
    sems = refs[3 * count]
    into, out = [], []
    for source, there, here in zip(sources, outs, held, strict=True):
        for first, rows in chunks_of(source.shape):
            at, n = pl.ds(first, rows), len(into)
            into.append(pltpu.make_async_copy(source.at[at, :], here.at[at, :], sems.at[0, n]))
            out.append(pltpu.make_async_copy(here.at[at, :], there.at[at, :], sems.at[1, n]))
    for cp in into:
        cp.start()
    for a, b in zip(into, out, strict=True):
        a.wait()
        b.start()
    for cp in out:
        cp.wait()


def hand_over(*arrays):
    hbm = pl.BlockSpec(memory_space=pl.ANY)
    total = sum(len(chunks_of(a.shape)) for a in arrays)
    return pl.pallas_call(
        functools.partial(hand_over_kernel, len(arrays)),
        in_specs=[hbm] * len(arrays),
        out_specs=[hbm] * len(arrays),
        out_shape=[jax.ShapeDtypeStruct(a.shape, a.dtype) for a in arrays],
        scratch_shapes=[pltpu.VMEM(a.shape, a.dtype) for a in arrays] + [pltpu.SemaphoreType.DMA((2, total))],
        compiler_params=pltpu.CompilerParams(vmem_limit_bytes=60 * 2**20),
        name="hand_over",
    )(*arrays)


def rms_scale(values):
    return lax.rsqrt(jnp.mean(values * values, axis=-1, keepdims=True) + EPSILON)


def rotate_t(values, cosine, sine):
    half = cosine.shape[0]
    shaped = values.reshape(-1, 2, half, values.shape[1])
    u, w = shaped[:, 0], shaped[:, 1]
    turned = jnp.stack([u * cosine - w * sine, w * cosine + u * sine], axis=1)
    return turned.reshape(values.shape)


def on_device(
    tokens,
    positions,
    expert_picks,
    priority,
    first_gain,
    query_weight,
    key_projection_matrix,
    value_projection_matrix,
    output_weight,
    second_gain,
    router_weight,
    gate_weight,
    up_weight,
    down_weight,
    cotangent,
):
    devices = lax.axis_size("dev")
    rows, model = tokens.shape
    split = devices // EXPERTS
    capacity = split * ((9 * rows * TOP + 8 * EXPERTS * split - 1) // (8 * EXPERTS * split))
    weight_rows = query_weight.shape[0]

    output_matrix = lax.all_gather(output_weight, "dev", axis=0, tiled=True)

    extra = [query_weight, key_projection_matrix, value_projection_matrix, router_weight]
    pad = (-(QKV + EXPERTS)) % 128
    packed = jnp.concatenate(extra + [jnp.zeros((weight_rows, pad), BF16)], axis=1)
    q_width, k_width = QUERY_HEADS * HEAD_DIM, KEY_HEADS * HEAD_DIM
    inputs = tokens.astype(F32)
    half_dim = HEAD_DIM // 2
    frequency = jnp.power(10000.0, -(jnp.arange(half_dim, dtype=F32) * 2.0) / HEAD_DIM)
    angle = positions.astype(F32)[None, :] * frequency[:, None]
    cos_t, sin_t = jnp.cos(angle), jnp.sin(angle)
    lo = (jnp.arange(rows, dtype=jnp.int32) - positions)[None, :]
    one_hot = expert_picks[:, :, None] == jnp.arange(EXPERTS, dtype=jnp.int32)
    picked_any = jnp.any(one_hot, axis=1)
    turn = jnp.sum(jnp.where(one_hot, priority[:, :, None], 0), axis=1).astype(F32)
    turn = jnp.where(picked_any, turn, UNPICKED)

    if meshed():
        query_t, attended_t, lse, window, plane_slots, expert_up, matrices, normed_one, gains, scale_one = front(
            lo, cos_t, sin_t, tokens, extra[:3], router_weight, cotangent, turn, first_gain[None, :], second_gain[None, :]
        )
        gain_first, gain_second = gains[0], gains[1]
    else:
        matrices, gain_first, gain_second = (
            lax.all_gather(v, "dev", axis=0, tiled=True) for v in (packed, first_gain, second_gain)
        )
        gain_first, gain_second = gain_first.astype(F32), gain_second.astype(F32)
        rank = jnp.sum((turn.T[:, None, :] < turn.T[:, :, None]).astype(jnp.int32), axis=2)
        slot_rows = jnp.where(picked_any.T & (rank < capacity), rank, -1).astype(F32)
        scale_one = rms_scale(inputs)
        normed_one = (inputs * scale_one * gain_first).astype(BF16)
        qkv_t = dims(matrices[:, :QKV], normed_one, 0, 1)
        query_t = rotate_t(qkv_t[:q_width], cos_t, sin_t).astype(BF16) * BF16(HEAD_DIM**-0.5)
        key = rotate_t(qkv_t[q_width : q_width + k_width], cos_t, sin_t).astype(BF16).T
        value = qkv_t[q_width + k_width :].astype(BF16).T
        window, offset = window_of(jnp.stack([key, value])), jnp.int32(0)
        attended_t, lse = attend(query_t, window, offset, lo)
    qkv_matrix = matrices[:, :QKV]
    router_matrix = matrices[:, QKV : QKV + EXPERTS]
    residual = inputs + dims(attended_t, output_matrix, 0, 0)
    scale_two = rms_scale(residual)
    normed_two = (residual * scale_two * gain_second).astype(BF16)

    logits = dims(normed_two, router_matrix, 1, 0)
    logits = jnp.where(picked_any, logits, MASKED)
    picked_exp = jnp.exp(logits - jnp.max(logits, axis=1, keepdims=True))
    gates = picked_exp / jnp.sum(picked_exp, axis=1, keepdims=True)

    if meshed():
        gate_rows = jnp.pad(gates.T.reshape(EXPERTS, rows // 128, 128), ((0, 0), (0, 8 - rows // 128), (0, 0)))
        expert_in, grad_rows, out_rows, gated_hidden, gate_in_grad, up_in_grad, gate_grad_rows = run_experts(
            normed_two, gate_rows, plane_slots, expert_up, gate_weight, up_weight, down_weight
        )
        returned_grad, gate_grad, gate_gradient, up_gradient, down_gradient = run_grads(
            grad_rows, plane_slots, gate_grad_rows, expert_in, expert_up, gated_hidden, gate_in_grad, up_in_grad
        )
        gate_grad = gate_grad[:, : rows // 128].reshape(EXPERTS, rows).T
    else:
        gate_rows, slot = (
            lax.all_to_all(jnp.repeat(v, split, axis=0), "dev", split_axis=0, concat_axis=0, tiled=True)
            for v in (gates.T, slot_rows)
        )
        pair_slot = jnp.where(
            slot.reshape(devices // 2, 2, rows) >= 0,
            slot.reshape(devices // 2, 2, rows) + jnp.array([[0], [capacity]], F32),
            -1.0,
        ).astype(jnp.int32).reshape(devices // 2, 1, 2 * rows)
        all_upstream = lax.all_gather(cotangent, "dev", axis=0, tiled=True)
        all_normed = lax.all_gather(normed_two, "dev", axis=0, tiled=True)
        expert_in, expert_up = dispatch(pair_slot, all_normed, all_upstream, 2 * capacity)
        slot_hit = slot[:, None, :] == jnp.arange(capacity, dtype=F32)[None, :, None]
        gate_of_slot = jnp.sum(jnp.where(slot_hit, gate_rows[:, None, :], 0.0), axis=2).reshape(-1, 1)
        gate_in = dims(expert_in, gate_weight, 1, 0)
        up_in = dims(expert_in, up_weight, 1, 0)
        sigmoid_gate = 1.0 / (1.0 + jnp.exp(-gate_in))
        silu_gate = gate_in * sigmoid_gate
        hidden = (silu_gate * up_in).astype(BF16)
        gated_hidden = (hidden.astype(F32) * gate_of_slot).astype(BF16)
        hidden_up = dims(expert_up, down_weight, 1, 1)
        hidden_grad = hidden_up * gate_of_slot
        gate_grad_slot = jnp.sum(hidden.astype(F32) * hidden_up, axis=1).reshape(devices, capacity)
        gate_in_grad = (hidden_grad * up_in * sigmoid_gate * (1.0 + gate_in * (1.0 - sigmoid_gate))).astype(BF16)
        up_in_grad = (hidden_grad * silu_gate).astype(BF16)
        partial_in = (dims(gate_in_grad, gate_weight, 1, 1) + dims(up_in_grad, up_weight, 1, 1)).astype(BF16)
        gate_grad_rows = jnp.sum(jnp.where(slot_hit, gate_grad_slot[:, :, None], 0.0), axis=1)
        returned_grad = lax.psum_scatter(
            combine(pair_slot, partial_in, 2 * capacity), "dev", scatter_dimension=0, tiled=True
        ).astype(F32)
        gate_grad = lax.all_to_all(gate_grad_rows, "dev", split_axis=0, concat_axis=0, tiled=True)
        gate_grad = jnp.sum(gate_grad.reshape(EXPERTS, split, rows), axis=1).T
        partial_out = dims(gated_hidden, down_weight, 1, 0).astype(BF16)
        dense_out = combine(pair_slot, partial_out, 2 * capacity)
        mixture = lax.psum_scatter(dense_out, "dev", scatter_dimension=0, tiled=True).astype(F32)
        down_gradient = dims(gated_hidden, expert_up, 0, 0)
        gate_gradient = dims(expert_in, gate_in_grad, 0, 0)
        up_gradient = dims(expert_in, up_in_grad, 0, 0)

    upstream = cotangent.astype(F32)
    logit_grad = (gates * (gate_grad - jnp.sum(gates * gate_grad, axis=1, keepdims=True))).astype(BF16)
    router_gradient = dims(normed_two, logit_grad, 0, 0)
    normed_two_grad = returned_grad + dims(logit_grad, router_matrix, 1, 1)
    weighted_two = normed_two_grad * gain_second
    second_gain_grad = jnp.sum(normed_two_grad * residual * scale_two, axis=0)
    residual_grad = (
        upstream
        + scale_two * weighted_two
        - residual * scale_two**3 * jnp.mean(weighted_two * residual, axis=-1, keepdims=True)
    )
    branch_grad = residual_grad.astype(BF16)
    output_gradient = dims(attended_t, branch_grad, 1, 0).astype(BF16)
    output_gradient = lax.psum_scatter(output_gradient, "dev", scatter_dimension=0, tiled=True).astype(F32)

    if meshed():
        qkv_grad, layer_output = attend_back_mesh(
            query_t, window, lo, branch_grad, output_matrix, lse, attended_t, cos_t, sin_t, out_rows, plane_slots, residual
        )
    else:
        grad_t = dims(output_matrix, branch_grad, 1, 1).astype(BF16)
        query_grad_t, window_grad = attend_back(query_t, window, offset, lo, grad_t, lse, attended_t, cos_t, sin_t)
        key_grad, value_grad = unwindow(window_grad)
        key_grad_t = rotate_t(key_grad.T, cos_t, -sin_t).astype(BF16)
        qkv_grad_t = jnp.concatenate([query_grad_t, key_grad_t, value_grad.T.astype(BF16)], axis=0)
        layer_output = (residual + mixture).astype(BF16)
    more = jnp.concatenate(
        [router_gradient, second_gain_grad[:, None], jnp.zeros((model, (-(EXPERTS + 1)) % 256), F32)], axis=1
    ).astype(BF16)
    if meshed():
        query_sums, key_sums, value_sums, more_sums, tokens_gradient, first_sums = finish(
            normed_one, qkv_grad, matrices, more, gain_first[None, :], scale_one, tokens, residual_grad
        )
        first_sums = first_sums[0, :weight_rows]
        (
            gate_gradient, up_gradient, down_gradient, layer_output, tokens_gradient, query_sums, key_sums, value_sums
        ) = hand_over(
            gate_gradient, up_gradient, down_gradient, layer_output, tokens_gradient, query_sums, key_sums, value_sums
        )
    else:
        qkv_gradient = dims(normed_one, qkv_grad_t, 0, 1).astype(BF16)
        normed_one_grad = dims(qkv_grad_t, qkv_matrix, 0, 1)
        weighted_one = normed_one_grad * gain_first
        tokens_gradient = (
            residual_grad
            + scale_one * weighted_one
            - inputs * scale_one**3 * jnp.mean(weighted_one * inputs, axis=-1, keepdims=True)
        )
        sums = lax.psum_scatter(
            jnp.concatenate([qkv_gradient, more], axis=1), "dev", scatter_dimension=0, tiled=True
        ).astype(F32)
        query_sums, key_sums, value_sums, more_sums = jnp.split(sums, [q_width, q_width + k_width, QKV], axis=1)
        first_sums = lax.psum_scatter(
            jnp.sum(normed_one_grad * inputs * scale_one, axis=0), "dev", scatter_dimension=0, tiled=True
        )
    return (
        layer_output,
        tokens_gradient,
        first_sums,
        query_sums,
        key_sums,
        value_sums,
        output_gradient,
        more_sums[:, EXPERTS],
        more_sums[:, :EXPERTS],
        gate_gradient,
        up_gradient,
        down_gradient,
    )


def solution(mesh):
    rows, whole = P("dev", None), P("dev")
    columns = P(None, "dev")
    return jax.shard_map(
        on_device,
        mesh=mesh,
        in_specs=(rows, whole, rows, rows, whole, rows, rows, rows, rows, whole, rows, columns, columns, rows, rows),
        out_specs=(rows, rows, whole, rows, rows, rows, rows, whole, rows, columns, columns, rows),
        check_vma=False,
    )
```

```python
import functools
import jax, jax.numpy as jnp
from jax import lax
from jax.experimental import pallas as pl
from jax.experimental.pallas import tpu as pltpu

MESH = pl.DeviceIdType.MESH


def place():
    me = lax.axis_index("dev")
    return lax.rem(me // 8, 4), lax.rem(me // 4, 2), lax.rem(me // 2, 2), lax.rem(me, 2)


def number(z, y, x, c):
    return ((z * 2 + y) * 2 + x) * 2 + c


def greet(partners):
    barrier = pltpu.get_barrier_semaphore()
    for partner in partners:
        pl.semaphore_signal(barrier, inc=1, device_id=(partner,), device_id_type=MESH)
    pl.semaphore_wait(barrier, len(partners))


def partners_of(z, y, x, c):
    return [
        number(z, y, x, 1 - c),
        number(z, y, 1 - x, c),
        number(z, 1 - y, x, c),
        number(lax.rem(z + 1, 4), y, x, c),
        number(lax.rem(z + 2, 4), y, x, c),
        number(lax.rem(z + 3, 4), y, x, c),
    ]


class Whole:
    scratch = [pltpu.SemaphoreType.DMA] + [
        pltpu.SemaphoreType.DMA(shape)
        for shape in ((2, 2, 4), (2, 4), (2, 3, 4), (2, 3, 4), (2, 4, 4), (2, 4, 4))
    ]

    def __init__(self, x_ref, o_ref, scratch):
        self.x_ref, self.o_ref = x_ref, o_ref
        self.local_sem, self.zs, self.zr, self.fs, self.fr, self.cs, self.cr = scratch
        self.z, self.y, self.x, self.c = z, y, x, c = place()
        self.rows, cols = x_ref.shape
        half = (cols // 256) * 128
        self.pieces = (pl.ds(0, half), pl.ds(half, cols - half))
        self.sibling = number(z, y, x, 1 - c)
        self.me = number(z, y, x, c)
        self.around = (number(z, 1 - y, x, c), number(z, y, 1 - x, c))
        self.far = ((1, 0), (0, 1))
        self.local = pltpu.make_async_copy(x_ref, self.there(self.me), self.local_sem)

    def turn(self, i):
        middle = i if i < 2 else 5 - i
        return jnp.where(self.z == 0, (4 - i) % 4, jnp.where(self.z == 3, i, middle))

    def there(self, block, p=None):
        at = pl.ds(pl.multiple_of(block * self.rows, 16), self.rows)
        return self.o_ref.at[at, :] if p is None else self.o_ref.at[at, self.pieces[p]]

    def copy(self, source, block, p, send_sem, recv_sem, target):
        return pltpu.make_async_remote_copy(
            src_ref=source, dst_ref=self.there(block, p), send_sem=send_sem, recv_sem=recv_sem,
            device_id=(target,), device_id_type=MESH)

    def block(self, k, fy=0, fx=0):
        return number(lax.rem(self.z + 4 - k, 4), (1 - self.y) if fy else self.y, (1 - self.x) if fx else self.x, self.c)

    def along(self, i, use):
        k = self.turn(i)
        zz = lax.rem(self.z + 4 - k, 4)
        for up, step in ((1, 1), (0, 3)):
            go = (zz <= self.z) & (self.z < 3) if up else (zz >= self.z) & (self.z > 0)

            @pl.when(go)
            def _(up=up, step=step):
                block = self.block(k)
                target = number(lax.rem(self.z + step, 4), self.y, self.x, self.c)
                for p in range(2):
                    source = self.x_ref.at[:, self.pieces[p]] if i == 0 else self.there(block, p)
                    use(self.copy(
                        source, block, p, self.zs.at[p, up, k], self.zr.at[p, lax.rem(k + step, 4)], target))

    def hop(self, p, n, k):
        block = self.block(k, *self.far[p]) if n == 2 else self.block(k)
        target = self.around[p] if n == 0 else self.around[1 - p]
        return self.copy(self.there(block, p), block, p, self.fs.at[p, n, k], self.fr.at[p, n, k], target)

    def across(self, p, n, k):
        fy, fx = ((0, 0), self.far[p], (1 - self.far[p][0], 1 - self.far[p][1]), (1, 1))[n]
        block = self.block(k, fy, fx)
        return self.copy(self.there(block, p), block, p, self.cs.at[p, n, k], self.cr.at[p, n, k], self.sibling)

    def start(self):
        self.local.start()
        self.along(0, lambda cp: cp.start())

    def one(self, i):
        k = self.turn(i)
        if i == 0:
            self.local.wait()
        else:
            block = self.block(k)
            for p in range(2):
                self.copy(self.there(block, p), block, p, self.zs.at[p, 0, 0], self.zr.at[p, k], self.sibling).wait_recv()
            self.along(i, lambda cp: cp.start())
        for p in range(2):
            self.hop(p, 0, k).start()
            self.hop(p, 1, k).start()
            self.across(p, 0, k).start()

    def two(self, i):
        k = self.turn(i)
        for p in range(2):
            self.hop(p, 0, k).wait_recv()
            self.hop(p, 2, k).start()
            self.across(p, 1, k).start()

    def three(self, i):
        k = self.turn(i)
        for n in (1, 2):
            for p in range(2):
                self.hop(p, n, k).wait_recv()
                self.across(p, n + 1, k).start()

    def end(self):
        for k in range(4):
            for p in range(2):
                for n in range(4):
                    self.across(p, n, k).wait_recv()

    def sent(self):
        for i in range(4):
            self.along(i, lambda cp: cp.wait_send())
        for k in range(4):
            for p in range(2):
                for n in range(3):
                    self.hop(p, n, k).wait_send()
                for n in range(4):
                    self.across(p, n, k).wait_send()


from jax.sharding import PartitionSpec as P

QUERY_HEADS = 24
KEY_HEADS = 8
HEAD_DIM = 64
GROUP = QUERY_HEADS // KEY_HEADS
TOP = 8
EXPERTS = 32
MAXDOC = 2000
EPSILON = 1e-06
UNPICKED = 1e9
CAPACITY = 72
MASKED = -1e30
QKV = (QUERY_HEADS + 2 * KEY_HEADS) * HEAD_DIM
F32 = jnp.float32
BF16 = jnp.bfloat16


def meshed():
    return lax.axis_size("dev") == 32


def dims(a, b, ca, cb):
    return lax.dot_general(a, b, (((ca,), (cb,)), ((), ())), preferred_element_type=F32)


class Window:
    scratch = [pltpu.SemaphoreType.DMA((2,)), pltpu.SemaphoreType.DMA((9,)), pltpu.SemaphoreType.DMA((9,))]

    def __init__(self, rows, kv_ref, out, scratch):
        self.rows, self.kv_ref, self.out = rows, kv_ref, out
        self.lsem, self.ss, self.rs = scratch
        self.z, self.y, self.x, self.c = place()
        self.p = self.y * 2 + self.x
        self.sibling = number(self.z, self.y, self.x, 1 - self.c)
        self.near = [(self.z * 4 + lax.rem(self.p + d, 4)) * 2 + self.c for d in (1, 2, 3)]
        self.own_in = pltpu.make_async_copy(kv_ref, self.slot(4, self.c), self.lsem.at[0])
        self.stand_in = pltpu.make_async_copy(kv_ref, self.slot(0, self.c), self.lsem.at[1])
        self.to_up = self.copy(kv_ref, 0, 0, number(lax.rem(self.z + 1, 4), self.y, self.x, self.c))

    def slot(self, s, core):
        return self.out.at[:, pl.ds(pl.multiple_of((2 * s + core) * self.rows, 16), self.rows), :]

    def copy(self, source, s, n, target):
        return pltpu.make_async_remote_copy(
            src_ref=source, dst_ref=self.slot(s, self.c), send_sem=self.ss.at[n], recv_sem=self.rs.at[n],
            device_id=(target,), device_id_type=MESH)

    def own_near(self, d):
        return self.copy(self.kv_ref, 4 - d, d, self.near[d - 1])

    def across(self, s):
        source = self.kv_ref if s == 4 else self.slot(s, self.c)
        return self.copy(source, s, {4: 4, 0: 5}.get(s, 9 - s), self.sibling)

    def start(self):
        self.own_in.start()

        @pl.when(self.z < 3)
        def _():
            self.to_up.start()

        @pl.when(self.z == 0)
        def _():
            self.stand_in.start()

        for d in (1, 3, 2):
            @pl.when(self.p + d < 4)
            def _(d=d):
                self.own_near(d).start()
        self.across(4).start()

    def previous(self):
        @pl.when(self.z == 0)
        def _():
            self.stand_in.wait()

        @pl.when(self.z > 0)
        def _():
            self.to_up.wait_recv()

        for d in (3, 1, 2):
            @pl.when(self.p + d >= 4)
            def _(d=d):
                self.copy(self.slot(0, self.c), 4 - d, d, self.near[d - 1]).start()
        self.across(0).start()

    def pass_on(self):
        for d in (1, 3, 2):
            self.own_near(d).wait_recv()
            self.across(4 - d).start()

    def end(self):
        for s in range(5):
            pltpu.make_async_remote_copy(
                src_ref=self.kv_ref, dst_ref=self.slot(s, 1 - self.c), send_sem=self.ss.at[0],
                recv_sem=self.rs.at[{4: 4, 0: 5}.get(s, 9 - s)], device_id=(self.sibling,), device_id_type=MESH).wait_recv()
        self.own_in.wait()

    def sent(self):
        @pl.when(self.z < 3)
        def _():
            self.to_up.wait_send()

        for d in (1, 2, 3):
            self.own_near(d).wait_send()
        for s in range(5):
            self.across(s).wait_send()


def window_of(kv):
    rows = kv.shape[1]
    devices = lax.axis_size("dev")
    back = (MAXDOC + rows - 2) // rows
    parts = [
        lax.ppermute(kv, "dev", [(i - d, i) for i in range(d, devices)]) for d in range(back, 0, -1)
    ]
    return jnp.concatenate(parts + [kv, jnp.zeros_like(kv)], axis=1)


class Unwindow:
    @staticmethod
    def scratch(rows, width):
        return [
            pltpu.VMEM((5, 2, rows, width), BF16),
            pltpu.VMEM((3, 2, rows, width), BF16),
            pltpu.VMEM((2, rows, width), BF16),
            pltpu.SemaphoreType.DMA((9,)), pltpu.SemaphoreType.DMA((9,)),
        ]

    n_scratch = 5
    order = (3, 1, 2, 0, 4)

    def __init__(self, rows, grads, o_ref, scratch):
        self.rows, self.grads, self.o_ref = rows, grads, o_ref
        self.got, self.near_got, self.far, self.ss, self.rs = scratch
        self.z, self.y, self.x, self.c = place()
        self.p = self.y * 2 + self.x
        self.sibling = number(self.z, self.y, self.x, 1 - self.c)
        self.to_down = pltpu.make_async_remote_copy(
            src_ref=self.got.at[0], dst_ref=self.far, send_sem=self.ss.at[8], recv_sem=self.rs.at[8],
            device_id=(number(lax.rem(self.z + 3, 4), self.y, self.x, self.c),), device_id_type=MESH)

    def to_sibling(self, s):
        at = pl.ds(pl.multiple_of((2 * s + 1 - self.c) * self.rows, 16), self.rows)
        return pltpu.make_async_remote_copy(
            src_ref=self.grads.at[:, at, :], dst_ref=self.got.at[s], send_sem=self.ss.at[s], recv_sem=self.rs.at[s],
            device_id=(self.sibling,), device_id_type=MESH)

    def to_owner(self, d):
        owner = (self.z * 4 + lax.rem(self.p + 4 - d, 4)) * 2 + self.c
        return pltpu.make_async_remote_copy(
            src_ref=self.got.at[4 - d], dst_ref=self.near_got.at[d - 1], send_sem=self.ss.at[4 + d], recv_sem=self.rs.at[4 + d],
            device_id=(owner,), device_id_type=MESH)

    def rowwise(self, body):
        for h in range(2):
            def step(i, _, h=h):
                body(h, pl.multiple_of(i * 32, 32))
                return 0
            lax.fori_loop(0, self.rows // 32, step, 0)

    def start(self):
        for s in self.order:
            self.to_sibling(s).start()

    def sums(self):
        for s in self.order:
            self.to_sibling(s).wait_recv()
            first = (2 * s + self.c) * self.rows

            def both(h, r, s=s, first=first):
                at = pl.ds(r, 32)
                mine = self.grads[h, pl.ds(pl.multiple_of(first + r, 32), 32), :]
                total = self.got[s, h, at, :].astype(F32) + mine.astype(F32)
                if s == 4:
                    self.o_ref[h, at, :] = total
                else:
                    self.got[s, h, at, :] = total.astype(BF16)
            self.rowwise(both)
            if 0 < s < 4:
                self.to_owner(4 - s).start()

    def near(self):
        for d in (1, 3, 2):
            self.to_owner(d).wait_recv()

            @pl.when(self.p + d < 4)
            def _(d=d):
                def body(h, r):
                    at = pl.ds(r, 32)
                    self.o_ref[h, at, :] += self.near_got[d - 1, h, at, :].astype(F32)
                self.rowwise(body)

            @pl.when(self.p + d >= 4)
            def _(d=d):
                def body(h, r):
                    at = pl.ds(r, 32)
                    total = self.got[0, h, at, :].astype(F32) + self.near_got[d - 1, h, at, :].astype(F32)
                    self.got[0, h, at, :] = total.astype(BF16)
                self.rowwise(body)

        @pl.when(self.z > 0)
        def _():
            self.to_down.start()

    def end(self):
        @pl.when(self.z < 3)
        def _():
            self.to_down.wait_recv()

            def body(h, r):
                at = pl.ds(r, 32)
                self.o_ref[h, at, :] += self.far[h, at, :].astype(F32)
            self.rowwise(body)

        @pl.when(self.z > 0)
        def _():
            self.to_down.wait_send()

        for s in range(5):
            self.to_sibling(s).wait_send()
        for d in (1, 2, 3):
            self.to_owner(d).wait_send()


def unwindow(grads):
    rows = grads.shape[1] // 10
    devices = lax.axis_size("dev")
    back = (MAXDOC + rows - 2) // rows
    total = grads[:, back * rows : (back + 1) * rows].astype(F32)
    for d in range(1, back + 1):
        piece = grads[:, (back - d) * rows : (back - d + 1) * rows]
        moved = lax.ppermute(piece, "dev", [(i, i - d) for i in range(d, devices)])
        total = total + moved.astype(F32)
    return total


def make_bias(bias, lo_ref, chunks, rows):
    def fill(ch, _):
        at = pl.ds(pl.multiple_of(ch * rows, rows), rows)
        relative = lax.broadcasted_iota(jnp.int32, (rows, rows), 0) + (ch - (chunks - 1)) * rows
        query = lax.broadcasted_iota(jnp.int32, (rows, rows), 1)
        allowed = (relative <= query) & (relative >= lo_ref[...])
        bias[at, :] = jnp.where(allowed, 0.0, MASKED)
        return 0
    lax.fori_loop(0, chunks, fill, 0)


def side_by_side(ref, half):
    first = half * GROUP
    return jnp.concatenate(
        [ref[(first + g) * HEAD_DIM : (first + g + 1) * HEAD_DIM, :] for g in range(GROUP)], axis=1
    )


def stats_of(ref, half):
    return jnp.concatenate([ref[0, half * GROUP + g : half * GROUP + g + 1, :] for g in range(GROUP)], axis=1)


def attend_pair(chunks, rows, off, q_ref, kv_ref, o_ref, lse_ref, bias, between):
    lse_ref[...] = jnp.zeros_like(lse_ref)
    width = GROUP * rows
    for half in range(2):
        lanes = slice(half * HEAD_DIM, (half + 1) * HEAD_DIM)
        queries = side_by_side(q_ref, half)

        def chunk(i, carry, lanes=lanes, queries=queries):
            ch = chunks - 1 - i
            at = pl.ds(pl.multiple_of((ch + off) * rows, rows), rows)
            key, value = kv_ref[0, at, lanes], kv_ref[1, at, lanes]
            shift = bias[pl.ds(pl.multiple_of(ch * rows, rows), rows), :]
            top, total, mixed = carry
            score = dims(key, queries, 1, 0) + jnp.concatenate([shift] * GROUP, axis=1)
            new_top = jnp.maximum(top, jnp.max(score, axis=0, keepdims=True))
            weight = jnp.exp(score - new_top)
            fade = jnp.exp(top - new_top)
            total = total * fade + jnp.sum(weight, axis=0, keepdims=True)
            mixed = mixed * fade + dims(value, weight.astype(BF16), 0, 0)
            return new_top, total, mixed

        start = (jnp.full((1, width), MASKED, F32), jnp.zeros((1, width), F32), jnp.zeros((HEAD_DIM, width), F32))
        top, total, mixed = lax.fori_loop(0, chunks, chunk, start, unroll=3)
        mixed = (mixed / total).astype(BF16)
        lse = top + jnp.log(total)
        for g in range(GROUP):
            n = half * GROUP + g
            o_ref[n * HEAD_DIM : (n + 1) * HEAD_DIM, :] = mixed[:, g * rows : (g + 1) * rows]
            lse_ref[0, n : n + 1, :] = lse[:, g * rows : (g + 1) * rows]
        between(half)


def attend_kernel(chunks, rows, off_ref, lo_ref, q_ref, kv_ref, o_ref, lse_ref, bias):
    @pl.when(pl.program_id(0) == 0)
    def _():
        make_bias(bias, lo_ref, chunks, rows)

    attend_pair(chunks, rows, off_ref[0], q_ref, kv_ref, o_ref, lse_ref, bias, lambda half: None)


def attend_back_pair(
    chunks, rows, off, cos_ref, sin_ref, q_ref, kv_ref, g_ref, lse_ref, out_ref, dq_ref, dkv_ref, bias, between
):
    unused = pl.ds(pl.multiple_of((1 - off) * chunks * rows, rows), rows)
    dkv_ref[:, unused, :] = jnp.zeros((2, rows, 2 * HEAD_DIM), BF16)
    for half in range(2):
        lanes = slice(half * HEAD_DIM, (half + 1) * HEAD_DIM)
        queries, grads = side_by_side(q_ref, half), side_by_side(g_ref, half)
        lse = stats_of(lse_ref, half)
        mixed = side_by_side(out_ref, half).astype(F32)
        delta = jnp.sum(mixed * grads.astype(F32), axis=0, keepdims=True)

        def chunk(ch, query_grad, lanes=lanes, queries=queries, grads=grads, lse=lse, delta=delta):
            at = pl.ds(pl.multiple_of((ch + off) * rows, rows), rows)
            key, value = kv_ref[0, at, lanes], kv_ref[1, at, lanes]
            shift = bias[pl.ds(pl.multiple_of(ch * rows, rows), rows), :]
            score = dims(key, queries, 1, 0) + jnp.concatenate([shift] * GROUP, axis=1)
            weight = jnp.exp(score - lse)
            score_grad = (weight * (dims(value, grads, 1, 0) - delta)).astype(BF16)
            dkv_ref[0, at, lanes] = dims(score_grad, queries, 1, 1).astype(BF16)
            dkv_ref[1, at, lanes] = dims(weight.astype(BF16), grads, 1, 1).astype(BF16)
            return query_grad + dims(key, score_grad, 0, 0)

        done = lax.fori_loop(0, chunks, chunk, jnp.zeros((HEAD_DIM, GROUP * rows), F32), unroll=3)
        done = done * (HEAD_DIM**-0.5)
        cosine, sine = cos_ref[...], sin_ref[...]
        for g in range(GROUP):
            grad = done[:, g * rows : (g + 1) * rows]
            u, w = grad[: HEAD_DIM // 2], grad[HEAD_DIM // 2 :]
            n = (half * GROUP + g) * HEAD_DIM
            dq_ref[n : n + HEAD_DIM // 2, :] = (u * cosine + w * sine).astype(BF16)
            dq_ref[n + HEAD_DIM // 2 : n + HEAD_DIM, :] = (w * cosine - u * sine).astype(BF16)
        between(half)


def attend_back_kernel(
    chunks, rows, off_ref, lo_ref, cos_ref, sin_ref, q_ref, kv_ref, g_ref, lse_ref, out_ref, dq_ref, dkv_ref, bias
):
    @pl.when(pl.program_id(0) == 0)
    def _():
        make_bias(bias, lo_ref, chunks, rows)

    attend_back_pair(
        chunks, rows, off_ref[0], cos_ref, sin_ref, q_ref, kv_ref, g_ref, lse_ref, out_ref, dq_ref, dkv_ref, bias,
        lambda half: None,
    )


def attention_specs(rows, span):
    width = 2 * GROUP * HEAD_DIM
    return dict(
        smem=pl.BlockSpec(memory_space=pltpu.SMEM),
        row=pl.BlockSpec((1, rows), lambda j: (0, 0)),
        table=pl.BlockSpec((HEAD_DIM // 2, rows), lambda j: (0, 0)),
        query=pl.BlockSpec((width, rows), lambda j: (j, 0)),
        kv=pl.BlockSpec((2, span, 2 * HEAD_DIM), lambda j: (0, 0, j)),
        stat=pl.BlockSpec((1, 8, rows), lambda j: (j, 0, 0)),
    )


def attend(query_t, window, offset, lo):
    rows, span = query_t.shape[1], window.shape[1]
    chunks = span // rows - 1
    s = attention_specs(rows, span)
    return pl.pallas_call(
        functools.partial(attend_kernel, chunks, rows),
        grid=(KEY_HEADS // 2,),
        in_specs=[s["smem"], s["row"], s["query"], s["kv"]],
        out_specs=[s["query"], s["stat"]],
        out_shape=[
            jax.ShapeDtypeStruct(query_t.shape, BF16),
            jax.ShapeDtypeStruct((KEY_HEADS // 2, 8, rows), F32),
        ],
        scratch_shapes=[pltpu.VMEM((chunks * rows, rows), F32)],
        compiler_params=pltpu.CompilerParams(vmem_limit_bytes=40 * 2**20),
        cost_estimate=pl.CostEstimate(flops=7 * 10**9, bytes_accessed=8 * 10**6, transcendentals=15 * 10**6),
        name="attend",
    )(offset.reshape(1), lo, query_t, window)


def attend_back(query_t, window, offset, lo, grad_t, lse, attended_t, cos_t, sin_t):
    rows, span = query_t.shape[1], window.shape[1]
    chunks = span // rows - 1
    s = attention_specs(rows, span)
    return pl.pallas_call(
        functools.partial(attend_back_kernel, chunks, rows),
        grid=(KEY_HEADS // 2,),
        in_specs=[s["smem"], s["row"], s["table"], s["table"], s["query"], s["kv"], s["query"], s["stat"], s["query"]],
        out_specs=[s["query"], s["kv"]],
        out_shape=[
            jax.ShapeDtypeStruct(query_t.shape, BF16),
            jax.ShapeDtypeStruct(window.shape, BF16),
        ],
        scratch_shapes=[pltpu.VMEM((chunks * rows, rows), F32)],
        compiler_params=pltpu.CompilerParams(vmem_limit_bytes=40 * 2**20),
        cost_estimate=pl.CostEstimate(flops=18 * 10**9, bytes_accessed=16 * 10**6, transcendentals=15 * 10**6),
        name="attend_back",
    )(offset.reshape(1), lo, cos_t, sin_t, query_t, window, grad_t, lse, attended_t)


def hits(slot_ref, slots):
    width = slot_ref.shape[-1]
    return slot_ref[0] == lax.broadcasted_iota(jnp.int32, (slots, width), 0)


def dispatch_kernel(slot_ref, x_ref, u_ref, xo_ref, uo_ref):
    chosen = jnp.where(hits(slot_ref, xo_ref.shape[0]), 1.0, 0.0).astype(BF16)
    xo_ref[...] = dims(chosen, x_ref[...], 1, 0).astype(BF16)
    uo_ref[...] = dims(chosen, u_ref[...], 1, 0).astype(BF16)


def dispatch(slot, normed, upstream, slots):
    pairs, _, width = slot.shape
    model = normed.shape[1]
    return pl.pallas_call(
        dispatch_kernel,
        grid=(pairs,),
        in_specs=[
            pl.BlockSpec((1, 1, width), lambda i: (i, 0, 0)),
            pl.BlockSpec((width, model), lambda i: (i, 0)),
            pl.BlockSpec((width, model), lambda i: (i, 0)),
        ],
        out_specs=[pl.BlockSpec((slots, model), lambda i: (i, 0))] * 2,
        out_shape=[jax.ShapeDtypeStruct((pairs * slots, model), BF16)] * 2,
        compiler_params=pltpu.CompilerParams(vmem_limit_bytes=40 * 2**20),
        cost_estimate=pl.CostEstimate(flops=2 * 10**9, bytes_accessed=65 * 10**6, transcendentals=0),
        name="dispatch",
    )(slot, normed, upstream)


def combine_kernel(slot_ref, r_ref, o_ref):
    chosen = jnp.where(hits(slot_ref, r_ref.shape[0]), 1.0, 0.0).astype(BF16)
    o_ref[...] = dims(chosen, r_ref[...], 0, 0).astype(BF16)


def combine(slot, rows, slots):
    pairs, _, width = slot.shape
    model = rows.shape[1]
    return pl.pallas_call(
        combine_kernel,
        grid=(pairs,),
        in_specs=[
            pl.BlockSpec((1, 1, width), lambda i: (i, 0, 0)),
            pl.BlockSpec((slots, model), lambda i: (i, 0)),
        ],
        out_specs=pl.BlockSpec((width, model), lambda i: (i, 0)),
        out_shape=jax.ShapeDtypeStruct((pairs * width, model), BF16),
        compiler_params=pltpu.CompilerParams(vmem_limit_bytes=40 * 2**20),
        cost_estimate=pl.CostEstimate(flops=10**9, bytes_accessed=33 * 10**6, transcendentals=0),
        name="combine",
    )(slot, rows)


SLOTS = 80


def far_first(i):
    return jnp.where(i == 0, 2, jnp.where(i == 3, 0, 2 * i - 1))


def greet_all():
    me = lax.axis_index("dev")
    barrier = pltpu.get_barrier_semaphore()

    def signal(d, _):
        pl.semaphore_signal(barrier, inc=1, device_id=(lax.rem(me + d, 32),), device_id_type=MESH)
        return 0
    lax.fori_loop(1, 32, signal, 0)
    pl.semaphore_wait(barrier, 31)


class Swap:
    def __init__(self, source, into, ss, rs):
        self.me = lax.axis_index("dev")
        self.source, self.into, self.ss, self.rs = source, into, ss, rs

    def copy(self, d):
        target = lax.rem(self.me + d, 32)
        return pltpu.make_async_remote_copy(
            src_ref=self.source(target), dst_ref=self.into.at[self.me], send_sem=self.ss.at[d], recv_sem=self.rs.at[d],
            device_id=(target,), device_id_type=MESH)

    def start(self):
        def one(d, _):
            self.copy(d).start()
            return 0
        lax.fori_loop(1, 32, one, 0)
        self.into[self.me] = self.source(self.me)[...]

    def wait_recv(self):
        def one(d, _):
            self.copy(d).wait_recv()
            return 0
        lax.fori_loop(1, 32, one, 0)

    def wait_send(self):
        def one(d, _):
            self.copy(d).wait_send()
            return 0
        lax.fori_loop(1, 32, one, 0)


def in_plane(y, x, c):
    return (y * 2 + x) * 2 + c


def chosen_rows(slots_ref, block, expert):
    row = slots_ref[block, pl.ds(expert, 1), :]
    return row == lax.broadcasted_iota(jnp.int32, (SLOTS, row.shape[1]), 0).astype(F32)


def greet_near():
    z, y, x, c = place()
    greet(
        [number(z, y, x, 1 - c)]
        + [number(z, 1 - y, x, cc) for cc in (c, 1 - c)]
        + [number(z, y, 1 - x, cc) for cc in (c, 1 - c)]
        + [number(z, 1 - y, 1 - x, c)]
        + [number(lax.rem(z + d, 4), y, x, c) for d in (1, 2, 3)]
    )


class Forth:
    scratch = staticmethod(lambda rows, half: [
        pltpu.VMEM((2, 2, 4, rows, half), BF16),
        pltpu.VMEM((2, 2, 4, 4, SLOTS, half), BF16),
        pltpu.SemaphoreType.DMA((2, 2, 4)), pltpu.SemaphoreType.DMA((2, 4)),
        pltpu.SemaphoreType.DMA((2, 4)), pltpu.SemaphoreType.DMA((2, 4)),
        pltpu.SemaphoreType.DMA((2, 2, 4, 4)), pltpu.SemaphoreType.DMA((2, 2, 4, 3)), pltpu.SemaphoreType.DMA((2,)),
    ])
    n_scratch = 9

    def __init__(self, x_ref, slots_ref, xi, scratch):
        self.x_ref, self.slots_ref, self.xi = x_ref, slots_ref, xi
        self.land, self.stage, self.zs, self.zr, self.fs, self.fr, self.cs, self.cr, self.own_sem = scratch
        self.z, self.y, self.x, self.c = place()
        half = x_ref.shape[1] // 2
        self.cols = [pl.ds(0, half), pl.ds(half, half)]

    def turn(self, i):
        middle = jnp.where(i < 2, i, 5 - i)
        return jnp.where(self.z == 0, lax.rem(4 - i, 4), jnp.where(self.z == 3, i, middle))

    def to_z(self, p, up, k, own=False):
        step = 1 if up else 3
        source = self.x_ref.at[:, self.cols[p]] if own else self.land.at[p, 0, k]
        there = lax.rem(k + step, 4)
        return pltpu.make_async_remote_copy(
            src_ref=source, dst_ref=self.land.at[p, 0, there],
            send_sem=self.zs.at[p, int(up), k], recv_sem=self.zr.at[p, there],
            device_id=(number(lax.rem(self.z + step, 4), self.y, self.x, self.c),), device_id_type=MESH)

    def hop(self, p, k):
        z, y, x, c = self.z, self.y, self.x, self.c
        beside = number(z, 1 - y, x, c) if p == 0 else number(z, y, 1 - x, c)
        return pltpu.make_async_remote_copy(
            src_ref=self.land.at[p, 0, k], dst_ref=self.land.at[p, 1, k],
            send_sem=self.fs.at[p, k], recv_sem=self.fr.at[p, k], device_id=(beside,), device_id_type=MESH)

    def block(self, p, h, k):
        zz = lax.rem(self.z + 4 - k, 4)
        if p == 0:
            return number(zz, (1 - self.y) if h else self.y, self.x, self.c)
        return number(zz, self.y, (1 - self.x) if h else self.x, self.c)

    def who(self, p):
        y, x, c = self.y, self.x, self.c
        ay, ax = (y, 1 - x) if p == 0 else (1 - y, x)
        return [(y, x, 1 - c), (ay, ax, c), (ay, ax, 1 - c), (y, x, c)]

    def slots_at(self, p, h, k):
        return self.xi.at[pl.ds(pl.multiple_of(self.block(p, h, k) * SLOTS, 16), SLOTS), self.cols[p]]

    def served(self, p, h, k, t):
        return pltpu.make_async_remote_copy(
            src_ref=self.stage.at[p, h, k, t], dst_ref=self.slots_at(p, h, k),
            send_sem=self.cs.at[p, h, k, t], recv_sem=self.cr.at[p, h, k, t],
            device_id=(number(self.z, *self.who(p)[t]),), device_id_type=MESH)

    def kept(self, p, h, k):
        return pltpu.make_async_copy(self.stage.at[p, h, k, 3], self.slots_at(p, h, k), self.cs.at[p, h, k, 3])

    def serve(self, p, h, k):
        block = self.block(p, h, k)
        source = self.land[p, h, k]
        for t, to in enumerate(self.who(p)):
            chosen = jnp.where(chosen_rows(self.slots_ref, block, in_plane(*to)), 1.0, 0.0).astype(BF16)
            self.stage[p, h, k, t] = dims(chosen, source, 1, 0).astype(BF16)
            if t < 3:
                self.served(p, h, k, t).start()
            else:
                self.kept(p, h, k).start()

    def own(self, p):
        return pltpu.make_async_copy(self.x_ref.at[:, self.cols[p]], self.land.at[p, 0, 0], self.own_sem.at[p])

    def along(self, i, use):
        k = self.turn(i)
        zz = lax.rem(self.z + 4 - k, 4)
        for p in range(2):
            @pl.when((zz < self.z) & (self.z < 3))
            def _(p=p):
                use(self.to_z(p, True, k))

            @pl.when((zz > self.z) & (self.z > 0))
            def _(p=p):
                use(self.to_z(p, False, k))

    def along_own(self, use):
        for p in range(2):
            @pl.when(self.z < 3)
            def _(p=p):
                use(self.to_z(p, True, 0, own=True))

            @pl.when(self.z > 0)
            def _(p=p):
                use(self.to_z(p, False, 0, own=True))

    def start(self):
        for p in range(2):
            self.own(p).start()
        self.along_own(lambda cp: cp.start())

    def come(self, i):
        k = self.turn(i)
        for p in range(2):
            self.to_z(p, True, lax.rem(k + 3, 4)).wait_recv()
        self.along(i, lambda cp: cp.start())

    def one(self, i, come=True):
        k = self.turn(i)

        @pl.when(i == 0)
        def _():
            for p in range(2):
                self.own(p).wait()

        if come:
            @pl.when(i > 0)
            def _():
                self.come(i)

        for p in range(2):
            self.hop(p, k).start()
        for p in range(2):
            self.serve(p, 0, k)

    def two(self, i):
        k = self.turn(i)
        for p in range(2):
            self.hop(p, k).wait_recv()
            self.serve(p, 1, k)

    def arrived(self, group, i):
        k = self.turn(i)

        @pl.when(group == 0)
        def _():
            for p in range(2):
                self.served(p, 0, k, 0).wait_recv()
                self.kept(p, 0, k).wait()

        @pl.when(group == 1)
        def _():
            self.kept(0, 1, k).wait()
            self.served(0, 1, k, 0).wait_recv()
            self.served(1, 0, k, 1).wait_recv()
            self.served(1, 0, k, 2).wait_recv()

        @pl.when(group == 2)
        def _():
            self.kept(1, 1, k).wait()
            self.served(1, 1, k, 0).wait_recv()
            self.served(0, 0, k, 1).wait_recv()
            self.served(0, 0, k, 2).wait_recv()

        @pl.when(group == 3)
        def _():
            for p in range(2):
                self.served(p, 1, k, 1).wait_recv()
                self.served(p, 1, k, 2).wait_recv()

    def chip(self, group, i):
        dy, dx = lax.rem(group, 2), group // 2
        zz = lax.rem(self.z + 4 - self.turn(i), 4)
        yy = jnp.where(dy == 1, 1 - self.y, self.y)
        xx = jnp.where(dx == 1, 1 - self.x, self.x)
        return (zz * 2 + yy) * 2 + xx

    def sent(self):
        self.along_own(lambda cp: cp.wait_send())

        def each(i, _):
            k = self.turn(i)
            self.along(i, lambda cp: cp.wait_send())
            for p in range(2):
                self.hop(p, k).wait_send()
                for h in range(2):
                    for t in range(3):
                        self.served(p, h, k, t).wait_send()
            return 0
        lax.fori_loop(0, 4, each, 0)


BEFORE_UNIT = {0: ("o1", "t0", "o2", "t1"), 4: ("o3", "t2"), 8: ("t3",)}


def experts_kernel(
    x_ref, gates_ref, slots_ref, ui_ref, wg_in, wu_in, wd_in,
    xi_out, dx_out, y_out, hg_out, dg_out, du_out, gg_ref,
    gates, xi, ubuf, dx_buf, y_buf, hg_ref, dg_ref, du_ref, wg_ref, wu_ref, wd_ref, wgt, wut, wdt,
    gs, gr, usem, xsem, osem, wsem, *scratch,
):
    z, y, x, c = place()
    rows = x_ref.shape[0]
    greet_all()
    swap = Swap(lambda t: gates_ref.at[t], gates, gs, gr)
    ag = Forth(x_ref, slots_ref, xi, scratch)
    ag.start()

    def chip_of(u):
        return ag.chip(lax.rem(u, 4), u // 4)

    def at_chip(u):
        return pl.ds(pl.multiple_of(chip_of(u) * 2 * SLOTS, 16), 2 * SLOTS)

    def load_up(u):
        return pltpu.make_async_copy(ui_ref.at[at_chip(u), :], ubuf.at[lax.rem(u, 2)], usem.at[lax.rem(u, 2)])

    load_up(0).start()
    swap.start()
    loads = [
        pltpu.make_async_copy(source, into, wsem.at[i])
        for i, (source, into) in enumerate(((wg_in, wg_ref), (wu_in, wu_ref), (wd_in, wd_ref)))
    ]
    for cp in loads:
        cp.start()
    ag.one(0)
    for cp, source, into in zip(loads, (wg_ref, wu_ref, wd_ref), (wgt, wut, wdt), strict=True):
        cp.wait()
        into[...] = source[...].T
    swap.wait_recv()

    def store(n, buf, out, u):
        return pltpu.make_async_copy(buf.at[lax.rem(u, 2)], out.at[at_chip(u), :], osem.at[n, lax.rem(u, 2)])

    def stores(u):
        return [store(0, dx_buf, dx_out, u), store(1, y_buf, y_out, u)]

    def keep(u):
        return [
            pltpu.make_async_copy(held.at[at_chip(u), :], out.at[at_chip(u), :], xsem.at[i, u])
            for i, (held, out) in enumerate(((xi, xi_out), (hg_ref, hg_out), (dg_ref, dg_out), (du_ref, du_out)))
        ]

    def unit(u):
        slot = lax.rem(u, 2)
        chip = chip_of(u)

        @pl.when(u < 15)
        def _():
            load_up(u + 1).start()

        ag.arrived(lax.rem(u, 4), u // 4)

        @pl.when(u >= 2)
        def _():
            for s in stores(u - 2):
                s.wait()

        load_up(u).wait()
        at = at_chip(u)
        expert = in_plane(y, x, c)
        picks, gate = [], []
        for core in range(2):
            block = chip * 2 + core
            hit = chosen_rows(slots_ref, block, expert)
            picks.append(hit)
            gate_row = jnp.concatenate([gates[block, 0:1, :], gates[block, 1:2, :]], axis=1)
            gate.append(jnp.sum(jnp.where(hit, gate_row, 0.0), axis=1, keepdims=True))
        gate_of_slot = jnp.concatenate(gate, axis=0)
        hidden_up = dims(ubuf[slot], wdt[...], 1, 0)
        rows_in = xi[at, :]
        gate_in = dims(rows_in, wg_ref[...], 1, 0)
        up_in = dims(rows_in, wu_ref[...], 1, 0)
        sig = 1.0 / (1.0 + jnp.exp(-gate_in))
        silu = gate_in * sig
        hidden = (silu * up_in).astype(BF16).astype(F32)
        gated = (hidden * gate_of_slot).astype(BF16)
        hidden_grad = hidden_up * gate_of_slot
        gate_back = (hidden_grad * up_in * sig * (1.0 + gate_in * (1.0 - sig))).astype(BF16)
        up_back = (hidden_grad * silu).astype(BF16)
        hg_ref[at, :] = gated
        dg_ref[at, :] = gate_back
        du_ref[at, :] = up_back
        dx_buf[slot] = (dims(gate_back, wgt[...], 1, 0) + dims(up_back, wut[...], 1, 0)).astype(BF16)
        y_buf[slot] = dims(gated, wd_ref[...], 1, 0).astype(BF16)
        gate_grad = jnp.sum(hidden * hidden_up, axis=1, keepdims=True)
        for core in range(2):
            block = chip * 2 + core
            row = jnp.sum(jnp.where(picks[core], gate_grad[core * SLOTS : (core + 1) * SLOTS], 0.0), axis=0, keepdims=True)
            gg_ref[block, 0:1, :] = row[:, :128]
            gg_ref[block, 1:2, :] = row[:, 128:]
        for s in stores(u):
            s.start()
        for s in keep(u):
            s.start()

    step = {}
    for i in range(4):
        step[f"o{i}"] = functools.partial(ag.one, jnp.int32(i))
        step[f"c{i}"] = functools.partial(ag.come, jnp.int32(i))
        step[f"s{i}"] = functools.partial(ag.one, jnp.int32(i), False)
        step[f"t{i}"] = functools.partial(ag.two, jnp.int32(i))

    def each(u, _):
        for when, names in BEFORE_UNIT.items():
            @pl.when(u == when)
            def _(names=names):
                for name in names:
                    step[name]()

        unit(u)
        return 0

    lax.fori_loop(0, 16, each, 0)
    for u in (14, 15):
        for s in stores(u):
            s.wait()

    def last(u, _):
        for s in keep(u):
            s.wait()
        return 0
    lax.fori_loop(0, 16, last, 0)
    ag.sent()
    swap.wait_send()


def run_experts(normed, gates, slots, ui, gate_weight, up_weight, down_weight):
    rows, model = normed.shape
    ff = gate_weight.shape[1]
    n = 32 * SLOTS
    hbm, vmem = pl.BlockSpec(memory_space=pl.ANY), pl.BlockSpec(memory_space=pltpu.VMEM)
    dma = pltpu.SemaphoreType.DMA
    long = jax.ShapeDtypeStruct((n, model), BF16)
    short = jax.ShapeDtypeStruct((n, ff), BF16)
    return pl.pallas_call(
        experts_kernel,
        in_specs=[hbm, vmem, vmem, hbm, hbm, hbm, hbm],
        out_specs=[hbm] * 6 + [vmem],
        out_shape=[long] * 3 + [short] * 3 + [jax.ShapeDtypeStruct((32, 8, 128), F32)],
        scratch_shapes=[
            pltpu.VMEM((32, 8, 128), F32),
            pltpu.VMEM((n, model), BF16),
            pltpu.VMEM((2, 2 * SLOTS, model), BF16),
            pltpu.VMEM((2, 2 * SLOTS, model), BF16),
            pltpu.VMEM((2, 2 * SLOTS, model), BF16),
            pltpu.VMEM((n, ff), BF16), pltpu.VMEM((n, ff), BF16), pltpu.VMEM((n, ff), BF16),
            pltpu.VMEM((model, ff), BF16), pltpu.VMEM((model, ff), BF16), pltpu.VMEM((ff, model), BF16),
            pltpu.VMEM((ff, model), BF16), pltpu.VMEM((ff, model), BF16), pltpu.VMEM((model, ff), BF16),
            dma((32,)), dma((32,)), dma((2,)), dma((4, 16)), dma((2, 2)), dma((3,)),
        ] + Forth.scratch(rows, model // 2),
        compiler_params=pltpu.CompilerParams(collective_id=13, has_side_effects=True, vmem_limit_bytes=56 * 2**20),
        name="experts",
    )(normed, gates, slots, ui, gate_weight, up_weight, down_weight)


class Back:
    scratch = staticmethod(lambda rows, half: [
        pltpu.VMEM((2, 2, 4, SLOTS, half), BF16),
        pltpu.VMEM((2, 3, 2, 4, SLOTS, half), BF16),
        pltpu.VMEM((2, 4, rows, half), BF16),
        pltpu.VMEM((2, 4, rows, half), BF16),
        pltpu.VMEM((2, 4, rows, half), BF16),
        pltpu.VMEM((2, 4, rows, half), BF16),
        pltpu.SemaphoreType.DMA((2, 2, 4)),
        pltpu.SemaphoreType.DMA((2, 3, 2, 4)), pltpu.SemaphoreType.DMA((2, 3, 2, 4)),
        pltpu.SemaphoreType.DMA((2, 4)), pltpu.SemaphoreType.DMA((2, 4)),
        pltpu.SemaphoreType.DMA((2, 4)), pltpu.SemaphoreType.DMA((2, 4)),
    ])
    n_scratch = 13

    def __init__(self, rows_ref, slots_ref, o_ref, scratch):
        self.rows_ref, self.slots_ref, self.o_ref = rows_ref, slots_ref, o_ref
        (self.own, self.rin, self.sout, self.rb, self.zout, self.rz,
         self.own_sem, self.ts, self.tr, self.bs, self.br, self.zs, self.zr) = scratch
        self.z, self.y, self.x, self.c = place()
        half = rows_ref.shape[1] // 2
        self.cols = [pl.ds(0, half), pl.ds(half, half)]

    def block(self, p, h, k, yy, xx, cc):
        zz = lax.rem(self.z + k, 4)
        if p == 0:
            return number(zz, (1 - yy) if h else yy, xx, cc)
        return number(zz, yy, (1 - xx) if h else xx, cc)

    def sources(self, p):
        y, x, c = self.y, self.x, self.c
        ay, ax = (y, 1 - x) if p == 0 else (1 - y, x)
        return [(y, x, 1 - c), (ay, ax, c), (ay, ax, 1 - c)]

    def slot_rows(self, block, p):
        return self.rows_ref.at[pl.ds(pl.multiple_of(block * SLOTS, 16), SLOTS), self.cols[p]]

    def to(self, p, t, h, k):
        place_of = self.sources(p)[t]
        return pltpu.make_async_remote_copy(
            src_ref=self.slot_rows(self.block(p, h, k, *place_of), p), dst_ref=self.rin.at[p, t, h, k],
            send_sem=self.ts.at[p, t, h, k], recv_sem=self.tr.at[p, t, h, k],
            device_id=(number(self.z, *place_of),), device_id_type=MESH)

    def mine(self, p, h, k):
        return pltpu.make_async_copy(
            self.slot_rows(self.block(p, h, k, self.y, self.x, self.c), p), self.own.at[p, h, k], self.own_sem.at[p, h, k])

    def second(self, p, k):
        z, y, x, c = self.z, self.y, self.x, self.c
        target = number(z, 1 - y, x, c) if p == 0 else number(z, y, 1 - x, c)
        return pltpu.make_async_remote_copy(
            src_ref=self.sout.at[p, k], dst_ref=self.rb.at[p, k], send_sem=self.bs.at[p, k], recv_sem=self.br.at[p, k],
            device_id=(target,), device_id_type=MESH)

    def order(self, i):
        return jnp.where(self.z < 2, 3 - i, lax.rem(i + 1, 4))

    def relay(self, k):
        zz = lax.rem(self.z + k, 4)
        adds = ((self.z == 1) & (zz >= 2)) | ((self.z == 2) & (zz <= 1))
        return adds, 2 + jnp.where(zz >= 2, zz - 2, 1 - zz)

    def third(self, p, k):
        z = self.z
        zz = lax.rem(z + k, 4)
        to = jnp.where(z == 0, 1, jnp.where(z == 3, 2, zz))
        passed = ((z == 0) & (zz >= 2)) | ((z == 3) & (zz <= 1))
        last = ((z == 2) & (zz <= 1)) | ((z == 3) & (zz == 2)) | ((z == 1) & (zz == 3))
        slot = jnp.where(passed, 2 + jnp.where(zz >= 2, zz - 2, 1 - zz), jnp.where(last, 1, 0))
        return pltpu.make_async_remote_copy(
            src_ref=self.zout.at[p, k], dst_ref=self.rz.at[p, slot], send_sem=self.zs.at[p, k], recv_sem=self.zr.at[p, slot],
            device_id=(number(to, self.y, self.x, self.c),), device_id_type=MESH)

    def along(self, p, slot):
        return pltpu.make_async_remote_copy(
            src_ref=self.zout.at[p, 0], dst_ref=self.rz.at[p, slot], send_sem=self.zs.at[p, 0], recv_sem=self.zr.at[p, slot],
            device_id=(number(self.z, self.y, self.x, 1 - self.c),), device_id_type=MESH)

    def issue(self, h, i):
        k = self.order(i)
        for p in range(2):
            for t in (1, 2, 0):
                self.to(p, t, h, k).start()
            self.mine(p, h, k).start()

    def start(self):
        self.issue(1, 0)
        self.issue(0, 0)

    def dense(self, p, h, k):
        self.mine(p, h, k).wait()
        for t in range(3):
            self.to(p, t, h, k).wait_recv()
        block = self.block(p, h, k, self.y, self.x, self.c)
        total = None
        for t, who in enumerate([(self.y, self.x, self.c)] + self.sources(p)):
            hit = chosen_rows(self.slots_ref, block, in_plane(*who))
            chosen = jnp.where(hit, 1.0, 0.0).astype(BF16)
            values = self.own[p, h, k] if t == 0 else self.rin[p, t - 1, h, k]
            term = dims(chosen, values, 0, 0)
            total = term if total is None else total + term
        return total

    def step(self, u):
        i = u // 2
        k = self.order(jnp.int32(i))
        early = u % 2 == 0

        @pl.when(early)
        def _():
            for p in range(2):
                self.sout[p, k] = self.dense(p, 1, k).astype(BF16)
                self.second(p, k).start()

            @pl.when(i < 3)
            def _():
                self.issue(1, i + 1)

        @pl.when(u % 2 == 1)
        def _():
            for p in range(2):
                total = self.dense(p, 0, k)
                self.second(p, k).wait_recv()
                total = total + self.rb[p, k].astype(F32)

                adds, slot = self.relay(k)

                @pl.when((k > 0) & adds)
                def _(p=p, total=total):
                    self.along(p, slot).wait_recv()
                    self.zout[p, k] = (total + self.rz[p, slot].astype(F32)).astype(BF16)
                    self.third(p, k).start()

                @pl.when((k > 0) & jnp.logical_not(adds))
                def _(p=p, total=total):
                    self.zout[p, k] = total.astype(BF16)
                    self.third(p, k).start()

                @pl.when(k == 0)
                def _(p=p, total=total):
                    self.o_ref[:, self.cols[p]] = total

            @pl.when(i < 3)
            def _():
                self.issue(0, i + 1)

    def finish(self):
        for p in range(2):
            for slot in range(2):
                self.along(p, slot).wait_recv()
            self.o_ref[:, self.cols[p]] += self.rz[p, 0].astype(F32) + self.rz[p, 1].astype(F32)

        def one(k, _):
            for p in range(2):
                self.second(p, k).wait_send()

                @pl.when(k > 0)
                def _(p=p):
                    self.third(p, k).wait_send()
                for t in range(3):
                    for h in range(2):
                        self.to(p, t, h, k).wait_send()
            return 0
        lax.fori_loop(0, 4, one, 0)


def grads_kernel(
    dx_ref, slots_ref, gg_ref, xi_ref, ui_ref, hg_in, dg_in, du_in,
    o_ref, back_ref, wg_out, wu_out, wd_out, xcol, ucol, gout, uout, dout, hg_ref, dg_ref, du_ref,
    gs, gr, isem, osem, wsem, *scratch,
):
    greet_all()
    swap = Swap(lambda t: gg_ref.at[t], back_ref, gs, gr)
    rs = Back(dx_ref, slots_ref, o_ref, scratch)
    rs.start()
    swap.start()

    def col(i):
        return pl.ds(pl.multiple_of(i * 256, 256), 256)

    def loads(i):
        s = lax.rem(i, 2)
        return [
            pltpu.make_async_copy(xi_ref.at[:, col(i)], xcol.at[s], isem.at[0, s]),
            pltpu.make_async_copy(ui_ref.at[:, col(i)], ucol.at[s], isem.at[1, s]),
        ]

    def stores(i):
        s = lax.rem(i, 2)
        return [
            pltpu.make_async_copy(gout.at[s], wg_out.at[col(i), :], osem.at[0, s]),
            pltpu.make_async_copy(uout.at[s], wu_out.at[col(i), :], osem.at[1, s]),
            pltpu.make_async_copy(dout.at[s], wd_out.at[:, col(i)], osem.at[2, s]),
        ]

    for cp in loads(0):
        cp.start()
    whole = [
        pltpu.make_async_copy(source, into, wsem.at[i])
        for i, (source, into) in enumerate(((hg_in, hg_ref), (dg_in, dg_ref), (du_in, du_ref)))
    ]
    for cp in whole:
        cp.start()
    for cp in whole:
        cp.wait()

    def one(u, _):
        @pl.when(u < 6)
        def _():
            s = lax.rem(u, 2)

            @pl.when(u < 5)
            def _():
                for cp in loads(u + 1):
                    cp.start()

            for cp in loads(u):
                cp.wait()

            @pl.when(u >= 2)
            def _():
                for cp in stores(u - 2):
                    cp.wait()

            rows_in = xcol[s]
            gout[s] = dims(rows_in, dg_ref[...], 0, 0)
            uout[s] = dims(rows_in, du_ref[...], 0, 0)
            dout[s] = dims(hg_ref[...], ucol[s], 0, 0)
            for cp in stores(u):
                cp.start()

        rs.step(u)
        return 0

    lax.fori_loop(0, 8, one, 0)
    for i in (4, 5):
        for cp in stores(i):
            cp.wait()
    swap.wait_recv()
    rs.finish()
    swap.wait_send()


def run_grads(dx, slots, gg, xi, ui, hg, dg, du):
    rows, model = slots.shape[2], dx.shape[1]
    ff = hg.shape[1]
    n = dx.shape[0]
    hbm, vmem = pl.BlockSpec(memory_space=pl.ANY), pl.BlockSpec(memory_space=pltpu.VMEM)
    dma = pltpu.SemaphoreType.DMA
    return pl.pallas_call(
        grads_kernel,
        in_specs=[hbm, vmem, vmem, hbm, hbm, hbm, hbm, hbm],
        out_specs=[vmem, vmem, hbm, hbm, hbm],
        out_shape=[
            jax.ShapeDtypeStruct((rows, model), F32),
            jax.ShapeDtypeStruct((32, 8, 128), F32),
            jax.ShapeDtypeStruct((model, ff), F32),
            jax.ShapeDtypeStruct((model, ff), F32),
            jax.ShapeDtypeStruct((ff, model), F32),
        ],
        scratch_shapes=[
            pltpu.VMEM((2, n, 256), BF16), pltpu.VMEM((2, n, 256), BF16),
            pltpu.VMEM((2, 256, ff), F32), pltpu.VMEM((2, 256, ff), F32), pltpu.VMEM((2, ff, 256), F32),
            pltpu.VMEM((n, ff), BF16), pltpu.VMEM((n, ff), BF16), pltpu.VMEM((n, ff), BF16),
            dma((32,)), dma((32,)), dma((2, 2)), dma((3, 2)), dma((3,)),
        ] + Back.scratch(rows, model // 2),
        compiler_params=pltpu.CompilerParams(collective_id=14, has_side_effects=True, vmem_limit_bytes=56 * 2**20),
        name="grads",
    )(dx, slots, gg, xi, ui, hg, dg, du)


BEFORE_HEADS = (
    "w0", "rank", "w1", "v0", "w2", "v1", "w3", "v2", "v3", "bias", "gains", "norm", "u0", "u1",
    "u2", "u3", "wend", "kv", "ag", "o0", "q", "prev", "o1", "pass", "t0", "kend",
)
AFTER_HEAD = ("o2", "t1", "o3", "t2", "", "t3", "", "")


def front_kernel(
    chunks, rows, lo_ref, cos_ref, sin_ref, x_ref, wq_ref, wk_ref, wv_ref, router_ref, u_ref, turn_ref, turn_t_ref,
    gain_one_ref, gain_two_ref, q_out, o_ref, lse_ref, window_out, slots_ref, ui_ref, w_out, n_ref, gains_ref, scale_ref,
    q_ref, window, w_ref, part_ref, bias, mine, kv, key_t, insem, outsem, gs, gr, lsem, ws, wr, *scratch,
):
    loads, at = [], 0
    for i, ref in enumerate((wq_ref, wk_ref, wv_ref)):
        loads.append(pltpu.make_async_copy(ref, part_ref.at[:, pl.ds(at, ref.shape[1])], insem.at[i]))
        at += ref.shape[1]
    for cp in loads:
        cp.start()
    part_ref[:, at:] = jnp.zeros((part_ref.shape[0], part_ref.shape[1] - at), BF16)
    part_ref[:, at : at + EXPERTS] = router_ref[...]
    greet_all()
    weights = Whole(part_ref, w_ref, scratch[:7])
    swap = Swap(lambda t: mine.at[t // 8], slots_ref, gs, gr)
    keys = Window(rows, kv, window, (lsem, ws, wr))
    ag = Forth(u_ref, slots_ref, ui_ref, scratch[7:])
    cosine, sine = cos_ref[...], sin_ref[...]
    q_width, k_width = QUERY_HEADS * HEAD_DIM, KEY_HEADS * HEAD_DIM

    def rank():
        for e in range(EXPERTS):
            own = turn_t_ref[e : e + 1, :]
            place_of = jnp.sum(jnp.where(turn_ref[:, e : e + 1] < own, 1.0, 0.0), axis=0, keepdims=True)
            slot = jnp.where((own < UNPICKED) & (place_of < CAPACITY), place_of, -1.0)
            mine[e // 8, e % 8 : e % 8 + 1, :] = slot
        mine[:, 8:16, :] = jnp.zeros((4, 8, rows), F32)
        for plane in range(4):
            mine[plane, 8:9, 0 : part_ref.shape[0]] = gain_one_ref[...].astype(F32)
            mine[plane, 9:10, 0 : part_ref.shape[0]] = gain_two_ref[...].astype(F32)
        swap.start()

    def gains():
        swap.wait_recv()
        part = part_ref.shape[0]
        for t in range(32):
            gains_ref[0:8, t * part : (t + 1) * part] = slots_ref[t, 8:16, 0:part]

    def norm():
        def some(i, _):
            at = pl.ds(pl.multiple_of(i * 32, 32), 32)
            values = x_ref[at, :].astype(F32)
            scale = lax.rsqrt(jnp.mean(values * values, axis=1, keepdims=True) + EPSILON)
            scale_ref[at, :] = scale
            n_ref[at, :] = (values * scale * gains_ref[0:1, :]).astype(BF16)
            return 0
        lax.fori_loop(0, rows // 32, some, 0)

    def roped(values, into, first):
        turned = values.T
        for n in range(256 // HEAD_DIM):
            u = turned[n * HEAD_DIM : n * HEAD_DIM + HEAD_DIM // 2]
            w = turned[n * HEAD_DIM + HEAD_DIM // 2 : (n + 1) * HEAD_DIM]
            at = first + n * HEAD_DIM
            into[pl.ds(pl.multiple_of(at, 32), 32), :] = (u * cosine - w * sine).astype(BF16)
            into[pl.ds(pl.multiple_of(at + 32, 32), 32), :] = (w * cosine + u * sine).astype(BF16)

    def keys_and_values():
        for n in range(k_width // 256):
            roped(dims(n_ref[...], w_ref[:, q_width + n * 256 : q_width + (n + 1) * 256], 1, 0), key_t, n * 256)
            kv[0, :, n * 256 : (n + 1) * 256] = key_t[n * 256 : (n + 1) * 256, :].T
        kv[1] = dims(n_ref[...], w_ref[:, q_width + k_width : QKV], 1, 0).astype(BF16)
        keys.start()

    def queries():
        def some(i, _):
            at = pl.ds(pl.multiple_of(i * 256, 256), 256)
            roped(dims(n_ref[...], w_ref[:, at], 1, 0), q_ref, i * 256)
            q_ref[at, :] = (q_ref[at, :].astype(F32) * HEAD_DIM**-0.5).astype(BF16)
            return 0
        lax.fori_loop(0, q_width // 256, some, 0)

    def whole():
        weights.end()
        outs[0].start()

    def queried():
        queries()
        outs[1].start()

    def windowed():
        keys.end()
        outs[2].start()

    outs = [
        pltpu.make_async_copy(held, out, outsem.at[i])
        for i, (held, out) in enumerate(((w_ref, w_out), (q_ref, q_out), (window, window_out)))
    ]
    step = {
        "rank": rank, "gains": gains, "norm": norm, "kv": keys_and_values, "q": queried,
        "ag": ag.start, "bias": lambda: make_bias(bias, lo_ref, chunks, rows), "wend": whole,
        "prev": keys.previous, "pass": keys.pass_on, "kend": windowed,
    }
    for i in range(4):
        step[f"w{i}"] = functools.partial(weights.one, i)
        step[f"v{i}"] = functools.partial(weights.two, i)
        step[f"u{i}"] = functools.partial(weights.three, i)
        step[f"c{i}"] = functools.partial(ag.come, jnp.int32(i))
        step[f"s{i}"] = functools.partial(ag.one, jnp.int32(i), False)
        step[f"o{i}"] = functools.partial(ag.one, jnp.int32(i))
        step[f"t{i}"] = functools.partial(ag.two, jnp.int32(i))

    for cp in loads:
        cp.wait()
    weights.start()
    for name in BEFORE_HEADS:
        step[name]()
    width = 2 * GROUP * HEAD_DIM

    def pair(j, _):
        lanes = pl.ds(pl.multiple_of(j * 2 * HEAD_DIM, 2 * HEAD_DIM), 2 * HEAD_DIM)
        head = pl.ds(pl.multiple_of(j * width, width), width)

        def between(half):
            for u in range(half, 8, 2):
                if AFTER_HEAD[u]:
                    @pl.when(2 * j + half == u)
                    def _(u=u):
                        step[AFTER_HEAD[u]]()

        attend_pair(
            chunks, rows, lax.rem(lax.axis_index("dev"), 2), q_ref.at[head, :], window.at[:, :, lanes],
            o_ref.at[head, :], lse_ref.at[pl.ds(j, 1)], bias, between,
        )
        return 0

    lax.fori_loop(0, KEY_HEADS // 2, pair, 0)

    def last(u, _):
        ag.arrived(lax.rem(u, 4), u // 4)
        return 0
    lax.fori_loop(0, 16, last, 0)
    ag.sent()
    keys.sent()
    swap.wait_send()
    weights.sent()
    for cp in outs:
        cp.wait()


def front(lo, cos_t, sin_t, tokens, projections, router, upstream, turn, gain_one, gain_two):
    rows, model = tokens.shape
    chunks = 9
    keys = KEY_HEADS * HEAD_DIM
    part = jax.ShapeDtypeStruct((router.shape[0], -(-(QKV + EXPERTS) // 128) * 128), BF16)
    hbm, vmem = pl.BlockSpec(memory_space=pl.ANY), pl.BlockSpec(memory_space=pltpu.VMEM)
    dma = pltpu.SemaphoreType.DMA
    return pl.pallas_call(
        functools.partial(front_kernel, chunks, rows),
        in_specs=[vmem] * 4 + [hbm] * 3 + [vmem, hbm] + [vmem] * 4,
        out_specs=[hbm, vmem, vmem, hbm, vmem, hbm, hbm, vmem, vmem, vmem],
        out_shape=[
            jax.ShapeDtypeStruct((QUERY_HEADS * HEAD_DIM, rows), BF16),
            jax.ShapeDtypeStruct((QUERY_HEADS * HEAD_DIM, rows), BF16),
            jax.ShapeDtypeStruct((KEY_HEADS // 2, 8, rows), F32),
            jax.ShapeDtypeStruct((2, 10 * rows, keys), BF16),
            jax.ShapeDtypeStruct((32, 16, rows), F32),
            jax.ShapeDtypeStruct((32 * SLOTS, model), BF16),
            jax.ShapeDtypeStruct((32 * part.shape[0], part.shape[1]), BF16),
            jax.ShapeDtypeStruct((rows, model), BF16),
            jax.ShapeDtypeStruct((8, model), F32),
            jax.ShapeDtypeStruct((rows, 1), F32),
        ],
        scratch_shapes=[
            pltpu.VMEM((QUERY_HEADS * HEAD_DIM, rows), BF16), pltpu.VMEM((2, 10 * rows, keys), BF16),
            pltpu.VMEM((32 * part.shape[0], part.shape[1]), BF16), pltpu.VMEM(part.shape, BF16),
            pltpu.VMEM((chunks * rows, rows), F32), pltpu.VMEM((4, 16, rows), F32), pltpu.VMEM((2, rows, keys), BF16),
            pltpu.VMEM((keys, rows), BF16), dma((3,)), dma((3,)), dma((32,)), dma((32,)),
        ]
        + Window.scratch + Whole.scratch + Forth.scratch(rows, model // 2),
        compiler_params=pltpu.CompilerParams(collective_id=16, has_side_effects=True, vmem_limit_bytes=58 * 2**20),
        name="front",
    )(lo, cos_t, sin_t, tokens, *projections, router, upstream, turn, turn.T, gain_one, gain_two)


IN_PAIRS = {0: (0,), 2: (1,), 4: (2,), 6: (3,)}
AFTER_PAIRS = (4, "sums", 5, 6, "near", "turn", 7)


def attend_back_mesh_kernel(
    chunks, rows, lo_ref, cos_ref, sin_ref, q_ref, kv_in, branch_ref, wo_in, lse_ref, out_ref, y_ref, slots_ref, residual_in,
    grad_out, layer_ref, wo, g_ref, wsem, kv_ref, residual_ref, insem, bias, dkv, sums_ref, gt_ref, o_ref, *scratch,
):
    greet_near()
    rs = Back(y_ref, slots_ref, o_ref, scratch[: Back.n_scratch])
    keys = Unwindow(rows, dkv, sums_ref, scratch[Back.n_scratch :])
    rs.start()
    kv_load = pltpu.make_async_copy(kv_in, kv_ref, insem.at[0])
    residual_load = pltpu.make_async_copy(residual_in, residual_ref, insem.at[1])
    kv_load.start()
    residual_load.start()
    step = wo.shape[1]

    def wo_load(i):
        return pltpu.make_async_copy(wo_in.at[pl.ds(i * step, step), :], wo.at[i % 2], wsem.at[i % 2])

    wo_load(0).start()
    make_bias(bias, lo_ref, chunks, rows)
    for i in range(wo_in.shape[0] // step):
        if (i + 1) * step < wo_in.shape[0]:
            wo_load(i + 1).start()
        wo_load(i).wait()
        g_ref[i * step : (i + 1) * step, :] = dims(wo[i % 2], branch_ref[...], 1, 1).astype(BF16)
    kv_load.wait()
    residual_load.wait()
    width = 2 * GROUP * HEAD_DIM

    def pair(j, _):
        lanes = pl.ds(pl.multiple_of(j * 2 * HEAD_DIM, 2 * HEAD_DIM), 2 * HEAD_DIM)
        head = pl.ds(pl.multiple_of(j * width, width), width)

        def between(half):
            for n, names in IN_PAIRS.items():
                if n % 2 == half:
                    @pl.when(2 * j + half == n)
                    def _(names=names):
                        for name in names:
                            rs.step(name)

        attend_back_pair(
            chunks, rows, lax.rem(lax.axis_index("dev"), 2), cos_ref, sin_ref, q_ref.at[head, :], kv_ref.at[:, :, lanes], g_ref.at[head, :],
            lse_ref.at[pl.ds(j, 1)], out_ref.at[head, :], gt_ref.at[head, :], dkv.at[:, :, lanes], bias, between,
        )
        return 0

    lax.fori_loop(0, KEY_HEADS // 2, pair, 0)

    def turned(first, last):
        for n in range(first, last, 256):
            grad_out[:, n : n + 256] = gt_ref[n : n + 256, :].T

    keys.start()
    for name in AFTER_PAIRS:
        if isinstance(name, int):
            rs.step(name)
        elif name == "sums":
            keys.sums()
        elif name == "turn":
            turned(0, QUERY_HEADS * HEAD_DIM)
        else:
            keys.near()
    keys.end()
    base = QUERY_HEADS * HEAD_DIM
    key_t = sums_ref[0].T
    cosine, sine = cos_ref[...], sin_ref[...]
    for n in range(KEY_HEADS):
        first, middle = n * HEAD_DIM, n * HEAD_DIM + HEAD_DIM // 2
        u, w = key_t[first:middle], key_t[middle : first + HEAD_DIM]
        gt_ref[base + first : base + middle, :] = (u * cosine + w * sine).astype(BF16)
        gt_ref[base + middle : base + first + HEAD_DIM, :] = (w * cosine - u * sine).astype(BF16)
    turned(base, base + KEY_HEADS * HEAD_DIM)
    grad_out[:, base + KEY_HEADS * HEAD_DIM :] = sums_ref[1].astype(BF16)
    rs.finish()
    layer_ref[...] = (residual_ref[...] + o_ref[...]).astype(BF16)


def attend_back_mesh(query_t, window, lo, branch_grad, output_matrix, lse, attended_t, cos_t, sin_t, y, slots, residual):
    rows, span, keys = query_t.shape[1], window.shape[1], window.shape[2]
    chunks = span // rows - 1
    model = y.shape[1]
    hbm, vmem = pl.BlockSpec(memory_space=pl.ANY), pl.BlockSpec(memory_space=pltpu.VMEM)
    return pl.pallas_call(
        functools.partial(attend_back_mesh_kernel, chunks, rows),
        in_specs=[vmem] * 4 + [hbm, vmem, hbm] + [vmem] * 2 + [hbm, vmem, hbm],
        out_specs=[vmem] * 2,
        out_shape=[
            jax.ShapeDtypeStruct((rows, QKV), BF16),
            jax.ShapeDtypeStruct((rows, model), BF16),
        ],
        scratch_shapes=[
            pltpu.VMEM((2, 384, model), BF16), pltpu.VMEM(query_t.shape, BF16), pltpu.SemaphoreType.DMA((2,)),
            pltpu.VMEM(window.shape, BF16), pltpu.VMEM((rows, model), F32), pltpu.SemaphoreType.DMA((2,)),
            pltpu.VMEM((chunks * rows, rows), F32), pltpu.VMEM(window.shape, BF16), pltpu.VMEM((2, rows, keys), F32),
            pltpu.VMEM((QKV, rows), BF16), pltpu.VMEM((rows, model), F32),
        ]
        + Back.scratch(rows, model // 2) + Unwindow.scratch(rows, keys),
        compiler_params=pltpu.CompilerParams(collective_id=15, has_side_effects=True, vmem_limit_bytes=60 * 2**20),
        name="attend_back",
    )(lo, cos_t, sin_t, query_t, window, branch_grad, output_matrix, lse, attended_t, y, slots, residual)


def finish_kernel(
    rows, n_ref, g_ref, w_in, more_ref, gain_ref, scale_ref, x_in, rg_in,
    oq_ref, ok_ref, ov_ref, om_ref, tg_ref, fg_ref, w_ref, x_ref, rg_ref, insem,
    dense, acc, ra, rb, rz, out, ng, mine, theirs, ssem, rsem, sa, ra_sem, sb, rb_sem, sz, rz_sem, gs, gr,
):
    z, y, x, c = place()
    greet_all()
    sibling = number(z, y, x, 1 - c)
    cols = acc.shape[2]
    main = g_ref.shape[1]
    half = cols // 2
    pieces = [pl.ds(0, half), pl.ds(half, half)]
    around = (number(z, y, 1 - x, c), number(z, 1 - y, x, c))
    swap = Swap(lambda t: mine.at[t], theirs, gs, gr)

    def lane(dy, dx, k):
        yy = 1 - y if dy else y
        xx = 1 - x if dx else x
        return (lax.rem(z + k, 4) * 2 + yy) * 2 + xx

    def to_sibling(dy, dx, k):
        chip = lane(dy, dx, k)
        n = (k, dy, dx)
        sides = (
            (dense.at[chip, pl.ds(pl.multiple_of((1 - c) * rows, 16), rows), :], pl.ds(0, main)),
            (more_ref.at[pl.ds(pl.multiple_of((2 * chip + 1 - c) * rows, 16), rows), :], pl.ds(main, cols - main)),
        )
        return [
            pltpu.make_async_remote_copy(
                src_ref=source, dst_ref=acc.at[chip, :, at], send_sem=ssem.at[(*n, i)], recv_sem=rsem.at[(*n, i)],
                device_id=(sibling,), device_id_type=MESH)
            for i, (source, at) in enumerate(sides)
        ]

    def first(p, d2, k, dy, dx):
        return pltpu.make_async_remote_copy(
            src_ref=acc.at[lane(dy, dx, k), :, pieces[p]], dst_ref=ra.at[p, d2, k],
            send_sem=sa.at[p, d2, k], recv_sem=ra_sem.at[p, d2, k], device_id=(around[p],), device_id_type=MESH)

    def second(p, k):
        dy, dx = (1, 0) if p == 0 else (0, 1)
        return pltpu.make_async_remote_copy(
            src_ref=acc.at[lane(dy, dx, k), :, pieces[p]], dst_ref=rb.at[p, k],
            send_sem=sb.at[p, k], recv_sem=rb_sem.at[p, k], device_id=(around[1 - p],), device_id_type=MESH)

    def third(p, k):
        return pltpu.make_async_remote_copy(
            src_ref=acc.at[lane(0, 0, k), :, pieces[p]], dst_ref=rz.at[p, k],
            send_sem=sz.at[p, k], recv_sem=rz_sem.at[p, k],
            device_id=(number(lax.rem(z + k, 4), y, x, c),), device_id_type=MESH)

    quarter = ((1, 1), (1, 0), (0, 1), (0, 0))

    def product(i, _):
        k = far_first(i)
        zz = lax.rem(z + k, 4)
        at = pl.ds(pl.multiple_of(zz * 8 * rows, 128), 8 * rows)
        part = dims(n_ref[:, at], g_ref[...], 0, 0).astype(BF16)
        for chip in range(4):
            dense[zz * 4 + chip] = part[chip * 2 * rows : (chip + 1) * 2 * rows]
        for dy, dx in quarter:
            for cp in to_sibling(dy, dx, k):
                cp.start()
        return 0

    def own_sums(k):
        for dy, dx in quarter:
            chip = lane(dy, dx, k)
            for cp in to_sibling(dy, dx, k):
                cp.wait_recv()
            acc[chip, :, :main] = (
                acc[chip, :, :main].astype(F32) + dense[chip, pl.ds(pl.multiple_of(c * rows, 16), rows), :].astype(F32)
            ).astype(BF16)
            acc[chip, :, main:] = (
                acc[chip, :, main:].astype(F32)
                + more_ref[pl.ds(pl.multiple_of((2 * chip + c) * rows, 16), rows), :].astype(F32)
            ).astype(BF16)
            if dx:
                first(0, dy, k, dy, dx).start()
            if dy:
                first(1, dx, k, dy, dx).start()

    def middle(k):
        for p in range(2):
            dy, dx = (1, 0) if p == 0 else (0, 1)
            first(p, 1, k, 1, 1).wait_recv()
            block = acc.at[lane(dy, dx, k), :, pieces[p]]
            block[...] = (block[...].astype(F32) + ra[p, 1, k].astype(F32)).astype(BF16)
            second(p, k).start()

    def late(k):
        for p in range(2):
            first(p, 0, k, 1 - p, p).wait_recv()
            second(p, k).wait_recv()
            block = acc.at[lane(0, 0, k), :, pieces[p]]
            total = block[...].astype(F32) + ra[p, 0, k].astype(F32) + rb[p, k].astype(F32)

            @pl.when(k > 0)
            def _(p=p, block=block, total=total):
                block[...] = total.astype(BF16)
                third(p, k).start()

            @pl.when(k == 0)
            def _(p=p, total=total):
                out[:, pieces[p]] = total

    def rest_of_tokens():
        ng[...] = dims(g_ref[...], w_ref[:, :main], 1, 1)

        def tail(i, total):
            at = pl.ds(pl.multiple_of(i * 32, 32), 32)
            grad, scale, values = ng[at, :], scale_ref[at, :], x_ref[at, :].astype(F32)
            weighted = grad * gain_ref[...]
            scaled = values * scale
            mean = jnp.mean(weighted * values, axis=1, keepdims=True)
            tg_ref[at, :] = rg_ref[at, :] + scale * weighted - scaled * (scale * scale * mean)
            return total + jnp.sum(grad * scaled, axis=0, keepdims=True)
        total = lax.fori_loop(0, x_ref.shape[0] // 32, tail, jnp.zeros(gain_ref.shape, F32))
        mine[...] = jnp.zeros_like(mine)
        for t in range(32):
            mine[t, 0:1, 0:rows] = total[:, t * rows : (t + 1) * rows]
        swap.start()

    loads = [
        pltpu.make_async_copy(source, into, insem.at[i])
        for i, (source, into) in enumerate(((w_in, w_ref), (x_in, x_ref), (rg_in, rg_ref)))
    ]
    for cp in loads:
        cp.start()
    lax.fori_loop(0, 4, product, 0)
    for cp in loads:
        cp.wait()

    def steps(i, _):
        @pl.when(i < 4)
        def _():
            own_sums(far_first(i))

        @pl.when(i == 3)
        def _():
            rest_of_tokens()

        @pl.when((i >= 1) & (i < 5))
        def _():
            middle(far_first(i - 1))

        @pl.when(i >= 2)
        def _():
            late(far_first(i - 2))
        return 0
    lax.fori_loop(0, 6, steps, 0)
    swap.wait_recv()
    fg_ref[...] = jnp.sum(theirs[...], axis=0)
    for p in range(2):
        for k in range(1, 4):
            third(p, k).wait_recv()
        out[:, pieces[p]] += rz[p, 1].astype(F32) + rz[p, 2].astype(F32) + rz[p, 3].astype(F32)
    at = 0
    for ref in (oq_ref, ok_ref, ov_ref, om_ref):
        ref[...] = out[:, at : at + ref.shape[1]]
        at += ref.shape[1]

    def sent(k, _):
        for dy, dx in quarter:
            for cp in to_sibling(dy, dx, k):
                cp.wait_send()
        for p in range(2):
            first(p, 0, k, 1 - p, p).wait_send()
            first(p, 1, k, 1, 1).wait_send()
            second(p, k).wait_send()

            @pl.when(k > 0)
            def _(p=p):
                third(p, k).wait_send()
        return 0
    lax.fori_loop(0, 4, sent, 0)
    swap.wait_send()


def finish(normed, grad, matrices, more, gain, scale, tokens, residual_grad):
    count, model = normed.shape
    rows = model // 32
    main, cols = grad.shape[1], grad.shape[1] + more.shape[1]
    half = cols // 2
    dma = pltpu.SemaphoreType.DMA
    hbm, vmem = pl.BlockSpec(memory_space=pl.ANY), pl.BlockSpec(memory_space=pltpu.VMEM)
    widths = [QUERY_HEADS * HEAD_DIM, KEY_HEADS * HEAD_DIM, KEY_HEADS * HEAD_DIM, more.shape[1]]
    return pl.pallas_call(
        functools.partial(finish_kernel, rows),
        in_specs=[vmem, vmem, hbm, vmem, vmem, vmem, hbm, hbm],
        out_specs=[vmem] * 6,
        out_shape=[jax.ShapeDtypeStruct((rows, w), F32) for w in widths] + [
            jax.ShapeDtypeStruct((count, model), F32),
            jax.ShapeDtypeStruct((8, 128), F32),
        ],
        scratch_shapes=[
            pltpu.VMEM(matrices.shape, BF16), pltpu.VMEM((count, model), BF16), pltpu.VMEM((count, model), F32), dma((3,)),
            pltpu.VMEM((16, 2 * rows, main), BF16),
            pltpu.VMEM((16, rows, cols), BF16),
            pltpu.VMEM((2, 2, 4, rows, half), BF16),
            pltpu.VMEM((2, 4, rows, half), BF16),
            pltpu.VMEM((2, 4, rows, half), BF16),
            pltpu.VMEM((rows, cols), F32),
            pltpu.VMEM((count, model), F32),
            pltpu.VMEM((32, 8, 128), F32),
            pltpu.VMEM((32, 8, 128), F32),
            dma((4, 2, 2, 2)), dma((4, 2, 2, 2)), dma((2, 2, 4)), dma((2, 2, 4)), dma((2, 4)), dma((2, 4)), dma((2, 4)), dma((2, 4)),
            dma((32,)), dma((32,)),
        ],
        compiler_params=pltpu.CompilerParams(collective_id=17, has_side_effects=True, vmem_limit_bytes=42 * 2**20),
        name="finish",
    )(normed, grad, matrices, more, gain, scale, tokens, residual_grad)


def chunks_of(shape):
    rows = shape[0]
    count = 1
    while rows % (32 * count) == 0 and rows // count * shape[1] > 2**18:
        count *= 2
    return [(i * (rows // count), rows // count) for i in range(count)]


def hand_over_kernel(count, *refs):
    sources, outs, held = refs[:count], refs[count : 2 * count], refs[2 * count : 3 * count]
    sems = refs[3 * count]
    into, out = [], []
    for source, there, here in zip(sources, outs, held, strict=True):
        for first, rows in chunks_of(source.shape):
            at, n = pl.ds(first, rows), len(into)
            into.append(pltpu.make_async_copy(source.at[at, :], here.at[at, :], sems.at[0, n]))
            out.append(pltpu.make_async_copy(here.at[at, :], there.at[at, :], sems.at[1, n]))
    for cp in into:
        cp.start()
    for a, b in zip(into, out, strict=True):
        a.wait()
        b.start()
    for cp in out:
        cp.wait()


def hand_over(*arrays):
    hbm = pl.BlockSpec(memory_space=pl.ANY)
    total = sum(len(chunks_of(a.shape)) for a in arrays)
    return pl.pallas_call(
        functools.partial(hand_over_kernel, len(arrays)),
        in_specs=[hbm] * len(arrays),
        out_specs=[hbm] * len(arrays),
        out_shape=[jax.ShapeDtypeStruct(a.shape, a.dtype) for a in arrays],
        scratch_shapes=[pltpu.VMEM(a.shape, a.dtype) for a in arrays] + [pltpu.SemaphoreType.DMA((2, total))],
        compiler_params=pltpu.CompilerParams(vmem_limit_bytes=60 * 2**20),
        name="hand_over",
    )(*arrays)


def rms_scale(values):
    return lax.rsqrt(jnp.mean(values * values, axis=-1, keepdims=True) + EPSILON)


def rotate_t(values, cosine, sine):
    half = cosine.shape[0]
    shaped = values.reshape(-1, 2, half, values.shape[1])
    u, w = shaped[:, 0], shaped[:, 1]
    turned = jnp.stack([u * cosine - w * sine, w * cosine + u * sine], axis=1)
    return turned.reshape(values.shape)


def on_device(
    tokens,
    positions,
    expert_picks,
    priority,
    first_gain,
    query_weight,
    key_projection_matrix,
    value_projection_matrix,
    output_weight,
    second_gain,
    router_weight,
    gate_weight,
    up_weight,
    down_weight,
    cotangent,
):
    devices = lax.axis_size("dev")
    rows, model = tokens.shape
    split = devices // EXPERTS
    capacity = split * ((9 * rows * TOP + 8 * EXPERTS * split - 1) // (8 * EXPERTS * split))
    weight_rows = query_weight.shape[0]

    output_matrix = lax.all_gather(output_weight, "dev", axis=0, tiled=True)

    extra = [query_weight, key_projection_matrix, value_projection_matrix, router_weight]
    pad = (-(QKV + EXPERTS)) % 128
    packed = jnp.concatenate(extra + [jnp.zeros((weight_rows, pad), BF16)], axis=1)
    q_width, k_width = QUERY_HEADS * HEAD_DIM, KEY_HEADS * HEAD_DIM
    inputs = tokens.astype(F32)
    half_dim = HEAD_DIM // 2
    frequency = jnp.power(10000.0, -(jnp.arange(half_dim, dtype=F32) * 2.0) / HEAD_DIM)
    angle = positions.astype(F32)[None, :] * frequency[:, None]
    cos_t, sin_t = jnp.cos(angle), jnp.sin(angle)
    lo = (jnp.arange(rows, dtype=jnp.int32) - positions)[None, :]
    one_hot = expert_picks[:, :, None] == jnp.arange(EXPERTS, dtype=jnp.int32)
    picked_any = jnp.any(one_hot, axis=1)
    turn = jnp.sum(jnp.where(one_hot, priority[:, :, None], 0), axis=1).astype(F32)
    turn = jnp.where(picked_any, turn, UNPICKED)

    if meshed():
        query_t, attended_t, lse, window, plane_slots, expert_up, matrices, normed_one, gains, scale_one = front(
            lo, cos_t, sin_t, tokens, extra[:3], router_weight, cotangent, turn, first_gain[None, :], second_gain[None, :]
        )
        gain_first, gain_second = gains[0], gains[1]
    else:
        matrices, gain_first, gain_second = (
            lax.all_gather(v, "dev", axis=0, tiled=True) for v in (packed, first_gain, second_gain)
        )
        gain_first, gain_second = gain_first.astype(F32), gain_second.astype(F32)
        rank = jnp.sum((turn.T[:, None, :] < turn.T[:, :, None]).astype(jnp.int32), axis=2)
        slot_rows = jnp.where(picked_any.T & (rank < capacity), rank, -1).astype(F32)
        scale_one = rms_scale(inputs)
        normed_one = (inputs * scale_one * gain_first).astype(BF16)
        qkv_t = dims(matrices[:, :QKV], normed_one, 0, 1)
        query_t = rotate_t(qkv_t[:q_width], cos_t, sin_t).astype(BF16) * BF16(HEAD_DIM**-0.5)
        key = rotate_t(qkv_t[q_width : q_width + k_width], cos_t, sin_t).astype(BF16).T
        value = qkv_t[q_width + k_width :].astype(BF16).T
        window, offset = window_of(jnp.stack([key, value])), jnp.int32(0)
        attended_t, lse = attend(query_t, window, offset, lo)
    qkv_matrix = matrices[:, :QKV]
    router_matrix = matrices[:, QKV : QKV + EXPERTS]
    residual = inputs + dims(attended_t, output_matrix, 0, 0)
    scale_two = rms_scale(residual)
    normed_two = (residual * scale_two * gain_second).astype(BF16)

    logits = dims(normed_two, router_matrix, 1, 0)
    logits = jnp.where(picked_any, logits, MASKED)
    picked_exp = jnp.exp(logits - jnp.max(logits, axis=1, keepdims=True))
    gates = picked_exp / jnp.sum(picked_exp, axis=1, keepdims=True)

    if meshed():
        gate_rows = jnp.pad(gates.T.reshape(EXPERTS, rows // 128, 128), ((0, 0), (0, 8 - rows // 128), (0, 0)))
        expert_in, grad_rows, out_rows, gated_hidden, gate_in_grad, up_in_grad, gate_grad_rows = run_experts(
            normed_two, gate_rows, plane_slots, expert_up, gate_weight, up_weight, down_weight
        )
        returned_grad, gate_grad, gate_gradient, up_gradient, down_gradient = run_grads(
            grad_rows, plane_slots, gate_grad_rows, expert_in, expert_up, gated_hidden, gate_in_grad, up_in_grad
        )
        gate_grad = gate_grad[:, : rows // 128].reshape(EXPERTS, rows).T
    else:
        gate_rows, slot = (
            lax.all_to_all(jnp.repeat(v, split, axis=0), "dev", split_axis=0, concat_axis=0, tiled=True)
            for v in (gates.T, slot_rows)
        )
        pair_slot = jnp.where(
            slot.reshape(devices // 2, 2, rows) >= 0,
            slot.reshape(devices // 2, 2, rows) + jnp.array([[0], [capacity]], F32),
            -1.0,
        ).astype(jnp.int32).reshape(devices // 2, 1, 2 * rows)
        all_upstream = lax.all_gather(cotangent, "dev", axis=0, tiled=True)
        all_normed = lax.all_gather(normed_two, "dev", axis=0, tiled=True)
        expert_in, expert_up = dispatch(pair_slot, all_normed, all_upstream, 2 * capacity)
        slot_hit = slot[:, None, :] == jnp.arange(capacity, dtype=F32)[None, :, None]
        gate_of_slot = jnp.sum(jnp.where(slot_hit, gate_rows[:, None, :], 0.0), axis=2).reshape(-1, 1)
        gate_in = dims(expert_in, gate_weight, 1, 0)
        up_in = dims(expert_in, up_weight, 1, 0)
        sigmoid_gate = 1.0 / (1.0 + jnp.exp(-gate_in))
        silu_gate = gate_in * sigmoid_gate
        hidden = (silu_gate * up_in).astype(BF16)
        gated_hidden = (hidden.astype(F32) * gate_of_slot).astype(BF16)
        hidden_up = dims(expert_up, down_weight, 1, 1)
        hidden_grad = hidden_up * gate_of_slot
        gate_grad_slot = jnp.sum(hidden.astype(F32) * hidden_up, axis=1).reshape(devices, capacity)
        gate_in_grad = (hidden_grad * up_in * sigmoid_gate * (1.0 + gate_in * (1.0 - sigmoid_gate))).astype(BF16)
        up_in_grad = (hidden_grad * silu_gate).astype(BF16)
        partial_in = (dims(gate_in_grad, gate_weight, 1, 1) + dims(up_in_grad, up_weight, 1, 1)).astype(BF16)
        gate_grad_rows = jnp.sum(jnp.where(slot_hit, gate_grad_slot[:, :, None], 0.0), axis=1)
        returned_grad = lax.psum_scatter(
            combine(pair_slot, partial_in, 2 * capacity), "dev", scatter_dimension=0, tiled=True
        ).astype(F32)
        gate_grad = lax.all_to_all(gate_grad_rows, "dev", split_axis=0, concat_axis=0, tiled=True)
        gate_grad = jnp.sum(gate_grad.reshape(EXPERTS, split, rows), axis=1).T
        partial_out = dims(gated_hidden, down_weight, 1, 0).astype(BF16)
        dense_out = combine(pair_slot, partial_out, 2 * capacity)
        mixture = lax.psum_scatter(dense_out, "dev", scatter_dimension=0, tiled=True).astype(F32)
        down_gradient = dims(gated_hidden, expert_up, 0, 0)
        gate_gradient = dims(expert_in, gate_in_grad, 0, 0)
        up_gradient = dims(expert_in, up_in_grad, 0, 0)

    upstream = cotangent.astype(F32)
    logit_grad = (gates * (gate_grad - jnp.sum(gates * gate_grad, axis=1, keepdims=True))).astype(BF16)
    router_gradient = dims(normed_two, logit_grad, 0, 0)
    normed_two_grad = returned_grad + dims(logit_grad, router_matrix, 1, 1)
    weighted_two = normed_two_grad * gain_second
    second_gain_grad = jnp.sum(normed_two_grad * residual * scale_two, axis=0)
    residual_grad = (
        upstream
        + scale_two * weighted_two
        - residual * scale_two**3 * jnp.mean(weighted_two * residual, axis=-1, keepdims=True)
    )
    branch_grad = residual_grad.astype(BF16)
    output_gradient = dims(attended_t, branch_grad, 1, 0).astype(BF16)
    output_gradient = lax.psum_scatter(output_gradient, "dev", scatter_dimension=0, tiled=True).astype(F32)

    if meshed():
        qkv_grad, layer_output = attend_back_mesh(
            query_t, window, lo, branch_grad, output_matrix, lse, attended_t, cos_t, sin_t, out_rows, plane_slots, residual
        )
    else:
        grad_t = dims(output_matrix, branch_grad, 1, 1).astype(BF16)
        query_grad_t, window_grad = attend_back(query_t, window, offset, lo, grad_t, lse, attended_t, cos_t, sin_t)
        key_grad, value_grad = unwindow(window_grad)
        key_grad_t = rotate_t(key_grad.T, cos_t, -sin_t).astype(BF16)
        qkv_grad_t = jnp.concatenate([query_grad_t, key_grad_t, value_grad.T.astype(BF16)], axis=0)
        layer_output = (residual + mixture).astype(BF16)
    more = jnp.concatenate(
        [router_gradient, second_gain_grad[:, None], jnp.zeros((model, (-(EXPERTS + 1)) % 256), F32)], axis=1
    ).astype(BF16)
    if meshed():
        query_sums, key_sums, value_sums, more_sums, tokens_gradient, first_sums = finish(
            normed_one, qkv_grad, matrices, more, gain_first[None, :], scale_one, tokens, residual_grad
        )
        first_sums = first_sums[0, :weight_rows]
        (
            gate_gradient, up_gradient, down_gradient, layer_output, tokens_gradient, query_sums, key_sums, value_sums
        ) = hand_over(
            gate_gradient, up_gradient, down_gradient, layer_output, tokens_gradient, query_sums, key_sums, value_sums
        )
    else:
        qkv_gradient = dims(normed_one, qkv_grad_t, 0, 1).astype(BF16)
        normed_one_grad = dims(qkv_grad_t, qkv_matrix, 0, 1)
        weighted_one = normed_one_grad * gain_first
        tokens_gradient = (
            residual_grad
            + scale_one * weighted_one
            - inputs * scale_one**3 * jnp.mean(weighted_one * inputs, axis=-1, keepdims=True)
        )
        sums = lax.psum_scatter(
            jnp.concatenate([qkv_gradient, more], axis=1), "dev", scatter_dimension=0, tiled=True
        ).astype(F32)
        query_sums, key_sums, value_sums, more_sums = jnp.split(sums, [q_width, q_width + k_width, QKV], axis=1)
        first_sums = lax.psum_scatter(
            jnp.sum(normed_one_grad * inputs * scale_one, axis=0), "dev", scatter_dimension=0, tiled=True
        )
    return (
        layer_output,
        tokens_gradient,
        first_sums,
        query_sums,
        key_sums,
        value_sums,
        output_gradient,
        more_sums[:, EXPERTS],
        more_sums[:, :EXPERTS],
        gate_gradient,
        up_gradient,
        down_gradient,
    )


def solution(mesh):
    rows, whole = P("dev", None), P("dev")
    columns = P(None, "dev")
    return jax.shard_map(
        on_device,
        mesh=mesh,
        in_specs=(rows, whole, rows, rows, whole, rows, rows, rows, rows, whole, rows, columns, columns, rows, rows),
        out_specs=(rows, rows, whole, rows, rows, rows, rows, whole, rows, columns, columns, rows),
        check_vma=False,
    )
```

```python
import functools
import jax, jax.numpy as jnp
from jax import lax
from jax.experimental import pallas as pl
from jax.experimental.pallas import tpu as pltpu

MESH = pl.DeviceIdType.MESH


def place():
    me = lax.axis_index("dev")
    return lax.rem(me // 8, 4), lax.rem(me // 4, 2), lax.rem(me // 2, 2), lax.rem(me, 2)


def number(z, y, x, c):
    return ((z * 2 + y) * 2 + x) * 2 + c


def greet(partners):
    barrier = pltpu.get_barrier_semaphore()
    for partner in partners:
        pl.semaphore_signal(barrier, inc=1, device_id=(partner,), device_id_type=MESH)
    pl.semaphore_wait(barrier, len(partners))


def partners_of(z, y, x, c):
    return [
        number(z, y, x, 1 - c),
        number(z, y, 1 - x, c),
        number(z, 1 - y, x, c),
        number(lax.rem(z + 1, 4), y, x, c),
        number(lax.rem(z + 2, 4), y, x, c),
        number(lax.rem(z + 3, 4), y, x, c),
    ]


class Whole:
    scratch = [pltpu.SemaphoreType.DMA] + [
        pltpu.SemaphoreType.DMA(shape)
        for shape in ((2, 2, 4), (2, 4), (2, 3, 4), (2, 3, 4), (2, 4, 4), (2, 4, 4))
    ]

    def __init__(self, x_ref, o_ref, scratch):
        self.x_ref, self.o_ref = x_ref, o_ref
        self.local_sem, self.zs, self.zr, self.fs, self.fr, self.cs, self.cr = scratch
        self.z, self.y, self.x, self.c = z, y, x, c = place()
        self.rows, cols = x_ref.shape
        half = (cols // 256) * 128
        self.pieces = (pl.ds(0, half), pl.ds(half, cols - half))
        self.sibling = number(z, y, x, 1 - c)
        self.me = number(z, y, x, c)
        self.around = (number(z, 1 - y, x, c), number(z, y, 1 - x, c))
        self.far = ((1, 0), (0, 1))
        self.local = pltpu.make_async_copy(x_ref, self.there(self.me), self.local_sem)

    def turn(self, i):
        middle = i if i < 2 else 5 - i
        return jnp.where(self.z == 0, (4 - i) % 4, jnp.where(self.z == 3, i, middle))

    def there(self, block, p=None):
        at = pl.ds(pl.multiple_of(block * self.rows, 16), self.rows)
        return self.o_ref.at[at, :] if p is None else self.o_ref.at[at, self.pieces[p]]

    def copy(self, source, block, p, send_sem, recv_sem, target):
        return pltpu.make_async_remote_copy(
            src_ref=source, dst_ref=self.there(block, p), send_sem=send_sem, recv_sem=recv_sem,
            device_id=(target,), device_id_type=MESH)

    def block(self, k, fy=0, fx=0):
        return number(lax.rem(self.z + 4 - k, 4), (1 - self.y) if fy else self.y, (1 - self.x) if fx else self.x, self.c)

    def along(self, i, use):
        k = self.turn(i)
        zz = lax.rem(self.z + 4 - k, 4)
        for up, step in ((1, 1), (0, 3)):
            go = (zz <= self.z) & (self.z < 3) if up else (zz >= self.z) & (self.z > 0)

            @pl.when(go)
            def _(up=up, step=step):
                block = self.block(k)
                target = number(lax.rem(self.z + step, 4), self.y, self.x, self.c)
                for p in range(2):
                    source = self.x_ref.at[:, self.pieces[p]] if i == 0 else self.there(block, p)
                    use(self.copy(
                        source, block, p, self.zs.at[p, up, k], self.zr.at[p, lax.rem(k + step, 4)], target))

    def hop(self, p, n, k):
        block = self.block(k, *self.far[p]) if n == 2 else self.block(k)
        target = self.around[p] if n == 0 else self.around[1 - p]
        return self.copy(self.there(block, p), block, p, self.fs.at[p, n, k], self.fr.at[p, n, k], target)

    def across(self, p, n, k):
        fy, fx = ((0, 0), self.far[p], (1 - self.far[p][0], 1 - self.far[p][1]), (1, 1))[n]
        block = self.block(k, fy, fx)
        return self.copy(self.there(block, p), block, p, self.cs.at[p, n, k], self.cr.at[p, n, k], self.sibling)

    def start(self):
        self.local.start()
        self.along(0, lambda cp: cp.start())

    def one(self, i):
        k = self.turn(i)
        if i == 0:
            self.local.wait()
        else:
            block = self.block(k)
            for p in range(2):
                self.copy(self.there(block, p), block, p, self.zs.at[p, 0, 0], self.zr.at[p, k], self.sibling).wait_recv()
            self.along(i, lambda cp: cp.start())
        for p in range(2):
            self.hop(p, 0, k).start()
            self.hop(p, 1, k).start()
            self.across(p, 0, k).start()

    def two(self, i):
        k = self.turn(i)
        for p in range(2):
            self.hop(p, 0, k).wait_recv()
            self.hop(p, 2, k).start()
            self.across(p, 1, k).start()

    def three(self, i):
        k = self.turn(i)
        for n in (1, 2):
            for p in range(2):
                self.hop(p, n, k).wait_recv()
                self.across(p, n + 1, k).start()

    def end(self):
        for k in range(4):
            for p in range(2):
                for n in range(4):
                    self.across(p, n, k).wait_recv()

    def sent(self):
        for i in range(4):
            self.along(i, lambda cp: cp.wait_send())
        for k in range(4):
            for p in range(2):
                for n in range(3):
                    self.hop(p, n, k).wait_send()
                for n in range(4):
                    self.across(p, n, k).wait_send()


from jax.sharding import PartitionSpec as P

QUERY_HEADS = 24
KEY_HEADS = 8
HEAD_DIM = 64
GROUP = QUERY_HEADS // KEY_HEADS
TOP = 8
EXPERTS = 32
MAXDOC = 2000
EPSILON = 1e-06
UNPICKED = 1e9
CAPACITY = 72
MASKED = -1e30
QKV = (QUERY_HEADS + 2 * KEY_HEADS) * HEAD_DIM
F32 = jnp.float32
BF16 = jnp.bfloat16


def meshed():
    return lax.axis_size("dev") == 32


def dims(a, b, ca, cb):
    return lax.dot_general(a, b, (((ca,), (cb,)), ((), ())), preferred_element_type=F32)


class Window:
    scratch = [pltpu.SemaphoreType.DMA((2,)), pltpu.SemaphoreType.DMA((9,)), pltpu.SemaphoreType.DMA((9,))]

    def __init__(self, rows, kv_ref, out, scratch):
        self.rows, self.kv_ref, self.out = rows, kv_ref, out
        self.lsem, self.ss, self.rs = scratch
        self.z, self.y, self.x, self.c = place()
        self.p = self.y * 2 + self.x
        self.sibling = number(self.z, self.y, self.x, 1 - self.c)
        self.near = [(self.z * 4 + lax.rem(self.p + d, 4)) * 2 + self.c for d in (1, 2, 3)]
        self.own_in = pltpu.make_async_copy(kv_ref, self.slot(4, self.c), self.lsem.at[0])
        self.stand_in = pltpu.make_async_copy(kv_ref, self.slot(0, self.c), self.lsem.at[1])
        self.to_up = self.copy(kv_ref, 0, 0, number(lax.rem(self.z + 1, 4), self.y, self.x, self.c))

    def slot(self, s, core):
        return self.out.at[:, pl.ds(pl.multiple_of((2 * s + core) * self.rows, 16), self.rows), :]

    def copy(self, source, s, n, target):
        return pltpu.make_async_remote_copy(
            src_ref=source, dst_ref=self.slot(s, self.c), send_sem=self.ss.at[n], recv_sem=self.rs.at[n],
            device_id=(target,), device_id_type=MESH)

    def own_near(self, d):
        return self.copy(self.kv_ref, 4 - d, d, self.near[d - 1])

    def across(self, s):
        source = self.kv_ref if s == 4 else self.slot(s, self.c)
        return self.copy(source, s, {4: 4, 0: 5}.get(s, 9 - s), self.sibling)

    def start(self):
        self.own_in.start()

        @pl.when(self.z < 3)
        def _():
            self.to_up.start()

        @pl.when(self.z == 0)
        def _():
            self.stand_in.start()

        for d in (1, 3, 2):
            @pl.when(self.p + d < 4)
            def _(d=d):
                self.own_near(d).start()
        self.across(4).start()

    def previous(self):
        @pl.when(self.z == 0)
        def _():
            self.stand_in.wait()

        @pl.when(self.z > 0)
        def _():
            self.to_up.wait_recv()

        for d in (3, 1, 2):
            @pl.when(self.p + d >= 4)
            def _(d=d):
                self.copy(self.slot(0, self.c), 4 - d, d, self.near[d - 1]).start()
        self.across(0).start()

    def pass_on(self):
        for d in (1, 3, 2):
            self.own_near(d).wait_recv()
            self.across(4 - d).start()

    def end(self):
        for s in range(5):
            pltpu.make_async_remote_copy(
                src_ref=self.kv_ref, dst_ref=self.slot(s, 1 - self.c), send_sem=self.ss.at[0],
                recv_sem=self.rs.at[{4: 4, 0: 5}.get(s, 9 - s)], device_id=(self.sibling,), device_id_type=MESH).wait_recv()
        self.own_in.wait()

    def sent(self):
        @pl.when(self.z < 3)
        def _():
            self.to_up.wait_send()

        for d in (1, 2, 3):
            self.own_near(d).wait_send()
        for s in range(5):
            self.across(s).wait_send()


def window_of(kv):
    rows = kv.shape[1]
    devices = lax.axis_size("dev")
    back = (MAXDOC + rows - 2) // rows
    parts = [
        lax.ppermute(kv, "dev", [(i - d, i) for i in range(d, devices)]) for d in range(back, 0, -1)
    ]
    return jnp.concatenate(parts + [kv, jnp.zeros_like(kv)], axis=1)


class Unwindow:
    @staticmethod
    def scratch(rows, width):
        return [
            pltpu.VMEM((5, 2, rows, width), BF16),
            pltpu.VMEM((3, 2, rows, width), BF16),
            pltpu.VMEM((2, rows, width), BF16),
            pltpu.SemaphoreType.DMA((9,)), pltpu.SemaphoreType.DMA((9,)),
        ]

    n_scratch = 5
    order = (3, 1, 2, 0, 4)

    def __init__(self, rows, grads, o_ref, scratch):
        self.rows, self.grads, self.o_ref = rows, grads, o_ref
        self.got, self.near_got, self.far, self.ss, self.rs = scratch
        self.z, self.y, self.x, self.c = place()
        self.p = self.y * 2 + self.x
        self.sibling = number(self.z, self.y, self.x, 1 - self.c)
        self.to_down = pltpu.make_async_remote_copy(
            src_ref=self.got.at[0], dst_ref=self.far, send_sem=self.ss.at[8], recv_sem=self.rs.at[8],
            device_id=(number(lax.rem(self.z + 3, 4), self.y, self.x, self.c),), device_id_type=MESH)

    def to_sibling(self, s):
        at = pl.ds(pl.multiple_of((2 * s + 1 - self.c) * self.rows, 16), self.rows)
        return pltpu.make_async_remote_copy(
            src_ref=self.grads.at[:, at, :], dst_ref=self.got.at[s], send_sem=self.ss.at[s], recv_sem=self.rs.at[s],
            device_id=(self.sibling,), device_id_type=MESH)

    def to_owner(self, d):
        owner = (self.z * 4 + lax.rem(self.p + 4 - d, 4)) * 2 + self.c
        return pltpu.make_async_remote_copy(
            src_ref=self.got.at[4 - d], dst_ref=self.near_got.at[d - 1], send_sem=self.ss.at[4 + d], recv_sem=self.rs.at[4 + d],
            device_id=(owner,), device_id_type=MESH)

    def rowwise(self, body):
        for h in range(2):
            def step(i, _, h=h):
                body(h, pl.multiple_of(i * 32, 32))
                return 0
            lax.fori_loop(0, self.rows // 32, step, 0)

    def start(self):
        for s in self.order:
            self.to_sibling(s).start()

    def sums(self):
        for s in self.order:
            self.to_sibling(s).wait_recv()
            first = (2 * s + self.c) * self.rows

            def both(h, r, s=s, first=first):
                at = pl.ds(r, 32)
                mine = self.grads[h, pl.ds(pl.multiple_of(first + r, 32), 32), :]
                total = self.got[s, h, at, :].astype(F32) + mine.astype(F32)
                if s == 4:
                    self.o_ref[h, at, :] = total
                else:
                    self.got[s, h, at, :] = total.astype(BF16)
            self.rowwise(both)
            if 0 < s < 4:
                self.to_owner(4 - s).start()

    def near(self):
        for d in (1, 3, 2):
            self.to_owner(d).wait_recv()

            @pl.when(self.p + d < 4)
            def _(d=d):
                def body(h, r):
                    at = pl.ds(r, 32)
                    self.o_ref[h, at, :] += self.near_got[d - 1, h, at, :].astype(F32)
                self.rowwise(body)

            @pl.when(self.p + d >= 4)
            def _(d=d):
                def body(h, r):
                    at = pl.ds(r, 32)
                    total = self.got[0, h, at, :].astype(F32) + self.near_got[d - 1, h, at, :].astype(F32)
                    self.got[0, h, at, :] = total.astype(BF16)
                self.rowwise(body)

        @pl.when(self.z > 0)
        def _():
            self.to_down.start()

    def end(self):
        @pl.when(self.z < 3)
        def _():
            self.to_down.wait_recv()

            def body(h, r):
                at = pl.ds(r, 32)
                self.o_ref[h, at, :] += self.far[h, at, :].astype(F32)
            self.rowwise(body)

        @pl.when(self.z > 0)
        def _():
            self.to_down.wait_send()

        for s in range(5):
            self.to_sibling(s).wait_send()
        for d in (1, 2, 3):
            self.to_owner(d).wait_send()


def unwindow(grads):
    rows = grads.shape[1] // 10
    devices = lax.axis_size("dev")
    back = (MAXDOC + rows - 2) // rows
    total = grads[:, back * rows : (back + 1) * rows].astype(F32)
    for d in range(1, back + 1):
        piece = grads[:, (back - d) * rows : (back - d + 1) * rows]
        moved = lax.ppermute(piece, "dev", [(i, i - d) for i in range(d, devices)])
        total = total + moved.astype(F32)
    return total


def make_bias(bias, lo_ref, chunks, rows):
    def fill(ch, _):
        at = pl.ds(pl.multiple_of(ch * rows, rows), rows)
        relative = lax.broadcasted_iota(jnp.int32, (rows, rows), 0) + (ch - (chunks - 1)) * rows
        query = lax.broadcasted_iota(jnp.int32, (rows, rows), 1)
        allowed = (relative <= query) & (relative >= lo_ref[...])
        bias[at, :] = jnp.where(allowed, 0.0, MASKED)
        return 0
    lax.fori_loop(0, chunks, fill, 0)


def side_by_side(ref, half):
    first = half * GROUP
    return jnp.concatenate(
        [ref[(first + g) * HEAD_DIM : (first + g + 1) * HEAD_DIM, :] for g in range(GROUP)], axis=1
    )


def stats_of(ref, half):
    return jnp.concatenate([ref[0, half * GROUP + g : half * GROUP + g + 1, :] for g in range(GROUP)], axis=1)


def attend_pair(chunks, rows, off, q_ref, kv_ref, o_ref, lse_ref, bias, between):
    lse_ref[...] = jnp.zeros_like(lse_ref)
    width = GROUP * rows
    for half in range(2):
        lanes = slice(half * HEAD_DIM, (half + 1) * HEAD_DIM)
        queries = side_by_side(q_ref, half)

        def chunk(i, carry, lanes=lanes, queries=queries):
            ch = chunks - 1 - i
            at = pl.ds(pl.multiple_of((ch + off) * rows, rows), rows)
            key, value = kv_ref[0, at, lanes], kv_ref[1, at, lanes]
            shift = bias[pl.ds(pl.multiple_of(ch * rows, rows), rows), :]
            top, total, mixed = carry
            score = dims(key, queries, 1, 0) + jnp.concatenate([shift] * GROUP, axis=1)
            new_top = jnp.maximum(top, jnp.max(score, axis=0, keepdims=True))
            weight = jnp.exp(score - new_top)
            fade = jnp.exp(top - new_top)
            total = total * fade + jnp.sum(weight, axis=0, keepdims=True)
            mixed = mixed * fade + dims(value, weight.astype(BF16), 0, 0)
            return new_top, total, mixed

        start = (jnp.full((1, width), MASKED, F32), jnp.zeros((1, width), F32), jnp.zeros((HEAD_DIM, width), F32))
        top, total, mixed = lax.fori_loop(0, chunks, chunk, start, unroll=3)
        mixed = (mixed / total).astype(BF16)
        lse = top + jnp.log(total)
        for g in range(GROUP):
            n = half * GROUP + g
            o_ref[n * HEAD_DIM : (n + 1) * HEAD_DIM, :] = mixed[:, g * rows : (g + 1) * rows]
            lse_ref[0, n : n + 1, :] = lse[:, g * rows : (g + 1) * rows]
        between(half)


def attend_kernel(chunks, rows, off_ref, lo_ref, q_ref, kv_ref, o_ref, lse_ref, bias):
    @pl.when(pl.program_id(0) == 0)
    def _():
        make_bias(bias, lo_ref, chunks, rows)

    attend_pair(chunks, rows, off_ref[0], q_ref, kv_ref, o_ref, lse_ref, bias, lambda half: None)


def attend_back_pair(
    chunks, rows, off, cos_ref, sin_ref, q_ref, kv_ref, g_ref, lse_ref, out_ref, dq_ref, dkv_ref, bias, between
):
    unused = pl.ds(pl.multiple_of((1 - off) * chunks * rows, rows), rows)
    dkv_ref[:, unused, :] = jnp.zeros((2, rows, 2 * HEAD_DIM), BF16)
    for half in range(2):
        lanes = slice(half * HEAD_DIM, (half + 1) * HEAD_DIM)
        queries, grads = side_by_side(q_ref, half), side_by_side(g_ref, half)
        lse = stats_of(lse_ref, half)
        mixed = side_by_side(out_ref, half).astype(F32)
        delta = jnp.sum(mixed * grads.astype(F32), axis=0, keepdims=True)

        def chunk(ch, query_grad, lanes=lanes, queries=queries, grads=grads, lse=lse, delta=delta):
            at = pl.ds(pl.multiple_of((ch + off) * rows, rows), rows)
            key, value = kv_ref[0, at, lanes], kv_ref[1, at, lanes]
            shift = bias[pl.ds(pl.multiple_of(ch * rows, rows), rows), :]
            score = dims(key, queries, 1, 0) + jnp.concatenate([shift] * GROUP, axis=1)
            weight = jnp.exp(score - lse)
            score_grad = (weight * (dims(value, grads, 1, 0) - delta)).astype(BF16)
            dkv_ref[0, at, lanes] = dims(score_grad, queries, 1, 1).astype(BF16)
            dkv_ref[1, at, lanes] = dims(weight.astype(BF16), grads, 1, 1).astype(BF16)
            return query_grad + dims(key, score_grad, 0, 0)

        done = lax.fori_loop(0, chunks, chunk, jnp.zeros((HEAD_DIM, GROUP * rows), F32), unroll=3)
        done = done * (HEAD_DIM**-0.5)
        cosine, sine = cos_ref[...], sin_ref[...]
        for g in range(GROUP):
            grad = done[:, g * rows : (g + 1) * rows]
            u, w = grad[: HEAD_DIM // 2], grad[HEAD_DIM // 2 :]
            n = (half * GROUP + g) * HEAD_DIM
            dq_ref[n : n + HEAD_DIM // 2, :] = (u * cosine + w * sine).astype(BF16)
            dq_ref[n + HEAD_DIM // 2 : n + HEAD_DIM, :] = (w * cosine - u * sine).astype(BF16)
        between(half)


def attend_back_kernel(
    chunks, rows, off_ref, lo_ref, cos_ref, sin_ref, q_ref, kv_ref, g_ref, lse_ref, out_ref, dq_ref, dkv_ref, bias
):
    @pl.when(pl.program_id(0) == 0)
    def _():
        make_bias(bias, lo_ref, chunks, rows)

    attend_back_pair(
        chunks, rows, off_ref[0], cos_ref, sin_ref, q_ref, kv_ref, g_ref, lse_ref, out_ref, dq_ref, dkv_ref, bias,
        lambda half: None,
    )


def attention_specs(rows, span):
    width = 2 * GROUP * HEAD_DIM
    return dict(
        smem=pl.BlockSpec(memory_space=pltpu.SMEM),
        row=pl.BlockSpec((1, rows), lambda j: (0, 0)),
        table=pl.BlockSpec((HEAD_DIM // 2, rows), lambda j: (0, 0)),
        query=pl.BlockSpec((width, rows), lambda j: (j, 0)),
        kv=pl.BlockSpec((2, span, 2 * HEAD_DIM), lambda j: (0, 0, j)),
        stat=pl.BlockSpec((1, 8, rows), lambda j: (j, 0, 0)),
    )


def attend(query_t, window, offset, lo):
    rows, span = query_t.shape[1], window.shape[1]
    chunks = span // rows - 1
    s = attention_specs(rows, span)
    return pl.pallas_call(
        functools.partial(attend_kernel, chunks, rows),
        grid=(KEY_HEADS // 2,),
        in_specs=[s["smem"], s["row"], s["query"], s["kv"]],
        out_specs=[s["query"], s["stat"]],
        out_shape=[
            jax.ShapeDtypeStruct(query_t.shape, BF16),
            jax.ShapeDtypeStruct((KEY_HEADS // 2, 8, rows), F32),
        ],
        scratch_shapes=[pltpu.VMEM((chunks * rows, rows), F32)],
        compiler_params=pltpu.CompilerParams(vmem_limit_bytes=40 * 2**20),
        cost_estimate=pl.CostEstimate(flops=7 * 10**9, bytes_accessed=8 * 10**6, transcendentals=15 * 10**6),
        name="attend",
    )(offset.reshape(1), lo, query_t, window)


def attend_back(query_t, window, offset, lo, grad_t, lse, attended_t, cos_t, sin_t):
    rows, span = query_t.shape[1], window.shape[1]
    chunks = span // rows - 1
    s = attention_specs(rows, span)
    return pl.pallas_call(
        functools.partial(attend_back_kernel, chunks, rows),
        grid=(KEY_HEADS // 2,),
        in_specs=[s["smem"], s["row"], s["table"], s["table"], s["query"], s["kv"], s["query"], s["stat"], s["query"]],
        out_specs=[s["query"], s["kv"]],
        out_shape=[
            jax.ShapeDtypeStruct(query_t.shape, BF16),
            jax.ShapeDtypeStruct(window.shape, BF16),
        ],
        scratch_shapes=[pltpu.VMEM((chunks * rows, rows), F32)],
        compiler_params=pltpu.CompilerParams(vmem_limit_bytes=40 * 2**20),
        cost_estimate=pl.CostEstimate(flops=18 * 10**9, bytes_accessed=16 * 10**6, transcendentals=15 * 10**6),
        name="attend_back",
    )(offset.reshape(1), lo, cos_t, sin_t, query_t, window, grad_t, lse, attended_t)


def hits(slot_ref, slots):
    width = slot_ref.shape[-1]
    return slot_ref[0] == lax.broadcasted_iota(jnp.int32, (slots, width), 0)


def dispatch_kernel(slot_ref, x_ref, u_ref, xo_ref, uo_ref):
    chosen = jnp.where(hits(slot_ref, xo_ref.shape[0]), 1.0, 0.0).astype(BF16)
    xo_ref[...] = dims(chosen, x_ref[...], 1, 0).astype(BF16)
    uo_ref[...] = dims(chosen, u_ref[...], 1, 0).astype(BF16)


def dispatch(slot, normed, upstream, slots):
    pairs, _, width = slot.shape
    model = normed.shape[1]
    return pl.pallas_call(
        dispatch_kernel,
        grid=(pairs,),
        in_specs=[
            pl.BlockSpec((1, 1, width), lambda i: (i, 0, 0)),
            pl.BlockSpec((width, model), lambda i: (i, 0)),
            pl.BlockSpec((width, model), lambda i: (i, 0)),
        ],
        out_specs=[pl.BlockSpec((slots, model), lambda i: (i, 0))] * 2,
        out_shape=[jax.ShapeDtypeStruct((pairs * slots, model), BF16)] * 2,
        compiler_params=pltpu.CompilerParams(vmem_limit_bytes=40 * 2**20),
        cost_estimate=pl.CostEstimate(flops=2 * 10**9, bytes_accessed=65 * 10**6, transcendentals=0),
        name="dispatch",
    )(slot, normed, upstream)


def combine_kernel(slot_ref, r_ref, o_ref):
    chosen = jnp.where(hits(slot_ref, r_ref.shape[0]), 1.0, 0.0).astype(BF16)
    o_ref[...] = dims(chosen, r_ref[...], 0, 0).astype(BF16)


def combine(slot, rows, slots):
    pairs, _, width = slot.shape
    model = rows.shape[1]
    return pl.pallas_call(
        combine_kernel,
        grid=(pairs,),
        in_specs=[
            pl.BlockSpec((1, 1, width), lambda i: (i, 0, 0)),
            pl.BlockSpec((slots, model), lambda i: (i, 0)),
        ],
        out_specs=pl.BlockSpec((width, model), lambda i: (i, 0)),
        out_shape=jax.ShapeDtypeStruct((pairs * width, model), BF16),
        compiler_params=pltpu.CompilerParams(vmem_limit_bytes=40 * 2**20),
        cost_estimate=pl.CostEstimate(flops=10**9, bytes_accessed=33 * 10**6, transcendentals=0),
        name="combine",
    )(slot, rows)


SLOTS = 80


def far_first(i):
    return jnp.where(i == 0, 2, jnp.where(i == 3, 0, 2 * i - 1))


def greet_all():
    me = lax.axis_index("dev")
    barrier = pltpu.get_barrier_semaphore()

    def signal(d, _):
        pl.semaphore_signal(barrier, inc=1, device_id=(lax.rem(me + d, 32),), device_id_type=MESH)
        return 0
    lax.fori_loop(1, 32, signal, 0)
    pl.semaphore_wait(barrier, 31)


class Swap:
    def __init__(self, source, into, ss, rs):
        self.me = lax.axis_index("dev")
        self.source, self.into, self.ss, self.rs = source, into, ss, rs

    def copy(self, d):
        target = lax.rem(self.me + d, 32)
        return pltpu.make_async_remote_copy(
            src_ref=self.source(target), dst_ref=self.into.at[self.me], send_sem=self.ss.at[d], recv_sem=self.rs.at[d],
            device_id=(target,), device_id_type=MESH)

    def start(self):
        def one(d, _):
            self.copy(d).start()
            return 0
        lax.fori_loop(1, 32, one, 0)
        self.into[self.me] = self.source(self.me)[...]

    def wait_recv(self):
        def one(d, _):
            self.copy(d).wait_recv()
            return 0
        lax.fori_loop(1, 32, one, 0)

    def wait_send(self):
        def one(d, _):
            self.copy(d).wait_send()
            return 0
        lax.fori_loop(1, 32, one, 0)


def in_plane(y, x, c):
    return (y * 2 + x) * 2 + c


def chosen_rows(slots_ref, block, expert):
    row = slots_ref[block, pl.ds(expert, 1), :]
    return row == lax.broadcasted_iota(jnp.int32, (SLOTS, row.shape[1]), 0).astype(F32)


def greet_near():
    z, y, x, c = place()
    greet(
        [number(z, y, x, 1 - c)]
        + [number(z, 1 - y, x, cc) for cc in (c, 1 - c)]
        + [number(z, y, 1 - x, cc) for cc in (c, 1 - c)]
        + [number(z, 1 - y, 1 - x, c)]
        + [number(lax.rem(z + d, 4), y, x, c) for d in (1, 2, 3)]
    )


class Forth:
    scratch = staticmethod(lambda rows, half: [
        pltpu.VMEM((2, 2, 4, rows, half), BF16),
        pltpu.VMEM((2, 2, 4, 4, SLOTS, half), BF16),
        pltpu.SemaphoreType.DMA((2, 2, 4)), pltpu.SemaphoreType.DMA((2, 4)),
        pltpu.SemaphoreType.DMA((2, 4)), pltpu.SemaphoreType.DMA((2, 4)),
        pltpu.SemaphoreType.DMA((2, 2, 4, 4)), pltpu.SemaphoreType.DMA((2, 2, 4, 3)), pltpu.SemaphoreType.DMA((2,)),
    ])
    n_scratch = 9

    def __init__(self, x_ref, slots_ref, xi, scratch):
        self.x_ref, self.slots_ref, self.xi = x_ref, slots_ref, xi
        self.land, self.stage, self.zs, self.zr, self.fs, self.fr, self.cs, self.cr, self.own_sem = scratch
        self.z, self.y, self.x, self.c = place()
        half = x_ref.shape[1] // 2
        self.cols = [pl.ds(0, half), pl.ds(half, half)]

    def turn(self, i):
        middle = jnp.where(i < 2, i, 5 - i)
        return jnp.where(self.z == 0, lax.rem(4 - i, 4), jnp.where(self.z == 3, i, middle))

    def to_z(self, p, up, k, own=False):
        step = 1 if up else 3
        source = self.x_ref.at[:, self.cols[p]] if own else self.land.at[p, 0, k]
        there = lax.rem(k + step, 4)
        return pltpu.make_async_remote_copy(
            src_ref=source, dst_ref=self.land.at[p, 0, there],
            send_sem=self.zs.at[p, int(up), k], recv_sem=self.zr.at[p, there],
            device_id=(number(lax.rem(self.z + step, 4), self.y, self.x, self.c),), device_id_type=MESH)

    def hop(self, p, k):
        z, y, x, c = self.z, self.y, self.x, self.c
        beside = number(z, 1 - y, x, c) if p == 0 else number(z, y, 1 - x, c)
        return pltpu.make_async_remote_copy(
            src_ref=self.land.at[p, 0, k], dst_ref=self.land.at[p, 1, k],
            send_sem=self.fs.at[p, k], recv_sem=self.fr.at[p, k], device_id=(beside,), device_id_type=MESH)

    def block(self, p, h, k):
        zz = lax.rem(self.z + 4 - k, 4)
        if p == 0:
            return number(zz, (1 - self.y) if h else self.y, self.x, self.c)
        return number(zz, self.y, (1 - self.x) if h else self.x, self.c)

    def who(self, p):
        y, x, c = self.y, self.x, self.c
        ay, ax = (y, 1 - x) if p == 0 else (1 - y, x)
        return [(y, x, 1 - c), (ay, ax, c), (ay, ax, 1 - c), (y, x, c)]

    def slots_at(self, p, h, k):
        return self.xi.at[pl.ds(pl.multiple_of(self.block(p, h, k) * SLOTS, 16), SLOTS), self.cols[p]]

    def served(self, p, h, k, t):
        return pltpu.make_async_remote_copy(
            src_ref=self.stage.at[p, h, k, t], dst_ref=self.slots_at(p, h, k),
            send_sem=self.cs.at[p, h, k, t], recv_sem=self.cr.at[p, h, k, t],
            device_id=(number(self.z, *self.who(p)[t]),), device_id_type=MESH)

    def kept(self, p, h, k):
        return pltpu.make_async_copy(self.stage.at[p, h, k, 3], self.slots_at(p, h, k), self.cs.at[p, h, k, 3])

    def serve(self, p, h, k):
        block = self.block(p, h, k)
        source = self.land[p, h, k]
        for t, to in enumerate(self.who(p)):
            chosen = jnp.where(chosen_rows(self.slots_ref, block, in_plane(*to)), 1.0, 0.0).astype(BF16)
            self.stage[p, h, k, t] = dims(chosen, source, 1, 0).astype(BF16)
            if t < 3:
                self.served(p, h, k, t).start()
            else:
                self.kept(p, h, k).start()

    def own(self, p):
        return pltpu.make_async_copy(self.x_ref.at[:, self.cols[p]], self.land.at[p, 0, 0], self.own_sem.at[p])

    def along(self, i, use):
        k = self.turn(i)
        zz = lax.rem(self.z + 4 - k, 4)
        for p in range(2):
            @pl.when((zz < self.z) & (self.z < 3))
            def _(p=p):
                use(self.to_z(p, True, k))

            @pl.when((zz > self.z) & (self.z > 0))
            def _(p=p):
                use(self.to_z(p, False, k))

    def along_own(self, use):
        for p in range(2):
            @pl.when(self.z < 3)
            def _(p=p):
                use(self.to_z(p, True, 0, own=True))

            @pl.when(self.z > 0)
            def _(p=p):
                use(self.to_z(p, False, 0, own=True))

    def start(self):
        for p in range(2):
            self.own(p).start()
        self.along_own(lambda cp: cp.start())

    def come(self, i):
        k = self.turn(i)
        for p in range(2):
            self.to_z(p, True, lax.rem(k + 3, 4)).wait_recv()
        self.along(i, lambda cp: cp.start())

    def one(self, i, come=True):
        k = self.turn(i)

        @pl.when(i == 0)
        def _():
            for p in range(2):
                self.own(p).wait()

        if come:
            @pl.when(i > 0)
            def _():
                self.come(i)

        for p in range(2):
            self.hop(p, k).start()
        for p in range(2):
            self.serve(p, 0, k)

    def two(self, i):
        k = self.turn(i)
        for p in range(2):
            self.hop(p, k).wait_recv()
            self.serve(p, 1, k)

    def arrived(self, group, i):
        k = self.turn(i)

        @pl.when(group == 0)
        def _():
            for p in range(2):
                self.served(p, 0, k, 0).wait_recv()
                self.kept(p, 0, k).wait()

        @pl.when(group == 1)
        def _():
            self.kept(0, 1, k).wait()
            self.served(0, 1, k, 0).wait_recv()
            self.served(1, 0, k, 1).wait_recv()
            self.served(1, 0, k, 2).wait_recv()

        @pl.when(group == 2)
        def _():
            self.kept(1, 1, k).wait()
            self.served(1, 1, k, 0).wait_recv()
            self.served(0, 0, k, 1).wait_recv()
            self.served(0, 0, k, 2).wait_recv()

        @pl.when(group == 3)
        def _():
            for p in range(2):
                self.served(p, 1, k, 1).wait_recv()
                self.served(p, 1, k, 2).wait_recv()

    def chip(self, group, i):
        dy, dx = lax.rem(group, 2), group // 2
        zz = lax.rem(self.z + 4 - self.turn(i), 4)
        yy = jnp.where(dy == 1, 1 - self.y, self.y)
        xx = jnp.where(dx == 1, 1 - self.x, self.x)
        return (zz * 2 + yy) * 2 + xx

    def sent(self):
        self.along_own(lambda cp: cp.wait_send())

        def each(i, _):
            k = self.turn(i)
            self.along(i, lambda cp: cp.wait_send())
            for p in range(2):
                self.hop(p, k).wait_send()
                for h in range(2):
                    for t in range(3):
                        self.served(p, h, k, t).wait_send()
            return 0
        lax.fori_loop(0, 4, each, 0)


BEFORE_UNIT = {0: ("o1", "t0", "o2", "t1"), 4: ("o3", "t2"), 8: ("t3",)}


def experts_kernel(
    x_ref, gates_ref, slots_ref, ui_ref, wg_in, wu_in, wd_in,
    xi_out, dx_out, y_out, hg_out, dg_out, du_out, gg_ref,
    gates, xi, ubuf, dx_buf, y_buf, hg_ref, dg_ref, du_ref, wg_ref, wu_ref, wd_ref, wgt, wut, wdt,
    gs, gr, usem, xsem, osem, wsem, *scratch,
):
    z, y, x, c = place()
    rows = x_ref.shape[0]
    greet_all()
    swap = Swap(lambda t: gates_ref.at[t], gates, gs, gr)
    ag = Forth(x_ref, slots_ref, xi, scratch)
    ag.start()

    def chip_of(u):
        return ag.chip(lax.rem(u, 4), u // 4)

    def at_chip(u):
        return pl.ds(pl.multiple_of(chip_of(u) * 2 * SLOTS, 16), 2 * SLOTS)

    def load_up(u):
        return pltpu.make_async_copy(ui_ref.at[at_chip(u), :], ubuf.at[lax.rem(u, 2)], usem.at[lax.rem(u, 2)])

    load_up(0).start()
    swap.start()
    loads = [
        pltpu.make_async_copy(source, into, wsem.at[i])
        for i, (source, into) in enumerate(((wg_in, wg_ref), (wu_in, wu_ref), (wd_in, wd_ref)))
    ]
    for cp in loads:
        cp.start()
    ag.one(0)
    for cp, source, into in zip(loads, (wg_ref, wu_ref, wd_ref), (wgt, wut, wdt), strict=True):
        cp.wait()
        into[...] = source[...].T
    swap.wait_recv()

    def store(n, buf, out, u):
        return pltpu.make_async_copy(buf.at[lax.rem(u, 2)], out.at[at_chip(u), :], osem.at[n, lax.rem(u, 2)])

    def stores(u):
        return [store(0, dx_buf, dx_out, u), store(1, y_buf, y_out, u)]

    def keep(u):
        return [
            pltpu.make_async_copy(held.at[at_chip(u), :], out.at[at_chip(u), :], xsem.at[i, u])
            for i, (held, out) in enumerate(((xi, xi_out), (hg_ref, hg_out), (dg_ref, dg_out), (du_ref, du_out)))
        ]

    def unit(u):
        slot = lax.rem(u, 2)
        chip = chip_of(u)

        @pl.when(u < 15)
        def _():
            load_up(u + 1).start()

        ag.arrived(lax.rem(u, 4), u // 4)

        @pl.when(u >= 2)
        def _():
            for s in stores(u - 2):
                s.wait()

        load_up(u).wait()
        at = at_chip(u)
        expert = in_plane(y, x, c)
        picks, gate = [], []
        for core in range(2):
            block = chip * 2 + core
            hit = chosen_rows(slots_ref, block, expert)
            picks.append(hit)
            gate_row = jnp.concatenate([gates[block, 0:1, :], gates[block, 1:2, :]], axis=1)
            gate.append(jnp.sum(jnp.where(hit, gate_row, 0.0), axis=1, keepdims=True))
        gate_of_slot = jnp.concatenate(gate, axis=0)
        hidden_up = dims(ubuf[slot], wdt[...], 1, 0)
        rows_in = xi[at, :]
        gate_in = dims(rows_in, wg_ref[...], 1, 0)
        up_in = dims(rows_in, wu_ref[...], 1, 0)
        sig = 1.0 / (1.0 + jnp.exp(-gate_in))
        silu = gate_in * sig
        hidden = (silu * up_in).astype(BF16).astype(F32)
        gated = (hidden * gate_of_slot).astype(BF16)
        hidden_grad = hidden_up * gate_of_slot
        gate_back = (hidden_grad * up_in * sig * (1.0 + gate_in * (1.0 - sig))).astype(BF16)
        up_back = (hidden_grad * silu).astype(BF16)
        hg_ref[at, :] = gated
        dg_ref[at, :] = gate_back
        du_ref[at, :] = up_back
        dx_buf[slot] = (dims(gate_back, wgt[...], 1, 0) + dims(up_back, wut[...], 1, 0)).astype(BF16)
        y_buf[slot] = dims(gated, wd_ref[...], 1, 0).astype(BF16)
        gate_grad = jnp.sum(hidden * hidden_up, axis=1, keepdims=True)
        for core in range(2):
            block = chip * 2 + core
            row = jnp.sum(jnp.where(picks[core], gate_grad[core * SLOTS : (core + 1) * SLOTS], 0.0), axis=0, keepdims=True)
            gg_ref[block, 0:1, :] = row[:, :128]
            gg_ref[block, 1:2, :] = row[:, 128:]
        for s in stores(u):
            s.start()
        for s in keep(u):
            s.start()

    step = {}
    for i in range(4):
        step[f"o{i}"] = functools.partial(ag.one, jnp.int32(i))
        step[f"c{i}"] = functools.partial(ag.come, jnp.int32(i))
        step[f"s{i}"] = functools.partial(ag.one, jnp.int32(i), False)
        step[f"t{i}"] = functools.partial(ag.two, jnp.int32(i))

    def each(u, _):
        for when, names in BEFORE_UNIT.items():
            @pl.when(u == when)
            def _(names=names):
                for name in names:
                    step[name]()

        unit(u)
        return 0

    lax.fori_loop(0, 16, each, 0)
    for u in (14, 15):
        for s in stores(u):
            s.wait()

    def last(u, _):
        for s in keep(u):
            s.wait()
        return 0
    lax.fori_loop(0, 16, last, 0)
    ag.sent()
    swap.wait_send()


def run_experts(normed, gates, slots, ui, gate_weight, up_weight, down_weight):
    rows, model = normed.shape
    ff = gate_weight.shape[1]
    n = 32 * SLOTS
    hbm, vmem = pl.BlockSpec(memory_space=pl.ANY), pl.BlockSpec(memory_space=pltpu.VMEM)
    dma = pltpu.SemaphoreType.DMA
    long = jax.ShapeDtypeStruct((n, model), BF16)
    short = jax.ShapeDtypeStruct((n, ff), BF16)
    return pl.pallas_call(
        experts_kernel,
        in_specs=[hbm, vmem, vmem, hbm, hbm, hbm, hbm],
        out_specs=[hbm] * 6 + [vmem],
        out_shape=[long] * 3 + [short] * 3 + [jax.ShapeDtypeStruct((32, 8, 128), F32)],
        scratch_shapes=[
            pltpu.VMEM((32, 8, 128), F32),
            pltpu.VMEM((n, model), BF16),
            pltpu.VMEM((2, 2 * SLOTS, model), BF16),
            pltpu.VMEM((2, 2 * SLOTS, model), BF16),
            pltpu.VMEM((2, 2 * SLOTS, model), BF16),
            pltpu.VMEM((n, ff), BF16), pltpu.VMEM((n, ff), BF16), pltpu.VMEM((n, ff), BF16),
            pltpu.VMEM((model, ff), BF16), pltpu.VMEM((model, ff), BF16), pltpu.VMEM((ff, model), BF16),
            pltpu.VMEM((ff, model), BF16), pltpu.VMEM((ff, model), BF16), pltpu.VMEM((model, ff), BF16),
            dma((32,)), dma((32,)), dma((2,)), dma((4, 16)), dma((2, 2)), dma((3,)),
        ] + Forth.scratch(rows, model // 2),
        compiler_params=pltpu.CompilerParams(collective_id=13, has_side_effects=True, vmem_limit_bytes=56 * 2**20),
        name="experts",
    )(normed, gates, slots, ui, gate_weight, up_weight, down_weight)


class Back:
    scratch = staticmethod(lambda rows, half: [
        pltpu.VMEM((2, 2, 4, SLOTS, half), BF16),
        pltpu.VMEM((2, 3, 2, 4, SLOTS, half), BF16),
        pltpu.VMEM((2, 4, rows, half), BF16),
        pltpu.VMEM((2, 4, rows, half), BF16),
        pltpu.VMEM((2, 4, rows, half), BF16),
        pltpu.VMEM((2, 4, rows, half), BF16),
        pltpu.SemaphoreType.DMA((2, 2, 4)),
        pltpu.SemaphoreType.DMA((2, 3, 2, 4)), pltpu.SemaphoreType.DMA((2, 3, 2, 4)),
        pltpu.SemaphoreType.DMA((2, 4)), pltpu.SemaphoreType.DMA((2, 4)),
        pltpu.SemaphoreType.DMA((2, 4)), pltpu.SemaphoreType.DMA((2, 4)),
    ])
    n_scratch = 13

    def __init__(self, rows_ref, slots_ref, o_ref, scratch):
        self.rows_ref, self.slots_ref, self.o_ref = rows_ref, slots_ref, o_ref
        (self.own, self.rin, self.sout, self.rb, self.zout, self.rz,
         self.own_sem, self.ts, self.tr, self.bs, self.br, self.zs, self.zr) = scratch
        self.z, self.y, self.x, self.c = place()
        half = rows_ref.shape[1] // 2
        self.cols = [pl.ds(0, half), pl.ds(half, half)]

    def block(self, p, h, k, yy, xx, cc):
        zz = lax.rem(self.z + k, 4)
        if p == 0:
            return number(zz, (1 - yy) if h else yy, xx, cc)
        return number(zz, yy, (1 - xx) if h else xx, cc)

    def sources(self, p):
        y, x, c = self.y, self.x, self.c
        ay, ax = (y, 1 - x) if p == 0 else (1 - y, x)
        return [(y, x, 1 - c), (ay, ax, c), (ay, ax, 1 - c)]

    def slot_rows(self, block, p):
        return self.rows_ref.at[pl.ds(pl.multiple_of(block * SLOTS, 16), SLOTS), self.cols[p]]

    def to(self, p, t, h, k):
        place_of = self.sources(p)[t]
        return pltpu.make_async_remote_copy(
            src_ref=self.slot_rows(self.block(p, h, k, *place_of), p), dst_ref=self.rin.at[p, t, h, k],
            send_sem=self.ts.at[p, t, h, k], recv_sem=self.tr.at[p, t, h, k],
            device_id=(number(self.z, *place_of),), device_id_type=MESH)

    def mine(self, p, h, k):
        return pltpu.make_async_copy(
            self.slot_rows(self.block(p, h, k, self.y, self.x, self.c), p), self.own.at[p, h, k], self.own_sem.at[p, h, k])

    def second(self, p, k):
        z, y, x, c = self.z, self.y, self.x, self.c
        target = number(z, 1 - y, x, c) if p == 0 else number(z, y, 1 - x, c)
        return pltpu.make_async_remote_copy(
            src_ref=self.sout.at[p, k], dst_ref=self.rb.at[p, k], send_sem=self.bs.at[p, k], recv_sem=self.br.at[p, k],
            device_id=(target,), device_id_type=MESH)

    def order(self, i):
        return jnp.where(self.z < 2, 3 - i, lax.rem(i + 1, 4))

    def relay(self, k):
        zz = lax.rem(self.z + k, 4)
        adds = ((self.z == 1) & (zz >= 2)) | ((self.z == 2) & (zz <= 1))
        return adds, 2 + jnp.where(zz >= 2, zz - 2, 1 - zz)

    def third(self, p, k):
        z = self.z
        zz = lax.rem(z + k, 4)
        to = jnp.where(z == 0, 1, jnp.where(z == 3, 2, zz))
        passed = ((z == 0) & (zz >= 2)) | ((z == 3) & (zz <= 1))
        last = ((z == 2) & (zz <= 1)) | ((z == 3) & (zz == 2)) | ((z == 1) & (zz == 3))
        slot = jnp.where(passed, 2 + jnp.where(zz >= 2, zz - 2, 1 - zz), jnp.where(last, 1, 0))
        return pltpu.make_async_remote_copy(
            src_ref=self.zout.at[p, k], dst_ref=self.rz.at[p, slot], send_sem=self.zs.at[p, k], recv_sem=self.zr.at[p, slot],
            device_id=(number(to, self.y, self.x, self.c),), device_id_type=MESH)

    def along(self, p, slot):
        return pltpu.make_async_remote_copy(
            src_ref=self.zout.at[p, 0], dst_ref=self.rz.at[p, slot], send_sem=self.zs.at[p, 0], recv_sem=self.zr.at[p, slot],
            device_id=(number(self.z, self.y, self.x, 1 - self.c),), device_id_type=MESH)

    def issue(self, h, i):
        k = self.order(i)
        for p in range(2):
            for t in (1, 2, 0):
                self.to(p, t, h, k).start()
            self.mine(p, h, k).start()

    def start(self):
        self.issue(1, 0)
        self.issue(0, 0)

    def dense(self, p, h, k):
        self.mine(p, h, k).wait()
        for t in range(3):
            self.to(p, t, h, k).wait_recv()
        block = self.block(p, h, k, self.y, self.x, self.c)
        total = None
        for t, who in enumerate([(self.y, self.x, self.c)] + self.sources(p)):
            hit = chosen_rows(self.slots_ref, block, in_plane(*who))
            chosen = jnp.where(hit, 1.0, 0.0).astype(BF16)
            values = self.own[p, h, k] if t == 0 else self.rin[p, t - 1, h, k]
            term = dims(chosen, values, 0, 0)
            total = term if total is None else total + term
        return total

    def step(self, u):
        i = u // 2
        k = self.order(jnp.int32(i))
        early = u % 2 == 0

        @pl.when(early)
        def _():
            for p in range(2):
                self.sout[p, k] = self.dense(p, 1, k).astype(BF16)
                self.second(p, k).start()

            @pl.when(i < 3)
            def _():
                self.issue(1, i + 1)

        @pl.when(u % 2 == 1)
        def _():
            for p in range(2):
                total = self.dense(p, 0, k)
                self.second(p, k).wait_recv()
                total = total + self.rb[p, k].astype(F32)

                adds, slot = self.relay(k)

                @pl.when((k > 0) & adds)
                def _(p=p, total=total):
                    self.along(p, slot).wait_recv()
                    self.zout[p, k] = (total + self.rz[p, slot].astype(F32)).astype(BF16)
                    self.third(p, k).start()

                @pl.when((k > 0) & jnp.logical_not(adds))
                def _(p=p, total=total):
                    self.zout[p, k] = total.astype(BF16)
                    self.third(p, k).start()

                @pl.when(k == 0)
                def _(p=p, total=total):
                    self.o_ref[:, self.cols[p]] = total

            @pl.when(i < 3)
            def _():
                self.issue(0, i + 1)

    def finish(self):
        for p in range(2):
            for slot in range(2):
                self.along(p, slot).wait_recv()
            self.o_ref[:, self.cols[p]] += self.rz[p, 0].astype(F32) + self.rz[p, 1].astype(F32)

        def one(k, _):
            for p in range(2):
                self.second(p, k).wait_send()

                @pl.when(k > 0)
                def _(p=p):
                    self.third(p, k).wait_send()
                for t in range(3):
                    for h in range(2):
                        self.to(p, t, h, k).wait_send()
            return 0
        lax.fori_loop(0, 4, one, 0)


def grads_kernel(
    dx_ref, slots_ref, gg_ref, xi_ref, ui_ref, hg_in, dg_in, du_in,
    o_ref, back_ref, wg_out, wu_out, wd_out, xcol, ucol, gout, uout, dout, hg_ref, dg_ref, du_ref,
    gs, gr, isem, osem, wsem, *scratch,
):
    greet_all()
    swap = Swap(lambda t: gg_ref.at[t], back_ref, gs, gr)
    rs = Back(dx_ref, slots_ref, o_ref, scratch)
    rs.start()
    swap.start()

    def col(i):
        return pl.ds(pl.multiple_of(i * 256, 256), 256)

    def loads(i):
        s = lax.rem(i, 2)
        return [
            pltpu.make_async_copy(xi_ref.at[:, col(i)], xcol.at[s], isem.at[0, s]),
            pltpu.make_async_copy(ui_ref.at[:, col(i)], ucol.at[s], isem.at[1, s]),
        ]

    def stores(i):
        s = lax.rem(i, 2)
        return [
            pltpu.make_async_copy(gout.at[s], wg_out.at[col(i), :], osem.at[0, s]),
            pltpu.make_async_copy(uout.at[s], wu_out.at[col(i), :], osem.at[1, s]),
            pltpu.make_async_copy(dout.at[s], wd_out.at[:, col(i)], osem.at[2, s]),
        ]

    for cp in loads(0):
        cp.start()
    whole = [
        pltpu.make_async_copy(source, into, wsem.at[i])
        for i, (source, into) in enumerate(((hg_in, hg_ref), (dg_in, dg_ref), (du_in, du_ref)))
    ]
    for cp in whole:
        cp.start()
    for cp in whole:
        cp.wait()

    def one(u, _):
        @pl.when(u < 6)
        def _():
            s = lax.rem(u, 2)

            @pl.when(u < 5)
            def _():
                for cp in loads(u + 1):
                    cp.start()

            for cp in loads(u):
                cp.wait()

            @pl.when(u >= 2)
            def _():
                for cp in stores(u - 2):
                    cp.wait()

            rows_in = xcol[s]
            gout[s] = dims(rows_in, dg_ref[...], 0, 0)
            uout[s] = dims(rows_in, du_ref[...], 0, 0)
            dout[s] = dims(hg_ref[...], ucol[s], 0, 0)
            for cp in stores(u):
                cp.start()

        rs.step(u)
        return 0

    lax.fori_loop(0, 8, one, 0)
    for i in (4, 5):
        for cp in stores(i):
            cp.wait()
    swap.wait_recv()
    rs.finish()
    swap.wait_send()


def run_grads(dx, slots, gg, xi, ui, hg, dg, du):
    rows, model = slots.shape[2], dx.shape[1]
    ff = hg.shape[1]
    n = dx.shape[0]
    hbm, vmem = pl.BlockSpec(memory_space=pl.ANY), pl.BlockSpec(memory_space=pltpu.VMEM)
    dma = pltpu.SemaphoreType.DMA
    return pl.pallas_call(
        grads_kernel,
        in_specs=[hbm, vmem, vmem, hbm, hbm, hbm, hbm, hbm],
        out_specs=[vmem, vmem, hbm, hbm, hbm],
        out_shape=[
            jax.ShapeDtypeStruct((rows, model), F32),
            jax.ShapeDtypeStruct((32, 8, 128), F32),
            jax.ShapeDtypeStruct((model, ff), F32),
            jax.ShapeDtypeStruct((model, ff), F32),
            jax.ShapeDtypeStruct((ff, model), F32),
        ],
        scratch_shapes=[
            pltpu.VMEM((2, n, 256), BF16), pltpu.VMEM((2, n, 256), BF16),
            pltpu.VMEM((2, 256, ff), F32), pltpu.VMEM((2, 256, ff), F32), pltpu.VMEM((2, ff, 256), F32),
            pltpu.VMEM((n, ff), BF16), pltpu.VMEM((n, ff), BF16), pltpu.VMEM((n, ff), BF16),
            dma((32,)), dma((32,)), dma((2, 2)), dma((3, 2)), dma((3,)),
        ] + Back.scratch(rows, model // 2),
        compiler_params=pltpu.CompilerParams(collective_id=14, has_side_effects=True, vmem_limit_bytes=56 * 2**20),
        name="grads",
    )(dx, slots, gg, xi, ui, hg, dg, du)


BEFORE_HEADS = (
    "w0", "rank", "w1", "v0", "w2", "v1", "w3", "v2", "v3", "bias", "gains", "norm", "u0", "u1",
    "u2", "u3", "wend", "kv", "ag", "o0", "q", "prev", "o1", "pass", "t0", "kend",
)
AFTER_HEAD = ("o2", "t1", "o3", "t2", "", "t3", "", "")


def front_kernel(
    chunks, rows, lo_ref, cos_ref, sin_ref, x_ref, wq_ref, wk_ref, wv_ref, router_ref, u_ref, turn_ref, turn_t_ref,
    gain_one_ref, gain_two_ref, q_out, o_ref, lse_ref, window_out, slots_ref, ui_ref, w_out, n_ref, gains_ref, scale_ref,
    q_ref, window, w_ref, part_ref, bias, mine, kv, key_t, insem, outsem, gs, gr, lsem, ws, wr, *scratch,
):
    loads, at = [], 0
    for i, ref in enumerate((wq_ref, wk_ref, wv_ref)):
        loads.append(pltpu.make_async_copy(ref, part_ref.at[:, pl.ds(at, ref.shape[1])], insem.at[i]))
        at += ref.shape[1]
    for cp in loads:
        cp.start()
    part_ref[:, at:] = jnp.zeros((part_ref.shape[0], part_ref.shape[1] - at), BF16)
    part_ref[:, at : at + EXPERTS] = router_ref[...]
    greet_all()
    weights = Whole(part_ref, w_ref, scratch[:7])
    swap = Swap(lambda t: mine.at[t // 8], slots_ref, gs, gr)
    keys = Window(rows, kv, window, (lsem, ws, wr))
    ag = Forth(u_ref, slots_ref, ui_ref, scratch[7:])
    cosine, sine = cos_ref[...], sin_ref[...]
    q_width, k_width = QUERY_HEADS * HEAD_DIM, KEY_HEADS * HEAD_DIM

    def rank():
        for e in range(EXPERTS):
            own = turn_t_ref[e : e + 1, :]
            place_of = jnp.sum(jnp.where(turn_ref[:, e : e + 1] < own, 1.0, 0.0), axis=0, keepdims=True)
            slot = jnp.where((own < UNPICKED) & (place_of < CAPACITY), place_of, -1.0)
            mine[e // 8, e % 8 : e % 8 + 1, :] = slot
        mine[:, 8:16, :] = jnp.zeros((4, 8, rows), F32)
        for plane in range(4):
            mine[plane, 8:9, 0 : part_ref.shape[0]] = gain_one_ref[...].astype(F32)
            mine[plane, 9:10, 0 : part_ref.shape[0]] = gain_two_ref[...].astype(F32)
        swap.start()

    def gains():
        swap.wait_recv()
        part = part_ref.shape[0]
        for t in range(32):
            gains_ref[0:8, t * part : (t + 1) * part] = slots_ref[t, 8:16, 0:part]

    def norm():
        def some(i, _):
            at = pl.ds(pl.multiple_of(i * 32, 32), 32)
            values = x_ref[at, :].astype(F32)
            scale = lax.rsqrt(jnp.mean(values * values, axis=1, keepdims=True) + EPSILON)
            scale_ref[at, :] = scale
            n_ref[at, :] = (values * scale * gains_ref[0:1, :]).astype(BF16)
            return 0
        lax.fori_loop(0, rows // 32, some, 0)

    def roped(values, into, first):
        turned = values.T
        for n in range(256 // HEAD_DIM):
            u = turned[n * HEAD_DIM : n * HEAD_DIM + HEAD_DIM // 2]
            w = turned[n * HEAD_DIM + HEAD_DIM // 2 : (n + 1) * HEAD_DIM]
            at = first + n * HEAD_DIM
            into[pl.ds(pl.multiple_of(at, 32), 32), :] = (u * cosine - w * sine).astype(BF16)
            into[pl.ds(pl.multiple_of(at + 32, 32), 32), :] = (w * cosine + u * sine).astype(BF16)

    def keys_and_values():
        for n in range(k_width // 256):
            roped(dims(n_ref[...], w_ref[:, q_width + n * 256 : q_width + (n + 1) * 256], 1, 0), key_t, n * 256)
            kv[0, :, n * 256 : (n + 1) * 256] = key_t[n * 256 : (n + 1) * 256, :].T
        kv[1] = dims(n_ref[...], w_ref[:, q_width + k_width : QKV], 1, 0).astype(BF16)
        keys.start()

    def queries():
        def some(i, _):
            at = pl.ds(pl.multiple_of(i * 256, 256), 256)
            roped(dims(n_ref[...], w_ref[:, at], 1, 0), q_ref, i * 256)
            q_ref[at, :] = (q_ref[at, :].astype(F32) * HEAD_DIM**-0.5).astype(BF16)
            return 0
        lax.fori_loop(0, q_width // 256, some, 0)

    def whole():
        weights.end()
        outs[0].start()

    def queried():
        queries()
        outs[1].start()

    def windowed():
        keys.end()
        outs[2].start()

    outs = [
        pltpu.make_async_copy(held, out, outsem.at[i])
        for i, (held, out) in enumerate(((w_ref, w_out), (q_ref, q_out), (window, window_out)))
    ]
    step = {
        "rank": rank, "gains": gains, "norm": norm, "kv": keys_and_values, "q": queried,
        "ag": ag.start, "bias": lambda: make_bias(bias, lo_ref, chunks, rows), "wend": whole,
        "prev": keys.previous, "pass": keys.pass_on, "kend": windowed,
    }
    for i in range(4):
        step[f"w{i}"] = functools.partial(weights.one, i)
        step[f"v{i}"] = functools.partial(weights.two, i)
        step[f"u{i}"] = functools.partial(weights.three, i)
        step[f"c{i}"] = functools.partial(ag.come, jnp.int32(i))
        step[f"s{i}"] = functools.partial(ag.one, jnp.int32(i), False)
        step[f"o{i}"] = functools.partial(ag.one, jnp.int32(i))
        step[f"t{i}"] = functools.partial(ag.two, jnp.int32(i))

    for cp in loads:
        cp.wait()
    weights.start()
    for name in BEFORE_HEADS:
        step[name]()
    width = 2 * GROUP * HEAD_DIM

    def pair(j, _):
        lanes = pl.ds(pl.multiple_of(j * 2 * HEAD_DIM, 2 * HEAD_DIM), 2 * HEAD_DIM)
        head = pl.ds(pl.multiple_of(j * width, width), width)

        def between(half):
            for u in range(half, 8, 2):
                if AFTER_HEAD[u]:
                    @pl.when(2 * j + half == u)
                    def _(u=u):
                        step[AFTER_HEAD[u]]()

        attend_pair(
            chunks, rows, lax.rem(lax.axis_index("dev"), 2), q_ref.at[head, :], window.at[:, :, lanes],
            o_ref.at[head, :], lse_ref.at[pl.ds(j, 1)], bias, between,
        )
        return 0

    lax.fori_loop(0, KEY_HEADS // 2, pair, 0)

    def last(u, _):
        ag.arrived(lax.rem(u, 4), u // 4)
        return 0
    lax.fori_loop(0, 16, last, 0)
    ag.sent()
    keys.sent()
    swap.wait_send()
    weights.sent()
    for cp in outs:
        cp.wait()


def front(lo, cos_t, sin_t, tokens, projections, router, upstream, turn, gain_one, gain_two):
    rows, model = tokens.shape
    chunks = 9
    keys = KEY_HEADS * HEAD_DIM
    part = jax.ShapeDtypeStruct((router.shape[0], -(-(QKV + EXPERTS) // 128) * 128), BF16)
    hbm, vmem = pl.BlockSpec(memory_space=pl.ANY), pl.BlockSpec(memory_space=pltpu.VMEM)
    dma = pltpu.SemaphoreType.DMA
    return pl.pallas_call(
        functools.partial(front_kernel, chunks, rows),
        in_specs=[vmem] * 4 + [hbm] * 3 + [vmem, hbm] + [vmem] * 4,
        out_specs=[hbm, vmem, vmem, hbm, vmem, hbm, hbm, vmem, vmem, vmem],
        out_shape=[
            jax.ShapeDtypeStruct((QUERY_HEADS * HEAD_DIM, rows), BF16),
            jax.ShapeDtypeStruct((QUERY_HEADS * HEAD_DIM, rows), BF16),
            jax.ShapeDtypeStruct((KEY_HEADS // 2, 8, rows), F32),
            jax.ShapeDtypeStruct((2, 10 * rows, keys), BF16),
            jax.ShapeDtypeStruct((32, 16, rows), F32),
            jax.ShapeDtypeStruct((32 * SLOTS, model), BF16),
            jax.ShapeDtypeStruct((32 * part.shape[0], part.shape[1]), BF16),
            jax.ShapeDtypeStruct((rows, model), BF16),
            jax.ShapeDtypeStruct((8, model), F32),
            jax.ShapeDtypeStruct((rows, 1), F32),
        ],
        scratch_shapes=[
            pltpu.VMEM((QUERY_HEADS * HEAD_DIM, rows), BF16), pltpu.VMEM((2, 10 * rows, keys), BF16),
            pltpu.VMEM((32 * part.shape[0], part.shape[1]), BF16), pltpu.VMEM(part.shape, BF16),
            pltpu.VMEM((chunks * rows, rows), F32), pltpu.VMEM((4, 16, rows), F32), pltpu.VMEM((2, rows, keys), BF16),
            pltpu.VMEM((keys, rows), BF16), dma((3,)), dma((3,)), dma((32,)), dma((32,)),
        ]
        + Window.scratch + Whole.scratch + Forth.scratch(rows, model // 2),
        compiler_params=pltpu.CompilerParams(collective_id=16, has_side_effects=True, vmem_limit_bytes=58 * 2**20),
        name="front",
    )(lo, cos_t, sin_t, tokens, *projections, router, upstream, turn, turn.T, gain_one, gain_two)


IN_PAIRS = {0: (0,), 2: (1,), 4: (2,), 6: (3,)}
AFTER_PAIRS = (4, "sums", 5, 6, "near", "turn", 7)


def attend_back_mesh_kernel(
    chunks, rows, lo_ref, cos_ref, sin_ref, q_ref, kv_in, branch_ref, wo_in, lse_ref, out_ref, y_ref, slots_ref, residual_in,
    grad_out, layer_ref, wo, g_ref, wsem, kv_ref, residual_ref, insem, bias, dkv, sums_ref, gt_ref, o_ref, *scratch,
):
    greet_near()
    rs = Back(y_ref, slots_ref, o_ref, scratch[: Back.n_scratch])
    keys = Unwindow(rows, dkv, sums_ref, scratch[Back.n_scratch :])
    rs.start()
    kv_load = pltpu.make_async_copy(kv_in, kv_ref, insem.at[0])
    residual_load = pltpu.make_async_copy(residual_in, residual_ref, insem.at[1])
    kv_load.start()
    residual_load.start()
    step = wo.shape[1]

    def wo_load(i):
        return pltpu.make_async_copy(wo_in.at[pl.ds(i * step, step), :], wo.at[i % 2], wsem.at[i % 2])

    wo_load(0).start()
    make_bias(bias, lo_ref, chunks, rows)
    for i in range(wo_in.shape[0] // step):
        if (i + 1) * step < wo_in.shape[0]:
            wo_load(i + 1).start()
        wo_load(i).wait()
        g_ref[i * step : (i + 1) * step, :] = dims(wo[i % 2], branch_ref[...], 1, 1).astype(BF16)
    kv_load.wait()
    residual_load.wait()
    width = 2 * GROUP * HEAD_DIM

    def pair(j, _):
        lanes = pl.ds(pl.multiple_of(j * 2 * HEAD_DIM, 2 * HEAD_DIM), 2 * HEAD_DIM)
        head = pl.ds(pl.multiple_of(j * width, width), width)

        def between(half):
            for n, names in IN_PAIRS.items():
                if n % 2 == half:
                    @pl.when(2 * j + half == n)
                    def _(names=names):
                        for name in names:
                            rs.step(name)

        attend_back_pair(
            chunks, rows, lax.rem(lax.axis_index("dev"), 2), cos_ref, sin_ref, q_ref.at[head, :], kv_ref.at[:, :, lanes], g_ref.at[head, :],
            lse_ref.at[pl.ds(j, 1)], out_ref.at[head, :], gt_ref.at[head, :], dkv.at[:, :, lanes], bias, between,
        )
        return 0

    lax.fori_loop(0, KEY_HEADS // 2, pair, 0)

    def turned(first, last):
        for n in range(first, last, 256):
            grad_out[:, n : n + 256] = gt_ref[n : n + 256, :].T

    keys.start()
    for name in AFTER_PAIRS:
        if isinstance(name, int):
            rs.step(name)
        elif name == "sums":
            keys.sums()
        elif name == "turn":
            turned(0, QUERY_HEADS * HEAD_DIM)
        else:
            keys.near()
    keys.end()
    base = QUERY_HEADS * HEAD_DIM
    key_t = sums_ref[0].T
    cosine, sine = cos_ref[...], sin_ref[...]
    for n in range(KEY_HEADS):
        first, middle = n * HEAD_DIM, n * HEAD_DIM + HEAD_DIM // 2
        u, w = key_t[first:middle], key_t[middle : first + HEAD_DIM]
        gt_ref[base + first : base + middle, :] = (u * cosine + w * sine).astype(BF16)
        gt_ref[base + middle : base + first + HEAD_DIM, :] = (w * cosine - u * sine).astype(BF16)
    turned(base, base + KEY_HEADS * HEAD_DIM)
    grad_out[:, base + KEY_HEADS * HEAD_DIM :] = sums_ref[1].astype(BF16)
    rs.finish()
    layer_ref[...] = (residual_ref[...] + o_ref[...]).astype(BF16)


def attend_back_mesh(query_t, window, lo, branch_grad, output_matrix, lse, attended_t, cos_t, sin_t, y, slots, residual):
    rows, span, keys = query_t.shape[1], window.shape[1], window.shape[2]
    chunks = span // rows - 1
    model = y.shape[1]
    hbm, vmem = pl.BlockSpec(memory_space=pl.ANY), pl.BlockSpec(memory_space=pltpu.VMEM)
    return pl.pallas_call(
        functools.partial(attend_back_mesh_kernel, chunks, rows),
        in_specs=[vmem] * 4 + [hbm, vmem, hbm] + [vmem] * 2 + [hbm, vmem, hbm],
        out_specs=[vmem] * 2,
        out_shape=[
            jax.ShapeDtypeStruct((rows, QKV), BF16),
            jax.ShapeDtypeStruct((rows, model), BF16),
        ],
        scratch_shapes=[
            pltpu.VMEM((2, 384, model), BF16), pltpu.VMEM(query_t.shape, BF16), pltpu.SemaphoreType.DMA((2,)),
            pltpu.VMEM(window.shape, BF16), pltpu.VMEM((rows, model), F32), pltpu.SemaphoreType.DMA((2,)),
            pltpu.VMEM((chunks * rows, rows), F32), pltpu.VMEM(window.shape, BF16), pltpu.VMEM((2, rows, keys), F32),
            pltpu.VMEM((QKV, rows), BF16), pltpu.VMEM((rows, model), F32),
        ]
        + Back.scratch(rows, model // 2) + Unwindow.scratch(rows, keys),
        compiler_params=pltpu.CompilerParams(collective_id=15, has_side_effects=True, vmem_limit_bytes=60 * 2**20),
        name="attend_back",
    )(lo, cos_t, sin_t, query_t, window, branch_grad, output_matrix, lse, attended_t, y, slots, residual)


def finish_kernel(
    rows, n_ref, g_ref, w_in, more_ref, gain_ref, scale_ref, x_in, rg_in,
    oq_ref, ok_ref, ov_ref, om_ref, tg_ref, fg_ref, w_ref, x_ref, rg_ref, insem,
    dense, acc, ra, rb, rz, out, ng, mine, theirs, ssem, rsem, sa, ra_sem, sb, rb_sem, sz, rz_sem, gs, gr,
):
    z, y, x, c = place()
    greet_all()
    sibling = number(z, y, x, 1 - c)
    cols = acc.shape[2]
    main = g_ref.shape[1]
    half = cols // 2
    pieces = [pl.ds(0, half), pl.ds(half, half)]
    around = (number(z, y, 1 - x, c), number(z, 1 - y, x, c))
    swap = Swap(lambda t: mine.at[t], theirs, gs, gr)

    def lane(dy, dx, k):
        yy = 1 - y if dy else y
        xx = 1 - x if dx else x
        return (lax.rem(z + k, 4) * 2 + yy) * 2 + xx

    def to_sibling(dy, dx, k):
        chip = lane(dy, dx, k)
        n = (k, dy, dx)
        sides = (
            (dense.at[chip, pl.ds(pl.multiple_of((1 - c) * rows, 16), rows), :], pl.ds(0, main)),
            (more_ref.at[pl.ds(pl.multiple_of((2 * chip + 1 - c) * rows, 16), rows), :], pl.ds(main, cols - main)),
        )
        return [
            pltpu.make_async_remote_copy(
                src_ref=source, dst_ref=acc.at[chip, :, at], send_sem=ssem.at[(*n, i)], recv_sem=rsem.at[(*n, i)],
                device_id=(sibling,), device_id_type=MESH)
            for i, (source, at) in enumerate(sides)
        ]

    def first(p, d2, k, dy, dx):
        return pltpu.make_async_remote_copy(
            src_ref=acc.at[lane(dy, dx, k), :, pieces[p]], dst_ref=ra.at[p, d2, k],
            send_sem=sa.at[p, d2, k], recv_sem=ra_sem.at[p, d2, k], device_id=(around[p],), device_id_type=MESH)

    def second(p, k):
        dy, dx = (1, 0) if p == 0 else (0, 1)
        return pltpu.make_async_remote_copy(
            src_ref=acc.at[lane(dy, dx, k), :, pieces[p]], dst_ref=rb.at[p, k],
            send_sem=sb.at[p, k], recv_sem=rb_sem.at[p, k], device_id=(around[1 - p],), device_id_type=MESH)

    def order(i):
        return jnp.where(z < 2, 3 - i, lax.rem(i + 1, 4))

    def third(p, k):
        zz = lax.rem(z + k, 4)
        to = jnp.where(z == 0, 1, jnp.where(z == 3, 2, zz))
        passed = ((z == 0) & (zz >= 2)) | ((z == 3) & (zz <= 1))
        last = ((z == 2) & (zz <= 1)) | ((z == 3) & (zz == 2)) | ((z == 1) & (zz == 3))
        slot = jnp.where(passed, 2 + jnp.where(zz >= 2, zz - 2, 1 - zz), jnp.where(last, 1, 0))
        return pltpu.make_async_remote_copy(
            src_ref=acc.at[lane(0, 0, k), :, pieces[p]], dst_ref=rz.at[p, slot],
            send_sem=sz.at[p, k], recv_sem=rz_sem.at[p, slot], device_id=(number(to, y, x, c),), device_id_type=MESH)

    def along(p, slot):
        return pltpu.make_async_remote_copy(
            src_ref=acc.at[lane(0, 0, 0), :, pieces[p]], dst_ref=rz.at[p, slot],
            send_sem=sz.at[p, 0], recv_sem=rz_sem.at[p, slot], device_id=(sibling,), device_id_type=MESH)

    quarter = ((1, 1), (1, 0), (0, 1), (0, 0))

    def product(i, _):
        k = order(i)
        zz = lax.rem(z + k, 4)
        at = pl.ds(pl.multiple_of(zz * 8 * rows, 128), 8 * rows)
        part = dims(n_ref[:, at], g_ref[...], 0, 0).astype(BF16)
        for chip in range(4):
            dense[zz * 4 + chip] = part[chip * 2 * rows : (chip + 1) * 2 * rows]
        for dy, dx in quarter:
            for cp in to_sibling(dy, dx, k):
                cp.start()
        return 0

    def own_sums(k):
        for dy, dx in quarter:
            chip = lane(dy, dx, k)
            for cp in to_sibling(dy, dx, k):
                cp.wait_recv()
            acc[chip, :, :main] = (
                acc[chip, :, :main].astype(F32) + dense[chip, pl.ds(pl.multiple_of(c * rows, 16), rows), :].astype(F32)
            ).astype(BF16)
            acc[chip, :, main:] = (
                acc[chip, :, main:].astype(F32)
                + more_ref[pl.ds(pl.multiple_of((2 * chip + c) * rows, 16), rows), :].astype(F32)
            ).astype(BF16)
            if dx:
                first(0, dy, k, dy, dx).start()
            if dy:
                first(1, dx, k, dy, dx).start()

    def middle(k):
        for p in range(2):
            dy, dx = (1, 0) if p == 0 else (0, 1)
            first(p, 1, k, 1, 1).wait_recv()
            block = acc.at[lane(dy, dx, k), :, pieces[p]]
            block[...] = (block[...].astype(F32) + ra[p, 1, k].astype(F32)).astype(BF16)
            second(p, k).start()

    def late(k):
        for p in range(2):
            first(p, 0, k, 1 - p, p).wait_recv()
            second(p, k).wait_recv()
            block = acc.at[lane(0, 0, k), :, pieces[p]]
            total = block[...].astype(F32) + ra[p, 0, k].astype(F32) + rb[p, k].astype(F32)

            zz = lax.rem(z + k, 4)
            adds = ((z == 1) & (zz >= 2)) | ((z == 2) & (zz <= 1))
            slot = 2 + jnp.where(zz >= 2, zz - 2, 1 - zz)

            @pl.when((k > 0) & adds)
            def _(p=p, block=block, total=total):
                along(p, slot).wait_recv()
                block[...] = (total + rz[p, slot].astype(F32)).astype(BF16)
                third(p, k).start()

            @pl.when((k > 0) & jnp.logical_not(adds))
            def _(p=p, block=block, total=total):
                block[...] = total.astype(BF16)
                third(p, k).start()

            @pl.when(k == 0)
            def _(p=p, total=total):
                out[:, pieces[p]] = total

    def rest_of_tokens():
        ng[...] = dims(g_ref[...], w_ref[:, :main], 1, 1)

        def tail(i, total):
            at = pl.ds(pl.multiple_of(i * 32, 32), 32)
            grad, scale, values = ng[at, :], scale_ref[at, :], x_ref[at, :].astype(F32)
            weighted = grad * gain_ref[...]
            scaled = values * scale
            mean = jnp.mean(weighted * values, axis=1, keepdims=True)
            tg_ref[at, :] = rg_ref[at, :] + scale * weighted - scaled * (scale * scale * mean)
            return total + jnp.sum(grad * scaled, axis=0, keepdims=True)
        total = lax.fori_loop(0, x_ref.shape[0] // 32, tail, jnp.zeros(gain_ref.shape, F32))
        mine[...] = jnp.zeros_like(mine)
        for t in range(32):
            mine[t, 0:1, 0:rows] = total[:, t * rows : (t + 1) * rows]
        swap.start()

    loads = [
        pltpu.make_async_copy(source, into, insem.at[i])
        for i, (source, into) in enumerate(((w_in, w_ref), (x_in, x_ref), (rg_in, rg_ref)))
    ]
    for cp in loads:
        cp.start()
    lax.fori_loop(0, 4, product, 0)
    for cp in loads:
        cp.wait()

    def steps(i, _):
        @pl.when(i < 4)
        def _():
            own_sums(order(i))

        @pl.when(i == 3)
        def _():
            rest_of_tokens()

        @pl.when(i < 4)
        def _():
            middle(order(i))

        @pl.when(i >= 1)
        def _():
            late(order(i - 1))
        return 0
    lax.fori_loop(0, 5, steps, 0)
    swap.wait_recv()
    fg_ref[...] = jnp.sum(theirs[...], axis=0)
    for p in range(2):
        for slot in range(2):
            along(p, slot).wait_recv()
        out[:, pieces[p]] += rz[p, 0].astype(F32) + rz[p, 1].astype(F32)
    at = 0
    for ref in (oq_ref, ok_ref, ov_ref, om_ref):
        ref[...] = out[:, at : at + ref.shape[1]]
        at += ref.shape[1]

    def sent(k, _):
        for dy, dx in quarter:
            for cp in to_sibling(dy, dx, k):
                cp.wait_send()
        for p in range(2):
            first(p, 0, k, 1 - p, p).wait_send()
            first(p, 1, k, 1, 1).wait_send()
            second(p, k).wait_send()

            @pl.when(k > 0)
            def _(p=p):
                third(p, k).wait_send()
        return 0
    lax.fori_loop(0, 4, sent, 0)
    swap.wait_send()


def finish(normed, grad, matrices, more, gain, scale, tokens, residual_grad):
    count, model = normed.shape
    rows = model // 32
    main, cols = grad.shape[1], grad.shape[1] + more.shape[1]
    half = cols // 2
    dma = pltpu.SemaphoreType.DMA
    hbm, vmem = pl.BlockSpec(memory_space=pl.ANY), pl.BlockSpec(memory_space=pltpu.VMEM)
    widths = [QUERY_HEADS * HEAD_DIM, KEY_HEADS * HEAD_DIM, KEY_HEADS * HEAD_DIM, more.shape[1]]
    return pl.pallas_call(
        functools.partial(finish_kernel, rows),
        in_specs=[vmem, vmem, hbm, vmem, vmem, vmem, hbm, hbm],
        out_specs=[vmem] * 6,
        out_shape=[jax.ShapeDtypeStruct((rows, w), F32) for w in widths] + [
            jax.ShapeDtypeStruct((count, model), F32),
            jax.ShapeDtypeStruct((8, 128), F32),
        ],
        scratch_shapes=[
            pltpu.VMEM(matrices.shape, BF16), pltpu.VMEM((count, model), BF16), pltpu.VMEM((count, model), F32), dma((3,)),
            pltpu.VMEM((16, 2 * rows, main), BF16),
            pltpu.VMEM((16, rows, cols), BF16),
            pltpu.VMEM((2, 2, 4, rows, half), BF16),
            pltpu.VMEM((2, 4, rows, half), BF16),
            pltpu.VMEM((2, 4, rows, half), BF16),
            pltpu.VMEM((rows, cols), F32),
            pltpu.VMEM((count, model), F32),
            pltpu.VMEM((32, 8, 128), F32),
            pltpu.VMEM((32, 8, 128), F32),
            dma((4, 2, 2, 2)), dma((4, 2, 2, 2)), dma((2, 2, 4)), dma((2, 2, 4)), dma((2, 4)), dma((2, 4)), dma((2, 4)), dma((2, 4)),
            dma((32,)), dma((32,)),
        ],
        compiler_params=pltpu.CompilerParams(collective_id=17, has_side_effects=True, vmem_limit_bytes=42 * 2**20),
        name="finish",
    )(normed, grad, matrices, more, gain, scale, tokens, residual_grad)


def chunks_of(shape):
    rows = shape[0]
    count = 1
    while rows % (32 * count) == 0 and rows // count * shape[1] > 2**18:
        count *= 2
    return [(i * (rows // count), rows // count) for i in range(count)]


def hand_over_kernel(count, *refs):
    sources, outs, held = refs[:count], refs[count : 2 * count], refs[2 * count : 3 * count]
    sems = refs[3 * count]
    into, out = [], []
    for source, there, here in zip(sources, outs, held, strict=True):
        for first, rows in chunks_of(source.shape):
            at, n = pl.ds(first, rows), len(into)
            into.append(pltpu.make_async_copy(source.at[at, :], here.at[at, :], sems.at[0, n]))
            out.append(pltpu.make_async_copy(here.at[at, :], there.at[at, :], sems.at[1, n]))
    for cp in into:
        cp.start()
    for a, b in zip(into, out, strict=True):
        a.wait()
        b.start()
    for cp in out:
        cp.wait()


def hand_over(*arrays):
    hbm = pl.BlockSpec(memory_space=pl.ANY)
    total = sum(len(chunks_of(a.shape)) for a in arrays)
    return pl.pallas_call(
        functools.partial(hand_over_kernel, len(arrays)),
        in_specs=[hbm] * len(arrays),
        out_specs=[hbm] * len(arrays),
        out_shape=[jax.ShapeDtypeStruct(a.shape, a.dtype) for a in arrays],
        scratch_shapes=[pltpu.VMEM(a.shape, a.dtype) for a in arrays] + [pltpu.SemaphoreType.DMA((2, total))],
        compiler_params=pltpu.CompilerParams(vmem_limit_bytes=60 * 2**20),
        name="hand_over",
    )(*arrays)


def rms_scale(values):
    return lax.rsqrt(jnp.mean(values * values, axis=-1, keepdims=True) + EPSILON)


def rotate_t(values, cosine, sine):
    half = cosine.shape[0]
    shaped = values.reshape(-1, 2, half, values.shape[1])
    u, w = shaped[:, 0], shaped[:, 1]
    turned = jnp.stack([u * cosine - w * sine, w * cosine + u * sine], axis=1)
    return turned.reshape(values.shape)


def on_device(
    tokens,
    positions,
    expert_picks,
    priority,
    first_gain,
    query_weight,
    key_projection_matrix,
    value_projection_matrix,
    output_weight,
    second_gain,
    router_weight,
    gate_weight,
    up_weight,
    down_weight,
    cotangent,
):
    devices = lax.axis_size("dev")
    rows, model = tokens.shape
    split = devices // EXPERTS
    capacity = split * ((9 * rows * TOP + 8 * EXPERTS * split - 1) // (8 * EXPERTS * split))
    weight_rows = query_weight.shape[0]

    output_matrix = lax.all_gather(output_weight, "dev", axis=0, tiled=True)

    extra = [query_weight, key_projection_matrix, value_projection_matrix, router_weight]
    pad = (-(QKV + EXPERTS)) % 128
    packed = jnp.concatenate(extra + [jnp.zeros((weight_rows, pad), BF16)], axis=1)
    q_width, k_width = QUERY_HEADS * HEAD_DIM, KEY_HEADS * HEAD_DIM
    inputs = tokens.astype(F32)
    half_dim = HEAD_DIM // 2
    frequency = jnp.power(10000.0, -(jnp.arange(half_dim, dtype=F32) * 2.0) / HEAD_DIM)
    angle = positions.astype(F32)[None, :] * frequency[:, None]
    cos_t, sin_t = jnp.cos(angle), jnp.sin(angle)
    lo = (jnp.arange(rows, dtype=jnp.int32) - positions)[None, :]
    one_hot = expert_picks[:, :, None] == jnp.arange(EXPERTS, dtype=jnp.int32)
    picked_any = jnp.any(one_hot, axis=1)
    turn = jnp.sum(jnp.where(one_hot, priority[:, :, None], 0), axis=1).astype(F32)
    turn = jnp.where(picked_any, turn, UNPICKED)

    if meshed():
        query_t, attended_t, lse, window, plane_slots, expert_up, matrices, normed_one, gains, scale_one = front(
            lo, cos_t, sin_t, tokens, extra[:3], router_weight, cotangent, turn, first_gain[None, :], second_gain[None, :]
        )
        gain_first, gain_second = gains[0], gains[1]
    else:
        matrices, gain_first, gain_second = (
            lax.all_gather(v, "dev", axis=0, tiled=True) for v in (packed, first_gain, second_gain)
        )
        gain_first, gain_second = gain_first.astype(F32), gain_second.astype(F32)
        rank = jnp.sum((turn.T[:, None, :] < turn.T[:, :, None]).astype(jnp.int32), axis=2)
        slot_rows = jnp.where(picked_any.T & (rank < capacity), rank, -1).astype(F32)
        scale_one = rms_scale(inputs)
        normed_one = (inputs * scale_one * gain_first).astype(BF16)
        qkv_t = dims(matrices[:, :QKV], normed_one, 0, 1)
        query_t = rotate_t(qkv_t[:q_width], cos_t, sin_t).astype(BF16) * BF16(HEAD_DIM**-0.5)
        key = rotate_t(qkv_t[q_width : q_width + k_width], cos_t, sin_t).astype(BF16).T
        value = qkv_t[q_width + k_width :].astype(BF16).T
        window, offset = window_of(jnp.stack([key, value])), jnp.int32(0)
        attended_t, lse = attend(query_t, window, offset, lo)
    qkv_matrix = matrices[:, :QKV]
    router_matrix = matrices[:, QKV : QKV + EXPERTS]
    residual = inputs + dims(attended_t, output_matrix, 0, 0)
    scale_two = rms_scale(residual)
    normed_two = (residual * scale_two * gain_second).astype(BF16)

    logits = dims(normed_two, router_matrix, 1, 0)
    logits = jnp.where(picked_any, logits, MASKED)
    picked_exp = jnp.exp(logits - jnp.max(logits, axis=1, keepdims=True))
    gates = picked_exp / jnp.sum(picked_exp, axis=1, keepdims=True)

    if meshed():
        gate_rows = jnp.pad(gates.T.reshape(EXPERTS, rows // 128, 128), ((0, 0), (0, 8 - rows // 128), (0, 0)))
        expert_in, grad_rows, out_rows, gated_hidden, gate_in_grad, up_in_grad, gate_grad_rows = run_experts(
            normed_two, gate_rows, plane_slots, expert_up, gate_weight, up_weight, down_weight
        )
        returned_grad, gate_grad, gate_gradient, up_gradient, down_gradient = run_grads(
            grad_rows, plane_slots, gate_grad_rows, expert_in, expert_up, gated_hidden, gate_in_grad, up_in_grad
        )
        gate_grad = gate_grad[:, : rows // 128].reshape(EXPERTS, rows).T
    else:
        gate_rows, slot = (
            lax.all_to_all(jnp.repeat(v, split, axis=0), "dev", split_axis=0, concat_axis=0, tiled=True)
            for v in (gates.T, slot_rows)
        )
        pair_slot = jnp.where(
            slot.reshape(devices // 2, 2, rows) >= 0,
            slot.reshape(devices // 2, 2, rows) + jnp.array([[0], [capacity]], F32),
            -1.0,
        ).astype(jnp.int32).reshape(devices // 2, 1, 2 * rows)
        all_upstream = lax.all_gather(cotangent, "dev", axis=0, tiled=True)
        all_normed = lax.all_gather(normed_two, "dev", axis=0, tiled=True)
        expert_in, expert_up = dispatch(pair_slot, all_normed, all_upstream, 2 * capacity)
        slot_hit = slot[:, None, :] == jnp.arange(capacity, dtype=F32)[None, :, None]
        gate_of_slot = jnp.sum(jnp.where(slot_hit, gate_rows[:, None, :], 0.0), axis=2).reshape(-1, 1)
        gate_in = dims(expert_in, gate_weight, 1, 0)
        up_in = dims(expert_in, up_weight, 1, 0)
        sigmoid_gate = 1.0 / (1.0 + jnp.exp(-gate_in))
        silu_gate = gate_in * sigmoid_gate
        hidden = (silu_gate * up_in).astype(BF16)
        gated_hidden = (hidden.astype(F32) * gate_of_slot).astype(BF16)
        hidden_up = dims(expert_up, down_weight, 1, 1)
        hidden_grad = hidden_up * gate_of_slot
        gate_grad_slot = jnp.sum(hidden.astype(F32) * hidden_up, axis=1).reshape(devices, capacity)
        gate_in_grad = (hidden_grad * up_in * sigmoid_gate * (1.0 + gate_in * (1.0 - sigmoid_gate))).astype(BF16)
        up_in_grad = (hidden_grad * silu_gate).astype(BF16)
        partial_in = (dims(gate_in_grad, gate_weight, 1, 1) + dims(up_in_grad, up_weight, 1, 1)).astype(BF16)
        gate_grad_rows = jnp.sum(jnp.where(slot_hit, gate_grad_slot[:, :, None], 0.0), axis=1)
        returned_grad = lax.psum_scatter(
            combine(pair_slot, partial_in, 2 * capacity), "dev", scatter_dimension=0, tiled=True
        ).astype(F32)
        gate_grad = lax.all_to_all(gate_grad_rows, "dev", split_axis=0, concat_axis=0, tiled=True)
        gate_grad = jnp.sum(gate_grad.reshape(EXPERTS, split, rows), axis=1).T
        partial_out = dims(gated_hidden, down_weight, 1, 0).astype(BF16)
        dense_out = combine(pair_slot, partial_out, 2 * capacity)
        mixture = lax.psum_scatter(dense_out, "dev", scatter_dimension=0, tiled=True).astype(F32)
        down_gradient = dims(gated_hidden, expert_up, 0, 0)
        gate_gradient = dims(expert_in, gate_in_grad, 0, 0)
        up_gradient = dims(expert_in, up_in_grad, 0, 0)

    upstream = cotangent.astype(F32)
    logit_grad = (gates * (gate_grad - jnp.sum(gates * gate_grad, axis=1, keepdims=True))).astype(BF16)
    router_gradient = dims(normed_two, logit_grad, 0, 0)
    normed_two_grad = returned_grad + dims(logit_grad, router_matrix, 1, 1)
    weighted_two = normed_two_grad * gain_second
    second_gain_grad = jnp.sum(normed_two_grad * residual * scale_two, axis=0)
    residual_grad = (
        upstream
        + scale_two * weighted_two
        - residual * scale_two**3 * jnp.mean(weighted_two * residual, axis=-1, keepdims=True)
    )
    branch_grad = residual_grad.astype(BF16)
    output_gradient = dims(attended_t, branch_grad, 1, 0).astype(BF16)
    output_gradient = lax.psum_scatter(output_gradient, "dev", scatter_dimension=0, tiled=True).astype(F32)

    if meshed():
        qkv_grad, layer_output = attend_back_mesh(
            query_t, window, lo, branch_grad, output_matrix, lse, attended_t, cos_t, sin_t, out_rows, plane_slots, residual
        )
    else:
        grad_t = dims(output_matrix, branch_grad, 1, 1).astype(BF16)
        query_grad_t, window_grad = attend_back(query_t, window, offset, lo, grad_t, lse, attended_t, cos_t, sin_t)
        key_grad, value_grad = unwindow(window_grad)
        key_grad_t = rotate_t(key_grad.T, cos_t, -sin_t).astype(BF16)
        qkv_grad_t = jnp.concatenate([query_grad_t, key_grad_t, value_grad.T.astype(BF16)], axis=0)
        layer_output = (residual + mixture).astype(BF16)
    more = jnp.concatenate(
        [router_gradient, second_gain_grad[:, None], jnp.zeros((model, (-(EXPERTS + 1)) % 256), F32)], axis=1
    ).astype(BF16)
    if meshed():
        query_sums, key_sums, value_sums, more_sums, tokens_gradient, first_sums = finish(
            normed_one, qkv_grad, matrices, more, gain_first[None, :], scale_one, tokens, residual_grad
        )
        first_sums = first_sums[0, :weight_rows]
        (
            gate_gradient, up_gradient, down_gradient, layer_output, tokens_gradient, query_sums, key_sums, value_sums
        ) = hand_over(
            gate_gradient, up_gradient, down_gradient, layer_output, tokens_gradient, query_sums, key_sums, value_sums
        )
    else:
        qkv_gradient = dims(normed_one, qkv_grad_t, 0, 1).astype(BF16)
        normed_one_grad = dims(qkv_grad_t, qkv_matrix, 0, 1)
        weighted_one = normed_one_grad * gain_first
        tokens_gradient = (
            residual_grad
            + scale_one * weighted_one
            - inputs * scale_one**3 * jnp.mean(weighted_one * inputs, axis=-1, keepdims=True)
        )
        sums = lax.psum_scatter(
            jnp.concatenate([qkv_gradient, more], axis=1), "dev", scatter_dimension=0, tiled=True
        ).astype(F32)
        query_sums, key_sums, value_sums, more_sums = jnp.split(sums, [q_width, q_width + k_width, QKV], axis=1)
        first_sums = lax.psum_scatter(
            jnp.sum(normed_one_grad * inputs * scale_one, axis=0), "dev", scatter_dimension=0, tiled=True
        )
    return (
        layer_output,
        tokens_gradient,
        first_sums,
        query_sums,
        key_sums,
        value_sums,
        output_gradient,
        more_sums[:, EXPERTS],
        more_sums[:, :EXPERTS],
        gate_gradient,
        up_gradient,
        down_gradient,
    )


def solution(mesh):
    rows, whole = P("dev", None), P("dev")
    columns = P(None, "dev")
    return jax.shard_map(
        on_device,
        mesh=mesh,
        in_specs=(rows, whole, rows, rows, whole, rows, rows, rows, rows, whole, rows, columns, columns, rows, rows),
        out_specs=(rows, rows, whole, rows, rows, rows, rows, whole, rows, columns, columns, rows),
        check_vma=False,
    )
```

```python
import functools
import jax, jax.numpy as jnp
from jax import lax
from jax.experimental import pallas as pl
from jax.experimental.pallas import tpu as pltpu

MESH = pl.DeviceIdType.MESH


def place():
    me = lax.axis_index("dev")
    return lax.rem(me // 8, 4), lax.rem(me // 4, 2), lax.rem(me // 2, 2), lax.rem(me, 2)


def number(z, y, x, c):
    return ((z * 2 + y) * 2 + x) * 2 + c


def greet(partners):
    barrier = pltpu.get_barrier_semaphore()
    for partner in partners:
        pl.semaphore_signal(barrier, inc=1, device_id=(partner,), device_id_type=MESH)
    pl.semaphore_wait(barrier, len(partners))


def partners_of(z, y, x, c):
    return [
        number(z, y, x, 1 - c),
        number(z, y, 1 - x, c),
        number(z, 1 - y, x, c),
        number(lax.rem(z + 1, 4), y, x, c),
        number(lax.rem(z + 2, 4), y, x, c),
        number(lax.rem(z + 3, 4), y, x, c),
    ]


class Whole:
    scratch = [pltpu.SemaphoreType.DMA] + [
        pltpu.SemaphoreType.DMA(shape)
        for shape in ((2, 2, 4), (2, 4), (2, 3, 4), (2, 3, 4), (2, 4, 4), (2, 4, 4))
    ]

    def __init__(self, x_ref, o_ref, scratch):
        self.x_ref, self.o_ref = x_ref, o_ref
        self.local_sem, self.zs, self.zr, self.fs, self.fr, self.cs, self.cr = scratch
        self.z, self.y, self.x, self.c = z, y, x, c = place()
        self.rows, cols = x_ref.shape
        half = (cols // 256) * 128
        self.pieces = (pl.ds(0, half), pl.ds(half, cols - half))
        self.sibling = number(z, y, x, 1 - c)
        self.me = number(z, y, x, c)
        self.around = (number(z, 1 - y, x, c), number(z, y, 1 - x, c))
        self.far = ((1, 0), (0, 1))
        self.local = pltpu.make_async_copy(x_ref, self.there(self.me), self.local_sem)

    def turn(self, i):
        middle = i if i < 2 else 5 - i
        return jnp.where(self.z == 0, (4 - i) % 4, jnp.where(self.z == 3, i, middle))

    def there(self, block, p=None):
        at = pl.ds(pl.multiple_of(block * self.rows, 16), self.rows)
        return self.o_ref.at[at, :] if p is None else self.o_ref.at[at, self.pieces[p]]

    def copy(self, source, block, p, send_sem, recv_sem, target):
        return pltpu.make_async_remote_copy(
            src_ref=source, dst_ref=self.there(block, p), send_sem=send_sem, recv_sem=recv_sem,
            device_id=(target,), device_id_type=MESH)

    def block(self, k, fy=0, fx=0):
        return number(lax.rem(self.z + 4 - k, 4), (1 - self.y) if fy else self.y, (1 - self.x) if fx else self.x, self.c)

    def along(self, i, use):
        k = self.turn(i)
        zz = lax.rem(self.z + 4 - k, 4)
        for up, step in ((1, 1), (0, 3)):
            go = (zz <= self.z) & (self.z < 3) if up else (zz >= self.z) & (self.z > 0)

            @pl.when(go)
            def _(up=up, step=step):
                block = self.block(k)
                target = number(lax.rem(self.z + step, 4), self.y, self.x, self.c)
                for p in range(2):
                    source = self.x_ref.at[:, self.pieces[p]] if i == 0 else self.there(block, p)
                    use(self.copy(
                        source, block, p, self.zs.at[p, up, k], self.zr.at[p, lax.rem(k + step, 4)], target))

    def hop(self, p, n, k):
        block = self.block(k, *self.far[p]) if n == 2 else self.block(k)
        target = self.around[p] if n == 0 else self.around[1 - p]
        return self.copy(self.there(block, p), block, p, self.fs.at[p, n, k], self.fr.at[p, n, k], target)

    def across(self, p, n, k):
        fy, fx = ((0, 0), self.far[p], (1 - self.far[p][0], 1 - self.far[p][1]), (1, 1))[n]
        block = self.block(k, fy, fx)
        return self.copy(self.there(block, p), block, p, self.cs.at[p, n, k], self.cr.at[p, n, k], self.sibling)

    def start(self):
        self.local.start()
        self.along(0, lambda cp: cp.start())

    def one(self, i):
        k = self.turn(i)
        if i == 0:
            self.local.wait()
        else:
            block = self.block(k)
            for p in range(2):
                self.copy(self.there(block, p), block, p, self.zs.at[p, 0, 0], self.zr.at[p, k], self.sibling).wait_recv()
            self.along(i, lambda cp: cp.start())
        for p in range(2):
            self.hop(p, 0, k).start()
            self.hop(p, 1, k).start()
            self.across(p, 0, k).start()

    def two(self, i):
        k = self.turn(i)
        for p in range(2):
            self.hop(p, 0, k).wait_recv()
            self.hop(p, 2, k).start()
            self.across(p, 1, k).start()

    def three(self, i):
        k = self.turn(i)
        for n in (1, 2):
            for p in range(2):
                self.hop(p, n, k).wait_recv()
                self.across(p, n + 1, k).start()

    def end(self):
        for k in range(4):
            for p in range(2):
                for n in range(4):
                    self.across(p, n, k).wait_recv()

    def sent(self):
        for i in range(4):
            self.along(i, lambda cp: cp.wait_send())
        for k in range(4):
            for p in range(2):
                for n in range(3):
                    self.hop(p, n, k).wait_send()
                for n in range(4):
                    self.across(p, n, k).wait_send()


from jax.sharding import PartitionSpec as P

QUERY_HEADS = 24
KEY_HEADS = 8
HEAD_DIM = 64
GROUP = QUERY_HEADS // KEY_HEADS
TOP = 8
EXPERTS = 32
MAXDOC = 2000
EPSILON = 1e-06
UNPICKED = 1e9
CAPACITY = 72
MASKED = -1e30
QKV = (QUERY_HEADS + 2 * KEY_HEADS) * HEAD_DIM
F32 = jnp.float32
BF16 = jnp.bfloat16


def meshed():
    return lax.axis_size("dev") == 32


def dims(a, b, ca, cb):
    return lax.dot_general(a, b, (((ca,), (cb,)), ((), ())), preferred_element_type=F32)


class Window:
    scratch = [pltpu.SemaphoreType.DMA((2,)), pltpu.SemaphoreType.DMA((9,)), pltpu.SemaphoreType.DMA((9,))]

    def __init__(self, rows, kv_ref, out, scratch):
        self.rows, self.kv_ref, self.out = rows, kv_ref, out
        self.lsem, self.ss, self.rs = scratch
        self.z, self.y, self.x, self.c = place()
        self.p = self.y * 2 + self.x
        self.sibling = number(self.z, self.y, self.x, 1 - self.c)
        self.near = [(self.z * 4 + lax.rem(self.p + d, 4)) * 2 + self.c for d in (1, 2, 3)]
        self.own_in = pltpu.make_async_copy(kv_ref, self.slot(4, self.c), self.lsem.at[0])
        self.stand_in = pltpu.make_async_copy(kv_ref, self.slot(0, self.c), self.lsem.at[1])
        self.to_up = self.copy(kv_ref, 0, 0, number(lax.rem(self.z + 1, 4), self.y, self.x, self.c))

    def slot(self, s, core):
        return self.out.at[:, pl.ds(pl.multiple_of((2 * s + core) * self.rows, 16), self.rows), :]

    def copy(self, source, s, n, target):
        return pltpu.make_async_remote_copy(
            src_ref=source, dst_ref=self.slot(s, self.c), send_sem=self.ss.at[n], recv_sem=self.rs.at[n],
            device_id=(target,), device_id_type=MESH)

    def own_near(self, d):
        return self.copy(self.kv_ref, 4 - d, d, self.near[d - 1])

    def across(self, s):
        source = self.kv_ref if s == 4 else self.slot(s, self.c)
        return self.copy(source, s, {4: 4, 0: 5}.get(s, 9 - s), self.sibling)

    def start(self):
        self.own_in.start()

        @pl.when(self.z < 3)
        def _():
            self.to_up.start()

        @pl.when(self.z == 0)
        def _():
            self.stand_in.start()

        for d in (1, 3, 2):
            @pl.when(self.p + d < 4)
            def _(d=d):
                self.own_near(d).start()
        self.across(4).start()

    def previous(self):
        @pl.when(self.z == 0)
        def _():
            self.stand_in.wait()

        @pl.when(self.z > 0)
        def _():
            self.to_up.wait_recv()

        for d in (3, 1, 2):
            @pl.when(self.p + d >= 4)
            def _(d=d):
                self.copy(self.slot(0, self.c), 4 - d, d, self.near[d - 1]).start()
        self.across(0).start()

    def pass_on(self):
        for d in (1, 3, 2):
            self.own_near(d).wait_recv()
            self.across(4 - d).start()

    def end(self):
        for s in range(5):
            pltpu.make_async_remote_copy(
                src_ref=self.kv_ref, dst_ref=self.slot(s, 1 - self.c), send_sem=self.ss.at[0],
                recv_sem=self.rs.at[{4: 4, 0: 5}.get(s, 9 - s)], device_id=(self.sibling,), device_id_type=MESH).wait_recv()
        self.own_in.wait()

    def sent(self):
        @pl.when(self.z < 3)
        def _():
            self.to_up.wait_send()

        for d in (1, 2, 3):
            self.own_near(d).wait_send()
        for s in range(5):
            self.across(s).wait_send()


def window_of(kv):
    rows = kv.shape[1]
    devices = lax.axis_size("dev")
    back = (MAXDOC + rows - 2) // rows
    parts = [
        lax.ppermute(kv, "dev", [(i - d, i) for i in range(d, devices)]) for d in range(back, 0, -1)
    ]
    return jnp.concatenate(parts + [kv, jnp.zeros_like(kv)], axis=1)


class Unwindow:
    @staticmethod
    def scratch(rows, width):
        return [
            pltpu.VMEM((5, 2, rows, width), BF16),
            pltpu.VMEM((3, 2, rows, width), BF16),
            pltpu.VMEM((2, rows, width), BF16),
            pltpu.SemaphoreType.DMA((9,)), pltpu.SemaphoreType.DMA((9,)),
        ]

    n_scratch = 5
    order = (3, 1, 2, 0, 4)

    def __init__(self, rows, grads, o_ref, scratch):
        self.rows, self.grads, self.o_ref = rows, grads, o_ref
        self.got, self.near_got, self.far, self.ss, self.rs = scratch
        self.z, self.y, self.x, self.c = place()
        self.p = self.y * 2 + self.x
        self.sibling = number(self.z, self.y, self.x, 1 - self.c)
        self.to_down = pltpu.make_async_remote_copy(
            src_ref=self.got.at[0], dst_ref=self.far, send_sem=self.ss.at[8], recv_sem=self.rs.at[8],
            device_id=(number(lax.rem(self.z + 3, 4), self.y, self.x, self.c),), device_id_type=MESH)

    def to_sibling(self, s):
        at = pl.ds(pl.multiple_of((2 * s + 1 - self.c) * self.rows, 16), self.rows)
        return pltpu.make_async_remote_copy(
            src_ref=self.grads.at[:, at, :], dst_ref=self.got.at[s], send_sem=self.ss.at[s], recv_sem=self.rs.at[s],
            device_id=(self.sibling,), device_id_type=MESH)

    def to_owner(self, d):
        owner = (self.z * 4 + lax.rem(self.p + 4 - d, 4)) * 2 + self.c
        return pltpu.make_async_remote_copy(
            src_ref=self.got.at[4 - d], dst_ref=self.near_got.at[d - 1], send_sem=self.ss.at[4 + d], recv_sem=self.rs.at[4 + d],
            device_id=(owner,), device_id_type=MESH)

    def rowwise(self, body):
        for h in range(2):
            def step(i, _, h=h):
                body(h, pl.multiple_of(i * 32, 32))
                return 0
            lax.fori_loop(0, self.rows // 32, step, 0)

    def start(self):
        for s in self.order:
            self.to_sibling(s).start()

    def sums(self):
        for s in self.order:
            self.to_sibling(s).wait_recv()
            first = (2 * s + self.c) * self.rows

            def both(h, r, s=s, first=first):
                at = pl.ds(r, 32)
                mine = self.grads[h, pl.ds(pl.multiple_of(first + r, 32), 32), :]
                total = self.got[s, h, at, :].astype(F32) + mine.astype(F32)
                if s == 4:
                    self.o_ref[h, at, :] = total
                else:
                    self.got[s, h, at, :] = total.astype(BF16)
            self.rowwise(both)
            if 0 < s < 4:
                self.to_owner(4 - s).start()

    def near(self):
        for d in (1, 3, 2):
            self.to_owner(d).wait_recv()

            @pl.when(self.p + d < 4)
            def _(d=d):
                def body(h, r):
                    at = pl.ds(r, 32)
                    self.o_ref[h, at, :] += self.near_got[d - 1, h, at, :].astype(F32)
                self.rowwise(body)

            @pl.when(self.p + d >= 4)
            def _(d=d):
                def body(h, r):
                    at = pl.ds(r, 32)
                    total = self.got[0, h, at, :].astype(F32) + self.near_got[d - 1, h, at, :].astype(F32)
                    self.got[0, h, at, :] = total.astype(BF16)
                self.rowwise(body)

        @pl.when(self.z > 0)
        def _():
            self.to_down.start()

    def end(self):
        @pl.when(self.z < 3)
        def _():
            self.to_down.wait_recv()

            def body(h, r):
                at = pl.ds(r, 32)
                self.o_ref[h, at, :] += self.far[h, at, :].astype(F32)
            self.rowwise(body)

        @pl.when(self.z > 0)
        def _():
            self.to_down.wait_send()

        for s in range(5):
            self.to_sibling(s).wait_send()
        for d in (1, 2, 3):
            self.to_owner(d).wait_send()


def unwindow(grads):
    rows = grads.shape[1] // 10
    devices = lax.axis_size("dev")
    back = (MAXDOC + rows - 2) // rows
    total = grads[:, back * rows : (back + 1) * rows].astype(F32)
    for d in range(1, back + 1):
        piece = grads[:, (back - d) * rows : (back - d + 1) * rows]
        moved = lax.ppermute(piece, "dev", [(i, i - d) for i in range(d, devices)])
        total = total + moved.astype(F32)
    return total


def make_bias(bias, lo_ref, chunks, rows):
    def fill(ch, _):
        at = pl.ds(pl.multiple_of(ch * rows, rows), rows)
        relative = lax.broadcasted_iota(jnp.int32, (rows, rows), 0) + (ch - (chunks - 1)) * rows
        query = lax.broadcasted_iota(jnp.int32, (rows, rows), 1)
        allowed = (relative <= query) & (relative >= lo_ref[...])
        bias[at, :] = jnp.where(allowed, 0.0, MASKED)
        return 0
    lax.fori_loop(0, chunks, fill, 0)


def side_by_side(ref, half):
    first = half * GROUP
    return jnp.concatenate(
        [ref[(first + g) * HEAD_DIM : (first + g + 1) * HEAD_DIM, :] for g in range(GROUP)], axis=1
    )


def stats_of(ref, half):
    return jnp.concatenate([ref[0, half * GROUP + g : half * GROUP + g + 1, :] for g in range(GROUP)], axis=1)


def attend_pair(chunks, rows, off, q_ref, kv_ref, o_ref, lse_ref, bias, between):
    lse_ref[...] = jnp.zeros_like(lse_ref)
    width = GROUP * rows
    for half in range(2):
        lanes = slice(half * HEAD_DIM, (half + 1) * HEAD_DIM)
        queries = side_by_side(q_ref, half)

        def chunk(i, carry, lanes=lanes, queries=queries):
            ch = chunks - 1 - i
            at = pl.ds(pl.multiple_of((ch + off) * rows, rows), rows)
            key, value = kv_ref[0, at, lanes], kv_ref[1, at, lanes]
            shift = bias[pl.ds(pl.multiple_of(ch * rows, rows), rows), :]
            top, total, mixed = carry
            score = dims(key, queries, 1, 0) + jnp.concatenate([shift] * GROUP, axis=1)
            new_top = jnp.maximum(top, jnp.max(score, axis=0, keepdims=True))
            weight = jnp.exp(score - new_top)
            fade = jnp.exp(top - new_top)
            total = total * fade + jnp.sum(weight, axis=0, keepdims=True)
            mixed = mixed * fade + dims(value, weight.astype(BF16), 0, 0)
            return new_top, total, mixed

        start = (jnp.full((1, width), MASKED, F32), jnp.zeros((1, width), F32), jnp.zeros((HEAD_DIM, width), F32))
        top, total, mixed = lax.fori_loop(0, chunks, chunk, start, unroll=3)
        mixed = (mixed / total).astype(BF16)
        lse = top + jnp.log(total)
        for g in range(GROUP):
            n = half * GROUP + g
            o_ref[n * HEAD_DIM : (n + 1) * HEAD_DIM, :] = mixed[:, g * rows : (g + 1) * rows]
            lse_ref[0, n : n + 1, :] = lse[:, g * rows : (g + 1) * rows]
        between(half)


def attend_kernel(chunks, rows, off_ref, lo_ref, q_ref, kv_ref, o_ref, lse_ref, bias):
    @pl.when(pl.program_id(0) == 0)
    def _():
        make_bias(bias, lo_ref, chunks, rows)

    attend_pair(chunks, rows, off_ref[0], q_ref, kv_ref, o_ref, lse_ref, bias, lambda half: None)


def attend_back_pair(
    chunks, rows, off, cos_ref, sin_ref, q_ref, kv_ref, g_ref, lse_ref, out_ref, dq_ref, dkv_ref, bias, between
):
    unused = pl.ds(pl.multiple_of((1 - off) * chunks * rows, rows), rows)
    dkv_ref[:, unused, :] = jnp.zeros((2, rows, 2 * HEAD_DIM), BF16)
    for half in range(2):
        lanes = slice(half * HEAD_DIM, (half + 1) * HEAD_DIM)
        queries, grads = side_by_side(q_ref, half), side_by_side(g_ref, half)
        lse = stats_of(lse_ref, half)
        mixed = side_by_side(out_ref, half).astype(F32)
        delta = jnp.sum(mixed * grads.astype(F32), axis=0, keepdims=True)

        def chunk(ch, query_grad, lanes=lanes, queries=queries, grads=grads, lse=lse, delta=delta):
            at = pl.ds(pl.multiple_of((ch + off) * rows, rows), rows)
            key, value = kv_ref[0, at, lanes], kv_ref[1, at, lanes]
            shift = bias[pl.ds(pl.multiple_of(ch * rows, rows), rows), :]
            score = dims(key, queries, 1, 0) + jnp.concatenate([shift] * GROUP, axis=1)
            weight = jnp.exp(score - lse)
            score_grad = (weight * (dims(value, grads, 1, 0) - delta)).astype(BF16)
            dkv_ref[0, at, lanes] = dims(score_grad, queries, 1, 1).astype(BF16)
            dkv_ref[1, at, lanes] = dims(weight.astype(BF16), grads, 1, 1).astype(BF16)
            return query_grad + dims(key, score_grad, 0, 0)

        done = lax.fori_loop(0, chunks, chunk, jnp.zeros((HEAD_DIM, GROUP * rows), F32), unroll=3)
        done = done * (HEAD_DIM**-0.5)
        cosine, sine = cos_ref[...], sin_ref[...]
        for g in range(GROUP):
            grad = done[:, g * rows : (g + 1) * rows]
            u, w = grad[: HEAD_DIM // 2], grad[HEAD_DIM // 2 :]
            n = (half * GROUP + g) * HEAD_DIM
            dq_ref[n : n + HEAD_DIM // 2, :] = (u * cosine + w * sine).astype(BF16)
            dq_ref[n + HEAD_DIM // 2 : n + HEAD_DIM, :] = (w * cosine - u * sine).astype(BF16)
        between(half)


def attend_back_kernel(
    chunks, rows, off_ref, lo_ref, cos_ref, sin_ref, q_ref, kv_ref, g_ref, lse_ref, out_ref, dq_ref, dkv_ref, bias
):
    @pl.when(pl.program_id(0) == 0)
    def _():
        make_bias(bias, lo_ref, chunks, rows)

    attend_back_pair(
        chunks, rows, off_ref[0], cos_ref, sin_ref, q_ref, kv_ref, g_ref, lse_ref, out_ref, dq_ref, dkv_ref, bias,
        lambda half: None,
    )


def attention_specs(rows, span):
    width = 2 * GROUP * HEAD_DIM
    return dict(
        smem=pl.BlockSpec(memory_space=pltpu.SMEM),
        row=pl.BlockSpec((1, rows), lambda j: (0, 0)),
        table=pl.BlockSpec((HEAD_DIM // 2, rows), lambda j: (0, 0)),
        query=pl.BlockSpec((width, rows), lambda j: (j, 0)),
        kv=pl.BlockSpec((2, span, 2 * HEAD_DIM), lambda j: (0, 0, j)),
        stat=pl.BlockSpec((1, 8, rows), lambda j: (j, 0, 0)),
    )


def attend(query_t, window, offset, lo):
    rows, span = query_t.shape[1], window.shape[1]
    chunks = span // rows - 1
    s = attention_specs(rows, span)
    return pl.pallas_call(
        functools.partial(attend_kernel, chunks, rows),
        grid=(KEY_HEADS // 2,),
        in_specs=[s["smem"], s["row"], s["query"], s["kv"]],
        out_specs=[s["query"], s["stat"]],
        out_shape=[
            jax.ShapeDtypeStruct(query_t.shape, BF16),
            jax.ShapeDtypeStruct((KEY_HEADS // 2, 8, rows), F32),
        ],
        scratch_shapes=[pltpu.VMEM((chunks * rows, rows), F32)],
        compiler_params=pltpu.CompilerParams(vmem_limit_bytes=40 * 2**20),
        cost_estimate=pl.CostEstimate(flops=7 * 10**9, bytes_accessed=8 * 10**6, transcendentals=15 * 10**6),
        name="attend",
    )(offset.reshape(1), lo, query_t, window)


def attend_back(query_t, window, offset, lo, grad_t, lse, attended_t, cos_t, sin_t):
    rows, span = query_t.shape[1], window.shape[1]
    chunks = span // rows - 1
    s = attention_specs(rows, span)
    return pl.pallas_call(
        functools.partial(attend_back_kernel, chunks, rows),
        grid=(KEY_HEADS // 2,),
        in_specs=[s["smem"], s["row"], s["table"], s["table"], s["query"], s["kv"], s["query"], s["stat"], s["query"]],
        out_specs=[s["query"], s["kv"]],
        out_shape=[
            jax.ShapeDtypeStruct(query_t.shape, BF16),
            jax.ShapeDtypeStruct(window.shape, BF16),
        ],
        scratch_shapes=[pltpu.VMEM((chunks * rows, rows), F32)],
        compiler_params=pltpu.CompilerParams(vmem_limit_bytes=40 * 2**20),
        cost_estimate=pl.CostEstimate(flops=18 * 10**9, bytes_accessed=16 * 10**6, transcendentals=15 * 10**6),
        name="attend_back",
    )(offset.reshape(1), lo, cos_t, sin_t, query_t, window, grad_t, lse, attended_t)


def hits(slot_ref, slots):
    width = slot_ref.shape[-1]
    return slot_ref[0] == lax.broadcasted_iota(jnp.int32, (slots, width), 0)


def dispatch_kernel(slot_ref, x_ref, u_ref, xo_ref, uo_ref):
    chosen = jnp.where(hits(slot_ref, xo_ref.shape[0]), 1.0, 0.0).astype(BF16)
    xo_ref[...] = dims(chosen, x_ref[...], 1, 0).astype(BF16)
    uo_ref[...] = dims(chosen, u_ref[...], 1, 0).astype(BF16)


def dispatch(slot, normed, upstream, slots):
    pairs, _, width = slot.shape
    model = normed.shape[1]
    return pl.pallas_call(
        dispatch_kernel,
        grid=(pairs,),
        in_specs=[
            pl.BlockSpec((1, 1, width), lambda i: (i, 0, 0)),
            pl.BlockSpec((width, model), lambda i: (i, 0)),
            pl.BlockSpec((width, model), lambda i: (i, 0)),
        ],
        out_specs=[pl.BlockSpec((slots, model), lambda i: (i, 0))] * 2,
        out_shape=[jax.ShapeDtypeStruct((pairs * slots, model), BF16)] * 2,
        compiler_params=pltpu.CompilerParams(vmem_limit_bytes=40 * 2**20),
        cost_estimate=pl.CostEstimate(flops=2 * 10**9, bytes_accessed=65 * 10**6, transcendentals=0),
        name="dispatch",
    )(slot, normed, upstream)


def combine_kernel(slot_ref, r_ref, o_ref):
    chosen = jnp.where(hits(slot_ref, r_ref.shape[0]), 1.0, 0.0).astype(BF16)
    o_ref[...] = dims(chosen, r_ref[...], 0, 0).astype(BF16)


def combine(slot, rows, slots):
    pairs, _, width = slot.shape
    model = rows.shape[1]
    return pl.pallas_call(
        combine_kernel,
        grid=(pairs,),
        in_specs=[
            pl.BlockSpec((1, 1, width), lambda i: (i, 0, 0)),
            pl.BlockSpec((slots, model), lambda i: (i, 0)),
        ],
        out_specs=pl.BlockSpec((width, model), lambda i: (i, 0)),
        out_shape=jax.ShapeDtypeStruct((pairs * width, model), BF16),
        compiler_params=pltpu.CompilerParams(vmem_limit_bytes=40 * 2**20),
        cost_estimate=pl.CostEstimate(flops=10**9, bytes_accessed=33 * 10**6, transcendentals=0),
        name="combine",
    )(slot, rows)


SLOTS = 80


def far_first(i):
    return jnp.where(i == 0, 2, jnp.where(i == 3, 0, 2 * i - 1))


def greet_all():
    me = lax.axis_index("dev")
    barrier = pltpu.get_barrier_semaphore()

    def signal(d, _):
        pl.semaphore_signal(barrier, inc=1, device_id=(lax.rem(me + d, 32),), device_id_type=MESH)
        return 0
    lax.fori_loop(1, 32, signal, 0)
    pl.semaphore_wait(barrier, 31)


class Swap:
    def __init__(self, source, into, ss, rs):
        self.me = lax.axis_index("dev")
        self.source, self.into, self.ss, self.rs = source, into, ss, rs

    def copy(self, d):
        target = lax.rem(self.me + d, 32)
        return pltpu.make_async_remote_copy(
            src_ref=self.source(target), dst_ref=self.into.at[self.me], send_sem=self.ss.at[d], recv_sem=self.rs.at[d],
            device_id=(target,), device_id_type=MESH)

    def start(self):
        def one(d, _):
            self.copy(d).start()
            return 0
        lax.fori_loop(1, 32, one, 0)
        self.into[self.me] = self.source(self.me)[...]

    def wait_recv(self):
        def one(d, _):
            self.copy(d).wait_recv()
            return 0
        lax.fori_loop(1, 32, one, 0)

    def wait_send(self):
        def one(d, _):
            self.copy(d).wait_send()
            return 0
        lax.fori_loop(1, 32, one, 0)


def in_plane(y, x, c):
    return (y * 2 + x) * 2 + c


def chosen_rows(slots_ref, block, expert):
    row = slots_ref[block, pl.ds(expert, 1), :]
    return row == lax.broadcasted_iota(jnp.int32, (SLOTS, row.shape[1]), 0).astype(F32)


def greet_near():
    z, y, x, c = place()
    greet(
        [number(z, y, x, 1 - c)]
        + [number(z, 1 - y, x, cc) for cc in (c, 1 - c)]
        + [number(z, y, 1 - x, cc) for cc in (c, 1 - c)]
        + [number(z, 1 - y, 1 - x, c)]
        + [number(lax.rem(z + d, 4), y, x, c) for d in (1, 2, 3)]
    )


class Forth:
    scratch = staticmethod(lambda rows, half: [
        pltpu.VMEM((2, 2, 4, rows, half), BF16),
        pltpu.VMEM((2, 2, 4, 4, SLOTS, half), BF16),
        pltpu.SemaphoreType.DMA((2, 2, 4)), pltpu.SemaphoreType.DMA((2, 4)),
        pltpu.SemaphoreType.DMA((2, 4)), pltpu.SemaphoreType.DMA((2, 4)),
        pltpu.SemaphoreType.DMA((2, 2, 4, 4)), pltpu.SemaphoreType.DMA((2, 2, 4, 3)), pltpu.SemaphoreType.DMA((2,)),
    ])
    n_scratch = 9

    def __init__(self, x_ref, slots_ref, xi, scratch):
        self.x_ref, self.slots_ref, self.xi = x_ref, slots_ref, xi
        self.land, self.stage, self.zs, self.zr, self.fs, self.fr, self.cs, self.cr, self.own_sem = scratch
        self.z, self.y, self.x, self.c = place()
        half = x_ref.shape[1] // 2
        self.cols = [pl.ds(0, half), pl.ds(half, half)]

    def turn(self, i):
        middle = jnp.where(i < 2, i, 5 - i)
        return jnp.where(self.z == 0, lax.rem(4 - i, 4), jnp.where(self.z == 3, i, middle))

    def to_z(self, p, up, k, own=False):
        step = 1 if up else 3
        source = self.x_ref.at[:, self.cols[p]] if own else self.land.at[p, 0, k]
        there = lax.rem(k + step, 4)
        return pltpu.make_async_remote_copy(
            src_ref=source, dst_ref=self.land.at[p, 0, there],
            send_sem=self.zs.at[p, int(up), k], recv_sem=self.zr.at[p, there],
            device_id=(number(lax.rem(self.z + step, 4), self.y, self.x, self.c),), device_id_type=MESH)

    def hop(self, p, k):
        z, y, x, c = self.z, self.y, self.x, self.c
        beside = number(z, 1 - y, x, c) if p == 0 else number(z, y, 1 - x, c)
        return pltpu.make_async_remote_copy(
            src_ref=self.land.at[p, 0, k], dst_ref=self.land.at[p, 1, k],
            send_sem=self.fs.at[p, k], recv_sem=self.fr.at[p, k], device_id=(beside,), device_id_type=MESH)

    def block(self, p, h, k):
        zz = lax.rem(self.z + 4 - k, 4)
        if p == 0:
            return number(zz, (1 - self.y) if h else self.y, self.x, self.c)
        return number(zz, self.y, (1 - self.x) if h else self.x, self.c)

    def who(self, p):
        y, x, c = self.y, self.x, self.c
        ay, ax = (y, 1 - x) if p == 0 else (1 - y, x)
        return [(y, x, 1 - c), (ay, ax, c), (ay, ax, 1 - c), (y, x, c)]

    def slots_at(self, p, h, k):
        return self.xi.at[pl.ds(pl.multiple_of(self.block(p, h, k) * SLOTS, 16), SLOTS), self.cols[p]]

    def served(self, p, h, k, t):
        return pltpu.make_async_remote_copy(
            src_ref=self.stage.at[p, h, k, t], dst_ref=self.slots_at(p, h, k),
            send_sem=self.cs.at[p, h, k, t], recv_sem=self.cr.at[p, h, k, t],
            device_id=(number(self.z, *self.who(p)[t]),), device_id_type=MESH)

    def kept(self, p, h, k):
        return pltpu.make_async_copy(self.stage.at[p, h, k, 3], self.slots_at(p, h, k), self.cs.at[p, h, k, 3])

    def serve(self, p, h, k):
        block = self.block(p, h, k)
        source = self.land[p, h, k]
        for t, to in enumerate(self.who(p)):
            chosen = jnp.where(chosen_rows(self.slots_ref, block, in_plane(*to)), 1.0, 0.0).astype(BF16)
            self.stage[p, h, k, t] = dims(chosen, source, 1, 0).astype(BF16)
            if t < 3:
                self.served(p, h, k, t).start()
            else:
                self.kept(p, h, k).start()

    def own(self, p):
        return pltpu.make_async_copy(self.x_ref.at[:, self.cols[p]], self.land.at[p, 0, 0], self.own_sem.at[p])

    def along(self, i, use):
        k = self.turn(i)
        zz = lax.rem(self.z + 4 - k, 4)
        for p in range(2):
            @pl.when((zz < self.z) & (self.z < 3))
            def _(p=p):
                use(self.to_z(p, True, k))

            @pl.when((zz > self.z) & (self.z > 0))
            def _(p=p):
                use(self.to_z(p, False, k))

    def along_own(self, use):
        for p in range(2):
            @pl.when(self.z < 3)
            def _(p=p):
                use(self.to_z(p, True, 0, own=True))

            @pl.when(self.z > 0)
            def _(p=p):
                use(self.to_z(p, False, 0, own=True))

    def start(self):
        for p in range(2):
            self.own(p).start()
        self.along_own(lambda cp: cp.start())

    def come(self, i):
        k = self.turn(i)
        for p in range(2):
            self.to_z(p, True, lax.rem(k + 3, 4)).wait_recv()
        self.along(i, lambda cp: cp.start())

    def one(self, i, come=True):
        k = self.turn(i)

        @pl.when(i == 0)
        def _():
            for p in range(2):
                self.own(p).wait()

        if come:
            @pl.when(i > 0)
            def _():
                self.come(i)

        for p in range(2):
            self.hop(p, k).start()
        for p in range(2):
            self.serve(p, 0, k)

    def two(self, i):
        k = self.turn(i)
        for p in range(2):
            self.hop(p, k).wait_recv()
            self.serve(p, 1, k)

    def arrived(self, group, i):
        k = self.turn(i)

        @pl.when(group == 0)
        def _():
            for p in range(2):
                self.served(p, 0, k, 0).wait_recv()
                self.kept(p, 0, k).wait()

        @pl.when(group == 1)
        def _():
            self.kept(0, 1, k).wait()
            self.served(0, 1, k, 0).wait_recv()
            self.served(1, 0, k, 1).wait_recv()
            self.served(1, 0, k, 2).wait_recv()

        @pl.when(group == 2)
        def _():
            self.kept(1, 1, k).wait()
            self.served(1, 1, k, 0).wait_recv()
            self.served(0, 0, k, 1).wait_recv()
            self.served(0, 0, k, 2).wait_recv()

        @pl.when(group == 3)
        def _():
            for p in range(2):
                self.served(p, 1, k, 1).wait_recv()
                self.served(p, 1, k, 2).wait_recv()

    def chip(self, group, i):
        dy, dx = lax.rem(group, 2), group // 2
        zz = lax.rem(self.z + 4 - self.turn(i), 4)
        yy = jnp.where(dy == 1, 1 - self.y, self.y)
        xx = jnp.where(dx == 1, 1 - self.x, self.x)
        return (zz * 2 + yy) * 2 + xx

    def sent(self):
        self.along_own(lambda cp: cp.wait_send())

        def each(i, _):
            k = self.turn(i)
            self.along(i, lambda cp: cp.wait_send())
            for p in range(2):
                self.hop(p, k).wait_send()
                for h in range(2):
                    for t in range(3):
                        self.served(p, h, k, t).wait_send()
            return 0
        lax.fori_loop(0, 4, each, 0)


BEFORE_UNIT = {0: ("o1", "t0", "o2", "t1"), 4: ("o3", "t2"), 8: ("t3",)}


def experts_kernel(
    x_ref, gates_ref, slots_ref, ui_ref, wg_in, wu_in, wd_in,
    xi_out, dx_out, y_out, hg_out, dg_out, du_out, gg_ref,
    gates, xi, ubuf, dx_buf, y_buf, hg_ref, dg_ref, du_ref, wg_ref, wu_ref, wd_ref, wgt, wut, wdt,
    gs, gr, usem, xsem, osem, wsem, *scratch,
):
    z, y, x, c = place()
    rows = x_ref.shape[0]
    greet_all()
    swap = Swap(lambda t: gates_ref.at[t], gates, gs, gr)
    ag = Forth(x_ref, slots_ref, xi, scratch)
    ag.start()

    def chip_of(u):
        return ag.chip(lax.rem(u, 4), u // 4)

    def at_chip(u):
        return pl.ds(pl.multiple_of(chip_of(u) * 2 * SLOTS, 16), 2 * SLOTS)

    def load_up(u):
        return pltpu.make_async_copy(ui_ref.at[at_chip(u), :], ubuf.at[lax.rem(u, 2)], usem.at[lax.rem(u, 2)])

    load_up(0).start()
    loads = [
        pltpu.make_async_copy(source, into, wsem.at[i])
        for i, (source, into) in enumerate(((wg_in, wg_ref), (wu_in, wu_ref), (wd_in, wd_ref)))
    ]
    for cp in loads:
        cp.start()
    ag.one(0)
    swap.start()
    for cp, source, into in zip(loads, (wg_ref, wu_ref, wd_ref), (wgt, wut, wdt), strict=True):
        cp.wait()
        into[...] = source[...].T

    def store(n, buf, out, u):
        return pltpu.make_async_copy(buf.at[lax.rem(u, 2)], out.at[at_chip(u), :], osem.at[n, lax.rem(u, 2)])

    def stores(u):
        return [store(0, dx_buf, dx_out, u), store(1, y_buf, y_out, u)]

    def keep(u):
        return [
            pltpu.make_async_copy(held.at[at_chip(u), :], out.at[at_chip(u), :], xsem.at[i, u])
            for i, (held, out) in enumerate(((xi, xi_out), (hg_ref, hg_out), (dg_ref, dg_out), (du_ref, du_out)))
        ]

    def unit(u):
        slot = lax.rem(u, 2)
        chip = chip_of(u)

        @pl.when(u < 15)
        def _():
            load_up(u + 1).start()

        ag.arrived(lax.rem(u, 4), u // 4)

        @pl.when(u >= 2)
        def _():
            for s in stores(u - 2):
                s.wait()

        load_up(u).wait()
        at = at_chip(u)
        expert = in_plane(y, x, c)
        picks, gate = [], []
        for core in range(2):
            block = chip * 2 + core
            hit = chosen_rows(slots_ref, block, expert)
            picks.append(hit)
            gate_row = jnp.concatenate([gates[block, 0:1, :], gates[block, 1:2, :]], axis=1)
            gate.append(jnp.sum(jnp.where(hit, gate_row, 0.0), axis=1, keepdims=True))
        gate_of_slot = jnp.concatenate(gate, axis=0)
        hidden_up = dims(ubuf[slot], wdt[...], 1, 0)
        rows_in = xi[at, :]
        gate_in = dims(rows_in, wg_ref[...], 1, 0)
        up_in = dims(rows_in, wu_ref[...], 1, 0)
        sig = 1.0 / (1.0 + jnp.exp(-gate_in))
        silu = gate_in * sig
        hidden = (silu * up_in).astype(BF16).astype(F32)
        gated = (hidden * gate_of_slot).astype(BF16)
        hidden_grad = hidden_up * gate_of_slot
        gate_back = (hidden_grad * up_in * sig * (1.0 + gate_in * (1.0 - sig))).astype(BF16)
        up_back = (hidden_grad * silu).astype(BF16)
        hg_ref[at, :] = gated
        dg_ref[at, :] = gate_back
        du_ref[at, :] = up_back
        dx_buf[slot] = (dims(gate_back, wgt[...], 1, 0) + dims(up_back, wut[...], 1, 0)).astype(BF16)
        y_buf[slot] = dims(gated, wd_ref[...], 1, 0).astype(BF16)
        gate_grad = jnp.sum(hidden * hidden_up, axis=1, keepdims=True)
        for core in range(2):
            block = chip * 2 + core
            row = jnp.sum(jnp.where(picks[core], gate_grad[core * SLOTS : (core + 1) * SLOTS], 0.0), axis=0, keepdims=True)
            gg_ref[block, 0:1, :] = row[:, :128]
            gg_ref[block, 1:2, :] = row[:, 128:]
        for s in stores(u):
            s.start()
        for s in keep(u):
            s.start()

    step = {}
    for i in range(4):
        step[f"o{i}"] = functools.partial(ag.one, jnp.int32(i))
        step[f"c{i}"] = functools.partial(ag.come, jnp.int32(i))
        step[f"s{i}"] = functools.partial(ag.one, jnp.int32(i), False)
        step[f"t{i}"] = functools.partial(ag.two, jnp.int32(i))

    def each(u, _):
        for when, names in BEFORE_UNIT.items():
            @pl.when(u == when)
            def _(names=names):
                for name in names:
                    step[name]()

        @pl.when(u == 0)
        def _():
            swap.wait_recv()

        unit(u)
        return 0

    lax.fori_loop(0, 16, each, 0)
    for u in (14, 15):
        for s in stores(u):
            s.wait()

    def last(u, _):
        for s in keep(u):
            s.wait()
        return 0
    lax.fori_loop(0, 16, last, 0)
    ag.sent()
    swap.wait_send()


def run_experts(normed, gates, slots, ui, gate_weight, up_weight, down_weight):
    rows, model = normed.shape
    ff = gate_weight.shape[1]
    n = 32 * SLOTS
    hbm, vmem = pl.BlockSpec(memory_space=pl.ANY), pl.BlockSpec(memory_space=pltpu.VMEM)
    dma = pltpu.SemaphoreType.DMA
    long = jax.ShapeDtypeStruct((n, model), BF16)
    short = jax.ShapeDtypeStruct((n, ff), BF16)
    return pl.pallas_call(
        experts_kernel,
        in_specs=[hbm, vmem, vmem, hbm, hbm, hbm, hbm],
        out_specs=[hbm] * 6 + [vmem],
        out_shape=[long] * 3 + [short] * 3 + [jax.ShapeDtypeStruct((32, 8, 128), F32)],
        scratch_shapes=[
            pltpu.VMEM((32, 8, 128), F32),
            pltpu.VMEM((n, model), BF16),
            pltpu.VMEM((2, 2 * SLOTS, model), BF16),
            pltpu.VMEM((2, 2 * SLOTS, model), BF16),
            pltpu.VMEM((2, 2 * SLOTS, model), BF16),
            pltpu.VMEM((n, ff), BF16), pltpu.VMEM((n, ff), BF16), pltpu.VMEM((n, ff), BF16),
            pltpu.VMEM((model, ff), BF16), pltpu.VMEM((model, ff), BF16), pltpu.VMEM((ff, model), BF16),
            pltpu.VMEM((ff, model), BF16), pltpu.VMEM((ff, model), BF16), pltpu.VMEM((model, ff), BF16),
            dma((32,)), dma((32,)), dma((2,)), dma((4, 16)), dma((2, 2)), dma((3,)),
        ] + Forth.scratch(rows, model // 2),
        compiler_params=pltpu.CompilerParams(collective_id=13, has_side_effects=True, vmem_limit_bytes=56 * 2**20),
        name="experts",
    )(normed, gates, slots, ui, gate_weight, up_weight, down_weight)


class Back:
    scratch = staticmethod(lambda rows, half: [
        pltpu.VMEM((2, 2, 4, SLOTS, half), BF16),
        pltpu.VMEM((2, 3, 2, 4, SLOTS, half), BF16),
        pltpu.VMEM((2, 4, rows, half), BF16),
        pltpu.VMEM((2, 4, rows, half), BF16),
        pltpu.VMEM((2, 4, rows, half), BF16),
        pltpu.VMEM((2, 4, rows, half), BF16),
        pltpu.SemaphoreType.DMA((2, 2, 4)),
        pltpu.SemaphoreType.DMA((2, 3, 2, 4)), pltpu.SemaphoreType.DMA((2, 3, 2, 4)),
        pltpu.SemaphoreType.DMA((2, 4)), pltpu.SemaphoreType.DMA((2, 4)),
        pltpu.SemaphoreType.DMA((2, 4)), pltpu.SemaphoreType.DMA((2, 4)),
    ])
    n_scratch = 13

    def __init__(self, rows_ref, slots_ref, o_ref, scratch):
        self.rows_ref, self.slots_ref, self.o_ref = rows_ref, slots_ref, o_ref
        (self.own, self.rin, self.sout, self.rb, self.zout, self.rz,
         self.own_sem, self.ts, self.tr, self.bs, self.br, self.zs, self.zr) = scratch
        self.z, self.y, self.x, self.c = place()
        half = rows_ref.shape[1] // 2
        self.cols = [pl.ds(0, half), pl.ds(half, half)]

    def block(self, p, h, k, yy, xx, cc):
        zz = lax.rem(self.z + k, 4)
        if p == 0:
            return number(zz, (1 - yy) if h else yy, xx, cc)
        return number(zz, yy, (1 - xx) if h else xx, cc)

    def sources(self, p):
        y, x, c = self.y, self.x, self.c
        ay, ax = (y, 1 - x) if p == 0 else (1 - y, x)
        return [(y, x, 1 - c), (ay, ax, c), (ay, ax, 1 - c)]

    def slot_rows(self, block, p):
        return self.rows_ref.at[pl.ds(pl.multiple_of(block * SLOTS, 16), SLOTS), self.cols[p]]

    def to(self, p, t, h, k):
        place_of = self.sources(p)[t]
        return pltpu.make_async_remote_copy(
            src_ref=self.slot_rows(self.block(p, h, k, *place_of), p), dst_ref=self.rin.at[p, t, h, k],
            send_sem=self.ts.at[p, t, h, k], recv_sem=self.tr.at[p, t, h, k],
            device_id=(number(self.z, *place_of),), device_id_type=MESH)

    def mine(self, p, h, k):
        return pltpu.make_async_copy(
            self.slot_rows(self.block(p, h, k, self.y, self.x, self.c), p), self.own.at[p, h, k], self.own_sem.at[p, h, k])

    def second(self, p, k):
        z, y, x, c = self.z, self.y, self.x, self.c
        target = number(z, 1 - y, x, c) if p == 0 else number(z, y, 1 - x, c)
        return pltpu.make_async_remote_copy(
            src_ref=self.sout.at[p, k], dst_ref=self.rb.at[p, k], send_sem=self.bs.at[p, k], recv_sem=self.br.at[p, k],
            device_id=(target,), device_id_type=MESH)

    def order(self, i):
        return jnp.where(self.z < 2, 3 - i, lax.rem(i + 1, 4))

    def relay(self, k):
        zz = lax.rem(self.z + k, 4)
        adds = ((self.z == 1) & (zz >= 2)) | ((self.z == 2) & (zz <= 1))
        return adds, 2 + jnp.where(zz >= 2, zz - 2, 1 - zz)

    def third(self, p, k):
        z = self.z
        zz = lax.rem(z + k, 4)
        to = jnp.where(z == 0, 1, jnp.where(z == 3, 2, zz))
        passed = ((z == 0) & (zz >= 2)) | ((z == 3) & (zz <= 1))
        last = ((z == 2) & (zz <= 1)) | ((z == 3) & (zz == 2)) | ((z == 1) & (zz == 3))
        slot = jnp.where(passed, 2 + jnp.where(zz >= 2, zz - 2, 1 - zz), jnp.where(last, 1, 0))
        return pltpu.make_async_remote_copy(
            src_ref=self.zout.at[p, k], dst_ref=self.rz.at[p, slot], send_sem=self.zs.at[p, k], recv_sem=self.zr.at[p, slot],
            device_id=(number(to, self.y, self.x, self.c),), device_id_type=MESH)

    def along(self, p, slot):
        return pltpu.make_async_remote_copy(
            src_ref=self.zout.at[p, 0], dst_ref=self.rz.at[p, slot], send_sem=self.zs.at[p, 0], recv_sem=self.zr.at[p, slot],
            device_id=(number(self.z, self.y, self.x, 1 - self.c),), device_id_type=MESH)

    def issue(self, h, i):
        k = self.order(i)
        for p in range(2):
            for t in (1, 2, 0):
                self.to(p, t, h, k).start()
            self.mine(p, h, k).start()

    def start(self):
        self.issue(1, 0)
        self.issue(0, 0)

    def dense(self, p, h, k):
        self.mine(p, h, k).wait()
        for t in range(3):
            self.to(p, t, h, k).wait_recv()
        block = self.block(p, h, k, self.y, self.x, self.c)
        total = None
        for t, who in enumerate([(self.y, self.x, self.c)] + self.sources(p)):
            hit = chosen_rows(self.slots_ref, block, in_plane(*who))
            chosen = jnp.where(hit, 1.0, 0.0).astype(BF16)
            values = self.own[p, h, k] if t == 0 else self.rin[p, t - 1, h, k]
            term = dims(chosen, values, 0, 0)
            total = term if total is None else total + term
        return total

    def step(self, u):
        i = u // 2
        k = self.order(jnp.int32(i))
        early = u % 2 == 0

        @pl.when(early)
        def _():
            for p in range(2):
                self.sout[p, k] = self.dense(p, 1, k).astype(BF16)
                self.second(p, k).start()

            @pl.when(i < 3)
            def _():
                self.issue(1, i + 1)

        @pl.when(u % 2 == 1)
        def _():
            for p in range(2):
                total = self.dense(p, 0, k)
                self.second(p, k).wait_recv()
                total = total + self.rb[p, k].astype(F32)

                adds, slot = self.relay(k)

                @pl.when((k > 0) & adds)
                def _(p=p, total=total):
                    self.along(p, slot).wait_recv()
                    self.zout[p, k] = (total + self.rz[p, slot].astype(F32)).astype(BF16)
                    self.third(p, k).start()

                @pl.when((k > 0) & jnp.logical_not(adds))
                def _(p=p, total=total):
                    self.zout[p, k] = total.astype(BF16)
                    self.third(p, k).start()

                @pl.when(k == 0)
                def _(p=p, total=total):
                    self.o_ref[:, self.cols[p]] = total

            @pl.when(i < 3)
            def _():
                self.issue(0, i + 1)

    def finish(self):
        for p in range(2):
            for slot in range(2):
                self.along(p, slot).wait_recv()
            self.o_ref[:, self.cols[p]] += self.rz[p, 0].astype(F32) + self.rz[p, 1].astype(F32)

        def one(k, _):
            for p in range(2):
                self.second(p, k).wait_send()

                @pl.when(k > 0)
                def _(p=p):
                    self.third(p, k).wait_send()
                for t in range(3):
                    for h in range(2):
                        self.to(p, t, h, k).wait_send()
            return 0
        lax.fori_loop(0, 4, one, 0)


def grads_kernel(
    dx_ref, slots_ref, gg_ref, xi_ref, ui_ref, hg_in, dg_in, du_in,
    o_ref, back_ref, wg_out, wu_out, wd_out, xcol, ucol, gout, uout, dout, hg_ref, dg_ref, du_ref,
    gs, gr, isem, osem, wsem, *scratch,
):
    greet_all()
    swap = Swap(lambda t: gg_ref.at[t], back_ref, gs, gr)
    rs = Back(dx_ref, slots_ref, o_ref, scratch)
    rs.start()
    swap.start()

    def col(i):
        return pl.ds(pl.multiple_of(i * 256, 256), 256)

    def loads(i):
        s = lax.rem(i, 2)
        return [
            pltpu.make_async_copy(xi_ref.at[:, col(i)], xcol.at[s], isem.at[0, s]),
            pltpu.make_async_copy(ui_ref.at[:, col(i)], ucol.at[s], isem.at[1, s]),
        ]

    def stores(i):
        s = lax.rem(i, 2)
        return [
            pltpu.make_async_copy(gout.at[s], wg_out.at[col(i), :], osem.at[0, s]),
            pltpu.make_async_copy(uout.at[s], wu_out.at[col(i), :], osem.at[1, s]),
            pltpu.make_async_copy(dout.at[s], wd_out.at[:, col(i)], osem.at[2, s]),
        ]

    for cp in loads(0):
        cp.start()
    whole = [
        pltpu.make_async_copy(source, into, wsem.at[i])
        for i, (source, into) in enumerate(((hg_in, hg_ref), (dg_in, dg_ref), (du_in, du_ref)))
    ]
    for cp in whole:
        cp.start()
    for cp in whole:
        cp.wait()

    def one(u, _):
        @pl.when(u < 6)
        def _():
            s = lax.rem(u, 2)

            @pl.when(u < 5)
            def _():
                for cp in loads(u + 1):
                    cp.start()

            for cp in loads(u):
                cp.wait()

            @pl.when(u >= 2)
            def _():
                for cp in stores(u - 2):
                    cp.wait()

            rows_in = xcol[s]
            gout[s] = dims(rows_in, dg_ref[...], 0, 0)
            uout[s] = dims(rows_in, du_ref[...], 0, 0)
            dout[s] = dims(hg_ref[...], ucol[s], 0, 0)
            for cp in stores(u):
                cp.start()

        rs.step(u)
        return 0

    lax.fori_loop(0, 8, one, 0)
    for i in (4, 5):
        for cp in stores(i):
            cp.wait()
    swap.wait_recv()
    rs.finish()
    swap.wait_send()


def run_grads(dx, slots, gg, xi, ui, hg, dg, du):
    rows, model = slots.shape[2], dx.shape[1]
    ff = hg.shape[1]
    n = dx.shape[0]
    hbm, vmem = pl.BlockSpec(memory_space=pl.ANY), pl.BlockSpec(memory_space=pltpu.VMEM)
    dma = pltpu.SemaphoreType.DMA
    return pl.pallas_call(
        grads_kernel,
        in_specs=[hbm, vmem, vmem, hbm, hbm, hbm, hbm, hbm],
        out_specs=[vmem, vmem, hbm, hbm, hbm],
        out_shape=[
            jax.ShapeDtypeStruct((rows, model), F32),
            jax.ShapeDtypeStruct((32, 8, 128), F32),
            jax.ShapeDtypeStruct((model, ff), F32),
            jax.ShapeDtypeStruct((model, ff), F32),
            jax.ShapeDtypeStruct((ff, model), F32),
        ],
        scratch_shapes=[
            pltpu.VMEM((2, n, 256), BF16), pltpu.VMEM((2, n, 256), BF16),
            pltpu.VMEM((2, 256, ff), F32), pltpu.VMEM((2, 256, ff), F32), pltpu.VMEM((2, ff, 256), F32),
            pltpu.VMEM((n, ff), BF16), pltpu.VMEM((n, ff), BF16), pltpu.VMEM((n, ff), BF16),
            dma((32,)), dma((32,)), dma((2, 2)), dma((3, 2)), dma((3,)),
        ] + Back.scratch(rows, model // 2),
        compiler_params=pltpu.CompilerParams(collective_id=14, has_side_effects=True, vmem_limit_bytes=56 * 2**20),
        name="grads",
    )(dx, slots, gg, xi, ui, hg, dg, du)


BEFORE_HEADS = (
    "w0", "rank", "w1", "v0", "w2", "v1", "w3", "v2", "v3", "bias", "gains", "norm", "u0", "u1",
    "u2", "u3", "wend", "kv", "ag", "o0", "q", "prev", "o1", "pass", "t0", "kend",
)
AFTER_HEAD = ("o2", "t1", "o3", "t2", "", "t3", "", "")


def front_kernel(
    chunks, rows, lo_ref, cos_ref, sin_ref, x_ref, wq_ref, wk_ref, wv_ref, router_ref, u_ref, turn_ref, turn_t_ref,
    gain_one_ref, gain_two_ref, q_out, o_ref, lse_ref, window_out, slots_ref, ui_ref, w_out, n_ref, gains_ref, scale_ref,
    q_ref, window, w_ref, part_ref, bias, mine, kv, key_t, insem, outsem, gs, gr, lsem, ws, wr, *scratch,
):
    loads, at = [], 0
    for i, ref in enumerate((wq_ref, wk_ref, wv_ref)):
        loads.append(pltpu.make_async_copy(ref, part_ref.at[:, pl.ds(at, ref.shape[1])], insem.at[i]))
        at += ref.shape[1]
    for cp in loads:
        cp.start()
    part_ref[:, at:] = jnp.zeros((part_ref.shape[0], part_ref.shape[1] - at), BF16)
    part_ref[:, at : at + EXPERTS] = router_ref[...]
    greet_all()
    weights = Whole(part_ref, w_ref, scratch[:7])
    swap = Swap(lambda t: mine.at[t // 8], slots_ref, gs, gr)
    keys = Window(rows, kv, window, (lsem, ws, wr))
    ag = Forth(u_ref, slots_ref, ui_ref, scratch[7:])
    cosine, sine = cos_ref[...], sin_ref[...]
    q_width, k_width = QUERY_HEADS * HEAD_DIM, KEY_HEADS * HEAD_DIM

    def rank():
        for e in range(EXPERTS):
            own = turn_t_ref[e : e + 1, :]
            place_of = jnp.sum(jnp.where(turn_ref[:, e : e + 1] < own, 1.0, 0.0), axis=0, keepdims=True)
            slot = jnp.where((own < UNPICKED) & (place_of < CAPACITY), place_of, -1.0)
            mine[e // 8, e % 8 : e % 8 + 1, :] = slot
        mine[:, 8:16, :] = jnp.zeros((4, 8, rows), F32)
        for plane in range(4):
            mine[plane, 8:9, 0 : part_ref.shape[0]] = gain_one_ref[...].astype(F32)
            mine[plane, 9:10, 0 : part_ref.shape[0]] = gain_two_ref[...].astype(F32)
        swap.start()

    def gains():
        swap.wait_recv()
        part = part_ref.shape[0]
        for t in range(32):
            gains_ref[0:8, t * part : (t + 1) * part] = slots_ref[t, 8:16, 0:part]

    def norm():
        def some(i, _):
            at = pl.ds(pl.multiple_of(i * 32, 32), 32)
            values = x_ref[at, :].astype(F32)
            scale = lax.rsqrt(jnp.mean(values * values, axis=1, keepdims=True) + EPSILON)
            scale_ref[at, :] = scale
            n_ref[at, :] = (values * scale * gains_ref[0:1, :]).astype(BF16)
            return 0
        lax.fori_loop(0, rows // 32, some, 0)

    def roped(values, into, first):
        turned = values.T
        for n in range(256 // HEAD_DIM):
            u = turned[n * HEAD_DIM : n * HEAD_DIM + HEAD_DIM // 2]
            w = turned[n * HEAD_DIM + HEAD_DIM // 2 : (n + 1) * HEAD_DIM]
            at = first + n * HEAD_DIM
            into[pl.ds(pl.multiple_of(at, 32), 32), :] = (u * cosine - w * sine).astype(BF16)
            into[pl.ds(pl.multiple_of(at + 32, 32), 32), :] = (w * cosine + u * sine).astype(BF16)

    def keys_and_values():
        for n in range(k_width // 256):
            roped(dims(n_ref[...], w_ref[:, q_width + n * 256 : q_width + (n + 1) * 256], 1, 0), key_t, n * 256)
            kv[0, :, n * 256 : (n + 1) * 256] = key_t[n * 256 : (n + 1) * 256, :].T
        kv[1] = dims(n_ref[...], w_ref[:, q_width + k_width : QKV], 1, 0).astype(BF16)
        keys.start()

    def queries():
        def some(i, _):
            at = pl.ds(pl.multiple_of(i * 256, 256), 256)
            roped(dims(n_ref[...], w_ref[:, at], 1, 0), q_ref, i * 256)
            q_ref[at, :] = (q_ref[at, :].astype(F32) * HEAD_DIM**-0.5).astype(BF16)
            return 0
        lax.fori_loop(0, q_width // 256, some, 0)

    def whole():
        weights.end()
        outs[0].start()

    def queried():
        queries()
        outs[1].start()

    def windowed():
        keys.end()
        outs[2].start()

    outs = [
        pltpu.make_async_copy(held, out, outsem.at[i])
        for i, (held, out) in enumerate(((w_ref, w_out), (q_ref, q_out), (window, window_out)))
    ]
    step = {
        "rank": rank, "gains": gains, "norm": norm, "kv": keys_and_values, "q": queried,
        "ag": ag.start, "bias": lambda: make_bias(bias, lo_ref, chunks, rows), "wend": whole,
        "prev": keys.previous, "pass": keys.pass_on, "kend": windowed,
    }
    for i in range(4):
        step[f"w{i}"] = functools.partial(weights.one, i)
        step[f"v{i}"] = functools.partial(weights.two, i)
        step[f"u{i}"] = functools.partial(weights.three, i)
        step[f"c{i}"] = functools.partial(ag.come, jnp.int32(i))
        step[f"s{i}"] = functools.partial(ag.one, jnp.int32(i), False)
        step[f"o{i}"] = functools.partial(ag.one, jnp.int32(i))
        step[f"t{i}"] = functools.partial(ag.two, jnp.int32(i))

    for cp in loads:
        cp.wait()
    weights.start()
    for name in BEFORE_HEADS:
        step[name]()
    width = 2 * GROUP * HEAD_DIM

    def pair(j, _):
        lanes = pl.ds(pl.multiple_of(j * 2 * HEAD_DIM, 2 * HEAD_DIM), 2 * HEAD_DIM)
        head = pl.ds(pl.multiple_of(j * width, width), width)

        def between(half):
            for u in range(half, 8, 2):
                if AFTER_HEAD[u]:
                    @pl.when(2 * j + half == u)
                    def _(u=u):
                        step[AFTER_HEAD[u]]()

        attend_pair(
            chunks, rows, lax.rem(lax.axis_index("dev"), 2), q_ref.at[head, :], window.at[:, :, lanes],
            o_ref.at[head, :], lse_ref.at[pl.ds(j, 1)], bias, between,
        )
        return 0

    lax.fori_loop(0, KEY_HEADS // 2, pair, 0)

    def last(u, _):
        ag.arrived(lax.rem(u, 4), u // 4)
        return 0
    lax.fori_loop(0, 16, last, 0)
    ag.sent()
    keys.sent()
    swap.wait_send()
    weights.sent()
    for cp in outs:
        cp.wait()


def front(lo, cos_t, sin_t, tokens, projections, router, upstream, turn, gain_one, gain_two):
    rows, model = tokens.shape
    chunks = 9
    keys = KEY_HEADS * HEAD_DIM
    part = jax.ShapeDtypeStruct((router.shape[0], -(-(QKV + EXPERTS) // 128) * 128), BF16)
    hbm, vmem = pl.BlockSpec(memory_space=pl.ANY), pl.BlockSpec(memory_space=pltpu.VMEM)
    dma = pltpu.SemaphoreType.DMA
    return pl.pallas_call(
        functools.partial(front_kernel, chunks, rows),
        in_specs=[vmem] * 4 + [hbm] * 3 + [vmem, hbm] + [vmem] * 4,
        out_specs=[hbm, vmem, vmem, hbm, vmem, hbm, hbm, vmem, vmem, vmem],
        out_shape=[
            jax.ShapeDtypeStruct((QUERY_HEADS * HEAD_DIM, rows), BF16),
            jax.ShapeDtypeStruct((QUERY_HEADS * HEAD_DIM, rows), BF16),
            jax.ShapeDtypeStruct((KEY_HEADS // 2, 8, rows), F32),
            jax.ShapeDtypeStruct((2, 10 * rows, keys), BF16),
            jax.ShapeDtypeStruct((32, 16, rows), F32),
            jax.ShapeDtypeStruct((32 * SLOTS, model), BF16),
            jax.ShapeDtypeStruct((32 * part.shape[0], part.shape[1]), BF16),
            jax.ShapeDtypeStruct((rows, model), BF16),
            jax.ShapeDtypeStruct((8, model), F32),
            jax.ShapeDtypeStruct((rows, 1), F32),
        ],
        scratch_shapes=[
            pltpu.VMEM((QUERY_HEADS * HEAD_DIM, rows), BF16), pltpu.VMEM((2, 10 * rows, keys), BF16),
            pltpu.VMEM((32 * part.shape[0], part.shape[1]), BF16), pltpu.VMEM(part.shape, BF16),
            pltpu.VMEM((chunks * rows, rows), F32), pltpu.VMEM((4, 16, rows), F32), pltpu.VMEM((2, rows, keys), BF16),
            pltpu.VMEM((keys, rows), BF16), dma((3,)), dma((3,)), dma((32,)), dma((32,)),
        ]
        + Window.scratch + Whole.scratch + Forth.scratch(rows, model // 2),
        compiler_params=pltpu.CompilerParams(collective_id=16, has_side_effects=True, vmem_limit_bytes=58 * 2**20),
        name="front",
    )(lo, cos_t, sin_t, tokens, *projections, router, upstream, turn, turn.T, gain_one, gain_two)


IN_PAIRS = {0: (0,), 2: (1,), 4: (2,), 6: (3,)}
AFTER_PAIRS = (4, "sums", 5, 6, "near", "turn", 7)


def attend_back_mesh_kernel(
    chunks, rows, lo_ref, cos_ref, sin_ref, q_ref, kv_in, branch_ref, wo_in, lse_ref, out_ref, y_ref, slots_ref, residual_in,
    grad_out, layer_ref, wo, g_ref, wsem, kv_ref, residual_ref, insem, bias, dkv, sums_ref, gt_ref, o_ref, *scratch,
):
    greet_near()
    rs = Back(y_ref, slots_ref, o_ref, scratch[: Back.n_scratch])
    keys = Unwindow(rows, dkv, sums_ref, scratch[Back.n_scratch :])
    rs.start()
    kv_load = pltpu.make_async_copy(kv_in, kv_ref, insem.at[0])
    residual_load = pltpu.make_async_copy(residual_in, residual_ref, insem.at[1])
    kv_load.start()
    residual_load.start()
    step = wo.shape[1]

    def wo_load(i):
        return pltpu.make_async_copy(wo_in.at[pl.ds(i * step, step), :], wo.at[i % 2], wsem.at[i % 2])

    wo_load(0).start()
    make_bias(bias, lo_ref, chunks, rows)
    for i in range(wo_in.shape[0] // step):
        if (i + 1) * step < wo_in.shape[0]:
            wo_load(i + 1).start()
        wo_load(i).wait()
        g_ref[i * step : (i + 1) * step, :] = dims(wo[i % 2], branch_ref[...], 1, 1).astype(BF16)
    kv_load.wait()
    residual_load.wait()
    width = 2 * GROUP * HEAD_DIM

    def pair(j, _):
        lanes = pl.ds(pl.multiple_of(j * 2 * HEAD_DIM, 2 * HEAD_DIM), 2 * HEAD_DIM)
        head = pl.ds(pl.multiple_of(j * width, width), width)

        def between(half):
            for n, names in IN_PAIRS.items():
                if n % 2 == half:
                    @pl.when(2 * j + half == n)
                    def _(names=names):
                        for name in names:
                            rs.step(name)

        attend_back_pair(
            chunks, rows, lax.rem(lax.axis_index("dev"), 2), cos_ref, sin_ref, q_ref.at[head, :], kv_ref.at[:, :, lanes], g_ref.at[head, :],
            lse_ref.at[pl.ds(j, 1)], out_ref.at[head, :], gt_ref.at[head, :], dkv.at[:, :, lanes], bias, between,
        )
        return 0

    lax.fori_loop(0, KEY_HEADS // 2, pair, 0)

    def turned(first, last):
        for n in range(first, last, 256):
            grad_out[:, n : n + 256] = gt_ref[n : n + 256, :].T

    keys.start()
    for name in AFTER_PAIRS:
        if isinstance(name, int):
            rs.step(name)
        elif name == "sums":
            keys.sums()
        elif name == "turn":
            turned(0, QUERY_HEADS * HEAD_DIM)
        else:
            keys.near()
    keys.end()
    base = QUERY_HEADS * HEAD_DIM
    key_t = sums_ref[0].T
    cosine, sine = cos_ref[...], sin_ref[...]
    for n in range(KEY_HEADS):
        first, middle = n * HEAD_DIM, n * HEAD_DIM + HEAD_DIM // 2
        u, w = key_t[first:middle], key_t[middle : first + HEAD_DIM]
        gt_ref[base + first : base + middle, :] = (u * cosine + w * sine).astype(BF16)
        gt_ref[base + middle : base + first + HEAD_DIM, :] = (w * cosine - u * sine).astype(BF16)
    turned(base, base + KEY_HEADS * HEAD_DIM)
    grad_out[:, base + KEY_HEADS * HEAD_DIM :] = sums_ref[1].astype(BF16)
    rs.finish()
    layer_ref[...] = (residual_ref[...] + o_ref[...]).astype(BF16)


def attend_back_mesh(query_t, window, lo, branch_grad, output_matrix, lse, attended_t, cos_t, sin_t, y, slots, residual):
    rows, span, keys = query_t.shape[1], window.shape[1], window.shape[2]
    chunks = span // rows - 1
    model = y.shape[1]
    hbm, vmem = pl.BlockSpec(memory_space=pl.ANY), pl.BlockSpec(memory_space=pltpu.VMEM)
    return pl.pallas_call(
        functools.partial(attend_back_mesh_kernel, chunks, rows),
        in_specs=[vmem] * 4 + [hbm, vmem, hbm] + [vmem] * 2 + [hbm, vmem, hbm],
        out_specs=[vmem] * 2,
        out_shape=[
            jax.ShapeDtypeStruct((rows, QKV), BF16),
            jax.ShapeDtypeStruct((rows, model), BF16),
        ],
        scratch_shapes=[
            pltpu.VMEM((2, 384, model), BF16), pltpu.VMEM(query_t.shape, BF16), pltpu.SemaphoreType.DMA((2,)),
            pltpu.VMEM(window.shape, BF16), pltpu.VMEM((rows, model), F32), pltpu.SemaphoreType.DMA((2,)),
            pltpu.VMEM((chunks * rows, rows), F32), pltpu.VMEM(window.shape, BF16), pltpu.VMEM((2, rows, keys), F32),
            pltpu.VMEM((QKV, rows), BF16), pltpu.VMEM((rows, model), F32),
        ]
        + Back.scratch(rows, model // 2) + Unwindow.scratch(rows, keys),
        compiler_params=pltpu.CompilerParams(collective_id=15, has_side_effects=True, vmem_limit_bytes=60 * 2**20),
        name="attend_back",
    )(lo, cos_t, sin_t, query_t, window, branch_grad, output_matrix, lse, attended_t, y, slots, residual)


def finish_kernel(
    rows, n_ref, g_ref, w_in, more_ref, gain_ref, scale_ref, x_in, rg_in,
    oq_ref, ok_ref, ov_ref, om_ref, tg_ref, fg_ref, w_ref, x_ref, rg_ref, insem,
    dense, acc, ra, rb, rz, out, ng, mine, theirs, ssem, rsem, sa, ra_sem, sb, rb_sem, sz, rz_sem, gs, gr,
):
    z, y, x, c = place()
    greet_all()
    sibling = number(z, y, x, 1 - c)
    cols = acc.shape[2]
    main = g_ref.shape[1]
    half = cols // 2
    pieces = [pl.ds(0, half), pl.ds(half, half)]
    around = (number(z, y, 1 - x, c), number(z, 1 - y, x, c))
    swap = Swap(lambda t: mine.at[t], theirs, gs, gr)

    def lane(dy, dx, k):
        yy = 1 - y if dy else y
        xx = 1 - x if dx else x
        return (lax.rem(z + k, 4) * 2 + yy) * 2 + xx

    def to_sibling(dy, dx, k):
        chip = lane(dy, dx, k)
        n = (k, dy, dx)
        sides = (
            (dense.at[chip, pl.ds(pl.multiple_of((1 - c) * rows, 16), rows), :], pl.ds(0, main)),
            (more_ref.at[pl.ds(pl.multiple_of((2 * chip + 1 - c) * rows, 16), rows), :], pl.ds(main, cols - main)),
        )
        return [
            pltpu.make_async_remote_copy(
                src_ref=source, dst_ref=acc.at[chip, :, at], send_sem=ssem.at[(*n, i)], recv_sem=rsem.at[(*n, i)],
                device_id=(sibling,), device_id_type=MESH)
            for i, (source, at) in enumerate(sides)
        ]

    def first(p, d2, k, dy, dx):
        return pltpu.make_async_remote_copy(
            src_ref=acc.at[lane(dy, dx, k), :, pieces[p]], dst_ref=ra.at[p, d2, k],
            send_sem=sa.at[p, d2, k], recv_sem=ra_sem.at[p, d2, k], device_id=(around[p],), device_id_type=MESH)

    def second(p, k):
        dy, dx = (1, 0) if p == 0 else (0, 1)
        return pltpu.make_async_remote_copy(
            src_ref=acc.at[lane(dy, dx, k), :, pieces[p]], dst_ref=rb.at[p, k],
            send_sem=sb.at[p, k], recv_sem=rb_sem.at[p, k], device_id=(around[1 - p],), device_id_type=MESH)

    def order(i):
        return jnp.where(z < 2, 3 - i, lax.rem(i + 1, 4))

    def third(p, k):
        zz = lax.rem(z + k, 4)
        to = jnp.where(z == 0, 1, jnp.where(z == 3, 2, zz))
        passed = ((z == 0) & (zz >= 2)) | ((z == 3) & (zz <= 1))
        last = ((z == 2) & (zz <= 1)) | ((z == 3) & (zz == 2)) | ((z == 1) & (zz == 3))
        slot = jnp.where(passed, 2 + jnp.where(zz >= 2, zz - 2, 1 - zz), jnp.where(last, 1, 0))
        return pltpu.make_async_remote_copy(
            src_ref=acc.at[lane(0, 0, k), :, pieces[p]], dst_ref=rz.at[p, slot],
            send_sem=sz.at[p, k], recv_sem=rz_sem.at[p, slot], device_id=(number(to, y, x, c),), device_id_type=MESH)

    def along(p, slot):
        return pltpu.make_async_remote_copy(
            src_ref=acc.at[lane(0, 0, 0), :, pieces[p]], dst_ref=rz.at[p, slot],
            send_sem=sz.at[p, 0], recv_sem=rz_sem.at[p, slot], device_id=(sibling,), device_id_type=MESH)

    quarter = ((1, 1), (1, 0), (0, 1), (0, 0))

    def product(i, _):
        k = order(i)
        zz = lax.rem(z + k, 4)
        at = pl.ds(pl.multiple_of(zz * 8 * rows, 128), 8 * rows)
        part = dims(n_ref[:, at], g_ref[...], 0, 0).astype(BF16)
        for chip in range(4):
            dense[zz * 4 + chip] = part[chip * 2 * rows : (chip + 1) * 2 * rows]
        for dy, dx in quarter:
            for cp in to_sibling(dy, dx, k):
                cp.start()
        return 0

    def own_sums(k):
        for dy, dx in quarter:
            chip = lane(dy, dx, k)
            for cp in to_sibling(dy, dx, k):
                cp.wait_recv()
            acc[chip, :, :main] = (
                acc[chip, :, :main].astype(F32) + dense[chip, pl.ds(pl.multiple_of(c * rows, 16), rows), :].astype(F32)
            ).astype(BF16)
            acc[chip, :, main:] = (
                acc[chip, :, main:].astype(F32)
                + more_ref[pl.ds(pl.multiple_of((2 * chip + c) * rows, 16), rows), :].astype(F32)
            ).astype(BF16)
            if dx:
                first(0, dy, k, dy, dx).start()
            if dy:
                first(1, dx, k, dy, dx).start()

    def middle(k):
        for p in range(2):
            dy, dx = (1, 0) if p == 0 else (0, 1)
            first(p, 1, k, 1, 1).wait_recv()
            block = acc.at[lane(dy, dx, k), :, pieces[p]]
            block[...] = (block[...].astype(F32) + ra[p, 1, k].astype(F32)).astype(BF16)
            second(p, k).start()

    def late(k):
        for p in range(2):
            first(p, 0, k, 1 - p, p).wait_recv()
            second(p, k).wait_recv()
            block = acc.at[lane(0, 0, k), :, pieces[p]]
            total = block[...].astype(F32) + ra[p, 0, k].astype(F32) + rb[p, k].astype(F32)

            zz = lax.rem(z + k, 4)
            adds = ((z == 1) & (zz >= 2)) | ((z == 2) & (zz <= 1))
            slot = 2 + jnp.where(zz >= 2, zz - 2, 1 - zz)

            @pl.when((k > 0) & adds)
            def _(p=p, block=block, total=total):
                along(p, slot).wait_recv()
                block[...] = (total + rz[p, slot].astype(F32)).astype(BF16)
                third(p, k).start()

            @pl.when((k > 0) & jnp.logical_not(adds))
            def _(p=p, block=block, total=total):
                block[...] = total.astype(BF16)
                third(p, k).start()

            @pl.when(k == 0)
            def _(p=p, total=total):
                out[:, pieces[p]] = total

    def rest_of_tokens():
        ng[...] = dims(g_ref[...], w_ref[:, :main], 1, 1)

        def tail(i, total):
            at = pl.ds(pl.multiple_of(i * 32, 32), 32)
            grad, scale, values = ng[at, :], scale_ref[at, :], x_ref[at, :].astype(F32)
            weighted = grad * gain_ref[...]
            scaled = values * scale
            mean = jnp.mean(weighted * values, axis=1, keepdims=True)
            tg_ref[at, :] = rg_ref[at, :] + scale * weighted - scaled * (scale * scale * mean)
            return total + jnp.sum(grad * scaled, axis=0, keepdims=True)
        total = lax.fori_loop(0, x_ref.shape[0] // 32, tail, jnp.zeros(gain_ref.shape, F32))
        mine[...] = jnp.zeros_like(mine)
        for t in range(32):
            mine[t, 0:1, 0:rows] = total[:, t * rows : (t + 1) * rows]
        swap.start()

    loads = [
        pltpu.make_async_copy(source, into, insem.at[i])
        for i, (source, into) in enumerate(((w_in, w_ref), (x_in, x_ref), (rg_in, rg_ref)))
    ]
    for cp in loads:
        cp.start()
    lax.fori_loop(0, 4, product, 0)
    for cp in loads:
        cp.wait()

    def steps(i, _):
        @pl.when(i < 4)
        def _():
            own_sums(order(i))

        @pl.when(i == 3)
        def _():
            rest_of_tokens()

        @pl.when(i < 4)
        def _():
            middle(order(i))

        @pl.when(i >= 1)
        def _():
            late(order(i - 1))
        return 0
    lax.fori_loop(0, 5, steps, 0)
    swap.wait_recv()
    fg_ref[...] = jnp.sum(theirs[...], axis=0)
    for p in range(2):
        for slot in range(2):
            along(p, slot).wait_recv()
        out[:, pieces[p]] += rz[p, 0].astype(F32) + rz[p, 1].astype(F32)
    at = 0
    for ref in (oq_ref, ok_ref, ov_ref, om_ref):
        ref[...] = out[:, at : at + ref.shape[1]]
        at += ref.shape[1]

    def sent(k, _):
        for dy, dx in quarter:
            for cp in to_sibling(dy, dx, k):
                cp.wait_send()
        for p in range(2):
            first(p, 0, k, 1 - p, p).wait_send()
            first(p, 1, k, 1, 1).wait_send()
            second(p, k).wait_send()

            @pl.when(k > 0)
            def _(p=p):
                third(p, k).wait_send()
        return 0
    lax.fori_loop(0, 4, sent, 0)
    swap.wait_send()


def finish(normed, grad, matrices, more, gain, scale, tokens, residual_grad):
    count, model = normed.shape
    rows = model // 32
    main, cols = grad.shape[1], grad.shape[1] + more.shape[1]
    half = cols // 2
    dma = pltpu.SemaphoreType.DMA
    hbm, vmem = pl.BlockSpec(memory_space=pl.ANY), pl.BlockSpec(memory_space=pltpu.VMEM)
    widths = [QUERY_HEADS * HEAD_DIM, KEY_HEADS * HEAD_DIM, KEY_HEADS * HEAD_DIM, more.shape[1]]
    return pl.pallas_call(
        functools.partial(finish_kernel, rows),
        in_specs=[vmem, vmem, hbm, vmem, vmem, vmem, hbm, hbm],
        out_specs=[vmem] * 6,
        out_shape=[jax.ShapeDtypeStruct((rows, w), F32) for w in widths] + [
            jax.ShapeDtypeStruct((count, model), F32),
            jax.ShapeDtypeStruct((8, 128), F32),
        ],
        scratch_shapes=[
            pltpu.VMEM(matrices.shape, BF16), pltpu.VMEM((count, model), BF16), pltpu.VMEM((count, model), F32), dma((3,)),
            pltpu.VMEM((16, 2 * rows, main), BF16),
            pltpu.VMEM((16, rows, cols), BF16),
            pltpu.VMEM((2, 2, 4, rows, half), BF16),
            pltpu.VMEM((2, 4, rows, half), BF16),
            pltpu.VMEM((2, 4, rows, half), BF16),
            pltpu.VMEM((rows, cols), F32),
            pltpu.VMEM((count, model), F32),
            pltpu.VMEM((32, 8, 128), F32),
            pltpu.VMEM((32, 8, 128), F32),
            dma((4, 2, 2, 2)), dma((4, 2, 2, 2)), dma((2, 2, 4)), dma((2, 2, 4)), dma((2, 4)), dma((2, 4)), dma((2, 4)), dma((2, 4)),
            dma((32,)), dma((32,)),
        ],
        compiler_params=pltpu.CompilerParams(collective_id=17, has_side_effects=True, vmem_limit_bytes=42 * 2**20),
        name="finish",
    )(normed, grad, matrices, more, gain, scale, tokens, residual_grad)


def chunks_of(shape):
    rows = shape[0]
    count = 1
    while rows % (32 * count) == 0 and rows // count * shape[1] > 2**18:
        count *= 2
    return [(i * (rows // count), rows // count) for i in range(count)]


def hand_over_kernel(count, *refs):
    sources, outs, held = refs[:count], refs[count : 2 * count], refs[2 * count : 3 * count]
    sems = refs[3 * count]
    into, out = [], []
    for source, there, here in zip(sources, outs, held, strict=True):
        for first, rows in chunks_of(source.shape):
            at, n = pl.ds(first, rows), len(into)
            into.append(pltpu.make_async_copy(source.at[at, :], here.at[at, :], sems.at[0, n]))
            out.append(pltpu.make_async_copy(here.at[at, :], there.at[at, :], sems.at[1, n]))
    for cp in into:
        cp.start()
    for a, b in zip(into, out, strict=True):
        a.wait()
        b.start()
    for cp in out:
        cp.wait()


def hand_over(*arrays):
    hbm = pl.BlockSpec(memory_space=pl.ANY)
    total = sum(len(chunks_of(a.shape)) for a in arrays)
    return pl.pallas_call(
        functools.partial(hand_over_kernel, len(arrays)),
        in_specs=[hbm] * len(arrays),
        out_specs=[hbm] * len(arrays),
        out_shape=[jax.ShapeDtypeStruct(a.shape, a.dtype) for a in arrays],
        scratch_shapes=[pltpu.VMEM(a.shape, a.dtype) for a in arrays] + [pltpu.SemaphoreType.DMA((2, total))],
        compiler_params=pltpu.CompilerParams(vmem_limit_bytes=60 * 2**20),
        name="hand_over",
    )(*arrays)


def rms_scale(values):
    return lax.rsqrt(jnp.mean(values * values, axis=-1, keepdims=True) + EPSILON)


def rotate_t(values, cosine, sine):
    half = cosine.shape[0]
    shaped = values.reshape(-1, 2, half, values.shape[1])
    u, w = shaped[:, 0], shaped[:, 1]
    turned = jnp.stack([u * cosine - w * sine, w * cosine + u * sine], axis=1)
    return turned.reshape(values.shape)


def on_device(
    tokens,
    positions,
    expert_picks,
    priority,
    first_gain,
    query_weight,
    key_projection_matrix,
    value_projection_matrix,
    output_weight,
    second_gain,
    router_weight,
    gate_weight,
    up_weight,
    down_weight,
    cotangent,
):
    devices = lax.axis_size("dev")
    rows, model = tokens.shape
    split = devices // EXPERTS
    capacity = split * ((9 * rows * TOP + 8 * EXPERTS * split - 1) // (8 * EXPERTS * split))
    weight_rows = query_weight.shape[0]

    output_matrix = lax.all_gather(output_weight, "dev", axis=0, tiled=True)

    extra = [query_weight, key_projection_matrix, value_projection_matrix, router_weight]
    pad = (-(QKV + EXPERTS)) % 128
    packed = jnp.concatenate(extra + [jnp.zeros((weight_rows, pad), BF16)], axis=1)
    q_width, k_width = QUERY_HEADS * HEAD_DIM, KEY_HEADS * HEAD_DIM
    inputs = tokens.astype(F32)
    half_dim = HEAD_DIM // 2
    frequency = jnp.power(10000.0, -(jnp.arange(half_dim, dtype=F32) * 2.0) / HEAD_DIM)
    angle = positions.astype(F32)[None, :] * frequency[:, None]
    cos_t, sin_t = jnp.cos(angle), jnp.sin(angle)
    lo = (jnp.arange(rows, dtype=jnp.int32) - positions)[None, :]
    one_hot = expert_picks[:, :, None] == jnp.arange(EXPERTS, dtype=jnp.int32)
    picked_any = jnp.any(one_hot, axis=1)
    turn = jnp.sum(jnp.where(one_hot, priority[:, :, None], 0), axis=1).astype(F32)
    turn = jnp.where(picked_any, turn, UNPICKED)

    if meshed():
        query_t, attended_t, lse, window, plane_slots, expert_up, matrices, normed_one, gains, scale_one = front(
            lo, cos_t, sin_t, tokens, extra[:3], router_weight, cotangent, turn, first_gain[None, :], second_gain[None, :]
        )
        gain_first, gain_second = gains[0], gains[1]
    else:
        matrices, gain_first, gain_second = (
            lax.all_gather(v, "dev", axis=0, tiled=True) for v in (packed, first_gain, second_gain)
        )
        gain_first, gain_second = gain_first.astype(F32), gain_second.astype(F32)
        rank = jnp.sum((turn.T[:, None, :] < turn.T[:, :, None]).astype(jnp.int32), axis=2)
        slot_rows = jnp.where(picked_any.T & (rank < capacity), rank, -1).astype(F32)
        scale_one = rms_scale(inputs)
        normed_one = (inputs * scale_one * gain_first).astype(BF16)
        qkv_t = dims(matrices[:, :QKV], normed_one, 0, 1)
        query_t = rotate_t(qkv_t[:q_width], cos_t, sin_t).astype(BF16) * BF16(HEAD_DIM**-0.5)
        key = rotate_t(qkv_t[q_width : q_width + k_width], cos_t, sin_t).astype(BF16).T
        value = qkv_t[q_width + k_width :].astype(BF16).T
        window, offset = window_of(jnp.stack([key, value])), jnp.int32(0)
        attended_t, lse = attend(query_t, window, offset, lo)
    qkv_matrix = matrices[:, :QKV]
    router_matrix = matrices[:, QKV : QKV + EXPERTS]
    residual = inputs + dims(attended_t, output_matrix, 0, 0)
    scale_two = rms_scale(residual)
    normed_two = (residual * scale_two * gain_second).astype(BF16)

    logits = dims(normed_two, router_matrix, 1, 0)
    logits = jnp.where(picked_any, logits, MASKED)
    picked_exp = jnp.exp(logits - jnp.max(logits, axis=1, keepdims=True))
    gates = picked_exp / jnp.sum(picked_exp, axis=1, keepdims=True)

    if meshed():
        gate_rows = jnp.pad(gates.T.reshape(EXPERTS, rows // 128, 128), ((0, 0), (0, 8 - rows // 128), (0, 0)))
        expert_in, grad_rows, out_rows, gated_hidden, gate_in_grad, up_in_grad, gate_grad_rows = run_experts(
            normed_two, gate_rows, plane_slots, expert_up, gate_weight, up_weight, down_weight
        )
        returned_grad, gate_grad, gate_gradient, up_gradient, down_gradient = run_grads(
            grad_rows, plane_slots, gate_grad_rows, expert_in, expert_up, gated_hidden, gate_in_grad, up_in_grad
        )
        gate_grad = gate_grad[:, : rows // 128].reshape(EXPERTS, rows).T
    else:
        gate_rows, slot = (
            lax.all_to_all(jnp.repeat(v, split, axis=0), "dev", split_axis=0, concat_axis=0, tiled=True)
            for v in (gates.T, slot_rows)
        )
        pair_slot = jnp.where(
            slot.reshape(devices // 2, 2, rows) >= 0,
            slot.reshape(devices // 2, 2, rows) + jnp.array([[0], [capacity]], F32),
            -1.0,
        ).astype(jnp.int32).reshape(devices // 2, 1, 2 * rows)
        all_upstream = lax.all_gather(cotangent, "dev", axis=0, tiled=True)
        all_normed = lax.all_gather(normed_two, "dev", axis=0, tiled=True)
        expert_in, expert_up = dispatch(pair_slot, all_normed, all_upstream, 2 * capacity)
        slot_hit = slot[:, None, :] == jnp.arange(capacity, dtype=F32)[None, :, None]
        gate_of_slot = jnp.sum(jnp.where(slot_hit, gate_rows[:, None, :], 0.0), axis=2).reshape(-1, 1)
        gate_in = dims(expert_in, gate_weight, 1, 0)
        up_in = dims(expert_in, up_weight, 1, 0)
        sigmoid_gate = 1.0 / (1.0 + jnp.exp(-gate_in))
        silu_gate = gate_in * sigmoid_gate
        hidden = (silu_gate * up_in).astype(BF16)
        gated_hidden = (hidden.astype(F32) * gate_of_slot).astype(BF16)
        hidden_up = dims(expert_up, down_weight, 1, 1)
        hidden_grad = hidden_up * gate_of_slot
        gate_grad_slot = jnp.sum(hidden.astype(F32) * hidden_up, axis=1).reshape(devices, capacity)
        gate_in_grad = (hidden_grad * up_in * sigmoid_gate * (1.0 + gate_in * (1.0 - sigmoid_gate))).astype(BF16)
        up_in_grad = (hidden_grad * silu_gate).astype(BF16)
        partial_in = (dims(gate_in_grad, gate_weight, 1, 1) + dims(up_in_grad, up_weight, 1, 1)).astype(BF16)
        gate_grad_rows = jnp.sum(jnp.where(slot_hit, gate_grad_slot[:, :, None], 0.0), axis=1)
        returned_grad = lax.psum_scatter(
            combine(pair_slot, partial_in, 2 * capacity), "dev", scatter_dimension=0, tiled=True
        ).astype(F32)
        gate_grad = lax.all_to_all(gate_grad_rows, "dev", split_axis=0, concat_axis=0, tiled=True)
        gate_grad = jnp.sum(gate_grad.reshape(EXPERTS, split, rows), axis=1).T
        partial_out = dims(gated_hidden, down_weight, 1, 0).astype(BF16)
        dense_out = combine(pair_slot, partial_out, 2 * capacity)
        mixture = lax.psum_scatter(dense_out, "dev", scatter_dimension=0, tiled=True).astype(F32)
        down_gradient = dims(gated_hidden, expert_up, 0, 0)
        gate_gradient = dims(expert_in, gate_in_grad, 0, 0)
        up_gradient = dims(expert_in, up_in_grad, 0, 0)

    upstream = cotangent.astype(F32)
    logit_grad = (gates * (gate_grad - jnp.sum(gates * gate_grad, axis=1, keepdims=True))).astype(BF16)
    router_gradient = dims(normed_two, logit_grad, 0, 0)
    normed_two_grad = returned_grad + dims(logit_grad, router_matrix, 1, 1)
    weighted_two = normed_two_grad * gain_second
    second_gain_grad = jnp.sum(normed_two_grad * residual * scale_two, axis=0)
    residual_grad = (
        upstream
        + scale_two * weighted_two
        - residual * scale_two**3 * jnp.mean(weighted_two * residual, axis=-1, keepdims=True)
    )
    branch_grad = residual_grad.astype(BF16)
    output_gradient = dims(attended_t, branch_grad, 1, 0).astype(BF16)
    output_gradient = lax.psum_scatter(output_gradient, "dev", scatter_dimension=0, tiled=True).astype(F32)

    if meshed():
        qkv_grad, layer_output = attend_back_mesh(
            query_t, window, lo, branch_grad, output_matrix, lse, attended_t, cos_t, sin_t, out_rows, plane_slots, residual
        )
    else:
        grad_t = dims(output_matrix, branch_grad, 1, 1).astype(BF16)
        query_grad_t, window_grad = attend_back(query_t, window, offset, lo, grad_t, lse, attended_t, cos_t, sin_t)
        key_grad, value_grad = unwindow(window_grad)
        key_grad_t = rotate_t(key_grad.T, cos_t, -sin_t).astype(BF16)
        qkv_grad_t = jnp.concatenate([query_grad_t, key_grad_t, value_grad.T.astype(BF16)], axis=0)
        layer_output = (residual + mixture).astype(BF16)
    more = jnp.concatenate(
        [router_gradient, second_gain_grad[:, None], jnp.zeros((model, (-(EXPERTS + 1)) % 256), F32)], axis=1
    ).astype(BF16)
    if meshed():
        query_sums, key_sums, value_sums, more_sums, tokens_gradient, first_sums = finish(
            normed_one, qkv_grad, matrices, more, gain_first[None, :], scale_one, tokens, residual_grad
        )
        first_sums = first_sums[0, :weight_rows]
        (
            gate_gradient, up_gradient, down_gradient, layer_output, tokens_gradient, query_sums, key_sums, value_sums
        ) = hand_over(
            gate_gradient, up_gradient, down_gradient, layer_output, tokens_gradient, query_sums, key_sums, value_sums
        )
    else:
        qkv_gradient = dims(normed_one, qkv_grad_t, 0, 1).astype(BF16)
        normed_one_grad = dims(qkv_grad_t, qkv_matrix, 0, 1)
        weighted_one = normed_one_grad * gain_first
        tokens_gradient = (
            residual_grad
            + scale_one * weighted_one
            - inputs * scale_one**3 * jnp.mean(weighted_one * inputs, axis=-1, keepdims=True)
        )
        sums = lax.psum_scatter(
            jnp.concatenate([qkv_gradient, more], axis=1), "dev", scatter_dimension=0, tiled=True
        ).astype(F32)
        query_sums, key_sums, value_sums, more_sums = jnp.split(sums, [q_width, q_width + k_width, QKV], axis=1)
        first_sums = lax.psum_scatter(
            jnp.sum(normed_one_grad * inputs * scale_one, axis=0), "dev", scatter_dimension=0, tiled=True
        )
    return (
        layer_output,
        tokens_gradient,
        first_sums,
        query_sums,
        key_sums,
        value_sums,
        output_gradient,
        more_sums[:, EXPERTS],
        more_sums[:, :EXPERTS],
        gate_gradient,
        up_gradient,
        down_gradient,
    )


def solution(mesh):
    rows, whole = P("dev", None), P("dev")
    columns = P(None, "dev")
    return jax.shard_map(
        on_device,
        mesh=mesh,
        in_specs=(rows, whole, rows, rows, whole, rows, rows, rows, rows, whole, rows, columns, columns, rows, rows),
        out_specs=(rows, rows, whole, rows, rows, rows, rows, whole, rows, columns, columns, rows),
        check_vma=False,
    )
```
